32 devices in a mesh: dp: 4 (over y, x), edge: 8 (over z, core).
Axes of the slice: x: 2, y: 2, z: 4, core: 2. Of those that a mesh axis runs over, the one named last changes fastest.
Arguments:
- nodes: bfloat16 [4096, 512], P(('dp', 'edge')), parts along dimension 0, may hold values from -6 to 6
- edges: bfloat16 [4096, 9984], P(('dp', 'edge')), parts along dimension 0, may hold values from -6 to 6
- nbr_owner: int32 [4096, 52, 1], P(('dp', 'edge')), parts along dimension 0, may hold values from 0 to 7; in each aligned block of 6656 rows (0 to 6655, 6656 to 13311, ..., all dimensions but the last counted through in order) at most 1664 rows name the same one
- nbr_slot: int32 [4096, 52], P(('dp', 'edge')), parts along dimension 0, may hold values from 0 to 127
- edge_mask: int32 [4096, 52], P(('dp', 'edge')), parts along dimension 0, may hold values 0 or 1
- w_msg1: bfloat16 [1216, 512], replicated, may hold values from -0.15625 to 0.15625
- w_msg2: bfloat16 [512, 512], replicated, may hold values from -0.25 to 0.25
- w_msg3: bfloat16 [512, 512], replicated, may hold values from -1.25 to 1.25
- gain_one: float32 [512], replicated, may hold values from 0.1 to 1.9
- offset_one: float32 [512], replicated, may hold values from -3 to 3
- w_ffn1: bfloat16 [512, 2048], replicated, may hold values from -0.25 to 0.25
- w_ffn2: bfloat16 [2048, 512], replicated, may hold values from -0.125 to 0.125
- gain_two: float32 [512], replicated, may hold values from 0.1 to 1.9
- offset_two: float32 [512], replicated, may hold values from -3 to 3
- w_edge1: bfloat16 [1216, 192], replicated, may hold values from -0.15625 to 0.15625
- w_edge2: bfloat16 [192, 192], replicated, may hold values from -0.4375 to 0.4375
- w_edge3: bfloat16 [192, 192], replicated, may hold values from -0.4375 to 0.4375
- gain_three: float32 [192], replicated, may hold values from 0.1 to 1.9
- offset_three: float32 [192], replicated, may hold values from -3 to 3
- node_cotangent: bfloat16 [4096, 512], P(('dp', 'edge')), parts along dimension 0, may hold values from -6 to 6
- edge_cotangent: bfloat16 [4096, 9984], P(('dp', 'edge')), parts along dimension 0, may hold values from -6 to 6
Outputs:
- node_out: bfloat16 [4096, 512], P(('dp', 'edge')), parts along dimension 0
- edge_out: bfloat16 [4096, 9984], P(('dp', 'edge')), parts along dimension 0
- grad_nodes: float32 [4096, 512], P(('dp', 'edge')), parts along dimension 0
- grad_edges: float32 [4096, 9984], P(('dp', 'edge')), parts along dimension 0
- grad_w_msg1: float32 [4864, 512], P('dp'), parts along dimension 0
- grad_w_msg2: float32 [2048, 512], P('dp'), parts along dimension 0
- grad_w_msg3: float32 [2048, 512], P('dp'), parts along dimension 0
- grad_gain_one: float32 [2048], P('dp'), parts along dimension 0
- grad_offset_one: float32 [2048], P('dp'), parts along dimension 0
- grad_w_ffn1: float32 [2048, 2048], P('dp'), parts along dimension 0
- grad_w_ffn2: float32 [8192, 512], P('dp'), parts along dimension 0
- grad_gain_two: float32 [2048], P('dp'), parts along dimension 0
- grad_offset_two: float32 [2048], P('dp'), parts along dimension 0
- grad_w_edge1: float32 [4864, 192], P('dp'), parts along dimension 0
- grad_w_edge2: float32 [768, 192], P('dp'), parts along dimension 0
- grad_w_edge3: float32 [768, 192], P('dp'), parts along dimension 0
- grad_gain_three: float32 [768], P('dp'), parts along dimension 0
- grad_offset_three: float32 [768], P('dp'), parts along dimension 0
The draws below stay inside these ranges and needn't reach their ends.
There are 4 independent parts, one for each index of `dp`. The reference program is written for one: setup_inputs(seed, part) draws one part's arguments, and reference() takes and returns one part's arrays. A program takes and returns all parts, laid end to end along the dimension named above; an argument that names none is the same for every part. Nothing has to cross between parts.
Inputs may be any that keep to these rules, and one draw needn't show every extreme that they name: `nbr_owner`: among the 6656 edges of one device (aligned blocks of rows), no value is named by more than 1664 edges, a bound that some block reaches.
All inputs are finite; a program needn't handle non-finite values. No bound on the sum of `edge_mask` on one device may be relied on, other than what follows from the above.
Results may differ from the reference program's by a relative error of at most 0.017.
Values may be sent and summed in bfloat16 or wider, within the bound.
A program may use at most 512 MiB of HBM per device.

```python
import math
import jax
import jax.numpy as jnp
import numpy as np
from jax import lax

D = 512
C = 192
FF = 2048
K = 52
RES_DEV = 128
NODES = 1024
CAP = 1664
N_EDGE = 8


def touch_ends(entries, rng, smallest, largest):
    place = [jax.random.randint(jax.random.fold_in(rng, axis), (), 0, length) for axis, length in enumerate(entries.shape)]
    main_axis = entries.shape.index(max(entries.shape))
    beside = place[:main_axis] + [(place[main_axis] + 1) % entries.shape[main_axis]] + place[main_axis + 1:]
    return entries.at[tuple(place)].set(smallest).at[tuple(beside)].set(largest)


def block_levels(key, extent, shards, smallest, high):
    factor_of, own = 1.0, jax.random.fold_in(key, 6)
    for axis_at, blocks in shards:
        heights = jnp.exp(jax.random.uniform(jax.random.fold_in(own, axis_at), (blocks,), jnp.float32, smallest / len(shards), high / len(shards)))
        factor_of = factor_of * jnp.repeat(heights, extent[axis_at] // blocks).reshape([-1 if axis == axis_at else 1 for axis in range(len(extent))])
    return factor_of


def deal_out(own_key, own, number, rows, count, top, reach, skew):
    order = jax.random.permutation(own_key, count)
    packed, common = load_shares(count, rows * top, reach, skew, True), load_shares(count, rows * top, reach, skew, False)
    places = jnp.arange(count)

    def named(tallies, turn):
        used = int((tallies > 0).sum())
        fixed = max(1, used // 4)
        shifted = fixed + (places - fixed + turn * (used - fixed)) % max(1, count - fixed)
        return jnp.zeros((count,), jnp.int32).at[order[jnp.where(places < fixed, places, shifted)]].set(jnp.asarray(tallies, jnp.int32))

    tallies = jnp.where(number % 4 == 0, named(packed, number // 4), named(common, number - number // 4 - 1))
    mixed = jax.random.permutation(jax.random.fold_in(own, 3), count)
    source_of, taker = mixed[0:count // 2 * 2:2], mixed[1:count // 2 * 2:2]
    margin = jnp.minimum(tallies[source_of] - 1, reach - tallies[taker]) // 2
    margin = jnp.where((source_of == order[0]) | (taker == order[0]) | (tallies[taker] == 0), 0, jnp.maximum(margin, 0))
    shifted = jax.random.randint(jax.random.fold_in(own, 4), (count // 2,), 0, 1 << 20) % (margin + 1)
    tallies = tallies.at[source_of].add(-shifted).at[taker].add(shifted)
    labels = jnp.searchsorted(jnp.cumsum(tallies), jnp.arange(rows * top), side="right").astype(jnp.int32)
    grid = labels.reshape(top, rows).T
    grid = grid[jax.random.permutation(jax.random.fold_in(own, 1), rows)]
    turn = jax.random.randint(jax.random.fold_in(own, 2), (rows, 1), 0, top)
    return jnp.take_along_axis(grid, (jnp.arange(top)[None, :] + turn) % top, axis=1)


def load_shares(number_of, total, bound, skew, full):
    loads = [(1 << 20) // math.isqrt(rank ** skew) + 1 for rank in range(1, number_of + 1)]
    largest = bound if full else min(bound, max(-(-total // number_of), total * loads[0] // sum(loads)))
    least = 1 if total - largest >= number_of - 1 else 0
    holding, spare = [largest] + [least] * (number_of - 1), total - largest - least * (number_of - 1)
    while spare > 0:
        candidates = [i for i in range(1, number_of) if holding[i] < largest] or [i for i in range(1, number_of) if holding[i] < bound]
        mass, left = sum([loads[i] for i in candidates]), spare
        for i in candidates:
            addition = min(bound - holding[i], max(1, left * loads[i] // mass), spare)
            holding[i] = holding[i] + addition
            spare = spare - addition
    return np.array(holding)


def scatter_about(rng, dims, scale, bound, split=(), held_as=jnp.bfloat16):
    level = block_levels(rng, dims, split, -0.22, 0.18) if split else 1.0
    entries = jax.random.normal(rng, dims, jnp.float32) * scale * level
    return jnp.minimum(jnp.maximum(entries, -bound), bound).astype(held_as)


def setup_inputs(seed: int = 0, part: int = 0) -> dict:
    key_of = jax.random.split(jax.random.key(seed), 22)
    part_splits = jax.random.split(jax.random.fold_in(key_of[21], part), 22)
    nodes = scatter_about(part_splits[0], (NODES, D), 1.0, 6.0, ((0, 8),))
    edges = scatter_about(part_splits[1], (NODES, K * C), 1.0, 6.0, ((0, 8),))
    nbr_owner_keys = jax.random.split(jax.random.fold_in(part_splits[2], 1), NODES * K // (RES_DEV * K))
    nbr_owner_turns = jax.random.permutation(jax.random.fold_in(part_splits[2], 3), NODES * K // (RES_DEV * K))
    nbr_owner = jax.vmap(lambda own, number: deal_out(jax.random.fold_in(part_splits[2], 2), own, number, RES_DEV * K, N_EDGE, 1, CAP, 1))(nbr_owner_keys, nbr_owner_turns).reshape((NODES, K, 1))
    nbr_slot = touch_ends(jax.random.randint(part_splits[3], (NODES, K), 0, RES_DEV), jax.random.fold_in(part_splits[3], 1), 0, RES_DEV - 1).astype(jnp.int32)
    edge_mask = touch_ends((jax.random.randint(part_splits[4], (NODES, K), 0, 8) < 7).astype(jnp.int32), jax.random.fold_in(part_splits[4], 1), 0, 1)
    w_msg1 = scatter_about(key_of[5], (2 * D + C, D), (2 * D + C) ** -0.5, 0.15625)
    w_msg2 = scatter_about(key_of[6], (D, D), D ** -0.5, 0.25)
    w_msg3 = scatter_about(key_of[7], (D, D), (max(1, 2 * D // K)) ** -0.5, 1.25)
    gain_one = jnp.clip(1.0 + 0.18 * jax.random.normal(key_of[8], (D,), jnp.float32), 0.1, 1.9)
    offset_one = scatter_about(key_of[9], (D,), 0.5, 3.0, (), jnp.float32)
    w_ffn1 = scatter_about(key_of[10], (D, FF), D ** -0.5, 0.25)
    w_ffn2 = scatter_about(key_of[11], (FF, D), FF ** -0.5, 0.125)
    gain_two = jnp.clip(1.0 + 0.18 * jax.random.normal(key_of[12], (D,), jnp.float32), 0.1, 1.9)
    offset_two = scatter_about(key_of[13], (D,), 0.5, 3.0, (), jnp.float32)
    w_edge1 = scatter_about(key_of[14], (2 * D + C, C), (2 * D + C) ** -0.5, 0.15625)
    w_edge2 = scatter_about(key_of[15], (C, C), C ** -0.5, 0.4375)
    w_edge3 = scatter_about(key_of[16], (C, C), C ** -0.5, 0.4375)
    gain_three = jnp.clip(1.0 + 0.18 * jax.random.normal(key_of[17], (C,), jnp.float32), 0.1, 1.9)
    offset_three = scatter_about(key_of[18], (C,), 0.5, 3.0, (), jnp.float32)
    node_cotangent = scatter_about(part_splits[19], (NODES, D), 1.0, 6.0, ((0, 8),))
    edge_cotangent = scatter_about(part_splits[20], (NODES, K * C), 1.0, 6.0, ((0, 8),))
    return {"nodes": nodes, "edges": edges, "nbr_owner": nbr_owner, "nbr_slot": nbr_slot, "edge_mask": edge_mask, "w_msg1": w_msg1, "w_msg2": w_msg2, "w_msg3": w_msg3, "gain_one": gain_one, "offset_one": offset_one, "w_ffn1": w_ffn1, "w_ffn2": w_ffn2, "gain_two": gain_two, "offset_two": offset_two, "w_edge1": w_edge1, "w_edge2": w_edge2, "w_edge3": w_edge3, "gain_three": gain_three, "offset_three": offset_three, "node_cotangent": node_cotangent, "edge_cotangent": edge_cotangent}


@jax.custom_vjp
def low(v):
    return lax.optimization_barrier(v.astype(jnp.bfloat16)).astype(jnp.float32)

@jax.custom_vjp
def low_back(v):
    return v

def low_keep(v):
    return (low(v), None)

def low_pass(kept, grad):
    return (grad,)

def back_keep(v):
    return (v, None)

def back_low(kept, grad):
    return (low(grad),)
low.defvjp(low_keep, low_pass)
low_back.defvjp(back_keep, back_low)

def gelu_act(values):
    return jax.nn.gelu(values, approximate=True)

def matmul(left, right):
    return jnp.dot(left, right, precision=lax.Precision.HIGHEST, preferred_element_type=jnp.float32)

def layer_norm(values, scale_gain, offset):
    average = lax.optimization_barrier(jnp.mean(values, axis=-1, keepdims=True))
    centred = values - average
    variance = lax.optimization_barrier(jnp.mean(centred * centred, axis=-1, keepdims=True))
    return centred * lax.rsqrt(variance + 1e-05) * scale_gain + offset

def reference(nodes, edges, nbr_owner, nbr_slot, edge_mask, w_msg1, w_msg2, w_msg3, gain_one, offset_one, w_ffn1, w_ffn2, gain_two, offset_two, w_edge1, w_edge2, w_edge3, gain_three, offset_three, node_cotangent, edge_cotangent):
    node_total = nodes.shape[0]
    edge_total = node_total * K
    target = (nbr_owner[:, :, 0] * RES_DEV + nbr_slot).reshape(edge_total).astype(jnp.int32)
    source = jnp.repeat(jnp.arange(node_total, dtype=jnp.int32), K)
    live = edge_mask.reshape(edge_total).astype(jnp.float32)
    divisor = 1.0 + jax.ops.segment_sum(live, target, node_total)

    def forward(node_in, edge_in, msg_one, msg_two, msg_three, gain_a, offset_a, ffn_one, ffn_two, gain_b, offset_b, edge_one, edge_two, edge_three, gain_c, offset_c):
        edge_rows = edge_in.reshape(edge_total, C)
        joined = jnp.concatenate([low_back(node_in[source]), node_in[target], low_back(edge_rows)], axis=1)
        act_one = low(gelu_act(low_back(matmul(joined, msg_one))))
        act_two = low(gelu_act(low_back(matmul(act_one, msg_two))))
        message = low_back(matmul(act_two, msg_three))
        summed = jax.ops.segment_sum(message * live[:, None], target, node_total)
        normed_one = layer_norm(node_in + summed / divisor[:, None], gain_a, offset_a)
        ffn_act = low(gelu_act(low_back(matmul(low(normed_one), ffn_one))))
        node_new = layer_norm(normed_one + low_back(matmul(ffn_act, ffn_two)), gain_b, offset_b)
        node_low = low(node_new)
        edge_join = jnp.concatenate([node_low[source], low_back(node_low[target]), edge_rows], axis=1)
        hidden_one = low(gelu_act(low_back(matmul(edge_join, edge_one))))
        hidden_two = low(gelu_act(low_back(matmul(hidden_one, edge_two))))
        edge_new = layer_norm(edge_rows + low_back(matmul(hidden_two, edge_three)), gain_c, offset_c)
        return (node_new, edge_new.reshape(node_total, K * C))
    floats = tuple((item.astype(jnp.float32) for item in (nodes, edges, w_msg1, w_msg2, w_msg3, gain_one, offset_one, w_ffn1, w_ffn2, gain_two, offset_two, w_edge1, w_edge2, w_edge3, gain_three, offset_three)))
    outputs, pullback = jax.vjp(forward, *floats)
    grads = pullback((node_cotangent.astype(jnp.float32), edge_cotangent.astype(jnp.float32)))
    return (outputs[0].astype(jnp.bfloat16), outputs[1].astype(jnp.bfloat16), grads[0], grads[1], grads[2], grads[3], grads[4], grads[5], grads[6], grads[7], grads[8], grads[9], grads[10], grads[11], grads[12], grads[13], grads[14], grads[15])
```

```python
import functools

import jax
import jax.numpy as jnp
from jax import lax
from jax.experimental import pallas as pl
from jax.experimental.pallas import tpu as pltpu
from jax.sharding import PartitionSpec as P

BF = jnp.bfloat16
F32 = jnp.float32
I32 = jnp.int32
MESH = pl.DeviceIdType.MESH
MIB = 1024 * 1024
LANES = 128
GROUP = 4
TABLE = 1024
EPS = 1e-05
ROOT = 0.7978845608028654
CUBE = 0.044715 * ROOT


def dot(a, b):
    return jnp.dot(a, b, preferred_element_type=F32)


def dot_tn(a, b):
    return lax.dot_general(a, b, (((0,), (0,)), ((), ())), preferred_element_type=F32)


def dot_nt(a, b):
    return lax.dot_general(a, b, (((1,), (1,)), ((), ())), preferred_element_type=F32)


def gelu_pair(v):
    z = v * v
    q = 0.5 + 0.5 * jnp.tanh(v * (ROOT + CUBE * z))
    act = v * q
    slope = q + (act - act * q) * (2.0 * ROOT + 6.0 * CUBE * z)
    return act, slope


def row_mean(v):
    return jnp.mean(v, axis=-1, keepdims=True)


def lane_column(ref, k):
    rows = ref.shape[0]
    return jnp.broadcast_to(pltpu.roll(ref[...], LANES - k, axis=1)[:, 0:1], (rows, LANES))


def pick_rows(target, width):
    lane = lax.broadcasted_iota(I32, target.shape, 1)
    return jnp.concatenate(
        [(target == lane + LANES * c).astype(F32).astype(BF) for c in range(width // LANES)],
        axis=1,
    )


def pick_cols(target, width):
    edges = target.shape[1]
    sub = lax.broadcasted_iota(I32, (width, edges), 0)
    return (jnp.broadcast_to(target, (width, edges)) == sub).astype(F32).astype(BF)


def gather_table(targets, table):
    count = table.shape[0]
    if count <= TABLE:
        hot = jnp.concatenate([pick_rows(t, count) for t in targets], axis=0)
        return dot(hot, table[...])

    def step(c, total):
        base = c * TABLE
        hot = jnp.concatenate([pick_rows(t - base, TABLE) for t in targets], axis=0)
        return total + dot(hot, table[pl.ds(pl.multiple_of(base, TABLE), TABLE), :])

    rows = sum(t.shape[0] for t in targets)
    return lax.fori_loop(0, count // TABLE, step, jnp.zeros((rows, table.shape[1]), F32))


def add_by_target(target, values, total):
    count = total.shape[0]
    if count <= TABLE:
        total[...] += dot(pick_cols(target, count), values)
        return

    def step(c, carry):
        base = c * TABLE
        part = pl.ds(pl.multiple_of(base, TABLE), TABLE)
        total[part, :] += dot(pick_cols(target - base, TABLE), values)
        return carry

    lax.fori_loop(0, count // TABLE, step, 0)


def by_chunks(count, step):
    if count <= TABLE:
        step(pl.ds(0, count))
        return

    def one(c, carry):
        step(pl.ds(pl.multiple_of(c * TABLE, TABLE), TABLE))
        return carry

    lax.fori_loop(0, count // TABLE, one, 0)


def remote(src, dst, send, recv, peer):
    return pltpu.make_async_remote_copy(
        src_ref=src,
        dst_ref=dst,
        send_sem=send,
        recv_sem=recv,
        device_id={"edge": peer},
        device_id_type=MESH,
    )


def greet(peers):
    barrier = pltpu.get_barrier_semaphore()
    for peer in peers:
        pl.semaphore_signal(barrier, inc=1, device_id={"edge": peer}, device_id_type=MESH)
    pl.semaphore_wait(barrier, len(peers))


def block(ref, index, rows):
    return ref.at[pl.ds(pl.multiple_of(index * rows, rows), rows)]


class Place:
    def __init__(self, n):
        self.me = lax.axis_index("edge")
        self.chips = n // 2
        self.chip = self.me // 2
        self.core = lax.rem(self.me, 2)
        self.sibling = self.chip * 2 + 1 - self.core
        self.mates = [self.at(d) for d in range(1, self.chips)]

    def at(self, d):
        return lax.rem(self.chip + d + self.chips, self.chips) * 2 + self.core


def gather_start(place, x, out, send, recv):
    rows, chips = x.shape[0], place.chips
    far = []
    for d in range(1, chips):
        far.append(
            remote(x, block(out, place.me, rows), send.at[d], recv.at[d], place.mates[d - 1])
        )
    near = remote(x, block(out, place.me, rows), send.at[0], recv.at[0], place.sibling)
    for copy in far:
        copy.start()
    near.start()
    return far, near


def gather_finish(place, handles, x, out, send, recv):
    far, near = handles
    rows, chips = x.shape[0], place.chips
    passed = []
    for d in range(1, chips):
        far[d - 1].wait_recv()
        got = block(out, place.at(-d), rows)
        copy = remote(got, got, send.at[chips + d], recv.at[chips + d], place.sibling)
        copy.start()
        passed.append(copy)
    near.wait()
    for copy in passed:
        copy.wait()
    for copy in far:
        copy.wait_send()


def scatter_sum(place, x, pair_buf, send_buf, far_buf, send, recv):
    chips, rows = place.chips, pair_buf.shape[1]
    pairs = []
    for d in range(chips):
        theirs = lax.rem(place.chip + d, chips) * 2 + 1 - place.core
        pairs.append(
            remote(block(x, theirs, rows), pair_buf.at[d], send.at[d], recv.at[d], place.sibling)
        )
    for d in range(1, chips):
        pairs[d].start()
    pairs[0].start()
    far = []
    for d in range(1, chips):
        pairs[d].wait_recv()
        mine = x[pl.ds(pl.multiple_of(place.at(d) * rows, rows), rows), :]
        send_buf[d] = (mine.astype(F32) + pair_buf[d].astype(F32)).astype(BF)
        copy = remote(
            send_buf.at[d], far_buf.at[d], send.at[chips + d], recv.at[chips + d], place.at(d)
        )
        copy.start()
        far.append(copy)
    pairs[0].wait_recv()
    own = x[pl.ds(pl.multiple_of(place.me * rows, rows), rows), :]
    total = own.astype(F32) + pair_buf[0].astype(F32)
    for d in range(1, chips):
        far[d - 1].wait_recv()
        total = total + far_buf[d].astype(F32)
    for d in range(chips):
        pairs[d].wait_send()
    for copy in far:
        copy.wait_send()
    return total


def comm_scratch(n, rows, width):
    return [pltpu.VMEM((n // 2, rows, width), BF)] * 3


def sems(count):
    return [pltpu.SemaphoreType.DMA((count,))] * 2


def remote_params(cid):
    return pltpu.CompilerParams(
        collective_id=cid, has_side_effects=True, vmem_limit_bytes=60 * MIB
    )


LOCAL = pltpu.CompilerParams(vmem_limit_bytes=62 * MIB)
WHOLE = pl.BlockSpec(memory_space=pltpu.VMEM)


def start_kernel(
    n, K, nodes, owner, slot, live, nodes_all, tcol, lcol, trow, count,
    orow, lrow, scol, hist, got, send, recv, hsend, hrecv, own_sem,
):
    place = Place(n)
    rows = nodes.shape[0]
    others = [lax.rem(place.me + d, n) for d in range(1, n)]
    greet(others)
    handles = gather_start(place, nodes, nodes_all, send, recv)
    own = pltpu.make_async_copy(nodes, block(nodes_all, place.me, rows), own_sem.at[0])
    own.start()
    spare = jnp.zeros((rows, LANES - K), I32)
    own_wide = jnp.concatenate([owner[...], spare], axis=1)
    slot_wide = jnp.concatenate([slot[...], spare], axis=1)
    live_wide = jnp.concatenate([live[...], spare], axis=1).astype(F32)
    target = own_wide * rows + slot_wide
    tcol[...] = target
    lcol[...] = live_wide
    scol[...] = slot_wide
    trow[...] = jnp.transpose(target)
    orow[...] = jnp.transpose(own_wide)
    lrow[...] = jnp.transpose(live_wide)

    def tally(g, total):
        ks = [g * GROUP + j for j in range(GROUP)]
        hot = jnp.concatenate([pick_rows(lane_column(scol, k), LANES) for k in ks], axis=0)
        owners = jnp.concatenate([orow[pl.ds(k, 1), :] for k in ks], axis=1)
        lives = jnp.concatenate([lrow[pl.ds(k, 1), :] for k in ks], axis=1)
        sub = lax.broadcasted_iota(I32, (n, GROUP * rows), 0)
        who = jnp.where(
            jnp.broadcast_to(owners, sub.shape) == sub, jnp.broadcast_to(lives, sub.shape), 0.0
        )
        return total + dot(who.astype(BF), hot)

    totals = lax.fori_loop(0, K // GROUP, tally, jnp.zeros((n, LANES), F32))
    for e in range(n):
        hist[e] = jnp.broadcast_to(totals[e : e + 1, :], (8, LANES))
    copies = []
    for d in range(1, n):
        copy = remote(
            hist.at[others[d - 1]], got.at[d], hsend.at[d], hrecv.at[d], others[d - 1]
        )
        copy.start()
        copies.append(copy)
    total = hist[place.me]
    for copy in copies:
        copy.wait_recv()
    for d in range(1, n):
        total = total + got[d]
    count[...] = total
    own.wait()
    gather_finish(place, handles, nodes, nodes_all, send, recv)
    for copy in copies:
        copy.wait_send()


def start_call(n, nodes, owner, slot, live):
    rows, D = nodes.shape
    K = slot.shape[1]
    shape = jax.ShapeDtypeStruct
    return pl.pallas_call(
        functools.partial(start_kernel, n, K),
        in_specs=[WHOLE] * 4,
        out_specs=[WHOLE] * 5,
        out_shape=[
            shape((n * rows, D), BF),
            shape((rows, LANES), I32),
            shape((rows, LANES), F32),
            shape((LANES, rows), I32),
            shape((8, LANES), F32),
        ],
        scratch_shapes=[
            pltpu.VMEM((LANES, rows), I32),
            pltpu.VMEM((LANES, rows), F32),
            pltpu.VMEM((rows, LANES), I32),
            pltpu.VMEM((n, 8, LANES), F32),
            pltpu.VMEM((n, 8, LANES), F32),
            *sems(n),
            *sems(n),
            pltpu.SemaphoreType.DMA((1,)),
        ],
        compiler_params=remote_params(0),
    )(nodes, owner, slot, live)


def slab_pairs(slab, C):
    pairs = slab.shape[1] // (2 * C)
    even = [slab[:, 2 * C * m : 2 * C * m + 256] for m in range(pairs)]
    odd = [slab[:, 2 * C * m + 2 * C - 256 : 2 * C * m + 2 * C] for m in range(pairs)]
    return jnp.concatenate(even, axis=0), jnp.concatenate(odd, axis=0)


def interleave(even, odd, rows):
    parts = []
    for m in range(even.shape[0] // rows):
        parts += [even[m * rows : (m + 1) * rows], odd[m * rows : (m + 1) * rows]]
    return jnp.concatenate(parts, axis=0)


def split_tiles(values, rows):
    count = values.shape[0] // rows
    pick = lambda first: jnp.concatenate(
        [values[k * rows : (k + 1) * rows] for k in range(first, count, 2)], axis=0
    )
    return pick(0), pick(1)


def join_slab(even, odd, rows, C):
    parts = []
    for m in range(even.shape[0] // rows):
        a = even[m * rows : (m + 1) * rows]
        b = odd[m * rows : (m + 1) * rows]
        parts += [a[:, :LANES], a[:, LANES:] + b[:, :LANES], b[:, LANES:]]
    return jnp.concatenate(parts, axis=1)


def message_kernel(
    tiles, C, tcol, lcol, trow, nodes_all, nodes, w1, w2, edges,
    act1, slope1, slope2, summed, p_all, p_own, w_own, total, pre1, pre2,
):
    i = pl.program_id(0)
    rows, D = nodes.shape
    count = nodes_all.shape[0]

    @pl.when(i == 0)
    def _():
        def project(part):
            p_all[part, :] = dot(nodes_all[part, :], w1[D : 2 * D, :]).astype(BF)

        by_chunks(count, project)
        p_own[...] = dot(nodes[...], w1[:D, :])
        w_own[...] = jnp.zeros_like(w_own)
        w_own[0, :C, :] = w1[2 * D :, :]
        w_own[1, 256 - C :, :] = w1[2 * D :, :]
        total[...] = jnp.zeros_like(total)
        pre1[...] = jnp.zeros_like(pre1)
        pre2[...] = jnp.zeros_like(pre2)

    last = jnp.clip(i - 2, 0, tiles - 1)
    ks = [last * GROUP + j for j in range(GROUP)]
    act, slope = gelu_pair(pre2[...])
    live = jnp.concatenate(
        [jnp.concatenate([lane_column(lcol, k)] * (D // LANES), axis=1) for k in ks], axis=0
    )
    slope2[...] = (slope * live).astype(BF)
    live = live * jnp.where(i >= 2, 1.0, 0.0)
    act = (act * live).astype(BF)
    target = jnp.concatenate([trow[pl.ds(k, 1), :] for k in ks], axis=1)
    add_by_target(target, act, total)

    act, slope = gelu_pair(pre1[...])
    act = act.astype(BF)
    act1[...] = act
    slope1[...] = slope.astype(BF)
    pre2[...] = dot(act, w2[...])

    now = jnp.minimum(i, tiles - 1)
    targets = [lane_column(tcol, now * GROUP + j) for j in range(GROUP)]
    even, odd = slab_pairs(edges[...], C)
    base = p_own[...]
    own = interleave(dot(even, w_own[0]), dot(odd, w_own[1]), rows)
    pre1[...] = gather_table(targets, p_all) + own + jnp.concatenate([base] * GROUP, axis=0)

    @pl.when(i == tiles + 1)
    def _():
        summed[...] = total[...].astype(BF)


def full(x):
    return pl.BlockSpec(
        x.shape, lambda g: (0,) * x.ndim, pipeline_mode=pl.Buffered(buffer_count=1)
    )


def message_call(C, tcol, lcol, trow, nodes_all, nodes, w1, w2, edges):
    rows, D = nodes.shape
    count = nodes_all.shape[0]
    K = edges.shape[1] // C
    tiles = K // GROUP
    size = GROUP * rows
    shape = jax.ShapeDtypeStruct
    lag = lambda d: pl.BlockSpec((size, D), lambda g: (jnp.clip(g - d, 0, tiles - 1), 0))
    return pl.pallas_call(
        functools.partial(message_kernel, tiles, C),
        grid=(tiles + 2,),
        in_specs=[full(x) for x in (tcol, lcol, trow, nodes_all, nodes, w1, w2)]
        + [pl.BlockSpec((rows, GROUP * C), lambda g: (0, jnp.minimum(g, tiles - 1)))],
        out_specs=[lag(1), lag(1), lag(2), pl.BlockSpec((count, D), lambda g: (0, 0))],
        out_shape=[shape((K * rows, D), BF)] * 3 + [shape((count, D), BF)],
        scratch_shapes=[
            pltpu.VMEM((count, D), BF),
            pltpu.VMEM((rows, D), F32),
            pltpu.VMEM((2, 256, D), BF),
            pltpu.VMEM((count, D), F32),
            pltpu.VMEM((size, D), F32),
            pltpu.VMEM((size, D), F32),
        ],
        compiler_params=LOCAL,
    )(tcol, lcol, trow, nodes_all, nodes, w1, w2, edges)


def column_of(row):
    return jnp.transpose(jnp.broadcast_to(row, (LANES, row.shape[1])))


def spread(column, width):
    return jnp.concatenate([column] * (width // LANES), axis=1)


def norm_parts(values):
    centred = values - row_mean(values)
    inverse = lax.rsqrt(row_mean(centred * centred) + EPS)
    return centred * inverse, inverse


def node_kernel(
    n, C, summed, count, nodes, w3, g1, o1, wf1, wf2, g2, o2, we1,
    node_out, far_all, near, low_out, n1_out, n2_out, inv_out, act_out, slope_out, sum_out,
    pair_buf, send_buf, far_buf, q_own, send, recv, gsend, grecv, own_sem,
):
    place = Place(n)
    rows, D = nodes.shape
    greet([place.sibling] + place.mates)
    total = scatter_sum(place, summed, pair_buf, send_buf, far_buf, send, recv).astype(BF)
    sum_out[...] = total
    divisor = 1.0 + column_of(count[0:1, :])
    inv_out[2] = divisor
    resid = nodes[...].astype(F32) + dot(total, w3[...]) / spread(divisor, D)
    n1, inv1 = norm_parts(resid)
    n1_out[...] = n1
    inv_out[0] = jnp.broadcast_to(inv1, (rows, LANES))
    normed = n1 * g1[...] + o1[...]
    low = normed.astype(BF)
    low_out[...] = low
    act, slope = gelu_pair(dot(low, wf1[...]))
    act = act.astype(BF)
    act_out[...] = act
    slope_out[...] = slope.astype(BF)
    n2, inv2 = norm_parts(normed + dot(act, wf2[...]))
    n2_out[...] = n2
    inv_out[1] = jnp.broadcast_to(inv2, (rows, LANES))
    node_low = (n2 * g2[...] + o2[...]).astype(BF)
    node_out[...] = node_low
    pad = jnp.zeros((rows, 256 - C), F32)
    far = dot(node_low, we1[D : 2 * D, :])
    q_own[...] = jnp.concatenate([far, pad], axis=1).astype(BF)
    handles = gather_start(place, q_own, far_all, gsend, grecv)
    own = pltpu.make_async_copy(q_own, block(far_all, place.me, rows), own_sem.at[0])
    own.start()
    near[...] = jnp.concatenate([dot(node_low, we1[:D, :]), pad], axis=1)
    own.wait()
    gather_finish(place, handles, q_own, far_all, gsend, grecv)


def node_call(n, C, summed, count, nodes, w3, g1, o1, wf1, wf2, g2, o2, we1):
    rows, D = nodes.shape
    FF = wf1.shape[1]
    shape = jax.ShapeDtypeStruct
    return pl.pallas_call(
        functools.partial(node_kernel, n, C),
        in_specs=[WHOLE] * 11,
        out_specs=[WHOLE] * 10,
        out_shape=[
            shape((rows, D), BF),
            shape((n * rows, 256), BF),
            shape((rows, 256), F32),
            shape((rows, D), BF),
            shape((rows, D), F32),
            shape((rows, D), F32),
            shape((3, rows, LANES), F32),
            shape((rows, FF), BF),
            shape((rows, FF), BF),
            shape((rows, D), BF),
        ],
        scratch_shapes=[
            *comm_scratch(n, rows, D),
            pltpu.VMEM((rows, 256), BF),
            *sems(n),
            *sems(n),
            pltpu.SemaphoreType.DMA((1,)),
        ],
        compiler_params=remote_params(1),
    )(summed, count, nodes, w3, g1, o1, wf1, wf2, g2, o2, we1)


def edge_kernel(
    tiles, C, tcol, trow, far_all, near, we1, we2, we3, gain, offset, edges, cot,
    edge_out, partial, far_sum, near_sum, dw1, dw2, dw3, dgain,
    w1o, w2p, w3o, w1t, w2t, w3t, gains, total, a1, a2, a3, ag,
):
    g = pl.program_id(0)
    rows = near.shape[0]
    D2 = we1.shape[0] - C
    gap = 256 - C

    @pl.when(g == 0)
    def _():
        for ref in (w1o, w2p, w3o, w1t, w2t, w3t, gains, total, a1, a2, a3, ag, near_sum):
            ref[...] = jnp.zeros_like(ref)
        own = we1[D2:, :]
        w1o[0, :C, :C] = own
        w1o[1, gap:, :C] = own
        w2p[:C, :C] = we2[...]
        w3o[0, :C, :C] = we3[...]
        w3o[1, :C, :] = jnp.concatenate([jnp.zeros((C, gap), F32), we3[...].astype(F32)], axis=1).astype(BF)
        for s in range(2):
            w1t[s] = jnp.transpose(w1o[s].astype(F32)).astype(BF)
            w3t[s] = jnp.transpose(w3o[s].astype(F32)).astype(BF)
        w2t[...] = jnp.transpose(w2p[...].astype(F32)).astype(BF)
        zero = jnp.zeros((1, gap), F32)
        gains[0, 0:1] = jnp.concatenate([gain[...], zero], axis=1)
        gains[0, 1:2] = jnp.concatenate([offset[...], zero], axis=1)
        gains[1, 0:1] = jnp.concatenate([zero, gain[...]], axis=1)
        gains[1, 1:2] = jnp.concatenate([zero, offset[...]], axis=1)

    ks = [g * GROUP + j for j in range(GROUP)]
    slabs = slab_pairs(edges[...], C)
    cots = slab_pairs(cot[...], C)
    half = slabs[0].shape[0]
    own = interleave(dot(slabs[0], w1o[0]), dot(slabs[1], w1o[1]), rows)
    base = near[...]
    pre1 = gather_table([lane_column(tcol, k) for k in ks], far_all)
    pre1 = pre1 + own + jnp.concatenate([base] * GROUP, axis=0)
    h1, s1 = gelu_pair(pre1)
    h1 = h1.astype(BF)
    h2, s2 = gelu_pair(dot(h1, w2p[...]))
    h2 = h2.astype(BF)
    h2s = split_tiles(h2, rows)
    lane = lax.broadcasted_iota(I32, (half, 256), 1)
    outs, thirds, lows = [], [], []
    for s in range(2):
        inside = (lane < C) if s == 0 else (lane >= gap)
        keep = lambda v: jnp.where(inside, v, 0.0)
        mean = lambda v: jnp.sum(v, axis=-1, keepdims=True) * (1.0 / C)
        value = keep(slabs[s].astype(F32)) + dot(h2s[s], w3o[s])
        centred = keep(value - mean(value))
        inverse = lax.rsqrt(mean(centred * centred) + EPS)
        normal = centred * inverse
        outs.append(normal * gains[s, 0:1] + gains[s, 1:2])
        upstream = keep(cots[s].astype(F32))
        moved = upstream * normal
        for r in range(half // rows):
            part = slice(r * rows, (r + 1) * rows)
            ag[s, 0] += moved[part]
            ag[s, 1] += upstream[part]
        scaled = upstream * gains[s, 0:1]
        third = inverse * (scaled - mean(scaled) - normal * mean(scaled * normal))
        third = keep(third)
        thirds.append(third)
        low = third.astype(BF)
        lows.append(low)
        a3[s] += dot_tn(h2s[s], low)
    edge_out[...] = join_slab(outs[0], outs[1], rows, C).astype(BF)
    low2 = interleave(dot(lows[0], w3t[0]), dot(lows[1], w3t[1]), rows)
    low2 = (low2 * s2).astype(BF)
    a2[...] += dot_tn(h1, low2)
    low1 = (dot(low2, w2t[...]) * s1).astype(BF)
    low1s = split_tiles(low1, rows)
    for s in range(2):
        a1[s] += dot_tn(low1s[s], slabs[s])
        thirds[s] = thirds[s] + dot(low1s[s], w1t[s])
    partial[...] = join_slab(thirds[0], thirds[1], rows, C)
    wide = low1.astype(F32)
    acc = wide[:rows]
    for j in range(1, GROUP):
        acc = acc + wide[j * rows : (j + 1) * rows]
    near_sum[...] += acc
    target = jnp.concatenate([trow[pl.ds(k, 1), :] for k in ks], axis=1)
    add_by_target(target, low1, total)

    @pl.when(g == tiles - 1)
    def _():
        far_sum[...] = total[...].astype(BF)
        dw1[...] = (jnp.transpose(a1[0])[:C,:] + jnp.transpose(a1[1])[gap:,:])
        dw2[...] = a2[...]
        shifted = a3[1][:, gap:]
        dw3[...] = a3[0] + jnp.concatenate([shifted, jnp.zeros((256, gap), F32)], axis=1)
        for r in range(2):
            even = jnp.sum(ag[0, r], axis=0, keepdims=True)
            odd = jnp.sum(ag[1, r], axis=0, keepdims=True)
            row = even + jnp.concatenate([odd[:, gap:], jnp.zeros((1, gap), F32)], axis=1)
            dgain[r * 8 : r * 8 + 8, :] = jnp.broadcast_to(row, (8, 256))


def edge_call(C, tcol, trow, far_all, near, we1, we2, we3, gain, offset, edges, cot):
    rows = near.shape[0]
    count = far_all.shape[0]
    K = edges.shape[1] // C
    tiles = K // GROUP
    shape = jax.ShapeDtypeStruct
    slab = pl.BlockSpec((rows, GROUP * C), lambda g: (0, g))
    fixed = lambda *s: pl.BlockSpec(s, lambda g: (0,) * len(s))
    return pl.pallas_call(
        functools.partial(edge_kernel, tiles, C),
        grid=(tiles,),
        in_specs=[full(x) for x in (tcol, trow, far_all, near, we1, we2, we3, gain, offset)]
        + [slab, slab],
        out_specs=[
            slab, slab, fixed(count, 256), fixed(rows, 256),
            fixed(C, 256), fixed(256, 256), fixed(256, 256), fixed(16, 256),
        ],
        out_shape=[
            shape((rows, K * C), BF),
            shape((rows, K * C), F32),
            shape((count, 256), BF),
            shape((rows, 256), F32),
            shape((C, 256), F32),
            shape((256, 256), F32),
            shape((256, 256), F32),
            shape((16, 256), F32),
        ],
        scratch_shapes=[
            pltpu.VMEM((2, 256, 256), BF),
            pltpu.VMEM((256, 256), BF),
            pltpu.VMEM((2, 256, 256), BF),
            pltpu.VMEM((2, 256, 256), BF),
            pltpu.VMEM((256, 256), BF),
            pltpu.VMEM((2, 256, 256), BF),
            pltpu.VMEM((2, 8, 256), F32),
            pltpu.VMEM((count, 256), F32),
            pltpu.VMEM((2, 256, 256), F32),
            pltpu.VMEM((256, 256), F32),
            pltpu.VMEM((2, 256, 256), F32),
            pltpu.VMEM((2, 2, rows, 256), F32),
        ],
        compiler_params=LOCAL,
    )(tcol, trow, far_all, near, we1, we2, we3, gain, offset, edges, cot)


def norm_back(upstream, normal, inverse, gain):
    scaled = upstream * gain
    return inverse * (scaled - row_mean(scaled) - normal * row_mean(scaled * normal))


def node_back_kernel(
    n, C, far_sum, near_sum, cot, node_low, n1, n2, inv, act, slope, low, summed,
    w3, g1, wf1, wf2, g2, we1,
    grad_one, vw_all, resid_out, dgain, dw3, dwe_near, dwe_far,
    pair_buf, send_buf, far_buf, v_own, send, recv, gsend, grecv, own_sem,
):
    place = Place(n)
    rows, D = cot.shape
    greet([place.sibling] + place.mates)
    far = scatter_sum(place, far_sum, pair_buf, send_buf, far_buf, send, recv)
    far = far.astype(BF)[:, :C]
    near = near_sum[...].astype(BF)[:, :C]
    grad = cot[...].astype(F32) + dot_nt(near, we1[:D, :]) + dot_nt(far, we1[D : 2 * D, :])
    two = norm_back(grad, n2[...], inv[1][:, 0:1], g2[...])
    dgain[16:24, :] = jnp.broadcast_to(jnp.sum(grad * n2[...], axis=0, keepdims=True), (8, D))
    dgain[24:32, :] = jnp.broadcast_to(jnp.sum(grad, axis=0, keepdims=True), (8, D))
    resid = two.astype(BF)
    resid_out[...] = resid
    inner = (dot_nt(resid, wf2[...]) * slope[...].astype(F32)).astype(BF)
    grad = two + dot_nt(inner, wf1[...])
    one = norm_back(grad, n1[...], inv[0][:, 0:1], g1[...])
    dgain[0:8, :] = jnp.broadcast_to(jnp.sum(grad * n1[...], axis=0, keepdims=True), (8, D))
    dgain[8:16, :] = jnp.broadcast_to(jnp.sum(grad, axis=0, keepdims=True), (8, D))
    grad_one[...] = one
    upper = (one / spread(inv[2], D)).astype(BF)
    v_own[...] = dot_nt(upper, w3[...]).astype(BF)
    handles = gather_start(place, v_own, vw_all, gsend, grecv)
    own = pltpu.make_async_copy(v_own, block(vw_all, place.me, rows), own_sem.at[0])
    own.start()
    dw3[...] = dot_tn(summed[...], upper)
    dwe_near[...] = dot_tn(node_low[...], near)
    dwe_far[...] = dot_tn(node_low[...], far)
    own.wait()
    gather_finish(place, handles, v_own, vw_all, gsend, grecv)


def node_back_call(n, C, *args):
    cot, wf1 = args[2], args[13]
    rows, D = cot.shape
    shape = jax.ShapeDtypeStruct
    return pl.pallas_call(
        functools.partial(node_back_kernel, n, C),
        in_specs=[WHOLE] * len(args),
        out_specs=[WHOLE] * 7,
        out_shape=[
            shape((rows, D), F32),
            shape((n * rows, D), BF),
            shape((rows, D), BF),
            shape((32, D), F32),
            shape((D, D), F32),
            shape((D, C), F32),
            shape((D, C), F32),
        ],
        scratch_shapes=[
            *comm_scratch(n, rows, 256),
            pltpu.VMEM((rows, D), BF),
            *sems(n),
            *sems(n),
            pltpu.SemaphoreType.DMA((1,)),
        ],
        compiler_params=remote_params(2),
    )(*args)


def message_back_kernel(
    tiles, C, tcol, trow, nodes, vw, w1, w2,
    act1, slope1, slope2, edges, partial,
    grad_edges, dw1, dw2, target_sum, source_sum,
    w2t, w_own, w_own_t, total, a2, ae,
):
    g = pl.program_id(0)
    rows, D = nodes.shape
    gap = 256 - C

    @pl.when(g == 0)
    def _():
        for ref in (w_own, total, a2, ae, source_sum):
            ref[...] = jnp.zeros_like(ref)
        w_own[0, :C, :] = w1[2 * D :, :]
        w_own[1, gap:, :] = w1[2 * D :, :]
        for s in range(2):
            w_own_t[s] = jnp.transpose(w_own[s].astype(F32)).astype(BF)
        w2t[...] = jnp.transpose(w2[...].astype(F32)).astype(BF)

    ks = [g * GROUP + j for j in range(GROUP)]
    up = gather_table([lane_column(tcol, k) for k in ks], vw)
    upper = (up * slope2[...].astype(F32)).astype(BF)
    a2[...] += dot_tn(act1[...], upper)
    lower = (dot(upper, w2t[...]) * slope1[...].astype(F32)).astype(BF)
    wide = lower.astype(F32)
    acc = wide[:rows]
    for j in range(1, GROUP):
        acc = acc + wide[j * rows : (j + 1) * rows]
    source_sum[...] += acc
    target = jnp.concatenate([trow[pl.ds(k, 1), :] for k in ks], axis=1)
    add_by_target(target, lower, total)
    slabs = slab_pairs(edges[...], C)
    lowers = split_tiles(lower, rows)
    own = []
    for s in range(2):
        ae[s] += dot_tn(slabs[s], lowers[s])
        own.append(dot(lowers[s], w_own_t[s]))
    grad_edges[...] = partial[...] + join_slab(own[0], own[1], rows, C)

    @pl.when(g == tiles - 1)
    def _():
        target_sum[...] = total[...].astype(BF)
        dw2[...] = a2[...].astype(BF)
        dw1[:D, :] = dot_tn(nodes[...], source_sum[...].astype(BF)).astype(BF)
        dw1[D:, :] = (ae[0][:C, :] + ae[1][gap:, :]).astype(BF)


def message_back_call(C, tcol, trow, nodes, vw, w1, w2, act1, slope1, slope2, edges, partial):
    rows, D = nodes.shape
    count = vw.shape[0]
    K = edges.shape[1] // C
    tiles = K // GROUP
    size = GROUP * rows
    shape = jax.ShapeDtypeStruct
    slab = pl.BlockSpec((rows, GROUP * C), lambda g: (0, g))
    tile = pl.BlockSpec((size, D), lambda g: (g, 0))
    fixed = lambda *s: pl.BlockSpec(
        s, lambda g: (0,) * len(s), pipeline_mode=pl.Buffered(buffer_count=1)
    )
    return pl.pallas_call(
        functools.partial(message_back_kernel, tiles, C),
        grid=(tiles,),
        in_specs=[full(x) for x in (tcol, trow, nodes, vw, w1, w2)]
        + [tile, tile, tile, slab, slab],
        out_specs=[slab, fixed(D + C, D), fixed(D, D), fixed(count, D), fixed(rows, D)],
        out_shape=[
            shape((rows, K * C), F32),
            shape((D + C, D), BF),
            shape((D, D), BF),
            shape((count, D), BF),
            shape((rows, D), F32),
        ],
        scratch_shapes=[
            pltpu.VMEM((D, D), BF),
            pltpu.VMEM((2, 256, D), BF),
            pltpu.VMEM((2, D, 256), BF),
            pltpu.VMEM((count, D), F32),
            pltpu.VMEM((D, D), F32),
            pltpu.VMEM((2, 256, D), F32),
        ],
        compiler_params=LOCAL,
    )(tcol, trow, nodes, vw, w1, w2, act1, slope1, slope2, edges, partial)


def feed_kernel(low, resid, wf1, wf2, dwf1, dwf2):
    @pl.when(pl.program_id(1) == 0)
    def _():
        dwf1[...] = jnp.zeros_like(dwf1)
        dwf2[...] = jnp.zeros_like(dwf2)

    act, slope = gelu_pair(dot(low[...], wf1[...]))
    dwf2[...] += dot_tn(act.astype(BF), resid[...])
    inner = (dot_nt(resid[...], wf2[...]) * slope).astype(BF)
    dwf1[...] += dot_tn(low[...], inner)


def feed_call(both, wf1, wf2):
    count = both.shape[0]
    D, FF = wf1.shape
    step, rows = min(FF, 512), min(count, TABLE)
    shape = jax.ShapeDtypeStruct
    return pl.pallas_call(
        feed_kernel,
        grid=(FF // step, count // rows),
        in_specs=[
            pl.BlockSpec((rows, D), lambda f, r: (r, 0)),
            pl.BlockSpec((rows, D), lambda f, r: (r, 1)),
            pl.BlockSpec((D, step), lambda f, r: (0, f)),
            pl.BlockSpec((step, D), lambda f, r: (f, 0)),
        ],
        out_specs=[
            pl.BlockSpec((D, step), lambda f, r: (0, f)),
            pl.BlockSpec((step, D), lambda f, r: (f, 0)),
        ],
        out_shape=[shape((D, FF), F32), shape((FF, D), F32)],
        compiler_params=LOCAL,
    )(both, both, wf1, wf2)


def total_kernel(n, pieces, lag, x, out, pair_buf, low_buf, high_buf, send_buf, send, recv):
    place = Place(n)
    chips, c, q = place.chips, place.chip, place.core
    root = chips // 2 - 1 + q
    right = jnp.minimum(c + 1, chips - 1) * 2 + q
    left = jnp.maximum(c - 1, 0) * 2 + q
    half = x.shape[0] // 2
    rows = half // pieces
    barrier = pltpu.get_barrier_semaphore()

    def hello(peer):
        pl.semaphore_signal(barrier, inc=1, device_id={"edge": peer}, device_id_type=MESH)

    hello(place.sibling)
    pl.when(c > 0)(lambda: hello(left))
    pl.when(c < chips - 1)(lambda: hello(right))
    inner = jnp.where((c > 0) & (c < chips - 1), 1, 0)
    pl.semaphore_wait(barrier, 2 + inner)

    def part(which, p):
        return pl.ds(pl.multiple_of(which * half + p * rows, rows), rows)

    def local(p):
        return pl.ds(p * rows, rows)

    def link(src, dst, p, sent, got, peer):
        return remote(src, dst, send.at[sent * pieces + p], recv.at[got * pieces + p], peer)

    def pair(p):
        return link(x.at[part(1 - q, p)], pair_buf.at[local(p)], p, 0, 0, place.sibling)

    def up(p):
        return link(send_buf.at[local(p)], low_buf.at[local(p)], p, 1, 1, right)

    def down(p):
        return link(send_buf.at[local(p)], high_buf.at[local(p)], p, 2, 2, left)

    def out_left(p):
        return link(out.at[part(q, p)], out.at[part(q, p)], p, 3, 3, left)

    def out_right(p):
        return link(out.at[part(q, p)], out.at[part(q, p)], p, 5, 3, right)

    def across(p):
        return link(out.at[part(q, p)], out.at[part(q, p)], p, 4, 4, place.sibling)

    for p in range(pieces):
        pair(p).start()

    def reduce(p):
        pair(p).wait_recv()
        here = local(p)
        mine = lambda: x[part(q, p), :].astype(F32) + pair_buf[here, :].astype(F32)

        def from_left():
            def first():
                send_buf[here, :] = mine().astype(BF)

            def inner():
                up(p).wait_recv()
                send_buf[here, :] = (mine() + low_buf[here, :].astype(F32)).astype(BF)

            pl.when(c == 0)(first)
            pl.when(c > 0)(inner)
            up(p).start()

        def from_right():
            def first():
                send_buf[here, :] = mine().astype(BF)

            def inner():
                down(p).wait_recv()
                send_buf[here, :] = (mine() + high_buf[here, :].astype(F32)).astype(BF)

            pl.when(c == chips - 1)(first)
            pl.when(c < chips - 1)(inner)
            down(p).start()

        def at_root():
            up(p).wait_recv()
            down(p).wait_recv()
            total = mine() + low_buf[here, :].astype(F32) + high_buf[here, :].astype(F32)
            out[part(q, p), :] = total.astype(BF)
            out_left(p).start()
            out_right(p).start()
            across(p).start()

        pl.when(c < root)(from_left)
        pl.when(c > root)(from_right)
        pl.when(c == root)(at_root)

    def spread_out(p):
        def leftward():
            out_left(p).wait_recv()
            pl.when(c > 0)(lambda: out_left(p).start())
            across(p).start()

        def rightward():
            out_right(p).wait_recv()
            pl.when(c < chips - 1)(lambda: out_right(p).start())
            across(p).start()

        pl.when(c < root)(leftward)
        pl.when(c > root)(rightward)

    for s in range(pieces + lag):
        if s < pieces:
            reduce(s)
        if s >= lag:
            spread_out(s - lag)
    for p in range(pieces):
        across(p).wait_recv()
    for p in range(pieces):
        pair(p).wait_send()
        across(p).wait_send()
        pl.when(c < root)(lambda: up(p).wait_send())
        pl.when(c > root)(lambda: down(p).wait_send())
        pl.when((c <= root) & (c > 0))(lambda: out_left(p).wait_send())
        pl.when((c >= root) & (c < chips - 1))(lambda: out_right(p).wait_send())


def total_call(n, x, pieces, lag):
    rows, width = x.shape
    return pl.pallas_call(
        functools.partial(total_kernel, n, pieces, lag),
        in_specs=[WHOLE],
        out_specs=WHOLE,
        out_shape=jax.ShapeDtypeStruct(x.shape, x.dtype),
        scratch_shapes=[pltpu.VMEM((rows // 2, width), BF)] * 4 + sems(6 * pieces),
        compiler_params=remote_params(3),
    )(x)


def final_kernel(n, target_sum, source_sum, grad_one, w1, nodes, out, dw1, pair_buf, send_buf, far_buf, send, recv):
    place = Place(n)
    D = grad_one.shape[1]
    greet([place.sibling] + place.mates)
    total = scatter_sum(place, target_sum, pair_buf, send_buf, far_buf, send, recv)
    source = dot_nt(source_sum[...].astype(BF), w1[:D, :])
    total = total.astype(BF)
    out[...] = grad_one[...] + source + dot_nt(total, w1[D : 2 * D, :])
    dw1[...] = dot_tn(nodes[...], total).astype(BF)


def final_call(n, target_sum, source_sum, grad_one, w1, nodes):
    rows, D = grad_one.shape
    return pl.pallas_call(
        functools.partial(final_kernel, n),
        in_specs=[WHOLE] * 5,
        out_specs=[WHOLE] * 2,
        out_shape=[jax.ShapeDtypeStruct((rows, D), F32), jax.ShapeDtypeStruct((D, D), BF)],
        scratch_shapes=[*comm_scratch(n, rows, D), *sems(n)],
        compiler_params=remote_params(4),
    )(target_sum, source_sum, grad_one, w1, nodes)


def body(
    nodes, edges, nbr_owner, nbr_slot, edge_mask, w_msg1, w_msg2, w_msg3, gain_one, offset_one,
    w_ffn1, w_ffn2, gain_two, offset_two, w_edge1, w_edge2, w_edge3, gain_three, offset_three,
    node_cotangent, edge_cotangent,
):
    n = lax.axis_size("edge")
    rows, D = nodes.shape
    C = w_edge2.shape[0]
    K = nbr_slot.shape[1]
    g1, o1, g2, o2 = (v.reshape(1, D) for v in (gain_one, offset_one, gain_two, offset_two))
    nodes_all, tcol, lcol, trow, count = start_call(
        n, nodes, nbr_owner.reshape(rows, K), nbr_slot, edge_mask
    )
    act1, slope1, slope2, summed = message_call(
        C, tcol, lcol, trow, nodes_all, nodes, w_msg1, w_msg2, edges
    )
    node_out, far_all, near, low, n1, n2, inv, act, slope, own_sum = node_call(
        n, C, summed, count, nodes, w_msg3, g1, o1, w_ffn1, w_ffn2, g2, o2, w_edge1
    )
    edge_out, partial, far_sum, near_sum, dwe1, dwe2, dwe3, dg3 = edge_call(
        C, tcol, trow, far_all, near, w_edge1, w_edge2, w_edge3,
        gain_three.reshape(1, C), offset_three.reshape(1, C), edges, edge_cotangent,
    )
    grad_one, vw_all, resid, dgain, dw3, dwe_near, dwe_far = node_back_call(
        n, C, far_sum, near_sum, node_cotangent, node_out, n1, n2, inv, act, slope, low, own_sum,
        w_msg3, g1, w_ffn1, w_ffn2, g2, w_edge1,
    )
    both = lax.all_gather(jnp.concatenate([low, resid], axis=1), "edge", axis=0, tiled=True)
    small = jnp.concatenate(
        [dgain[0::8], jnp.concatenate([dg3[0::8], jnp.zeros((2, D - 256), F32)], axis=1)], axis=0
    )
    small = lax.psum(small, "edge")
    grad_edges, dw1, dw2, target_sum, source_sum = message_back_call(
        C, tcol, trow, nodes, vw_all, w_msg1, w_msg2, act1, slope1, slope2, edges, partial,
    )
    dwf1, dwf2 = feed_call(both, w_ffn1, w_ffn2)
    grad_nodes, dw1t = final_call(n, target_sum, source_sum, grad_one, w_msg1, nodes)
    wide = lambda v: jnp.pad(v, ((0, 0), (0, 256 - v.shape[1])))
    edge1 = jnp.concatenate([wide(dwe_near), wide(dwe_far), dwe1], axis=0).astype(BF)
    split = edge1.shape[0] // 2
    edge1 = jnp.concatenate([edge1[:split], edge1[split:]], axis=1)
    edge23 = jnp.concatenate([dwe2[:C], dwe3[:C]], axis=1).astype(BF)
    packed = jnp.concatenate([dw1[:D], dw1t, dw1[D:], dw2, dw3.astype(BF), edge1, edge23], axis=0)
    packed = total_call(n, packed, 5, 4).astype(F32)
    at = 0
    pieces = []
    for size in (2 * D + C, D, D, split, C):
        pieces.append(packed[at : at + size])
        at += size
    tot1, tot2, tot3, tot_e1, tot_e23 = pieces
    grad_we1 = jnp.concatenate([tot_e1[:, :C], tot_e1[:, 256 : 256 + C]], axis=0)
    return (
        node_out, edge_out, grad_nodes, grad_edges,
        tot1, tot2, tot3, small[0], small[1], dwf1, dwf2, small[2], small[3],
        grad_we1, tot_e23[:, :C], tot_e23[:, 256 : 256 + C], small[4, :C], small[5, :C],
    )


def solution(mesh):
    rows = P(("dp", "edge"), None)
    return jax.shard_map(
        body,
        mesh=mesh,
        in_specs=(rows, rows, P(("dp", "edge"), None, None), rows, rows)
        + (P(),) * 14
        + (rows, rows),
        out_specs=(rows,) * 4
        + (P("dp", None),) * 3
        + (P("dp"),) * 2
        + (P("dp", None),) * 2
        + (P("dp"),) * 2
        + (P("dp", None),) * 3
        + (P("dp"),) * 2,
        check_vma=False,
    )
```

```python
import functools

import jax
import jax.numpy as jnp
from jax import lax
from jax.experimental import pallas as pl
from jax.experimental.pallas import tpu as pltpu
from jax.sharding import PartitionSpec as P

BF = jnp.bfloat16
F32 = jnp.float32
I32 = jnp.int32
MESH = pl.DeviceIdType.MESH
MIB = 1024 * 1024
LANES = 128
GROUP = 4
TABLE = 1024
EPS = 1e-05
ROOT = 0.7978845608028654
CUBE = 0.044715 * ROOT


def dot(a, b):
    return jnp.dot(a, b, preferred_element_type=F32)


def dot_tn(a, b):
    return lax.dot_general(a, b, (((0,), (0,)), ((), ())), preferred_element_type=F32)


def dot_nt(a, b):
    return lax.dot_general(a, b, (((1,), (1,)), ((), ())), preferred_element_type=F32)


def gelu_pair(v):
    z = v * v
    q = 0.5 + 0.5 * jnp.tanh(v * (ROOT + CUBE * z))
    act = v * q
    slope = q + (act - act * q) * (2.0 * ROOT + 6.0 * CUBE * z)
    return act, slope


def row_mean(v):
    return jnp.mean(v, axis=-1, keepdims=True)


def lane_column(ref, k):
    rows = ref.shape[0]
    return jnp.broadcast_to(pltpu.roll(ref[...], LANES - k, axis=1)[:, 0:1], (rows, LANES))


def pick_rows(target, width):
    lane = lax.broadcasted_iota(I32, target.shape, 1)
    return jnp.concatenate(
        [(target == lane + LANES * c).astype(F32).astype(BF) for c in range(width // LANES)],
        axis=1,
    )


def pick_cols(target, width):
    edges = target.shape[1]
    sub = lax.broadcasted_iota(I32, (width, edges), 0)
    return (jnp.broadcast_to(target, (width, edges)) == sub).astype(F32).astype(BF)


def gather_table(targets, table):
    count = table.shape[0]
    if count <= TABLE:
        hot = jnp.concatenate([pick_rows(t, count) for t in targets], axis=0)
        return dot(hot, table[...])

    def step(c, total):
        base = c * TABLE
        hot = jnp.concatenate([pick_rows(t - base, TABLE) for t in targets], axis=0)
        return total + dot(hot, table[pl.ds(pl.multiple_of(base, TABLE), TABLE), :])

    rows = sum(t.shape[0] for t in targets)
    return lax.fori_loop(0, count // TABLE, step, jnp.zeros((rows, table.shape[1]), F32))


def add_by_target(target, values, total):
    count = total.shape[0]
    if count <= TABLE:
        total[...] += dot(pick_cols(target, count), values)
        return

    def step(c, carry):
        base = c * TABLE
        part = pl.ds(pl.multiple_of(base, TABLE), TABLE)
        total[part, :] += dot(pick_cols(target - base, TABLE), values)
        return carry

    lax.fori_loop(0, count // TABLE, step, 0)


def by_chunks(count, step):
    if count <= TABLE:
        step(pl.ds(0, count))
        return

    def one(c, carry):
        step(pl.ds(pl.multiple_of(c * TABLE, TABLE), TABLE))
        return carry

    lax.fori_loop(0, count // TABLE, one, 0)


def remote(src, dst, send, recv, peer):
    return pltpu.make_async_remote_copy(
        src_ref=src,
        dst_ref=dst,
        send_sem=send,
        recv_sem=recv,
        device_id={"edge": peer},
        device_id_type=MESH,
    )


def greet(peers):
    barrier = pltpu.get_barrier_semaphore()
    for peer in peers:
        pl.semaphore_signal(barrier, inc=1, device_id={"edge": peer}, device_id_type=MESH)
    pl.semaphore_wait(barrier, len(peers))


def block(ref, index, rows):
    return ref.at[pl.ds(pl.multiple_of(index * rows, rows), rows)]


class Place:
    def __init__(self, n):
        self.me = lax.axis_index("edge")
        self.chips = n // 2
        self.chip = self.me // 2
        self.core = lax.rem(self.me, 2)
        self.sibling = self.chip * 2 + 1 - self.core
        self.mates = [self.at(d) for d in range(1, self.chips)]

    def at(self, d):
        return lax.rem(self.chip + d + self.chips, self.chips) * 2 + self.core


def gather_start(place, x, out, send, recv):
    rows, chips = x.shape[0], place.chips
    far = []
    for d in range(1, chips):
        far.append(
            remote(x, block(out, place.me, rows), send.at[d], recv.at[d], place.mates[d - 1])
        )
    near = remote(x, block(out, place.me, rows), send.at[0], recv.at[0], place.sibling)
    for copy in far:
        copy.start()
    near.start()
    return far, near


def gather_finish(place, handles, x, out, send, recv):
    far, near = handles
    rows, chips = x.shape[0], place.chips
    passed = []
    for d in range(1, chips):
        far[d - 1].wait_recv()
        got = block(out, place.at(-d), rows)
        copy = remote(got, got, send.at[chips + d], recv.at[chips + d], place.sibling)
        copy.start()
        passed.append(copy)
    near.wait()
    for copy in passed:
        copy.wait()
    for copy in far:
        copy.wait_send()


def scatter_sum(place, x, pair_buf, send_buf, far_buf, send, recv):
    chips, rows = place.chips, pair_buf.shape[1]
    pairs = []
    for d in range(chips):
        theirs = lax.rem(place.chip + d, chips) * 2 + 1 - place.core
        pairs.append(
            remote(block(x, theirs, rows), pair_buf.at[d], send.at[d], recv.at[d], place.sibling)
        )
    for d in range(1, chips):
        pairs[d].start()
    pairs[0].start()
    far = []
    for d in range(1, chips):
        pairs[d].wait_recv()
        mine = x[pl.ds(pl.multiple_of(place.at(d) * rows, rows), rows), :]
        send_buf[d] = (mine.astype(F32) + pair_buf[d].astype(F32)).astype(BF)
        copy = remote(
            send_buf.at[d], far_buf.at[d], send.at[chips + d], recv.at[chips + d], place.at(d)
        )
        copy.start()
        far.append(copy)
    pairs[0].wait_recv()
    own = x[pl.ds(pl.multiple_of(place.me * rows, rows), rows), :]
    total = own.astype(F32) + pair_buf[0].astype(F32)
    for d in range(1, chips):
        far[d - 1].wait_recv()
        total = total + far_buf[d].astype(F32)
    for d in range(chips):
        pairs[d].wait_send()
    for copy in far:
        copy.wait_send()
    return total


def comm_scratch(n, rows, width):
    return [pltpu.VMEM((n // 2, rows, width), BF)] * 3


def sems(count):
    return [pltpu.SemaphoreType.DMA((count,))] * 2


def remote_params(cid):
    return pltpu.CompilerParams(
        collective_id=cid, has_side_effects=True, vmem_limit_bytes=60 * MIB
    )


LOCAL = pltpu.CompilerParams(vmem_limit_bytes=62 * MIB)
WHOLE = pl.BlockSpec(memory_space=pltpu.VMEM)


def start_kernel(
    n, K, nodes, owner, slot, live, nodes_all, tcol, lcol, trow, count,
    orow, lrow, scol, hist, got, send, recv, hsend, hrecv, own_sem,
):
    place = Place(n)
    rows = nodes.shape[0]
    others = [lax.rem(place.me + d, n) for d in range(1, n)]
    greet(others)
    handles = gather_start(place, nodes, nodes_all, send, recv)
    own = pltpu.make_async_copy(nodes, block(nodes_all, place.me, rows), own_sem.at[0])
    own.start()
    spare = jnp.zeros((LANES - K, rows), I32)
    own_wide = jnp.concatenate([owner[...], spare], axis=0)
    slot_wide = jnp.concatenate([slot[...], spare], axis=0)
    live_wide = jnp.concatenate([live[...], spare], axis=0).astype(F32)
    target = own_wide * rows + slot_wide
    trow[...] = target
    orow[...] = own_wide
    lrow[...] = live_wide
    tcol[...] = jnp.transpose(target)
    lcol[...] = jnp.transpose(live_wide)
    scol[...] = jnp.transpose(slot_wide)

    def tally(g, total):
        ks = [g * GROUP + j for j in range(GROUP)]
        hot = jnp.concatenate([pick_rows(lane_column(scol, k), LANES) for k in ks], axis=0)
        owners = jnp.concatenate([orow[pl.ds(k, 1), :] for k in ks], axis=1)
        lives = jnp.concatenate([lrow[pl.ds(k, 1), :] for k in ks], axis=1)
        sub = lax.broadcasted_iota(I32, (n, GROUP * rows), 0)
        who = jnp.where(
            jnp.broadcast_to(owners, sub.shape) == sub, jnp.broadcast_to(lives, sub.shape), 0.0
        )
        return total + dot(who.astype(BF), hot)

    totals = lax.fori_loop(0, K // GROUP, tally, jnp.zeros((n, LANES), F32))
    for e in range(n):
        hist[e] = jnp.broadcast_to(totals[e : e + 1, :], (8, LANES))
    copies = []
    for d in range(1, n):
        copy = remote(
            hist.at[others[d - 1]], got.at[d], hsend.at[d], hrecv.at[d], others[d - 1]
        )
        copy.start()
        copies.append(copy)
    total = hist[place.me]
    for copy in copies:
        copy.wait_recv()
    for d in range(1, n):
        total = total + got[d]
    count[...] = total
    own.wait()
    gather_finish(place, handles, nodes, nodes_all, send, recv)
    for copy in copies:
        copy.wait_send()


def start_call(n, nodes, owner, slot, live):
    rows, D = nodes.shape
    K = slot.shape[0]
    shape = jax.ShapeDtypeStruct
    return pl.pallas_call(
        functools.partial(start_kernel, n, K),
        in_specs=[WHOLE] * 4,
        out_specs=[WHOLE] * 5,
        out_shape=[
            shape((n * rows, D), BF),
            shape((rows, LANES), I32),
            shape((rows, LANES), F32),
            shape((LANES, rows), I32),
            shape((8, LANES), F32),
        ],
        scratch_shapes=[
            pltpu.VMEM((LANES, rows), I32),
            pltpu.VMEM((LANES, rows), F32),
            pltpu.VMEM((rows, LANES), I32),
            pltpu.VMEM((n, 8, LANES), F32),
            pltpu.VMEM((n, 8, LANES), F32),
            *sems(n),
            *sems(n),
            pltpu.SemaphoreType.DMA((1,)),
        ],
        compiler_params=remote_params(0),
    )(nodes, owner, slot, live)


def slab_pairs(slab, C):
    pairs = slab.shape[1] // (2 * C)
    even = [slab[:, 2 * C * m : 2 * C * m + 256] for m in range(pairs)]
    odd = [slab[:, 2 * C * m + 2 * C - 256 : 2 * C * m + 2 * C] for m in range(pairs)]
    return jnp.concatenate(even, axis=0), jnp.concatenate(odd, axis=0)


def interleave(even, odd, rows):
    parts = []
    for m in range(even.shape[0] // rows):
        parts += [even[m * rows : (m + 1) * rows], odd[m * rows : (m + 1) * rows]]
    return jnp.concatenate(parts, axis=0)


def split_tiles(values, rows):
    count = values.shape[0] // rows
    pick = lambda first: jnp.concatenate(
        [values[k * rows : (k + 1) * rows] for k in range(first, count, 2)], axis=0
    )
    return pick(0), pick(1)


def join_slab(even, odd, rows, C):
    parts = []
    for m in range(even.shape[0] // rows):
        a = even[m * rows : (m + 1) * rows]
        b = odd[m * rows : (m + 1) * rows]
        parts += [a[:, :LANES], a[:, LANES:] + b[:, :LANES], b[:, LANES:]]
    return jnp.concatenate(parts, axis=1)


def message_kernel(
    tiles, C, tcol, lcol, trow, nodes_all, nodes, w1, w2, edges,
    act1, slope1, slope2, summed, p_all, p_own, w_own, total, pre1, pre2,
):
    i = pl.program_id(0)
    rows, D = nodes.shape
    count = nodes_all.shape[0]

    @pl.when(i == 0)
    def _():
        def project(part):
            p_all[part, :] = dot(nodes_all[part, :], w1[D : 2 * D, :]).astype(BF)

        by_chunks(count, project)
        p_own[...] = dot(nodes[...], w1[:D, :])
        w_own[...] = jnp.zeros_like(w_own)
        w_own[0, :C, :] = w1[2 * D :, :]
        w_own[1, 256 - C :, :] = w1[2 * D :, :]
        total[...] = jnp.zeros_like(total)
        pre1[...] = jnp.zeros_like(pre1)
        pre2[...] = jnp.zeros_like(pre2)

    last = jnp.clip(i - 2, 0, tiles - 1)
    ks = [last * GROUP + j for j in range(GROUP)]
    act, slope = gelu_pair(pre2[...])
    live = jnp.concatenate(
        [jnp.concatenate([lane_column(lcol, k)] * (D // LANES), axis=1) for k in ks], axis=0
    )
    slope2[...] = (slope * live).astype(BF)
    live = live * jnp.where(i >= 2, 1.0, 0.0)
    act = (act * live).astype(BF)
    target = jnp.concatenate([trow[pl.ds(k, 1), :] for k in ks], axis=1)
    add_by_target(target, act, total)

    act, slope = gelu_pair(pre1[...])
    act = act.astype(BF)
    act1[...] = act
    slope1[...] = slope.astype(BF)
    pre2[...] = dot(act, w2[...])

    now = jnp.minimum(i, tiles - 1)
    targets = [lane_column(tcol, now * GROUP + j) for j in range(GROUP)]
    even, odd = slab_pairs(edges[...], C)
    base = p_own[...]
    own = interleave(dot(even, w_own[0]), dot(odd, w_own[1]), rows)
    pre1[...] = gather_table(targets, p_all) + own + jnp.concatenate([base] * GROUP, axis=0)

    @pl.when(i == tiles + 1)
    def _():
        summed[...] = total[...].astype(BF)


def full(x):
    return pl.BlockSpec(
        x.shape, lambda g: (0,) * x.ndim, pipeline_mode=pl.Buffered(buffer_count=1)
    )


def message_call(C, tcol, lcol, trow, nodes_all, nodes, w1, w2, edges):
    rows, D = nodes.shape
    count = nodes_all.shape[0]
    K = edges.shape[1] // C
    tiles = K // GROUP
    size = GROUP * rows
    shape = jax.ShapeDtypeStruct
    lag = lambda d: pl.BlockSpec((size, D), lambda g: (jnp.clip(g - d, 0, tiles - 1), 0))
    return pl.pallas_call(
        functools.partial(message_kernel, tiles, C),
        grid=(tiles + 2,),
        in_specs=[full(x) for x in (tcol, lcol, trow, nodes_all, nodes, w1, w2)]
        + [pl.BlockSpec((rows, GROUP * C), lambda g: (0, jnp.minimum(g, tiles - 1)))],
        out_specs=[lag(1), lag(1), lag(2), pl.BlockSpec((count, D), lambda g: (0, 0))],
        out_shape=[shape((K * rows, D), BF)] * 3 + [shape((count, D), BF)],
        scratch_shapes=[
            pltpu.VMEM((count, D), BF),
            pltpu.VMEM((rows, D), F32),
            pltpu.VMEM((2, 256, D), BF),
            pltpu.VMEM((count, D), F32),
            pltpu.VMEM((size, D), F32),
            pltpu.VMEM((size, D), F32),
        ],
        compiler_params=LOCAL,
    )(tcol, lcol, trow, nodes_all, nodes, w1, w2, edges)


def column_of(row):
    return jnp.transpose(jnp.broadcast_to(row, (LANES, row.shape[1])))


def spread(column, width):
    return jnp.concatenate([column] * (width // LANES), axis=1)


def norm_parts(values):
    centred = values - row_mean(values)
    inverse = lax.rsqrt(row_mean(centred * centred) + EPS)
    return centred * inverse, inverse


def node_kernel(
    n, C, summed, count, nodes, w3, g1, o1, wf1, wf2, g2, o2, we1,
    node_out, far_all, near, low_out, n1_out, n2_out, inv_out, act_out, slope_out, sum_out,
    pair_buf, send_buf, far_buf, q_own, send, recv, gsend, grecv, own_sem,
):
    place = Place(n)
    rows, D = nodes.shape
    greet([place.sibling] + place.mates)
    total = scatter_sum(place, summed, pair_buf, send_buf, far_buf, send, recv).astype(BF)
    sum_out[...] = total
    divisor = 1.0 + column_of(count[0:1, :])
    inv_out[2] = divisor
    resid = nodes[...].astype(F32) + dot(total, w3[...]) / spread(divisor, D)
    n1, inv1 = norm_parts(resid)
    n1_out[...] = n1
    inv_out[0] = jnp.broadcast_to(inv1, (rows, LANES))
    normed = n1 * g1[...] + o1[...]
    low = normed.astype(BF)
    low_out[...] = low
    act, slope = gelu_pair(dot(low, wf1[...]))
    act = act.astype(BF)
    act_out[...] = act
    slope_out[...] = slope.astype(BF)
    n2, inv2 = norm_parts(normed + dot(act, wf2[...]))
    n2_out[...] = n2
    inv_out[1] = jnp.broadcast_to(inv2, (rows, LANES))
    node_low = (n2 * g2[...] + o2[...]).astype(BF)
    node_out[...] = node_low
    pad = jnp.zeros((rows, 256 - C), F32)
    far = dot_nt(node_low, we1[:, D : 2 * D])
    q_own[...] = jnp.concatenate([far, pad], axis=1).astype(BF)
    handles = gather_start(place, q_own, far_all, gsend, grecv)
    own = pltpu.make_async_copy(q_own, block(far_all, place.me, rows), own_sem.at[0])
    own.start()
    near[...] = jnp.concatenate([dot_nt(node_low, we1[:, :D]), pad], axis=1)
    own.wait()
    gather_finish(place, handles, q_own, far_all, gsend, grecv)


def node_call(n, C, summed, count, nodes, w3, g1, o1, wf1, wf2, g2, o2, we1):
    rows, D = nodes.shape
    FF = wf1.shape[1]
    shape = jax.ShapeDtypeStruct
    return pl.pallas_call(
        functools.partial(node_kernel, n, C),
        in_specs=[WHOLE] * 11,
        out_specs=[WHOLE] * 10,
        out_shape=[
            shape((rows, D), BF),
            shape((n * rows, 256), BF),
            shape((rows, 256), F32),
            shape((rows, D), BF),
            shape((rows, D), F32),
            shape((rows, D), F32),
            shape((3, rows, LANES), F32),
            shape((rows, FF), BF),
            shape((rows, FF), BF),
            shape((rows, D), BF),
        ],
        scratch_shapes=[
            *comm_scratch(n, rows, D),
            pltpu.VMEM((rows, 256), BF),
            *sems(n),
            *sems(n),
            pltpu.SemaphoreType.DMA((1,)),
        ],
        compiler_params=remote_params(1),
    )(summed, count, nodes, w3, g1, o1, wf1, wf2, g2, o2, we1)


def edge_kernel(
    tiles, C, tcol, trow, far_all, near, we1, we2, we3, gain, offset, edges, cot,
    edge_out, partial, far_sum, near_sum, dw1, dw2, dw3, dgain,
    w1o, w2p, w3o, w1t, w2t, w3t, gains, total, a1, a2, a3, ag,
):
    g = pl.program_id(0)
    rows = near.shape[0]
    D2 = we1.shape[1] - C
    gap = 256 - C

    @pl.when(g == 0)
    def _():
        for ref in (w1o, w2p, w3o, w1t, w2t, w3t, gains, total, a1, a2, a3, ag, near_sum):
            ref[...] = jnp.zeros_like(ref)
        own = jnp.transpose(we1[:, D2:].astype(F32)).astype(BF)
        w1o[0, :C, :C] = own
        w1o[1, gap:, :C] = own
        w2p[:C, :C] = we2[...]
        w3o[0, :C, :C] = we3[...]
        w3o[1, :C, :] = jnp.concatenate([jnp.zeros((C, gap), F32), we3[...].astype(F32)], axis=1).astype(BF)
        for s in range(2):
            w1t[s] = jnp.transpose(w1o[s].astype(F32)).astype(BF)
            w3t[s] = jnp.transpose(w3o[s].astype(F32)).astype(BF)
        w2t[...] = jnp.transpose(w2p[...].astype(F32)).astype(BF)
        zero = jnp.zeros((1, gap), F32)
        gains[0, 0:1] = jnp.concatenate([gain[...], zero], axis=1)
        gains[0, 1:2] = jnp.concatenate([offset[...], zero], axis=1)
        gains[1, 0:1] = jnp.concatenate([zero, gain[...]], axis=1)
        gains[1, 1:2] = jnp.concatenate([zero, offset[...]], axis=1)

    ks = [g * GROUP + j for j in range(GROUP)]
    slabs = slab_pairs(edges[...], C)
    cots = slab_pairs(cot[...], C)
    half = slabs[0].shape[0]
    own = interleave(dot(slabs[0], w1o[0]), dot(slabs[1], w1o[1]), rows)
    base = near[...]
    pre1 = gather_table([lane_column(tcol, k) for k in ks], far_all)
    pre1 = pre1 + own + jnp.concatenate([base] * GROUP, axis=0)
    h1, s1 = gelu_pair(pre1)
    h1 = h1.astype(BF)
    h2, s2 = gelu_pair(dot(h1, w2p[...]))
    h2 = h2.astype(BF)
    h2s = split_tiles(h2, rows)
    lane = lax.broadcasted_iota(I32, (half, 256), 1)
    outs, thirds, lows = [], [], []
    for s in range(2):
        inside = (lane < C) if s == 0 else (lane >= gap)
        keep = lambda v: jnp.where(inside, v, 0.0)
        mean = lambda v: jnp.sum(v, axis=-1, keepdims=True) * (1.0 / C)
        value = keep(slabs[s].astype(F32)) + dot(h2s[s], w3o[s])
        centred = keep(value - mean(value))
        inverse = lax.rsqrt(mean(centred * centred) + EPS)
        normal = centred * inverse
        outs.append(normal * gains[s, 0:1] + gains[s, 1:2])
        upstream = keep(cots[s].astype(F32))
        moved = upstream * normal
        for r in range(half // rows):
            part = slice(r * rows, (r + 1) * rows)
            ag[s, 0] += moved[part]
            ag[s, 1] += upstream[part]
        scaled = upstream * gains[s, 0:1]
        third = inverse * (scaled - mean(scaled) - normal * mean(scaled * normal))
        third = keep(third)
        thirds.append(third)
        low = third.astype(BF)
        lows.append(low)
        a3[s] += dot_tn(h2s[s], low)
    edge_out[...] = join_slab(outs[0], outs[1], rows, C).astype(BF)
    low2 = interleave(dot(lows[0], w3t[0]), dot(lows[1], w3t[1]), rows)
    low2 = (low2 * s2).astype(BF)
    a2[...] += dot_tn(h1, low2)
    low1 = (dot(low2, w2t[...]) * s1).astype(BF)
    low1s = split_tiles(low1, rows)
    for s in range(2):
        a1[s] += dot_tn(low1s[s], slabs[s])
        thirds[s] = thirds[s] + dot(low1s[s], w1t[s])
    partial[...] = join_slab(thirds[0], thirds[1], rows, C)
    wide = low1.astype(F32)
    acc = wide[:rows]
    for j in range(1, GROUP):
        acc = acc + wide[j * rows : (j + 1) * rows]
    near_sum[...] += acc
    target = jnp.concatenate([trow[pl.ds(k, 1), :] for k in ks], axis=1)
    add_by_target(target, low1, total)

    @pl.when(g == tiles - 1)
    def _():
        far_sum[...] = total[...].astype(BF)
        dw1[...] = (jnp.transpose(a1[0])[:C,:] + jnp.transpose(a1[1])[gap:,:])
        dw2[...] = a2[...]
        shifted = a3[1][:, gap:]
        dw3[...] = a3[0] + jnp.concatenate([shifted, jnp.zeros((256, gap), F32)], axis=1)
        for r in range(2):
            even = jnp.sum(ag[0, r], axis=0, keepdims=True)
            odd = jnp.sum(ag[1, r], axis=0, keepdims=True)
            row = even + jnp.concatenate([odd[:, gap:], jnp.zeros((1, gap), F32)], axis=1)
            dgain[r * 8 : r * 8 + 8, :] = jnp.broadcast_to(row, (8, 256))


def edge_call(C, tcol, trow, far_all, near, we1, we2, we3, gain, offset, edges, cot):
    rows = near.shape[0]
    count = far_all.shape[0]
    K = edges.shape[1] // C
    tiles = K // GROUP
    shape = jax.ShapeDtypeStruct
    slab = pl.BlockSpec((rows, GROUP * C), lambda g: (0, g))
    fixed = lambda *s: pl.BlockSpec(s, lambda g: (0,) * len(s))
    return pl.pallas_call(
        functools.partial(edge_kernel, tiles, C),
        grid=(tiles,),
        in_specs=[full(x) for x in (tcol, trow, far_all, near, we1, we2, we3, gain, offset)]
        + [slab, slab],
        out_specs=[
            slab, slab, fixed(count, 256), fixed(rows, 256),
            fixed(C, 256), fixed(256, 256), fixed(256, 256), fixed(16, 256),
        ],
        out_shape=[
            shape((rows, K * C), BF),
            shape((rows, K * C), F32),
            shape((count, 256), BF),
            shape((rows, 256), F32),
            shape((C, 256), F32),
            shape((256, 256), F32),
            shape((256, 256), F32),
            shape((16, 256), F32),
        ],
        scratch_shapes=[
            pltpu.VMEM((2, 256, 256), BF),
            pltpu.VMEM((256, 256), BF),
            pltpu.VMEM((2, 256, 256), BF),
            pltpu.VMEM((2, 256, 256), BF),
            pltpu.VMEM((256, 256), BF),
            pltpu.VMEM((2, 256, 256), BF),
            pltpu.VMEM((2, 8, 256), F32),
            pltpu.VMEM((count, 256), F32),
            pltpu.VMEM((2, 256, 256), F32),
            pltpu.VMEM((256, 256), F32),
            pltpu.VMEM((2, 256, 256), F32),
            pltpu.VMEM((2, 2, rows, 256), F32),
        ],
        compiler_params=LOCAL,
    )(tcol, trow, far_all, near, we1, we2, we3, gain, offset, edges, cot)


def norm_back(upstream, normal, inverse, gain):
    scaled = upstream * gain
    return inverse * (scaled - row_mean(scaled) - normal * row_mean(scaled * normal))


def node_back_kernel(
    n, C, far_sum, near_sum, cot, node_low, n1, n2, inv, act, slope, low, summed,
    w3, g1, wf1, wf2, g2, we1,
    grad_one, vw_all, both, dgain, dw3, dwe_near, dwe_far,
    pair_buf, send_buf, far_buf, v_own, send, recv, gsend, grecv, own_sem,
):
    place = Place(n)
    rows, D = cot.shape
    greet([place.sibling] + place.mates)
    far = scatter_sum(place, far_sum, pair_buf, send_buf, far_buf, send, recv)
    far = far.astype(BF)[:, :C]
    near = near_sum[...].astype(BF)[:, :C]
    grad = cot[...].astype(F32) + dot(near, we1[:, :D]) + dot(far, we1[:, D : 2 * D])
    two = norm_back(grad, n2[...], inv[1][:, 0:1], g2[...])
    dgain[16:24, :] = jnp.broadcast_to(jnp.sum(grad * n2[...], axis=0, keepdims=True), (8, D))
    dgain[24:32, :] = jnp.broadcast_to(jnp.sum(grad, axis=0, keepdims=True), (8, D))
    resid = two.astype(BF)
    both[:, :D] = low[...]
    both[:, D:] = resid
    inner = (dot_nt(resid, wf2[...]) * slope[...].astype(F32)).astype(BF)
    grad = two + dot_nt(inner, wf1[...])
    one = norm_back(grad, n1[...], inv[0][:, 0:1], g1[...])
    dgain[0:8, :] = jnp.broadcast_to(jnp.sum(grad * n1[...], axis=0, keepdims=True), (8, D))
    dgain[8:16, :] = jnp.broadcast_to(jnp.sum(grad, axis=0, keepdims=True), (8, D))
    grad_one[...] = one
    upper = (one / spread(inv[2], D)).astype(BF)
    v_own[...] = dot_nt(upper, w3[...]).astype(BF)
    handles = gather_start(place, v_own, vw_all, gsend, grecv)
    own = pltpu.make_async_copy(v_own, block(vw_all, place.me, rows), own_sem.at[0])
    own.start()
    dw3[...] = dot_tn(summed[...], upper)
    dwe_near[...] = dot_tn(node_low[...], near)
    dwe_far[...] = dot_tn(node_low[...], far)
    own.wait()
    gather_finish(place, handles, v_own, vw_all, gsend, grecv)


def node_back_call(n, C, *args):
    cot, wf1 = args[2], args[13]
    rows, D = cot.shape
    shape = jax.ShapeDtypeStruct
    return pl.pallas_call(
        functools.partial(node_back_kernel, n, C),
        in_specs=[WHOLE] * len(args),
        out_specs=[WHOLE] * 7,
        out_shape=[
            shape((rows, D), F32),
            shape((n * rows, D), BF),
            shape((rows, 2 * D), BF),
            shape((32, D), F32),
            shape((D, D), F32),
            shape((D, C), F32),
            shape((D, C), F32),
        ],
        scratch_shapes=[
            *comm_scratch(n, rows, 256),
            pltpu.VMEM((rows, D), BF),
            *sems(n),
            *sems(n),
            pltpu.SemaphoreType.DMA((1,)),
        ],
        compiler_params=remote_params(2),
    )(*args)


def message_back_kernel(
    tiles, C, tcol, trow, nodes_all, nodes, vw, w1, w2,
    act1, slope1, slope2, edges, partial,
    grad_edges, dw1, dw2, target_sum, source_sum,
    w2t, w_own, w_own_t, total, a2, ae,
):
    g = pl.program_id(0)
    rows, D = nodes.shape
    gap = 256 - C

    @pl.when(g == 0)
    def _():
        for ref in (w_own, total, a2, ae, source_sum):
            ref[...] = jnp.zeros_like(ref)
        w_own[0, :C, :] = w1[2 * D :, :]
        w_own[1, gap:, :] = w1[2 * D :, :]
        for s in range(2):
            w_own_t[s] = jnp.transpose(w_own[s].astype(F32)).astype(BF)
        w2t[...] = jnp.transpose(w2[...].astype(F32)).astype(BF)

    ks = [g * GROUP + j for j in range(GROUP)]
    up = gather_table([lane_column(tcol, k) for k in ks], vw)
    upper = (up * slope2[...].astype(F32)).astype(BF)
    a2[...] += dot_tn(act1[...], upper)
    lower = (dot(upper, w2t[...]) * slope1[...].astype(F32)).astype(BF)
    wide = lower.astype(F32)
    acc = wide[:rows]
    for j in range(1, GROUP):
        acc = acc + wide[j * rows : (j + 1) * rows]
    source_sum[...] += acc
    target = jnp.concatenate([trow[pl.ds(k, 1), :] for k in ks], axis=1)
    add_by_target(target, lower, total)
    slabs = slab_pairs(edges[...], C)
    lowers = split_tiles(lower, rows)
    own = []
    for s in range(2):
        ae[s] += dot_tn(slabs[s], lowers[s])
        own.append(dot(lowers[s], w_own_t[s]))
    grad_edges[...] = partial[...] + join_slab(own[0], own[1], rows, C)

    @pl.when(g == tiles - 1)
    def _():
        target_sum[...] = total[...].astype(BF)
        dw2[...] = a2[...].astype(BF)
        dw1[:D, :] = dot_tn(nodes[...], source_sum[...].astype(BF)).astype(BF)
        dw1[2 * D :, :] = (ae[0][:C, :] + ae[1][gap:, :]).astype(BF)
        a2[...] = jnp.zeros_like(a2)

        def weigh(part):
            a2[...] += dot_tn(nodes_all[part, :], total[part, :].astype(BF))

        by_chunks(vw.shape[0], weigh)
        dw1[D : 2 * D, :] = a2[...].astype(BF)


def message_back_call(C, tcol, trow, nodes_all, nodes, vw, w1, w2, act1, slope1, slope2, edges, partial):
    rows, D = nodes.shape
    count = vw.shape[0]
    K = edges.shape[1] // C
    tiles = K // GROUP
    size = GROUP * rows
    shape = jax.ShapeDtypeStruct
    slab = pl.BlockSpec((rows, GROUP * C), lambda g: (0, g))
    tile = pl.BlockSpec((size, D), lambda g: (g, 0))
    fixed = lambda *s: pl.BlockSpec(
        s, lambda g: (0,) * len(s), pipeline_mode=pl.Buffered(buffer_count=1)
    )
    return pl.pallas_call(
        functools.partial(message_back_kernel, tiles, C),
        grid=(tiles,),
        in_specs=[full(x) for x in (tcol, trow, nodes_all, nodes, vw, w1, w2)]
        + [tile, tile, tile, slab, slab],
        out_specs=[slab, fixed(2 * D + C, D), fixed(D, D), fixed(count, D), fixed(rows, D)],
        out_shape=[
            shape((rows, K * C), F32),
            shape((2 * D + C, D), BF),
            shape((D, D), BF),
            shape((count, D), BF),
            shape((rows, D), F32),
        ],
        scratch_shapes=[
            pltpu.VMEM((D, D), BF),
            pltpu.VMEM((2, 256, D), BF),
            pltpu.VMEM((2, D, 256), BF),
            pltpu.VMEM((count, D), F32),
            pltpu.VMEM((D, D), F32),
            pltpu.VMEM((2, 256, D), F32),
        ],
        compiler_params=LOCAL,
    )(tcol, trow, nodes_all, nodes, vw, w1, w2, act1, slope1, slope2, edges, partial)


def feed_kernel(low, resid, wf1, wf2, dwf1, dwf2):
    @pl.when(pl.program_id(1) == 0)
    def _():
        dwf1[...] = jnp.zeros_like(dwf1)
        dwf2[...] = jnp.zeros_like(dwf2)

    act, slope = gelu_pair(dot(low[...], wf1[...]))
    dwf2[...] += dot_tn(act.astype(BF), resid[...])
    inner = (dot_nt(resid[...], wf2[...]) * slope).astype(BF)
    dwf1[...] += dot_tn(low[...], inner)


def feed_call(both, wf1, wf2):
    count = both.shape[0]
    D, FF = wf1.shape
    step, rows = min(FF, 512), min(count, TABLE)
    shape = jax.ShapeDtypeStruct
    return pl.pallas_call(
        feed_kernel,
        grid=(FF // step, count // rows),
        in_specs=[
            pl.BlockSpec((rows, D), lambda f, r: (r, 0)),
            pl.BlockSpec((rows, D), lambda f, r: (r, 1)),
            pl.BlockSpec((D, step), lambda f, r: (0, f)),
            pl.BlockSpec((step, D), lambda f, r: (f, 0)),
        ],
        out_specs=[
            pl.BlockSpec((D, step), lambda f, r: (0, f)),
            pl.BlockSpec((step, D), lambda f, r: (f, 0)),
        ],
        out_shape=[shape((D, FF), F32), shape((FF, D), F32)],
        compiler_params=LOCAL,
    )(both, both, wf1, wf2)


class Line:
    def __init__(self, place, pieces, x, out, pair_buf, low_buf, high_buf, send_buf, send, recv):
        self.place, self.pieces, self.x, self.out = place, pieces, x, out
        self.pair_buf, self.low_buf, self.high_buf = pair_buf, low_buf, high_buf
        self.send_buf, self.send, self.recv = send_buf, send, recv
        c, q, chips = place.chip, place.core, place.chips
        self.root = chips // 2 - 1 + q
        self.away = jnp.abs(c - self.root)
        self.right = jnp.minimum(c + 1, chips - 1) * 2 + q
        self.left = jnp.maximum(c - 1, 0) * 2 + q
        self.half = x.shape[0] // 2
        self.rows = self.half // pieces

    def part(self, which, p):
        return pl.ds(pl.multiple_of(which * self.half + p * self.rows, self.rows), self.rows)

    def here(self, p):
        return pl.ds(pl.multiple_of(p * self.rows, self.rows), self.rows)

    def link(self, src, dst, p, sent, got, peer):
        n = self.pieces
        return remote(src, dst, self.send.at[sent * n + p], self.recv.at[got * n + p], peer)

    def pair(self, p):
        src = self.x.at[self.part(1 - self.place.core, p)]
        return self.link(src, self.pair_buf.at[self.here(p)], p, 0, 0, self.place.sibling)

    def up(self, p):
        here = self.here(p)
        return self.link(self.send_buf.at[here], self.low_buf.at[here], p, 1, 1, self.right)

    def down(self, p):
        here = self.here(p)
        return self.link(self.send_buf.at[here], self.high_buf.at[here], p, 2, 2, self.left)

    def outward(self, p, sent, got, peer):
        mine = self.out.at[self.part(self.place.core, p)]
        return self.link(mine, mine, p, sent, got, peer)

    def out_left(self, p):
        return self.outward(p, 3, 3, self.left)

    def out_right(self, p):
        return self.outward(p, 5, 3, self.right)

    def across(self, p):
        return self.outward(p, 4, 4, self.place.sibling)

    def each(self, step):
        lax.fori_loop(0, self.pieces, lambda p, z: (step(p), z)[1], 0)

    def start(self):
        self.each(lambda p: self.pair(p).start())

    def reduce(self, p):
        c, root, last = self.place.chip, self.root, self.place.chips - 1
        here, mine_at = self.here(p), self.part(self.place.core, p)
        self.pair(p).wait_recv()
        mine = lambda: self.x[mine_at, :].astype(F32) + self.pair_buf[here, :].astype(F32)

        def end():
            self.send_buf[here, :] = mine().astype(BF)

        def from_low():
            self.up(p).wait_recv()
            self.send_buf[here, :] = (mine() + self.low_buf[here, :].astype(F32)).astype(BF)

        def from_high():
            self.down(p).wait_recv()
            self.send_buf[here, :] = (mine() + self.high_buf[here, :].astype(F32)).astype(BF)

        def at_root():
            self.up(p).wait_recv()
            self.down(p).wait_recv()
            total = mine() + self.low_buf[here, :].astype(F32) + self.high_buf[here, :].astype(F32)
            self.out[mine_at, :] = total.astype(BF)
            self.out_left(p).start()
            self.out_right(p).start()
            self.across(p).start()

        pl.when((c == 0) | (c == last))(end)
        pl.when((c > 0) & (c < root))(from_low)
        pl.when((c > root) & (c < last))(from_high)
        pl.when(c < root)(lambda: self.up(p).start())
        pl.when(c > root)(lambda: self.down(p).start())
        pl.when(c == root)(at_root)

    def spread(self, p):
        c, root, last = self.place.chip, self.root, self.place.chips - 1

        def leftward():
            self.out_left(p).wait_recv()
            pl.when(c > 0)(lambda: self.out_left(p).start())
            self.across(p).start()

        def rightward():
            self.out_right(p).wait_recv()
            pl.when(c < last)(lambda: self.out_right(p).start())
            self.across(p).start()

        pl.when(c < root)(leftward)
        pl.when(c > root)(rightward)

    def slots(self, lag):
        return self.pieces + lag * (self.place.chips // 2)

    def slot(self, s, lag):
        pl.when(s < self.pieces)(lambda: self.reduce(s))
        p = s - lag * self.away
        pl.when((p >= 0) & (p < self.pieces) & (self.away > 0))(lambda: self.spread(p))

    def finish(self):
        c, root, last = self.place.chip, self.root, self.place.chips - 1

        def end(p):
            self.pair(p).wait_send()
            self.across(p).wait_send()
            pl.when(c < root)(lambda: self.up(p).wait_send())
            pl.when(c > root)(lambda: self.down(p).wait_send())
            pl.when((c <= root) & (c > 0))(lambda: self.out_left(p).wait_send())
            pl.when((c >= root) & (c < last))(lambda: self.out_right(p).wait_send())

        self.each(lambda p: self.across(p).wait_recv())
        self.each(end)


def line_scratch(rows, width, pieces):
    return [pltpu.VMEM((rows // 2, width), BF)] * 4 + sems(6 * pieces)


PIECES = 19
LAG = 4


def final_kernel(
    n, C, feed, target_sum, source_sum, grad_one, w1, dw1, dw2, dw3, dwe_near, dwe_far, dwe1, dwe2,
    dwe3, dgain, dg3, *rest,
):
    if feed:
        both, wf1, wf2, grad_nodes, out, small, dwf1, dwf2, *rest = rest
    else:
        grad_nodes, out, small, *rest = rest
    x, gains, others_gains, pair_buf, send_buf, far_buf, send, recv, gsend, grecv, *line_refs = rest
    place = Place(n)
    rows, D = grad_one.shape
    others = [lax.rem(place.me + d, n) for d in range(1, n)]
    greet(others)
    at = 2 * D + C
    x[:at, :] = dw1[...]
    x[at : at + D, :] = dw2[...]
    x[at + D : at + 2 * D, :] = dw3[...].astype(BF)
    at += 2 * D
    spare = jnp.zeros((D, 256 - C), F32)
    edge1 = jnp.concatenate(
        [
            jnp.concatenate([dwe_near[...], spare], axis=1),
            jnp.concatenate([dwe_far[...], spare], axis=1),
            dwe1[...],
        ],
        axis=0,
    ).astype(BF)
    half = edge1.shape[0] // 2
    x[at : at + half, :256] = edge1[:half]
    x[at : at + half, 256:] = edge1[half:]
    at += half
    x[at : at + C, :256] = dwe2[:C, :].astype(BF)
    x[at : at + C, 256:] = dwe3[:C, :].astype(BF)
    line = Line(place, PIECES, x, out, *line_refs)
    line.start()
    gains[...] = jnp.zeros_like(gains)
    for r in range(4):
        gains[r : r + 1, :] = dgain[8 * r : 8 * r + 1, :]
    for r in range(2):
        gains[4 + r : 5 + r, :256] = dg3[8 * r : 8 * r + 1, :]
    copies = []
    for d in range(1, n):
        copy = remote(gains, others_gains.at[place.me], gsend.at[d], grecv.at[d], others[d - 1])
        copy.start()
        copies.append(copy)
    others_gains[place.me] = gains[...]

    def feed_part(f):
        step = 256
        cols = pl.ds(pl.multiple_of(f * step, step), step)
        low, resid = both[:, :D], both[:, D:]
        act, slope = gelu_pair(dot(low, wf1[:, cols]))
        dwf2[cols, :] = dot_tn(act.astype(BF), resid).astype(BF)
        inner = (dot_nt(resid, wf2[cols, :]) * slope).astype(BF)
        dwf1[:, cols] = dot_tn(low, inner).astype(BF)

    parts = wf1.shape[1] // 256 if feed else 0

    def slot(s, carry):
        line.slot(s, LAG)
        if feed:
            pl.when((s % 2 == 1) & (s // 2 < parts))(lambda: feed_part(s // 2))
        return carry

    lax.fori_loop(0, line.slots(LAG), slot, 0)
    total = scatter_sum(place, target_sum, pair_buf, send_buf, far_buf, send, recv)
    source = dot_nt(source_sum[...].astype(BF), w1[:D, :])
    grad_nodes[...] = grad_one[...] + source + dot_nt(total.astype(BF), w1[D : 2 * D, :])
    for copy in copies:
        copy.wait_recv()
    total = others_gains[0]
    for e in range(1, n):
        total = total + others_gains[e]
    small[...] = total
    line.finish()
    for copy in copies:
        copy.wait_send()


def final_call(n, C, feed, args, both, wf1, wf2):
    rows, D = args[2].shape
    FF = wf1.shape[1]
    size = 4 * D + C + (2 * D + C) // 2 + C
    shape = jax.ShapeDtypeStruct
    outs = [shape((rows, D), F32), shape((size, D), BF), shape((8, D), F32)]
    if feed:
        args = [*args, both, wf1, wf2]
        outs += [shape((D, FF), BF), shape((FF, D), BF)]
    return pl.pallas_call(
        functools.partial(final_kernel, n, C, feed),
        in_specs=[WHOLE] * len(args),
        out_specs=[WHOLE] * len(outs),
        out_shape=outs,
        scratch_shapes=[
            pltpu.VMEM((size, D), BF),
            pltpu.VMEM((8, D), F32),
            pltpu.VMEM((n, 8, D), F32),
            *comm_scratch(n, rows, D),
            *sems(n),
            *sems(n),
            *line_scratch(size, D, PIECES),
        ],
        compiler_params=remote_params(3),
    )(*args)


def unpack_kernel(C, steps, sizes, packed, *refs):
    g = pl.program_id(0)
    count = len(sizes)
    plain = refs[: (len(refs) - 3 - count) // 2]
    outs = refs[len(plain) :]
    at = 0
    for size, b in zip(sizes, outs):
        step = size // steps
        b[...] = packed[pl.ds(pl.multiple_of(at + g * step, 16), step), :].astype(F32)
        at += size
    for a, b in zip(plain, outs[count:]):
        b[...] = a[...].astype(F32)
    one, two, three = outs[-3:]

    @pl.when(g == steps - 1)
    def _():
        half = packed.shape[0] - at - C
        for r in range(2):
            left = 256 * r
            flipped = jnp.transpose(packed[at : at + half, left : left + 256].astype(F32))
            one[:, half * r : half * r + half] = flipped[:C, :]
        two[...] = packed[at + half :, :C].astype(F32)
        three[...] = packed[at + half :, 256 : 256 + C].astype(F32)


def unpack_call(C, sizes, packed, arrays):
    steps = 4
    D = packed.shape[1]
    shape = jax.ShapeDtypeStruct
    cut = lambda r, c: pl.BlockSpec((r // steps, c), lambda g: (g, 0))
    fixed = lambda *s: pl.BlockSpec(s, lambda g: (0,) * len(s))
    half = packed.shape[0] - sum(sizes) - C
    last = [(C, 2 * half), (C, C), (C, C)]
    first = [(size, D) for size in sizes] + [v.shape for v in arrays]
    return pl.pallas_call(
        functools.partial(unpack_kernel, C, steps, sizes),
        grid=(steps,),
        in_specs=[full(packed)] + [cut(*v.shape) for v in arrays],
        out_specs=[cut(*v) for v in first] + [fixed(*s) for s in last],
        out_shape=[shape(v, F32) for v in first + last],
        compiler_params=LOCAL,
    )(packed, *arrays)


def body(
    nodes, edges, nbr_owner, nbr_slot, edge_mask, w_msg1, w_msg2, w_msg3, gain_one, offset_one,
    w_ffn1, w_ffn2, gain_two, offset_two, w_edge1, w_edge2, w_edge3, gain_three, offset_three,
    node_cotangent, edge_cotangent,
):
    n = lax.axis_size("edge")
    rows, D = nodes.shape
    C = w_edge2.shape[0]
    we1 = w_edge1.T
    g1, o1, g2, o2 = (v.reshape(1, D) for v in (gain_one, offset_one, gain_two, offset_two))
    nodes_all, tcol, lcol, trow, count = start_call(
        n, nodes, nbr_owner[:, :, 0].T, nbr_slot.T, edge_mask.T
    )
    act1, slope1, slope2, summed = message_call(
        C, tcol, lcol, trow, nodes_all, nodes, w_msg1, w_msg2, edges
    )
    node_out, far_all, near, low, n1, n2, inv, act, slope, own_sum = node_call(
        n, C, summed, count, nodes, w_msg3, g1, o1, w_ffn1, w_ffn2, g2, o2, we1
    )
    edge_out, partial, far_sum, near_sum, dwe1, dwe2, dwe3, dg3 = edge_call(
        C, tcol, trow, far_all, near, we1, w_edge2, w_edge3,
        gain_three.reshape(1, C), offset_three.reshape(1, C), edges, edge_cotangent,
    )
    grad_one, vw_all, both, dgain, dw3, dwe_near, dwe_far = node_back_call(
        n, C, far_sum, near_sum, node_cotangent, node_out, n1, n2, inv, act, slope, low, own_sum,
        w_msg3, g1, w_ffn1, w_ffn2, g2, we1,
    )
    both = lax.all_gather(both, "edge", axis=0, tiled=True)
    grad_edges, dw1, dw2, target_sum, source_sum = message_back_call(
        C, tcol, trow, nodes_all, nodes, vw_all, w_msg1, w_msg2, act1, slope1, slope2, edges, partial,
    )
    feed = both.shape[0] <= TABLE
    grad_nodes, packed, small, *dwf = final_call(
        n, C, feed,
        [target_sum, source_sum, grad_one, w_msg1, dw1, dw2, dw3, dwe_near, dwe_far, dwe1, dwe2, dwe3, dgain, dg3],
        both, w_ffn1, w_ffn2,
    )
    if not feed:
        dwf = feed_call(both, w_ffn1, w_ffn2)
    tot1, tot2, tot3, *dwf_out, we1_t, tot_e2, tot_e3 = unpack_call(
        C, [2 * D + C, D, D], packed, dwf if feed else []
    )
    dwf1, dwf2 = dwf_out if feed else dwf
    return (
        node_out, edge_out, grad_nodes, grad_edges,
        tot1, tot2, tot3, small[0], small[1], dwf1, dwf2, small[2], small[3],
        we1_t.T, tot_e2, tot_e3, small[4, :C], small[5, :C],
    )


def solution(mesh):
    rows = P(("dp", "edge"), None)
    return jax.shard_map(
        body,
        mesh=mesh,
        in_specs=(rows, rows, P(("dp", "edge"), None, None), rows, rows)
        + (P(),) * 14
        + (rows, rows),
        out_specs=(rows,) * 4
        + (P("dp", None),) * 3
        + (P("dp"),) * 2
        + (P("dp", None),) * 2
        + (P("dp"),) * 2
        + (P("dp", None),) * 3
        + (P("dp"),) * 2,
        check_vma=False,
    )
```

```python
import functools

import jax
import jax.numpy as jnp
from jax import lax
from jax.experimental import pallas as pl
from jax.experimental.pallas import tpu as pltpu
from jax.sharding import PartitionSpec as P

BF = jnp.bfloat16
F32 = jnp.float32
I32 = jnp.int32
MESH = pl.DeviceIdType.MESH
MIB = 1024 * 1024
LANES = 128
GROUP = 4
ORDER = (0, 2, 1, 3)
TABLE = 1024
EPS = 1e-05
ROOT = 0.7978845608028654
CUBE = 0.044715 * ROOT


def dot(a, b):
    return jnp.dot(a, b, preferred_element_type=F32)


def dot_tn(a, b):
    return lax.dot_general(a, b, (((0,), (0,)), ((), ())), preferred_element_type=F32)


def dot_nt(a, b):
    return lax.dot_general(a, b, (((1,), (1,)), ((), ())), preferred_element_type=F32)


def gelu_pair(v):
    v = v.astype(BF)
    c = lambda x: jnp.asarray(x, BF)
    z = v * v
    q = c(0.5) + c(0.5) * jnp.tanh(v * (c(ROOT) + c(CUBE) * z))
    act = v * q
    slope = q + (act - act * q) * (c(2.0 * ROOT) + c(6.0 * CUBE) * z)
    return act, slope


def gelu_full(v):
    z = v * v
    q = 0.5 + 0.5 * jnp.tanh(v * (ROOT + CUBE * z))
    act = v * q
    slope = q + (act - act * q) * (2.0 * ROOT + 6.0 * CUBE * z)
    return act.astype(BF), slope.astype(BF)


def row_mean(v):
    return jnp.mean(v, axis=-1, keepdims=True)


def lane_column(ref, k):
    rows = ref.shape[0]
    return jnp.broadcast_to(pltpu.roll(ref[...], LANES - k, axis=1)[:, 0:1], (rows, LANES))


def pick_rows(target, width):
    lane = lax.broadcasted_iota(I32, target.shape, 1)
    one, nil = jnp.ones((), BF), jnp.zeros((), BF)
    t16, l16 = target.astype(jnp.int16), lane.astype(jnp.int16)
    return jnp.concatenate(
        [jnp.where(t16 == l16 + jnp.int16(LANES * c), one, nil) for c in range(width // LANES)], axis=1)


def pick_cols(target, width):
    edges = target.shape[1]
    sub = lax.broadcasted_iota(I32, (width, edges), 0)
    return jnp.where(jnp.broadcast_to(target, (width, edges)).astype(jnp.int16) == sub.astype(jnp.int16), jnp.ones((), BF), jnp.zeros((), BF))


def gather_table(targets, table):
    count = table.shape[0]
    if count <= TABLE:
        hot = jnp.concatenate([pick_rows(t, count) for t in targets], axis=0)
        return dot(hot, table[...])

    def step(c, total):
        base = c * TABLE
        hot = jnp.concatenate([pick_rows(t - base, TABLE) for t in targets], axis=0)
        return total + dot(hot, table[pl.ds(pl.multiple_of(base, TABLE), TABLE), :])

    rows = sum(t.shape[0] for t in targets)
    return lax.fori_loop(0, count // TABLE, step, jnp.zeros((rows, table.shape[1]), F32))


def add_by_target(target, values, total):
    count = total.shape[0]
    if count <= TABLE:
        total[...] += dot(pick_cols(target, count), values)
        return

    def step(c, carry):
        base = c * TABLE
        part = pl.ds(pl.multiple_of(base, TABLE), TABLE)
        total[part, :] += dot(pick_cols(target - base, TABLE), values)
        return carry

    lax.fori_loop(0, count // TABLE, step, 0)


def by_chunks(count, step):
    if count <= TABLE:
        step(pl.ds(0, count))
        return

    def one(c, carry):
        step(pl.ds(pl.multiple_of(c * TABLE, TABLE), TABLE))
        return carry

    lax.fori_loop(0, count // TABLE, one, 0)


def remote(src, dst, send, recv, peer):
    return pltpu.make_async_remote_copy(
        src_ref=src,
        dst_ref=dst,
        send_sem=send,
        recv_sem=recv,
        device_id={"edge": peer},
        device_id_type=MESH,
    )


def greet(peers):
    barrier = pltpu.get_barrier_semaphore()
    for peer in peers:
        pl.semaphore_signal(barrier, inc=1, device_id={"edge": peer}, device_id_type=MESH)
    pl.semaphore_wait(barrier, len(peers))


def block(ref, index, rows):
    return ref.at[pl.ds(pl.multiple_of(index * rows, rows), rows)]


class Place:
    def __init__(self, n):
        self.me = lax.axis_index("edge")
        self.chips = n // 2
        self.chip = self.me // 2
        self.core = lax.rem(self.me, 2)
        self.sibling = self.chip * 2 + 1 - self.core
        self.mates = [self.at(d) for d in range(1, self.chips)]

    def at(self, d):
        return lax.rem(self.chip + d + self.chips, self.chips) * 2 + self.core


class Gather:
    def __init__(self, place, x, out, send, recv):
        rows, chips = x.shape[0], place.chips
        mine = block(out, place.me, rows)
        self.near = remote(x, mine, send.at[0], recv.at[0], place.sibling)
        self.far, self.passed = [], []
        for d in range(1, chips):
            self.far.append(remote(x, mine, send.at[d], recv.at[d], place.mates[d - 1]))
            got = block(out, place.at(-d), rows)
            at = chips + d
            self.passed.append(remote(got, got, send.at[at], recv.at[at], place.sibling))

    def start(self):
        for copy in self.far:
            copy.start()
        self.near.start()

    def finish(self):
        for far, passed in zip(self.far, self.passed):
            far.wait_recv()
            passed.start()
        self.near.wait()
        for copy in self.passed:
            copy.wait()
        for copy in self.far:
            copy.wait_send()


class Scatter:
    def __init__(self, place, x, pair_buf, far_buf, send, recv):
        self.place, self.x = place, x
        self.pair_buf, self.far_buf = pair_buf, far_buf
        chips, self.rows = place.chips, pair_buf.shape[1]
        self.pairs, self.far = [], []
        for d in range(chips):
            theirs = lax.rem(place.chip + d, chips) * 2 + 1 - place.core
            src = block(x, theirs, self.rows)
            self.pairs.append(remote(src, pair_buf.at[d], send.at[d], recv.at[d], place.sibling))
        for d in range(1, chips):
            at = chips + d
            self.far.append(
                remote(pair_buf.at[d], far_buf.at[d], send.at[at], recv.at[at], place.at(d))
            )

    def start(self):
        for copy in self.pairs[1:]:
            copy.start()
        self.pairs[0].start()

    def pass_on(self):
        for d in range(1, self.place.chips):
            self.pairs[d].wait_recv()
            at = pl.ds(pl.multiple_of(self.place.at(d) * self.rows, self.rows), self.rows)
            mine = self.x[at, :].astype(F32) + self.pair_buf[d].astype(F32)
            self.pair_buf[d] = mine.astype(BF)
            self.far[d - 1].start()

    def finish(self):
        self.pairs[0].wait_recv()
        at = pl.ds(pl.multiple_of(self.place.me * self.rows, self.rows), self.rows)
        total = self.x[at, :].astype(F32) + self.pair_buf[0].astype(F32)
        for d in range(1, self.place.chips):
            self.far[d - 1].wait_recv()
            total = total + self.far_buf[d].astype(F32)
        for copy in self.pairs + self.far:
            copy.wait_send()
        return total


def scatter_sum(*refs):
    scatter = Scatter(*refs)
    scatter.start()
    scatter.pass_on()
    return scatter.finish()


def comm_scratch(n, rows, width):
    return [pltpu.VMEM((n // 2, rows, width), BF)] * 2


def sems(count):
    return [pltpu.SemaphoreType.DMA((count,))] * 2


def remote_params(cid):
    return pltpu.CompilerParams(
        collective_id=cid, has_side_effects=True, vmem_limit_bytes=62 * MIB
    )


LOCAL = pltpu.CompilerParams(vmem_limit_bytes=62 * MIB)
WHOLE = pl.BlockSpec(memory_space=pltpu.VMEM)


def slab_pairs(slab, C):
    pairs = slab.shape[1] // (2 * C)
    even = [slab[:, 2 * C * m : 2 * C * m + 256] for m in range(pairs)]
    odd = [slab[:, 2 * C * m + 2 * C - 256 : 2 * C * m + 2 * C] for m in range(pairs)]
    return jnp.concatenate(even, axis=0), jnp.concatenate(odd, axis=0)


def interleave(even, odd, rows):
    parts = []
    for m in range(even.shape[0] // rows):
        parts += [even[m * rows : (m + 1) * rows], odd[m * rows : (m + 1) * rows]]
    return jnp.concatenate(parts, axis=0)


def split_tiles(values, rows):
    count = values.shape[0] // rows
    pick = lambda first: jnp.concatenate(
        [values[k * rows : (k + 1) * rows] for k in range(first, count, 2)], axis=0
    )
    return pick(0), pick(1)


def join_slab(even, odd, rows, C):
    parts = []
    for m in range(even.shape[0] // rows):
        a = even[m * rows : (m + 1) * rows]
        b = odd[m * rows : (m + 1) * rows]
        parts += [a[:, :LANES], a[:, LANES:] + b[:, :LANES], b[:, LANES:]]
    return jnp.concatenate(parts, axis=1)


class Loads:
    def __init__(self, pairs, sem):
        self.copies = [
            pltpu.make_async_copy(src, dst, sem.at[j]) for j, (src, dst) in enumerate(pairs)
        ]

    def start(self):
        for copy in self.copies:
            copy.start()

    def wait(self, first=0, last=None):
        for copy in self.copies[first:last]:
            copy.wait()


def column_of(row):
    return jnp.transpose(jnp.broadcast_to(row, (LANES, row.shape[1])))


def spread(column, width):
    return jnp.concatenate([column] * (width // LANES), axis=1)


def norm_parts(values):
    centred = values - row_mean(values)
    inverse = lax.rsqrt(row_mean(centred * centred) + EPS)
    return centred * inverse, inverse


def forward_kernel(
    n, K, C, nodes, owner, slot, live, g1, o1, g2, o2, w1_h, w2_h, w3_h, wf1_h, wf2_h, we1_h, edges,
    act1, slope1, slope2, tcol, trow, node_out, near, low_out, n1_out, n2_out, inv_out, act_out,
    slope_out, sum_out, nodes_h, far_h,
    w1, w2, w3, wf1, wf2, we1, load_sem,
    nodes_all, far_all, lcol, orow, lrow, scol, hist, hist_got, count,
    p_all, p_own, w_own, pre2, total, summed, q_own, pair_buf, far_buf,
    send, recv, hsend, hrecv, rsend, rrecv, qsend, qrecv, own_sem,
):
    i = pl.program_id(0)
    rows, D = nodes.shape
    tiles = K // GROUP
    size = GROUP * rows
    if n * rows > TABLE:
        p_all = summed = nodes_all
    place = Place(n)
    others = [lax.rem(place.me + d, n) for d in range(1, n)]
    loads = Loads(
        [(w1_h, w1), (w2_h, w2), (w3_h, w3), (wf1_h, wf1), (wf2_h, wf2), (we1_h, we1)], load_sem
    )
    keep_nodes = pltpu.make_async_copy(nodes_all, nodes_h, own_sem.at[1])

    @pl.when(i == 0)
    def _():
        loads.start()
        spare = jnp.zeros((LANES - K, rows), I32)
        own_wide = jnp.concatenate([owner[...], spare], axis=0)
        slot_wide = jnp.concatenate([slot[...], spare], axis=0)
        live_wide = jnp.concatenate([live[...], spare], axis=0).astype(F32)
        target = own_wide * rows + slot_wide
        trow[...] = target
        orow[...] = own_wide
        lrow[...] = live_wide
        tcol[...] = jnp.transpose(target)
        lcol[...] = jnp.transpose(live_wide)
        scol[...] = jnp.transpose(slot_wide)
        pre2[...] = jnp.zeros_like(pre2)
        total[...] = jnp.zeros_like(total)
        w_own[...] = jnp.zeros_like(w_own)
        greet(others)
        gather = Gather(place, nodes, nodes_all, send, recv)
        gather.start()
        own = pltpu.make_async_copy(nodes, block(nodes_all, place.me, rows), own_sem.at[0])
        own.start()

        def tally(g, total):
            ks = [g * GROUP + j for j in range(GROUP)]
            hot = jnp.concatenate([pick_rows(lane_column(scol, k), LANES) for k in ks], axis=0)
            owners = jnp.concatenate([orow[pl.ds(k, 1), :] for k in ks], axis=1)
            lives = jnp.concatenate([lrow[pl.ds(k, 1), :] for k in ks], axis=1)
            sub = lax.broadcasted_iota(I32, (n, size), 0)
            who = jnp.where(
                jnp.broadcast_to(owners, sub.shape) == sub, jnp.broadcast_to(lives, sub.shape), 0.0
            )
            return total + dot(who.astype(BF), hot)

        totals = lax.fori_loop(0, tiles, tally, jnp.zeros((n, LANES), F32))
        for e in range(n):
            hist[e] = jnp.broadcast_to(totals[e : e + 1, :], (8, LANES))
        copies = []
        for d in range(1, n):
            peer = others[d - 1]
            copy = remote(hist.at[peer], hist_got.at[d], hsend.at[d], hrecv.at[d], peer)
            copy.start()
            copies.append(copy)
        loads.wait(0, 2)
        p_own[...] = dot(nodes[...], w1[:D, :])
        w_own[0, :C, :] = w1[2 * D :, :]
        w_own[1, 256 - C :, :] = w1[2 * D :, :]
        tallied = hist[place.me]
        for copy in copies:
            copy.wait_recv()
        for d in range(1, n):
            tallied = tallied + hist_got[d]
        count[...] = tallied
        own.wait()
        gather.finish()
        for copy in copies:
            copy.wait_send()
        keep_nodes.start()
        if n * rows > TABLE:
            keep_nodes.wait()

        def project(part):
            p_all[part, :] = dot(nodes_all[part, :], w1[D : 2 * D, :]).astype(BF)

        by_chunks(n * rows, project)

    last = jnp.clip(i - 1, 0, tiles - 1)
    ks = [last * GROUP + j for j in ORDER]
    act, slope = gelu_pair(pre2[...])
    alive = jnp.concatenate(
        [jnp.concatenate([lane_column(lcol, k)] * (D // LANES), axis=1) for k in ks], axis=0
    ).astype(BF)
    slope2[...] = slope * alive
    act = act * (alive * jnp.where(i >= 1, 1.0, 0.0).astype(BF))
    target = jnp.concatenate([trow[pl.ds(k, 1), :] for k in ks], axis=1)
    add_by_target(target, act, total)

    now = jnp.minimum(i, tiles - 1)
    targets = [lane_column(tcol, now * GROUP + j) for j in ORDER]
    even, odd = slab_pairs(edges[...], C)
    own = jnp.concatenate([dot(even, w_own[0]), dot(odd, w_own[1])], axis=0)
    act, slope = gelu_pair(
        gather_table(targets, p_all) + own + jnp.concatenate([p_own[...]] * GROUP, axis=0)
    )
    act1[...] = act
    slope1[...] = slope
    pre2[...] = dot(act, w2[...])

    @pl.when(i == tiles)
    def _():
        summed[...] = total[...].astype(BF)
        scatter = Scatter(place, summed, pair_buf, far_buf, rsend, rrecv)
        scatter.start()
        scatter.pass_on()
        if n * rows <= TABLE:
            keep_nodes.wait()
        loads.wait(2)
        divisor = 1.0 + column_of(count[0:1, :])
        inv_out[2] = divisor
        mine = scatter.finish().astype(BF)
        sum_out[...] = mine
        resid = nodes[...].astype(F32) + dot(mine, w3[...]) / spread(divisor, D)
        n1, inv1 = norm_parts(resid)
        n1_out[...] = n1
        inv_out[0] = jnp.broadcast_to(inv1, (rows, LANES))
        normed = n1 * g1[...] + o1[...]
        low = normed.astype(BF)
        low_out[...] = low
        act, slope = gelu_full(dot(low, wf1[...]))
        act_out[...] = act
        slope_out[...] = slope
        n2, inv2 = norm_parts(normed + dot(act, wf2[...]))
        n2_out[...] = n2
        inv_out[1] = jnp.broadcast_to(inv2, (rows, LANES))
        node_low = (n2 * g2[...] + o2[...]).astype(BF)
        node_out[...] = node_low
        pad = jnp.zeros((rows, 256 - C), F32)
        far = dot_nt(node_low, we1[:, D : 2 * D])
        q_own[...] = jnp.concatenate([far, pad], axis=1).astype(BF)
        gather = Gather(place, q_own, far_all, qsend, qrecv)
        gather.start()
        own = pltpu.make_async_copy(q_own, block(far_all, place.me, rows), own_sem.at[0])
        own.start()
        near[...] = jnp.concatenate([dot_nt(node_low, we1[:, :D]), pad], axis=1)
        own.wait()
        gather.finish()
        keep_far = pltpu.make_async_copy(far_all, far_h, own_sem.at[2])
        keep_far.start()
        keep_far.wait()


def full(x):
    return pl.BlockSpec(
        x.shape, lambda g: (0,) * x.ndim, pipeline_mode=pl.Buffered(buffer_count=1)
    )


def fixed(*s):
    return pl.BlockSpec(s, lambda g: (0,) * len(s), pipeline_mode=pl.Buffered(buffer_count=1))


HBM = pl.BlockSpec(memory_space=pl.ANY)


def forward_call(n, C, nodes, owner, slot, live, g1, o1, g2, o2, weights, edges):
    rows, D = nodes.shape
    K = slot.shape[0]
    FF = weights[3].shape[1]
    tiles = K // GROUP
    size = GROUP * rows
    count = n * rows
    other = count if count <= TABLE else 16
    shape = jax.ShapeDtypeStruct
    lag = lambda d: pl.BlockSpec((size, D), lambda g: (jnp.clip(g - d, 0, tiles - 1), 0))
    small = [nodes, owner, slot, live, g1, o1, g2, o2]
    outs = [
        shape((LANES, rows), I32),
        shape((LANES, rows), I32),
        shape((rows, D), BF),
        shape((rows, 256), F32),
        shape((rows, D), BF),
        shape((rows, D), F32),
        shape((rows, D), F32),
        shape((3, rows, LANES), F32),
        shape((rows, FF), BF),
        shape((rows, FF), BF),
        shape((rows, D), BF),
    ]
    outs[0] = shape((rows, LANES), I32)
    return pl.pallas_call(
        functools.partial(forward_kernel, n, K, C),
        grid=(tiles + 1,),
        in_specs=[full(v) for v in small]
        + [HBM] * 6
        + [pl.BlockSpec((rows, GROUP * C), lambda g: (0, jnp.minimum(g, tiles - 1)))],
        out_specs=[lag(0), lag(0), lag(1)] + [fixed(*v.shape) for v in outs] + [HBM] * 2,
        out_shape=[shape((K * rows, D), BF)] * 3
        + outs
        + [shape((count, D), BF), shape((count, 256), BF)],
        scratch_shapes=[pltpu.VMEM(v.shape, BF) for v in weights]
        + [
            pltpu.SemaphoreType.DMA((6,)),
            pltpu.VMEM((count, D), BF),
            pltpu.VMEM((count, 256), BF),
            pltpu.VMEM((rows, LANES), F32),
            pltpu.VMEM((LANES, rows), I32),
            pltpu.VMEM((LANES, rows), F32),
            pltpu.VMEM((rows, LANES), I32),
            pltpu.VMEM((n, 8, LANES), F32),
            pltpu.VMEM((n, 8, LANES), F32),
            pltpu.VMEM((8, LANES), F32),
            pltpu.VMEM((other, D), BF),
            pltpu.VMEM((rows, D), F32),
            pltpu.VMEM((2, 256, D), BF),
            pltpu.VMEM((size, D), F32),
            pltpu.VMEM((count, D), F32),
            pltpu.VMEM((other, D), BF),
            pltpu.VMEM((rows, 256), BF),
            *comm_scratch(n, rows, D),
            *sems(n),
            *sems(n),
            *sems(n),
            *sems(n),
            pltpu.SemaphoreType.DMA((3,)),
        ],
        compiler_params=remote_params(0),
    )(*small, *weights, edges)


def edge_kernel(
    tiles, C, tcol, trow, far_all, near, we1, we2, we3, gain, offset, edges1, edges4, edges6, cot,
    edge_out, partial, far_sum, near_sum, dw1, dw2, dw3, dgain,
    w1o, w2p, w3o, w1t, w2t, w3t, gains, total, a1, a2, a3, ag,
    pre1, hid1, slope1, pre2, hid2, slope2, res3, third, up2, up1,
):
    i = pl.program_id(0)
    rows = near.shape[0]
    D2 = we1.shape[1] - C
    gap = 256 - C
    half = GROUP // 2 * rows

    @pl.when(i == 0)
    def _():
        for ref in (w1o, w2p, w3o, w1t, w2t, w3t, gains, total, a1, a2, a3, ag, near_sum,
                    pre1, hid1, slope1, pre2, hid2, slope2, res3, third, up2, up1):
            ref[...] = jnp.zeros_like(ref)
        own = jnp.transpose(we1[:, D2:].astype(F32)).astype(BF)
        w1o[0, :C, :C] = own
        w1o[1, gap:, :C] = own
        w2p[:C, :C] = we2[...]
        w3o[0, :C, :C] = we3[...]
        w3o[1, :C, :] = jnp.concatenate([jnp.zeros((C, gap), F32), we3[...].astype(F32)], axis=1).astype(BF)
        for s in range(2):
            w1t[s] = jnp.transpose(w1o[s].astype(F32)).astype(BF)
            w3t[s] = jnp.transpose(w3o[s].astype(F32)).astype(BF)
        w2t[...] = jnp.transpose(w2p[...].astype(F32)).astype(BF)
        zero = jnp.zeros((1, gap), F32)
        gains[0, 0:1] = jnp.concatenate([gain[...], zero], axis=1)
        gains[0, 1:2] = jnp.concatenate([offset[...], zero], axis=1)
        gains[1, 0:1] = jnp.concatenate([zero, gain[...]], axis=1)
        gains[1, 1:2] = jnp.concatenate([zero, offset[...]], axis=1)

    tile = lambda d: jnp.clip(i - d, 0, tiles - 1)
    sides = [slice(0, half), slice(half, 2 * half)]

    t4 = tile(1)
    valid = jnp.where(i >= 1, 1.0, 0.0)
    slabs = slab_pairs(edges4[...], C)
    cots = slab_pairs(cot[...], C)
    lane = lax.broadcasted_iota(I32, (half, 256), 1)
    outs, grads, ups = [], [], []
    for s in range(2):
        inside = (lane < C) if s == 0 else (lane >= gap)
        keep = lambda v: jnp.where(inside, v, 0.0)
        mean = lambda v: jnp.sum(v, axis=-1, keepdims=True) * (1.0 / C)
        value = keep(slabs[s].astype(F32)) + res3[sides[s], :]
        centred = keep(value - mean(value))
        inverse = lax.rsqrt(mean(centred * centred) + EPS)
        normal = centred * inverse
        outs.append(normal * gains[s, 0:1] + gains[s, 1:2])
        upstream = keep(cots[s].astype(F32)) * valid
        moved = upstream * normal
        for r in range(half // rows):
            part = slice(r * rows, (r + 1) * rows)
            ag[s, 0] += moved[part]
            ag[s, 1] += upstream[part]
        scaled = upstream * gains[s, 0:1]
        grad = inverse * (scaled - mean(scaled) - normal * mean(scaled * normal))
        grad = keep(grad)
        grads.append(grad)
        low3 = grad.astype(BF)
        a3[s] += dot_tn(hid2[sides[s], :], low3)
        ups.append(dot(low3, w3t[s]))
    edge_out[...] = join_slab(outs[0], outs[1], rows, C).astype(BF)

    t5 = tile(1)
    low2 = (jnp.concatenate(ups, axis=0) * slope2[0].astype(F32)).astype(BF)
    a2[...] += dot_tn(hid1[0], low2)
    up1v = dot(low2, w2t[...])

    t6 = tile(1)
    low1 = (up1v * slope1[0].astype(F32)).astype(BF)
    slabs = slab_pairs(edges4[...], C)
    outs = []
    for s in range(2):
        a1[s] += dot_tn(low1[sides[s]], slabs[s])
        outs.append(grads[s] + dot(low1[sides[s]], w1t[s]))
    partial[...] = join_slab(outs[0], outs[1], rows, C).astype(BF)
    wide = low1.astype(F32)
    acc = wide[:rows]
    for j in range(1, GROUP):
        acc = acc + wide[j * rows : (j + 1) * rows]
    near_sum[...] += acc
    target = jnp.concatenate([trow[pl.ds(t6 * GROUP + j, 1), :] for j in ORDER], axis=1)
    add_by_target(target, low1, total)

    t1 = tile(0)
    slabs = slab_pairs(edges1[...], C)
    own = jnp.concatenate([dot(slabs[0], w1o[0]), dot(slabs[1], w1o[1])], axis=0)
    got = gather_table([lane_column(tcol, t1 * GROUP + j) for j in ORDER], far_all)
    pre1v = got + own + jnp.concatenate([near[...]] * GROUP, axis=0)

    t2 = tile(0)
    act, slope = gelu_pair(pre1v)
    hid1[0] = act
    slope1[0] = slope
    pre2v = dot(act, w2p[...])

    t3 = tile(0)
    act, slope = gelu_pair(pre2v)
    hid2[...] = act
    slope2[0] = slope
    for s in range(2):
        res3[sides[s], :] = dot(act[sides[s]], w3o[s])

    @pl.when(i == tiles)
    def _():
        far_sum[...] = total[...].astype(BF)
        dw1[...] = jnp.transpose(a1[0])[:C, :] + jnp.transpose(a1[1])[gap:, :]
        dw2[...] = a2[...]
        shifted = a3[1][:, gap:]
        dw3[...] = a3[0] + jnp.concatenate([shifted, jnp.zeros((256, gap), F32)], axis=1)
        for r in range(2):
            even = jnp.sum(ag[0, r], axis=0, keepdims=True)
            odd = jnp.sum(ag[1, r], axis=0, keepdims=True)
            row = even + jnp.concatenate([odd[:, gap:], jnp.zeros((1, gap), F32)], axis=1)
            dgain[r * 8 : r * 8 + 8, :] = jnp.broadcast_to(row, (8, 256))


def edge_call(C, tcol, trow, far_all, near, we1, we2, we3, gain, offset, edges, cot):
    rows = near.shape[0]
    count = far_all.shape[0]
    K = edges.shape[1] // C
    tiles = K // GROUP
    size = GROUP * rows
    shape = jax.ShapeDtypeStruct
    slab = lambda d: pl.BlockSpec(
        (rows, GROUP * C), lambda g: (0, jnp.clip(g - d, 0, tiles - 1))
    )
    fixed = lambda *s: pl.BlockSpec(
        s, lambda g: (0,) * len(s), pipeline_mode=pl.Buffered(buffer_count=1)
    )
    return pl.pallas_call(
        functools.partial(edge_kernel, tiles, C),
        grid=(tiles + 1,),
        in_specs=[full(x) for x in (tcol, trow, far_all, near, we1, we2, we3, gain, offset)]
        + [slab(0), slab(1), slab(99), slab(1)],
        out_specs=[
            slab(1), slab(1), fixed(count, 256), fixed(rows, 256),
            fixed(C, 256), fixed(256, 256), fixed(256, 256), fixed(16, 256),
        ],
        out_shape=[
            shape((rows, K * C), BF),
            shape((rows, K * C), BF),
            shape((count, 256), BF),
            shape((rows, 256), F32),
            shape((C, 256), F32),
            shape((256, 256), F32),
            shape((256, 256), F32),
            shape((16, 256), F32),
        ],
        scratch_shapes=[
            pltpu.VMEM((2, 256, 256), BF),
            pltpu.VMEM((256, 256), BF),
            pltpu.VMEM((2, 256, 256), BF),
            pltpu.VMEM((2, 256, 256), BF),
            pltpu.VMEM((256, 256), BF),
            pltpu.VMEM((2, 256, 256), BF),
            pltpu.VMEM((2, 8, 256), F32),
            pltpu.VMEM((count, 256), F32),
            pltpu.VMEM((2, 256, 256), F32),
            pltpu.VMEM((256, 256), F32),
            pltpu.VMEM((2, 256, 256), F32),
            pltpu.VMEM((2, 2, rows, 256), F32),
            pltpu.VMEM((size, 256), F32),
            pltpu.VMEM((3, size, 256), BF),
            pltpu.VMEM((4, size, 256), BF),
            pltpu.VMEM((size, 256), F32),
            pltpu.VMEM((size, 256), BF),
            pltpu.VMEM((2, size, 256), BF),
            pltpu.VMEM((size, 256), F32),
            pltpu.VMEM((2, size, 256), F32),
            pltpu.VMEM((size, 256), F32),
            pltpu.VMEM((size, 256), F32),
        ],
        compiler_params=LOCAL,
    )(tcol, trow, far_all, near, we1, we2, we3, gain, offset, edges, edges, edges, cot)


def norm_back(upstream, normal, inverse, gain):
    scaled = upstream * gain
    return inverse * (scaled - row_mean(scaled) - normal * row_mean(scaled * normal))


def node_back_kernel(
    n, C, far_sum, near_sum, cot, node_low, n1, n2, inv, act, slope, low, summed,
    w3, g1, wf1, wf2, g2, we1,
    grad_one, vw_all, both, dgain, dw3, dwe_near, dwe_far,
    pair_buf, far_buf, v_own, send, recv, gsend, grecv, own_sem,
):
    place = Place(n)
    rows, D = cot.shape
    greet([place.sibling] + place.mates)
    far = scatter_sum(place, far_sum, pair_buf, far_buf, send, recv)
    far = far.astype(BF)[:, :C]
    near = near_sum[...].astype(BF)[:, :C]
    grad = cot[...].astype(F32) + dot(near, we1[:, :D]) + dot(far, we1[:, D : 2 * D])
    two = norm_back(grad, n2[...], inv[1][:, 0:1], g2[...])
    dgain[16:24, :] = jnp.broadcast_to(jnp.sum(grad * n2[...], axis=0, keepdims=True), (8, D))
    dgain[24:32, :] = jnp.broadcast_to(jnp.sum(grad, axis=0, keepdims=True), (8, D))
    resid = two.astype(BF)
    both[:, :D] = low[...]
    both[:, D:] = resid
    inner = (dot_nt(resid, wf2[...]) * slope[...].astype(F32)).astype(BF)
    grad = two + dot_nt(inner, wf1[...])
    one = norm_back(grad, n1[...], inv[0][:, 0:1], g1[...])
    dgain[0:8, :] = jnp.broadcast_to(jnp.sum(grad * n1[...], axis=0, keepdims=True), (8, D))
    dgain[8:16, :] = jnp.broadcast_to(jnp.sum(grad, axis=0, keepdims=True), (8, D))
    grad_one[...] = one
    upper = (one / spread(inv[2], D)).astype(BF)
    v_own[...] = dot_nt(upper, w3[...]).astype(BF)
    gather = Gather(place, v_own, vw_all, gsend, grecv)
    gather.start()
    own = pltpu.make_async_copy(v_own, block(vw_all, place.me, rows), own_sem.at[0])
    own.start()
    dw3[...] = dot_tn(summed[...], upper)
    dwe_near[...] = dot_tn(node_low[...], near)
    dwe_far[...] = dot_tn(node_low[...], far)
    own.wait()
    gather.finish()


def node_back_call(n, C, *args):
    cot, wf1 = args[2], args[13]
    rows, D = cot.shape
    shape = jax.ShapeDtypeStruct
    return pl.pallas_call(
        functools.partial(node_back_kernel, n, C),
        in_specs=[WHOLE] * len(args),
        out_specs=[WHOLE] * 7,
        out_shape=[
            shape((rows, D), F32),
            shape((n * rows, D), BF),
            shape((rows, 2 * D), BF),
            shape((32, D), F32),
            shape((D, D), F32),
            shape((D, C), F32),
            shape((D, C), F32),
        ],
        scratch_shapes=[
            *comm_scratch(n, rows, 256),
            pltpu.VMEM((rows, D), BF),
            *sems(n),
            *sems(n),
            pltpu.SemaphoreType.DMA((1,)),
        ],
        compiler_params=remote_params(2),
    )(*args)


class Line:
    def __init__(self, place, pieces, x, out, pair_buf, low_buf, high_buf, send_buf, send, recv):
        self.place, self.pieces, self.x, self.out = place, pieces, x, out
        self.pair_buf, self.low_buf, self.high_buf = pair_buf, low_buf, high_buf
        self.send_buf, self.send, self.recv = send_buf, send, recv
        c, q, chips = place.chip, place.core, place.chips
        self.root = chips // 2 - 1 + q
        self.away = jnp.abs(c - self.root)
        self.right = jnp.minimum(c + 1, chips - 1) * 2 + q
        self.left = jnp.maximum(c - 1, 0) * 2 + q
        self.half = x.shape[0] // 2
        self.rows = self.half // pieces

    def part(self, which, p):
        return pl.ds(pl.multiple_of(which * self.half + p * self.rows, self.rows), self.rows)

    def here(self, p):
        return pl.ds(pl.multiple_of(p * self.rows, self.rows), self.rows)

    def link(self, src, dst, p, sent, got, peer):
        n = self.pieces
        return remote(src, dst, self.send.at[sent * n + p], self.recv.at[got * n + p], peer)

    def pair(self, p):
        src = self.x.at[self.part(1 - self.place.core, p)]
        return self.link(src, self.pair_buf.at[self.here(p)], p, 0, 0, self.place.sibling)

    def up(self, p):
        here = self.here(p)
        return self.link(self.send_buf.at[here], self.low_buf.at[here], p, 1, 1, self.right)

    def down(self, p):
        here = self.here(p)
        return self.link(self.send_buf.at[here], self.high_buf.at[here], p, 2, 2, self.left)

    def outward(self, p, sent, got, peer):
        mine = self.out.at[self.part(self.place.core, p)]
        return self.link(mine, mine, p, sent, got, peer)

    def out_left(self, p):
        return self.outward(p, 3, 3, self.left)

    def out_right(self, p):
        return self.outward(p, 5, 3, self.right)

    def across(self, p):
        return self.outward(p, 4, 4, self.place.sibling)

    def each(self, step):
        lax.fori_loop(0, self.pieces, lambda p, z: (step(p), z)[1], 0)

    def start(self):
        self.each(lambda p: self.pair(p).start())

    def reduce(self, p):
        c, root, last = self.place.chip, self.root, self.place.chips - 1
        here, mine_at = self.here(p), self.part(self.place.core, p)
        self.pair(p).wait_recv()
        mine = lambda: self.x[mine_at, :].astype(F32) + self.pair_buf[here, :].astype(F32)

        def end():
            self.send_buf[here, :] = mine().astype(BF)

        def from_low():
            self.up(p).wait_recv()
            self.send_buf[here, :] = (mine() + self.low_buf[here, :].astype(F32)).astype(BF)

        def from_high():
            self.down(p).wait_recv()
            self.send_buf[here, :] = (mine() + self.high_buf[here, :].astype(F32)).astype(BF)

        def at_root():
            self.up(p).wait_recv()
            self.down(p).wait_recv()
            total = mine() + self.low_buf[here, :].astype(F32) + self.high_buf[here, :].astype(F32)
            self.out[mine_at, :] = total.astype(BF)
            self.out_left(p).start()
            self.out_right(p).start()
            self.across(p).start()

        pl.when((c == 0) | (c == last))(end)
        pl.when((c > 0) & (c < root))(from_low)
        pl.when((c > root) & (c < last))(from_high)
        pl.when(c < root)(lambda: self.up(p).start())
        pl.when(c > root)(lambda: self.down(p).start())
        pl.when(c == root)(at_root)

    def spread(self, p):
        c, root, last = self.place.chip, self.root, self.place.chips - 1

        def leftward():
            self.out_left(p).wait_recv()
            pl.when(c > 0)(lambda: self.out_left(p).start())
            self.across(p).start()

        def rightward():
            self.out_right(p).wait_recv()
            pl.when(c < last)(lambda: self.out_right(p).start())
            self.across(p).start()

        pl.when(c < root)(leftward)
        pl.when(c > root)(rightward)

    def slots(self, lag):
        return self.pieces + 2 * lag * (self.place.chips // 2)

    def slot(self, s, lag):
        deep = self.place.chips // 2
        p = s - lag * (deep - self.away)
        pl.when((p >= 0) & (p < self.pieces))(lambda: self.reduce(p))
        o = s - lag * (deep + self.away)
        pl.when((o >= 0) & (o < self.pieces) & (self.away > 0))(lambda: self.spread(o))

    def finish(self):
        c, root, last = self.place.chip, self.root, self.place.chips - 1

        def end(p):
            self.pair(p).wait_send()
            self.across(p).wait_send()
            pl.when(c < root)(lambda: self.up(p).wait_send())
            pl.when(c > root)(lambda: self.down(p).wait_send())
            pl.when((c <= root) & (c > 0))(lambda: self.out_left(p).wait_send())
            pl.when((c >= root) & (c < last))(lambda: self.out_right(p).wait_send())

        self.each(lambda p: self.across(p).wait_recv())
        self.each(end)


def line_scratch(rows, width, pieces):
    return [pltpu.VMEM((rows // 2, width), BF)] * 4 + sems(6 * pieces)


class Exchange:
    def __init__(self, place, n, mine, got, send, recv):
        self.place, self.n, self.mine, self.got = place, n, mine, got
        self.copies = []
        for d in range(1, n):
            peer = lax.rem(place.me + d, n)
            self.copies.append(remote(mine, got.at[place.me], send.at[d], recv.at[d], peer))

    def start(self):
        for copy in self.copies:
            copy.start()
        self.got[self.place.me] = self.mine[...]

    def finish(self):
        for copy in self.copies:
            copy.wait_recv()
        total = self.got[0]
        for e in range(1, self.n):
            total = total + self.got[e]
        for copy in self.copies:
            copy.wait_send()
        return total


PIECES = 19
LAG = 4


def pack_sums(C, x, gains, dw1, dw2, dw3, dwe_near, dwe_far, dwe1, dwe2, dwe3, dgain, dg3):
    D = dw3.shape[0]
    at = 2 * D + C
    if dw1 is not x:
        x[:at, :] = dw1[...]
        x[at : at + D, :] = dw2[...]
    at += D
    x[at : at + D, :] = dw3[...].astype(BF)
    at += D
    spare = jnp.zeros((D, 256 - C), F32)
    edge1 = jnp.concatenate(
        [
            jnp.concatenate([dwe_near[...], spare], axis=1),
            jnp.concatenate([dwe_far[...], spare], axis=1),
            dwe1[...],
        ],
        axis=0,
    ).astype(BF)
    half = edge1.shape[0] // 2
    x[at : at + half, :256] = edge1[:half]
    x[at : at + half, 256:] = edge1[half:]
    at += half
    x[at : at + C, :256] = dwe2[:C, :].astype(BF)
    x[at : at + C, 256:] = dwe3[:C, :].astype(BF)
    gains[...] = jnp.zeros_like(gains)
    for r in range(4):
        gains[r : r + 1, :] = dgain[8 * r : 8 * r + 1, :]
    for r in range(2):
        gains[4 + r : 5 + r, :256] = dg3[8 * r : 8 * r + 1, :]


def back_start(C, w1, w2, w2t, w_own, w_own_t, zeroed):
    D = w2.shape[0]
    gap = 256 - C
    for ref in (w_own, *zeroed):
        ref[...] = jnp.zeros_like(ref)
    w_own[0, :C, :] = w1[2 * D :, :]
    w_own[1, gap:, :] = w1[2 * D :, :]
    for s in range(2):
        w_own_t[s] = jnp.transpose(w_own[s].astype(F32)).astype(BF)
    w2t[...] = jnp.transpose(w2[...].astype(F32)).astype(BF)


def back_tile(
    g, rows, C, tcol, trow, vw, act1, slope1, slope2, edges, partial, grad_edges,
    w2t, w_own_t, total, a2, ae, source_sum,
):
    half = GROUP // 2 * rows
    ks = [g * GROUP + j for j in ORDER]
    up = gather_table([lane_column(tcol, k) for k in ks], vw)
    upper = up.astype(BF) * slope2[...]
    a2[...] += dot_tn(act1[...], upper)
    lower = dot(upper, w2t[...]).astype(BF) * slope1[...]
    wide = lower.astype(F32)
    acc = wide[:rows]
    for j in range(1, GROUP):
        acc = acc + wide[j * rows : (j + 1) * rows]
    source_sum[...] += acc
    target = jnp.concatenate([trow[pl.ds(k, 1), :] for k in ks], axis=1)
    add_by_target(target, lower, total)
    slabs = slab_pairs(edges[...], C)
    lowers = [lower[:half], lower[half:]]
    own = []
    for s in range(2):
        ae[s] += dot_tn(slabs[s], lowers[s])
        own.append(dot(lowers[s], w_own_t[s]))
    grad_edges[...] = (partial[...].astype(F32) + join_slab(own[0], own[1], rows, C)).astype(BF)


def back_weights(C, dw1, dw2, nodes_all, nodes, total, a2, ae, source_sum):
    D = nodes.shape[1]
    gap = 256 - C
    dw2[...] = a2[...].astype(BF)
    dw1[:D, :] = dot_tn(nodes[...], source_sum[...].astype(BF)).astype(BF)
    dw1[2 * D :, :] = (ae[0][:C, :] + ae[1][gap:, :]).astype(BF)
    a2[...] = jnp.zeros_like(a2)

    def weigh(part):
        a2[...] += dot_tn(nodes_all[part, :], total[part, :].astype(BF))

    by_chunks(total.shape[0], weigh)
    dw1[D : 2 * D, :] = a2[...].astype(BF)


def tail(
    place, n, line, scatter, exchange, source_sum, grad_one, w1, grad_nodes, small, feed,
):
    D = grad_one.shape[1]
    line.start()
    scatter.start()
    exchange.start()
    scatter.pass_on()

    def feed_part(f):
        both, wf1, wf2, dwf1, dwf2 = feed
        step = 256
        cols = pl.ds(pl.multiple_of(f * step, step), step)
        low, resid = both[:, :D], both[:, D:]
        act, slope = gelu_full(dot(low, wf1[:, cols]))
        dwf2[cols, :] = dot_tn(act, resid).astype(BF)
        inner = (dot_nt(resid, wf2[cols, :]) * slope.astype(F32)).astype(BF)
        dwf1[:, cols] = dot_tn(low, inner).astype(BF)

    parts = feed[1].shape[1] // 256 if feed else 0

    def slot(s, carry):
        line.slot(s, LAG)
        if feed:
            pl.when((s % 2 == 1) & (s // 2 < parts))(lambda: feed_part(s // 2))
        return carry

    lax.fori_loop(0, line.slots(LAG), slot, 0)
    source = dot_nt(source_sum[...].astype(BF), w1[:D, :])
    total = scatter.finish()
    grad_nodes[...] = grad_one[...] + source + dot_nt(total.astype(BF), w1[D : 2 * D, :])
    small[...] = exchange.finish()
    line.finish()


def back_kernel(
    n, tiles, C, tcol, trow, nodes, vw, w1, w2,
    dw3, dwe_near, dwe_far, dwe1, dwe2, dwe3, dgain, dg3, both_own,
    nodes_all_h, grad_one_h, wf1_h, wf2_h, act1, slope1, slope2, edges, partial,
    grad_edges, grad_nodes, small, dwf1, dwf2, out_h,
    nodes_all, grad_one, wf1, wf2, load_sem, both, bsend, brecv, out,
    w2t, w_own, w_own_t, total, a2, ae, source_sum, target_sum, x, gains, got, gsend, grecv,
    pair_buf, far_buf, send, recv, *line_refs,
):
    g = pl.program_id(0)
    rows, D = nodes.shape
    place = Place(n)
    loads = Loads(
        [(nodes_all_h, nodes_all), (grad_one_h, grad_one), (wf1_h, wf1), (wf2_h, wf2)], load_sem
    )
    gather = Gather(place, both_own, both, bsend, brecv)
    keep_own = pltpu.make_async_copy(both_own, block(both, place.me, rows), load_sem.at[4])

    @pl.when(g == 0)
    def _():
        loads.start()
        keep_own.start()
        greet([lax.rem(place.me + d, n) for d in range(1, n)])
        gather.start()
        back_start(C, w1, w2, w2t, w_own, w_own_t, (total, a2, ae, source_sum))

    back_tile(
        g, rows, C, tcol, trow, vw, act1, slope1, slope2, edges, partial, grad_edges,
        w2t, w_own_t, total, a2, ae, source_sum,
    )

    @pl.when(g == tiles - 1)
    def _():
        target_sum[...] = total[...].astype(BF)
        loads.wait()
        keep_own.wait()
        gather.finish()
        at = 2 * D + C
        back_weights(
            C, x.at[pl.ds(0, at)], x.at[pl.ds(at, D)], nodes_all, nodes, total, a2, ae, source_sum
        )
        pack_sums(C, x, gains, x, x, dw3, dwe_near, dwe_far, dwe1, dwe2, dwe3, dgain, dg3)
        tail(
            place, n, Line(place, PIECES, x, out, *line_refs),
            Scatter(place, target_sum, pair_buf, far_buf, send, recv),
            Exchange(place, n, gains, got, gsend, grecv),
            source_sum, grad_one, w1, grad_nodes, small, (both, wf1, wf2, dwf1, dwf2),
        )
        keep_out = pltpu.make_async_copy(out, out_h, load_sem.at[5])
        keep_out.start()
        keep_out.wait()


def sum_rows(D, C):
    return 4 * D + C + (2 * D + C) // 2 + C


def back_call(n, C, tcol, trow, nodes, vw, w1, w2, sums, both_own, loaded, act1, slope1, slope2, edges, partial):
    rows, D = nodes.shape
    count = vw.shape[0]
    K = edges.shape[1] // C
    tiles = K // GROUP
    size = GROUP * rows
    FF = loaded[2].shape[1]
    total = sum_rows(D, C)
    shape = jax.ShapeDtypeStruct
    slab = pl.BlockSpec((rows, GROUP * C), lambda g: (0, g))
    tile = pl.BlockSpec((size, D), lambda g: (g, 0))
    whole = [tcol, trow, nodes, vw, w1, w2, *sums, both_own]
    outs = [
        shape((rows, D), F32),
        shape((8, D), F32),
        shape((D, FF), BF),
        shape((FF, D), BF),
    ]
    return pl.pallas_call(
        functools.partial(back_kernel, n, tiles, C),
        grid=(tiles,),
        in_specs=[full(v) for v in whole] + [HBM] * 4 + [tile, tile, tile, slab, slab],
        out_specs=[slab] + [fixed(*v.shape) for v in outs] + [HBM],
        out_shape=[shape((rows, K * C), BF)] + outs + [shape((total, D), BF)],
        scratch_shapes=[pltpu.VMEM(v.shape, v.dtype) for v in loaded]
        + [
            pltpu.SemaphoreType.DMA((6,)),
            pltpu.VMEM((count, 2 * D), BF),
            *sems(n),
            pltpu.VMEM((total, D), BF),
            pltpu.VMEM((D, D), BF),
            pltpu.VMEM((2, 256, D), BF),
            pltpu.VMEM((2, D, 256), BF),
            pltpu.VMEM((count, D), F32),
            pltpu.VMEM((D, D), F32),
            pltpu.VMEM((2, 256, D), F32),
            pltpu.VMEM((rows, D), F32),
            pltpu.VMEM((count, D), BF),
            pltpu.VMEM((total, D), BF),
            pltpu.VMEM((8, D), F32),
            pltpu.VMEM((n, 8, D), F32),
            *sems(n),
            *comm_scratch(n, rows, D),
            *sems(n),
            *line_scratch(total, D, PIECES),
        ],
        compiler_params=remote_params(3),
    )(*whole, *loaded, act1, slope1, slope2, edges, partial)


def message_back_kernel(
    tiles, C, tcol, trow, nodes_all, nodes, vw, w1, w2, act1, slope1, slope2, edges, partial,
    grad_edges, dw1, dw2, target_sum, source_sum, w2t, w_own, w_own_t, total, a2, ae,
):
    g = pl.program_id(0)

    @pl.when(g == 0)
    def _():
        back_start(C, w1, w2, w2t, w_own, w_own_t, (total, a2, ae, source_sum))

    back_tile(
        g, nodes.shape[0], C, tcol, trow, vw, act1, slope1, slope2, edges, partial, grad_edges,
        w2t, w_own_t, total, a2, ae, source_sum,
    )

    @pl.when(g == tiles - 1)
    def _():
        target_sum[...] = total[...].astype(BF)
        back_weights(C, dw1, dw2, nodes_all, nodes, total, a2, ae, source_sum)


def message_back_call(C, tcol, trow, nodes_all, nodes, vw, w1, w2, act1, slope1, slope2, edges, partial):
    rows, D = nodes.shape
    count = vw.shape[0]
    K = edges.shape[1] // C
    tiles = K // GROUP
    size = GROUP * rows
    shape = jax.ShapeDtypeStruct
    slab = pl.BlockSpec((rows, GROUP * C), lambda g: (0, g))
    tile = pl.BlockSpec((size, D), lambda g: (g, 0))
    return pl.pallas_call(
        functools.partial(message_back_kernel, tiles, C),
        grid=(tiles,),
        in_specs=[full(x) for x in (tcol, trow, nodes_all, nodes, vw, w1, w2)]
        + [tile, tile, tile, slab, slab],
        out_specs=[slab, fixed(2 * D + C, D), fixed(D, D), fixed(count, D), fixed(rows, D)],
        out_shape=[
            shape((rows, K * C), BF),
            shape((2 * D + C, D), BF),
            shape((D, D), BF),
            shape((count, D), BF),
            shape((rows, D), F32),
        ],
        scratch_shapes=[
            pltpu.VMEM((D, D), BF),
            pltpu.VMEM((2, 256, D), BF),
            pltpu.VMEM((2, D, 256), BF),
            pltpu.VMEM((count, D), F32),
            pltpu.VMEM((D, D), F32),
            pltpu.VMEM((2, 256, D), F32),
        ],
        compiler_params=LOCAL,
    )(tcol, trow, nodes_all, nodes, vw, w1, w2, act1, slope1, slope2, edges, partial)


def final_kernel(
    n, C, target_sum, source_sum, grad_one, w1, dw1, dw2, dw3, dwe_near, dwe_far, dwe1, dwe2, dwe3,
    dgain, dg3, grad_nodes, out, small,
    x, gains, got, gsend, grecv, pair_buf, far_buf, send, recv, *line_refs,
):
    place = Place(n)
    greet([lax.rem(place.me + d, n) for d in range(1, n)])
    pack_sums(C, x, gains, dw1, dw2, dw3, dwe_near, dwe_far, dwe1, dwe2, dwe3, dgain, dg3)
    tail(
        place, n, Line(place, PIECES, x, out, *line_refs),
        Scatter(place, target_sum, pair_buf, far_buf, send, recv),
        Exchange(place, n, gains, got, gsend, grecv),
        source_sum, grad_one, w1, grad_nodes, small, None,
    )


def final_call(n, C, args):
    rows, D = args[2].shape
    size = sum_rows(D, C)
    shape = jax.ShapeDtypeStruct
    return pl.pallas_call(
        functools.partial(final_kernel, n, C),
        in_specs=[WHOLE] * len(args),
        out_specs=[WHOLE] * 3,
        out_shape=[shape((rows, D), F32), shape((size, D), BF), shape((8, D), F32)],
        scratch_shapes=[
            pltpu.VMEM((size, D), BF),
            pltpu.VMEM((8, D), F32),
            pltpu.VMEM((n, 8, D), F32),
            *sems(n),
            *comm_scratch(n, rows, D),
            *sems(n),
            *line_scratch(size, D, PIECES),
        ],
        compiler_params=remote_params(4),
    )(*args)


def feed_kernel(low, resid, wf1, wf2, dwf1, dwf2):
    @pl.when(pl.program_id(1) == 0)
    def _():
        dwf1[...] = jnp.zeros_like(dwf1)
        dwf2[...] = jnp.zeros_like(dwf2)

    act, slope = gelu_full(dot(low[...], wf1[...]))
    dwf2[...] += dot_tn(act, resid[...])
    inner = (dot_nt(resid[...], wf2[...]) * slope.astype(F32)).astype(BF)
    dwf1[...] += dot_tn(low[...], inner)


def feed_call(both, wf1, wf2):
    count = both.shape[0]
    D, FF = wf1.shape
    step, rows = min(FF, 512), min(count, TABLE)
    shape = jax.ShapeDtypeStruct
    return pl.pallas_call(
        feed_kernel,
        grid=(FF // step, count // rows),
        in_specs=[
            pl.BlockSpec((rows, D), lambda f, r: (r, 0)),
            pl.BlockSpec((rows, D), lambda f, r: (r, 1)),
            pl.BlockSpec((D, step), lambda f, r: (0, f)),
            pl.BlockSpec((step, D), lambda f, r: (f, 0)),
        ],
        out_specs=[
            pl.BlockSpec((D, step), lambda f, r: (0, f)),
            pl.BlockSpec((step, D), lambda f, r: (f, 0)),
        ],
        out_shape=[shape((D, FF), F32), shape((FF, D), F32)],
        compiler_params=LOCAL,
    )(both, both, wf1, wf2)


def unpack_kernel(C, steps, packed, small, edges, *refs):
    g = pl.program_id(0)
    D = packed.shape[1]
    plain = refs[: (len(refs) - 13) // 2]
    w1, w2, w3, grad_edges, one, two, three, *outs = refs[len(plain) :]
    gains = outs[len(plain) :]
    grad_edges[...] = edges[...].astype(F32)
    at = 0
    for ref, size in ((w1, 2 * D + C), (w2, D), (w3, D)):
        step = size // steps
        ref[...] = packed[pl.ds(pl.multiple_of(at + g * step, 16), step), :].astype(F32)
        at += size
    for a, b in zip(plain, outs):
        b[...] = a[...].astype(F32)

    @pl.when(g == steps - 1)
    def _():
        half = (2 * D + C) // 2
        for r in range(2):
            left = 256 * r
            flipped = jnp.transpose(packed[at : at + half, left : left + 256].astype(F32))
            one[:, half * r : half * r + half] = flipped[:C, :]
        end = at + half
        two[...] = packed[end : end + C, :C].astype(F32)
        three[...] = packed[end : end + C, 256 : 256 + C].astype(F32)
        for r in range(6):
            width = D if r < 4 else C
            gains[r][...] = small[r : r + 1, :width]


def unpack_call(C, packed, small, edges, arrays):
    steps = 4
    D = packed.shape[1]
    first = 2 * D + C
    shape = jax.ShapeDtypeStruct
    cut = lambda r, c: pl.BlockSpec((r // steps, c), lambda g: (g, 0))
    head = [(first, D), (D, D), (D, D), edges.shape]
    last = [(C, first), (C, C), (C, C)]
    plain = [v.shape for v in arrays]
    gains = [(1, D)] * 4 + [(1, C)] * 2
    return pl.pallas_call(
        functools.partial(unpack_kernel, C, steps),
        grid=(steps,),
        in_specs=[full(packed), full(small)] + [cut(*v.shape) for v in (edges, *arrays)],
        out_specs=[cut(*v) for v in head]
        + [fixed(*v) for v in last]
        + [cut(*v) for v in plain]
        + [fixed(*v) for v in gains],
        out_shape=[shape(v, F32) for v in head + last + plain + gains],
        compiler_params=LOCAL,
    )(packed, small, edges, *arrays)


def body(
    nodes, edges, nbr_owner, nbr_slot, edge_mask, w_msg1, w_msg2, w_msg3, gain_one, offset_one,
    w_ffn1, w_ffn2, gain_two, offset_two, w_edge1, w_edge2, w_edge3, gain_three, offset_three,
    node_cotangent, edge_cotangent,
):
    n = lax.axis_size("edge")
    rows, D = nodes.shape
    C = w_edge2.shape[0]
    we1 = w_edge1.T
    g1, o1, g2, o2 = (v.reshape(1, D) for v in (gain_one, offset_one, gain_two, offset_two))
    (
        act1, slope1, slope2, tcol, trow, node_out, near, low, n1, n2, inv, act, slope, own_sum,
        nodes_all, far_all,
    ) = forward_call(
        n, C, nodes, nbr_owner[:, :, 0].T, nbr_slot.T, edge_mask.T, g1, o1, g2, o2,
        [w_msg1, w_msg2, w_msg3, w_ffn1, w_ffn2, we1], edges,
    )
    edge_out, partial, far_sum, near_sum, dwe1, dwe2, dwe3, dg3 = edge_call(
        C, tcol, trow, far_all, near, we1, w_edge2, w_edge3,
        gain_three.reshape(1, C), offset_three.reshape(1, C), edges, edge_cotangent,
    )
    grad_one, vw_all, both, dgain, dw3, dwe_near, dwe_far = node_back_call(
        n, C, far_sum, near_sum, node_cotangent, node_out, n1, n2, inv, act, slope, low, own_sum,
        w_msg3, g1, w_ffn1, w_ffn2, g2, we1,
    )
    sums = [dw3, dwe_near, dwe_far, dwe1, dwe2, dwe3, dgain, dg3]
    kept = [act1, slope1, slope2, edges, partial]
    if n * rows <= TABLE:
        grad_edges, grad_nodes, small, *dwf, packed = back_call(
            n, C, tcol, trow, nodes, vw_all, w_msg1, w_msg2, sums, both,
            [nodes_all, grad_one, w_ffn1, w_ffn2], *kept,
        )
        tot1, tot2, tot3, grad_edges, we1_t, tot_e2, tot_e3, dwf1, dwf2, *gains = unpack_call(
            C, packed, small, grad_edges, dwf
        )
    else:
        grad_edges, dw1, dw2, target_sum, source_sum = message_back_call(
            C, tcol, trow, nodes_all, nodes, vw_all, w_msg1, w_msg2, *kept
        )
        grad_nodes, packed, small = final_call(
            n, C, [target_sum, source_sum, grad_one, w_msg1, dw1, dw2, *sums]
        )
        tot1, tot2, tot3, grad_edges, we1_t, tot_e2, tot_e3, *gains = unpack_call(
            C, packed, small, grad_edges, []
        )
        both = lax.all_gather(both, "edge", axis=0, tiled=True)
        dwf1, dwf2 = feed_call(both, w_ffn1, w_ffn2)
    gains = [v.reshape(v.shape[1]) for v in gains]
    return (
        node_out, edge_out, grad_nodes, grad_edges,
        tot1, tot2, tot3, gains[0], gains[1], dwf1, dwf2, gains[2], gains[3],
        we1_t.T, tot_e2, tot_e3, gains[4], gains[5],
    )


def solution(mesh):
    rows = P(("dp", "edge"), None)
    return jax.shard_map(
        body,
        mesh=mesh,
        in_specs=(rows, rows, P(("dp", "edge"), None, None), rows, rows)
        + (P(),) * 14
        + (rows, rows),
        out_specs=(rows,) * 4
        + (P("dp", None),) * 3
        + (P("dp"),) * 2
        + (P("dp", None),) * 2
        + (P("dp"),) * 2
        + (P("dp", None),) * 3
        + (P("dp"),) * 2,
        check_vma=False,
    )
```

```python
import functools

import jax
import jax.numpy as jnp
from jax import lax
from jax.experimental import pallas as pl
from jax.experimental.pallas import tpu as pltpu
from jax.sharding import PartitionSpec as P

BF = jnp.bfloat16
F32 = jnp.float32
I32 = jnp.int32
MESH = pl.DeviceIdType.MESH
MIB = 1024 * 1024
LANES = 128
GROUP = 4
ORDER = (0, 2, 1, 3)
TABLE = 1024
EPS = 1e-05
ROOT = 0.7978845608028654
CUBE = 0.044715 * ROOT


def dot(a, b):
    return jnp.dot(a, b, preferred_element_type=F32)


def dot_tn(a, b):
    return lax.dot_general(a, b, (((0,), (0,)), ((), ())), preferred_element_type=F32)


def dot_nt(a, b):
    return lax.dot_general(a, b, (((1,), (1,)), ((), ())), preferred_element_type=F32)


def gelu_pair(v):
    v = v.astype(BF)
    c = lambda x: jnp.asarray(x, BF)
    z = v * v
    q = c(0.5) + c(0.5) * jnp.tanh(v * (c(ROOT) + c(CUBE) * z))
    act = v * q
    slope = q + (act - act * q) * (c(2.0 * ROOT) + c(6.0 * CUBE) * z)
    return act, slope


def gelu_full(v):
    z = v * v
    q = 0.5 + 0.5 * jnp.tanh(v * (ROOT + CUBE * z))
    act = v * q
    slope = q + (act - act * q) * (2.0 * ROOT + 6.0 * CUBE * z)
    return act.astype(BF), slope.astype(BF)


def row_mean(v):
    return jnp.mean(v, axis=-1, keepdims=True)


def lane_column(ref, k):
    rows = ref.shape[0]
    return jnp.broadcast_to(pltpu.roll(ref[...], LANES - k, axis=1)[:, 0:1], (rows, LANES))


def pick_rows(target, width):
    lane = lax.broadcasted_iota(I32, target.shape, 1)
    one, nil = jnp.ones((), BF), jnp.zeros((), BF)
    t16, l16 = target.astype(jnp.int16), lane.astype(jnp.int16)
    return jnp.concatenate(
        [jnp.where(t16 == l16 + jnp.int16(LANES * c), one, nil) for c in range(width // LANES)], axis=1)


def pick_cols(target, width):
    edges = target.shape[1]
    sub = lax.broadcasted_iota(I32, (width, edges), 0)
    return jnp.where(jnp.broadcast_to(target, (width, edges)).astype(jnp.int16) == sub.astype(jnp.int16), jnp.ones((), BF), jnp.zeros((), BF))


def gather_table(targets, table):
    count = table.shape[0]
    if count <= TABLE:
        hot = jnp.concatenate([pick_rows(t, count) for t in targets], axis=0)
        return dot(hot, table[...])

    def step(c, total):
        base = c * TABLE
        hot = jnp.concatenate([pick_rows(t - base, TABLE) for t in targets], axis=0)
        return total + dot(hot, table[pl.ds(pl.multiple_of(base, TABLE), TABLE), :])

    rows = sum(t.shape[0] for t in targets)
    return lax.fori_loop(0, count // TABLE, step, jnp.zeros((rows, table.shape[1]), F32))


def add_by_target(target, values, total):
    count = total.shape[0]
    if count <= TABLE:
        total[...] += dot(pick_cols(target, count), values)
        return

    def step(c, carry):
        base = c * TABLE
        part = pl.ds(pl.multiple_of(base, TABLE), TABLE)
        total[part, :] += dot(pick_cols(target - base, TABLE), values)
        return carry

    lax.fori_loop(0, count // TABLE, step, 0)


def by_chunks(count, step):
    if count <= TABLE:
        step(pl.ds(0, count))
        return

    def one(c, carry):
        step(pl.ds(pl.multiple_of(c * TABLE, TABLE), TABLE))
        return carry

    lax.fori_loop(0, count // TABLE, one, 0)


def remote(src, dst, send, recv, peer):
    return pltpu.make_async_remote_copy(
        src_ref=src,
        dst_ref=dst,
        send_sem=send,
        recv_sem=recv,
        device_id={"edge": peer},
        device_id_type=MESH,
    )


def greet(peers):
    barrier = pltpu.get_barrier_semaphore()
    for peer in peers:
        pl.semaphore_signal(barrier, inc=1, device_id={"edge": peer}, device_id_type=MESH)
    pl.semaphore_wait(barrier, len(peers))


def block(ref, index, rows):
    return ref.at[pl.ds(pl.multiple_of(index * rows, rows), rows)]


class Place:
    def __init__(self, n):
        self.me = lax.axis_index("edge")
        self.chips = n // 2
        self.chip = self.me // 2
        self.core = lax.rem(self.me, 2)
        self.sibling = self.chip * 2 + 1 - self.core
        self.mates = [self.at(d) for d in range(1, self.chips)]

    def at(self, d):
        return lax.rem(self.chip + d + self.chips, self.chips) * 2 + self.core


class Gather:
    def __init__(self, place, x, out, send, recv):
        rows, chips = x.shape[0], place.chips
        mine = block(out, place.me, rows)
        self.near = remote(x, mine, send.at[0], recv.at[0], place.sibling)
        self.far, self.passed = [], []
        for d in range(1, chips):
            self.far.append(remote(x, mine, send.at[d], recv.at[d], place.mates[d - 1]))
            got = block(out, place.at(-d), rows)
            at = chips + d
            self.passed.append(remote(got, got, send.at[at], recv.at[at], place.sibling))

    def start(self):
        for copy in self.far:
            copy.start()
        self.near.start()

    def finish(self):
        for far, passed in zip(self.far, self.passed):
            far.wait_recv()
            passed.start()
        self.near.wait()
        for copy in self.passed:
            copy.wait()
        for copy in self.far:
            copy.wait_send()


class Scatter:
    def __init__(self, place, x, pair_buf, far_buf, send, recv):
        self.place, self.x = place, x
        self.pair_buf, self.far_buf = pair_buf, far_buf
        chips, self.rows = place.chips, pair_buf.shape[1]
        self.pairs, self.far = [], []
        for d in range(chips):
            theirs = lax.rem(place.chip + d, chips) * 2 + 1 - place.core
            src = block(x, theirs, self.rows)
            self.pairs.append(remote(src, pair_buf.at[d], send.at[d], recv.at[d], place.sibling))
        for d in range(1, chips):
            at = chips + d
            self.far.append(
                remote(pair_buf.at[d], far_buf.at[d], send.at[at], recv.at[at], place.at(d))
            )

    def start(self):
        for copy in self.pairs[1:]:
            copy.start()
        self.pairs[0].start()

    def pass_on(self):
        for d in range(1, self.place.chips):
            self.pairs[d].wait_recv()
            at = pl.ds(pl.multiple_of(self.place.at(d) * self.rows, self.rows), self.rows)
            mine = self.x[at, :].astype(F32) + self.pair_buf[d].astype(F32)
            self.pair_buf[d] = mine.astype(BF)
            self.far[d - 1].start()

    def finish(self):
        self.pairs[0].wait_recv()
        at = pl.ds(pl.multiple_of(self.place.me * self.rows, self.rows), self.rows)
        total = self.x[at, :].astype(F32) + self.pair_buf[0].astype(F32)
        for d in range(1, self.place.chips):
            self.far[d - 1].wait_recv()
            total = total + self.far_buf[d].astype(F32)
        for copy in self.pairs + self.far:
            copy.wait_send()
        return total


def scatter_sum(*refs):
    scatter = Scatter(*refs)
    scatter.start()
    scatter.pass_on()
    return scatter.finish()


def comm_scratch(n, rows, width):
    return [pltpu.VMEM((n // 2, rows, width), BF)] * 2


def sems(count):
    return [pltpu.SemaphoreType.DMA((count,))] * 2


def remote_params(cid):
    return pltpu.CompilerParams(
        collective_id=cid, has_side_effects=True, vmem_limit_bytes=62 * MIB
    )


LOCAL = pltpu.CompilerParams(vmem_limit_bytes=62 * MIB)
WHOLE = pl.BlockSpec(memory_space=pltpu.VMEM)


def slab_pairs(slab, C):
    pairs = slab.shape[1] // (2 * C)
    even = [slab[:, 2 * C * m : 2 * C * m + 256] for m in range(pairs)]
    odd = [slab[:, 2 * C * m + 2 * C - 256 : 2 * C * m + 2 * C] for m in range(pairs)]
    return jnp.concatenate(even, axis=0), jnp.concatenate(odd, axis=0)


def interleave(even, odd, rows):
    parts = []
    for m in range(even.shape[0] // rows):
        parts += [even[m * rows : (m + 1) * rows], odd[m * rows : (m + 1) * rows]]
    return jnp.concatenate(parts, axis=0)


def split_tiles(values, rows):
    count = values.shape[0] // rows
    pick = lambda first: jnp.concatenate(
        [values[k * rows : (k + 1) * rows] for k in range(first, count, 2)], axis=0
    )
    return pick(0), pick(1)


def join_slab(even, odd, rows, C):
    parts = []
    for m in range(even.shape[0] // rows):
        a = even[m * rows : (m + 1) * rows]
        b = odd[m * rows : (m + 1) * rows]
        parts += [a[:, :LANES], a[:, LANES:] + b[:, :LANES], b[:, LANES:]]
    return jnp.concatenate(parts, axis=1)


class Loads:
    def __init__(self, pairs, sem):
        self.copies = [
            pltpu.make_async_copy(src, dst, sem.at[j]) for j, (src, dst) in enumerate(pairs)
        ]

    def start(self):
        for copy in self.copies:
            copy.start()

    def wait(self, first=0, last=None):
        for copy in self.copies[first:last]:
            copy.wait()


def column_of(row):
    return jnp.transpose(jnp.broadcast_to(row, (LANES, row.shape[1])))


def spread(column, width):
    return jnp.concatenate([column] * (width // LANES), axis=1)


def norm_parts(values):
    centred = values - row_mean(values)
    inverse = lax.rsqrt(row_mean(centred * centred) + EPS)
    return centred * inverse, inverse


def forward_kernel(
    n, K, C, nodes, owner, slot, live, g1, o1, g2, o2, w1_h, w2_h, w3_h, wf1_h, wf2_h, we1_h, edges,
    act1, slope1, slope2, tcol, trow, node_out, near, low_out, n1_out, n2_out, inv_out,
    slope_out, sum_out, nodes_h, far_h,
    w1, w2, w3, wf1, wf2, we1, load_sem,
    nodes_all, far_all, lcol, orow, lrow, scol, hist, hist_got, count,
    p_all, p_own, w_own, pre2, total, summed, q_own, pair_buf, far_buf,
    send, recv, hsend, hrecv, rsend, rrecv, qsend, qrecv, own_sem,
):
    i = pl.program_id(0)
    rows, D = nodes.shape
    tiles = K // GROUP
    size = GROUP * rows
    if n * rows > TABLE:
        p_all = summed = nodes_all
    place = Place(n)
    others = [lax.rem(place.me + d, n) for d in range(1, n)]
    loads = Loads(
        [(w1_h, w1), (w2_h, w2), (w3_h, w3), (wf1_h, wf1), (wf2_h, wf2), (we1_h, we1)], load_sem
    )
    keep_nodes = pltpu.make_async_copy(nodes_all, nodes_h, own_sem.at[1])

    @pl.when(i == 0)
    def _():
        loads.start()
        spare = jnp.zeros((LANES - K, rows), I32)
        own_rows = jnp.concatenate([owner[...], jnp.zeros((rows, LANES - K), I32)], axis=1)
        own_wide = jnp.transpose(own_rows)
        slot_wide = jnp.concatenate([slot[...], spare], axis=0)
        live_wide = jnp.concatenate([live[...], spare], axis=0).astype(F32)
        target = own_wide * rows + slot_wide
        trow[...] = target
        orow[...] = own_wide
        lrow[...] = live_wide
        tcol[...] = jnp.transpose(target)
        lcol[...] = jnp.transpose(live_wide)
        scol[...] = jnp.transpose(slot_wide)
        pre2[...] = jnp.zeros_like(pre2)
        total[...] = jnp.zeros_like(total)
        w_own[...] = jnp.zeros_like(w_own)
        greet(others)
        gather = Gather(place, nodes, nodes_all, send, recv)
        gather.start()
        own = pltpu.make_async_copy(nodes, block(nodes_all, place.me, rows), own_sem.at[0])
        own.start()

        def tally(g, total):
            ks = [g * GROUP + j for j in range(GROUP)]
            hot = jnp.concatenate([pick_rows(lane_column(scol, k), LANES) for k in ks], axis=0)
            owners = jnp.concatenate([orow[pl.ds(k, 1), :] for k in ks], axis=1)
            lives = jnp.concatenate([lrow[pl.ds(k, 1), :] for k in ks], axis=1)
            sub = lax.broadcasted_iota(I32, (n, size), 0)
            who = jnp.where(
                jnp.broadcast_to(owners, sub.shape) == sub, jnp.broadcast_to(lives, sub.shape), 0.0
            )
            return total + dot(who.astype(BF), hot)

        totals = lax.fori_loop(0, tiles, tally, jnp.zeros((n, LANES), F32))
        for e in range(n):
            hist[e] = jnp.broadcast_to(totals[e : e + 1, :], (8, LANES))
        copies = []
        for d in range(1, n):
            peer = others[d - 1]
            copy = remote(hist.at[peer], hist_got.at[d], hsend.at[d], hrecv.at[d], peer)
            copy.start()
            copies.append(copy)
        loads.wait(0, 2)
        p_own[...] = dot(nodes[...], w1[:D, :])
        w_own[0, :C, :] = w1[2 * D :, :]
        w_own[1, 256 - C :, :] = w1[2 * D :, :]
        tallied = hist[place.me]
        for copy in copies:
            copy.wait_recv()
        for d in range(1, n):
            tallied = tallied + hist_got[d]
        count[...] = tallied
        own.wait()
        gather.finish()
        for copy in copies:
            copy.wait_send()
        keep_nodes.start()
        if n * rows > TABLE:
            keep_nodes.wait()

        def project(part):
            p_all[part, :] = dot(nodes_all[part, :], w1[D : 2 * D, :]).astype(BF)

        by_chunks(n * rows, project)

    last = jnp.clip(i - 1, 0, tiles - 1)
    ks = [last * GROUP + j for j in ORDER]
    act, slope = gelu_pair(pre2[...])
    alive = jnp.concatenate(
        [jnp.concatenate([lane_column(lcol, k)] * (D // LANES), axis=1) for k in ks], axis=0
    ).astype(BF)
    slope2[...] = slope * alive
    act = act * (alive * jnp.where(i >= 1, 1.0, 0.0).astype(BF))
    target = jnp.concatenate([trow[pl.ds(k, 1), :] for k in ks], axis=1)
    add_by_target(target, act, total)

    now = jnp.minimum(i, tiles - 1)
    targets = [lane_column(tcol, now * GROUP + j) for j in ORDER]
    even, odd = slab_pairs(edges[...], C)
    own = jnp.concatenate([dot(even, w_own[0]), dot(odd, w_own[1])], axis=0)
    act, slope = gelu_pair(
        gather_table(targets, p_all) + own + jnp.concatenate([p_own[...]] * GROUP, axis=0)
    )
    act1[...] = act
    slope1[...] = slope
    pre2[...] = dot(act, w2[...])

    @pl.when(i == tiles)
    def _():
        summed[...] = total[...].astype(BF)
        scatter = Scatter(place, summed, pair_buf, far_buf, rsend, rrecv)
        scatter.start()
        scatter.pass_on()
        if n * rows <= TABLE:
            keep_nodes.wait()
        loads.wait(2)
        divisor = 1.0 + column_of(count[0:1, :])
        inv_out[2] = divisor
        mine = scatter.finish().astype(BF)
        sum_out[...] = mine
        resid = nodes[...].astype(F32) + dot(mine, w3[...]) / spread(divisor, D)
        n1, inv1 = norm_parts(resid)
        n1_out[...] = n1
        inv_out[0] = jnp.broadcast_to(inv1, (rows, LANES))
        normed = n1 * g1[...] + o1[...]
        low = normed.astype(BF)
        low_out[...] = low
        act, slope = gelu_full(dot(low, wf1[...]))
        slope_out[...] = slope
        n2, inv2 = norm_parts(normed + dot(act, wf2[...]))
        n2_out[...] = n2
        inv_out[1] = jnp.broadcast_to(inv2, (rows, LANES))
        node_low = (n2 * g2[...] + o2[...]).astype(BF)
        node_out[...] = node_low
        pad = jnp.zeros((rows, 256 - C), F32)
        far = dot_nt(node_low, we1[:, D : 2 * D])
        q_own[...] = jnp.concatenate([far, pad], axis=1).astype(BF)
        gather = Gather(place, q_own, far_all, qsend, qrecv)
        gather.start()
        own = pltpu.make_async_copy(q_own, block(far_all, place.me, rows), own_sem.at[0])
        own.start()
        near[...] = jnp.concatenate([dot_nt(node_low, we1[:, :D]), pad], axis=1)
        own.wait()
        gather.finish()
        keep_far = pltpu.make_async_copy(far_all, far_h, own_sem.at[2])
        keep_far.start()
        keep_far.wait()


def full(x):
    return pl.BlockSpec(
        x.shape, lambda g: (0,) * x.ndim, pipeline_mode=pl.Buffered(buffer_count=1)
    )


def fixed(*s):
    return pl.BlockSpec(s, lambda g: (0,) * len(s), pipeline_mode=pl.Buffered(buffer_count=1))


HBM = pl.BlockSpec(memory_space=pl.ANY)


def forward_call(n, C, nodes, owner, slot, live, g1, o1, g2, o2, weights, edges):
    rows, D = nodes.shape
    K = slot.shape[0]
    FF = weights[3].shape[1]
    tiles = K // GROUP
    size = GROUP * rows
    count = n * rows
    other = count if count <= TABLE else 16
    shape = jax.ShapeDtypeStruct
    lag = lambda d: pl.BlockSpec((size, D), lambda g: (jnp.clip(g - d, 0, tiles - 1), 0))
    small = [nodes, owner, slot, live, g1, o1, g2, o2]
    outs = [
        shape((LANES, rows), I32),
        shape((LANES, rows), I32),
        shape((rows, D), BF),
        shape((rows, 256), F32),
        shape((rows, D), BF),
        shape((rows, D), F32),
        shape((rows, D), F32),
        shape((3, rows, LANES), F32),
        shape((rows, FF), BF),
        shape((rows, D), BF),
    ]
    outs[0] = shape((rows, LANES), I32)
    return pl.pallas_call(
        functools.partial(forward_kernel, n, K, C),
        grid=(tiles + 1,),
        in_specs=[full(v) for v in small]
        + [HBM] * 6
        + [pl.BlockSpec((rows, GROUP * C), lambda g: (0, jnp.minimum(g, tiles - 1)))],
        out_specs=[lag(0), lag(0), lag(1)] + [fixed(*v.shape) for v in outs] + [HBM] * 2,
        out_shape=[shape((K * rows, D), BF)] * 3
        + outs
        + [shape((count, D), BF), shape((count, 256), BF)],
        scratch_shapes=[pltpu.VMEM(v.shape, BF) for v in weights]
        + [
            pltpu.SemaphoreType.DMA((6,)),
            pltpu.VMEM((count, D), BF),
            pltpu.VMEM((count, 256), BF),
            pltpu.VMEM((rows, LANES), F32),
            pltpu.VMEM((LANES, rows), I32),
            pltpu.VMEM((LANES, rows), F32),
            pltpu.VMEM((rows, LANES), I32),
            pltpu.VMEM((n, 8, LANES), F32),
            pltpu.VMEM((n, 8, LANES), F32),
            pltpu.VMEM((8, LANES), F32),
            pltpu.VMEM((other, D), BF),
            pltpu.VMEM((rows, D), F32),
            pltpu.VMEM((2, 256, D), BF),
            pltpu.VMEM((size, D), F32),
            pltpu.VMEM((count, D), F32),
            pltpu.VMEM((other, D), BF),
            pltpu.VMEM((rows, 256), BF),
            *comm_scratch(n, rows, D),
            *sems(n),
            *sems(n),
            *sems(n),
            *sems(n),
            pltpu.SemaphoreType.DMA((3,)),
        ],
        compiler_params=remote_params(0),
    )(*small, *weights, edges)


def edge_kernel(
    tiles, C, tcol, trow, far_all, near, we1, we2, we3, gain, offset, edges1, edges4, edges6, cot,
    edge_out, partial, far_sum, near_sum, dw1, dw2, dw3, dgain,
    w1o, w2p, w3o, w1t, w2t, w3t, gains, total, a1, a2, a3, ag,
    pre1, hid1, slope1, pre2, hid2, slope2, res3, third, up2, up1,
):
    i = pl.program_id(0)
    rows = near.shape[0]
    D2 = we1.shape[1] - C
    gap = 256 - C
    half = GROUP // 2 * rows

    @pl.when(i == 0)
    def _():
        for ref in (w1o, w2p, w3o, w1t, w2t, w3t, gains, total, a1, a2, a3, ag, near_sum,
                    pre1, hid1, slope1, pre2, hid2, slope2, res3, third, up2, up1):
            ref[...] = jnp.zeros_like(ref)
        own = jnp.transpose(we1[:, D2:].astype(F32)).astype(BF)
        w1o[0, :C, :C] = own
        w1o[1, gap:, :C] = own
        w2p[:C, :C] = we2[...]
        w3o[0, :C, :C] = we3[...]
        w3o[1, :C, :] = jnp.concatenate([jnp.zeros((C, gap), F32), we3[...].astype(F32)], axis=1).astype(BF)
        for s in range(2):
            w1t[s] = jnp.transpose(w1o[s].astype(F32)).astype(BF)
            w3t[s] = jnp.transpose(w3o[s].astype(F32)).astype(BF)
        w2t[...] = jnp.transpose(w2p[...].astype(F32)).astype(BF)
        zero = jnp.zeros((1, gap), F32)
        gains[0, 0:1] = jnp.concatenate([gain[...], zero], axis=1)
        gains[0, 1:2] = jnp.concatenate([offset[...], zero], axis=1)
        gains[1, 0:1] = jnp.concatenate([zero, gain[...]], axis=1)
        gains[1, 1:2] = jnp.concatenate([zero, offset[...]], axis=1)

    tile = lambda d: jnp.clip(i - d, 0, tiles - 1)
    sides = [slice(0, half), slice(half, 2 * half)]

    t4 = tile(1)
    valid = jnp.where(i >= 1, 1.0, 0.0)
    slabs = slab_pairs(edges4[...], C)
    cots = slab_pairs(cot[...], C)
    lane = lax.broadcasted_iota(I32, (half, 256), 1)
    outs, grads, ups = [], [], []
    for s in range(2):
        inside = (lane < C) if s == 0 else (lane >= gap)
        keep = lambda v: jnp.where(inside, v, 0.0)
        mean = lambda v: jnp.sum(v, axis=-1, keepdims=True) * (1.0 / C)
        value = keep(slabs[s].astype(F32)) + res3[sides[s], :]
        centred = keep(value - mean(value))
        inverse = lax.rsqrt(mean(centred * centred) + EPS)
        normal = centred * inverse
        outs.append(normal * gains[s, 0:1] + gains[s, 1:2])
        upstream = keep(cots[s].astype(F32)) * valid
        moved = upstream * normal
        for r in range(half // rows):
            part = slice(r * rows, (r + 1) * rows)
            ag[s, 0] += moved[part]
            ag[s, 1] += upstream[part]
        scaled = upstream * gains[s, 0:1]
        grad = inverse * (scaled - mean(scaled) - normal * mean(scaled * normal))
        grad = keep(grad)
        grads.append(grad)
        low3 = grad.astype(BF)
        a3[s] += dot_tn(hid2[sides[s], :], low3)
        ups.append(dot(low3, w3t[s]))
    edge_out[...] = join_slab(outs[0], outs[1], rows, C).astype(BF)

    t5 = tile(1)
    low2 = (jnp.concatenate(ups, axis=0) * slope2[0].astype(F32)).astype(BF)
    a2[...] += dot_tn(hid1[0], low2)
    up1v = dot(low2, w2t[...])

    t6 = tile(1)
    low1 = (up1v * slope1[0].astype(F32)).astype(BF)
    slabs = slab_pairs(edges4[...], C)
    outs = []
    for s in range(2):
        a1[s] += dot_tn(low1[sides[s]], slabs[s])
        outs.append(grads[s] + dot(low1[sides[s]], w1t[s]))
    partial[...] = join_slab(outs[0], outs[1], rows, C).astype(BF)
    wide = low1.astype(F32)
    acc = wide[:rows]
    for j in range(1, GROUP):
        acc = acc + wide[j * rows : (j + 1) * rows]
    near_sum[...] += acc
    target = jnp.concatenate([trow[pl.ds(t6 * GROUP + j, 1), :] for j in ORDER], axis=1)
    add_by_target(target, low1, total)

    t1 = tile(0)
    slabs = slab_pairs(edges1[...], C)
    own = jnp.concatenate([dot(slabs[0], w1o[0]), dot(slabs[1], w1o[1])], axis=0)
    got = gather_table([lane_column(tcol, t1 * GROUP + j) for j in ORDER], far_all)
    pre1v = got + own + jnp.concatenate([near[...]] * GROUP, axis=0)

    t2 = tile(0)
    act, slope = gelu_pair(pre1v)
    hid1[0] = act
    slope1[0] = slope
    pre2v = dot(act, w2p[...])

    t3 = tile(0)
    act, slope = gelu_pair(pre2v)
    hid2[...] = act
    slope2[0] = slope
    for s in range(2):
        res3[sides[s], :] = dot(act[sides[s]], w3o[s])

    @pl.when(i == tiles)
    def _():
        far_sum[...] = total[...].astype(BF)
        dw1[...] = jnp.transpose(a1[0])[:C, :] + jnp.transpose(a1[1])[gap:, :]
        dw2[...] = a2[...]
        shifted = a3[1][:, gap:]
        dw3[...] = a3[0] + jnp.concatenate([shifted, jnp.zeros((256, gap), F32)], axis=1)
        for r in range(2):
            even = jnp.sum(ag[0, r], axis=0, keepdims=True)
            odd = jnp.sum(ag[1, r], axis=0, keepdims=True)
            row = even + jnp.concatenate([odd[:, gap:], jnp.zeros((1, gap), F32)], axis=1)
            dgain[r * 8 : r * 8 + 8, :] = jnp.broadcast_to(row, (8, 256))


def edge_call(C, tcol, trow, far_all, near, we1, we2, we3, gain, offset, edges, cot):
    rows = near.shape[0]
    count = far_all.shape[0]
    K = edges.shape[1] // C
    tiles = K // GROUP
    size = GROUP * rows
    shape = jax.ShapeDtypeStruct
    slab = lambda d: pl.BlockSpec(
        (rows, GROUP * C), lambda g: (0, jnp.clip(g - d, 0, tiles - 1))
    )
    fixed = lambda *s: pl.BlockSpec(
        s, lambda g: (0,) * len(s), pipeline_mode=pl.Buffered(buffer_count=1)
    )
    return pl.pallas_call(
        functools.partial(edge_kernel, tiles, C),
        grid=(tiles + 1,),
        in_specs=[full(x) for x in (tcol, trow, far_all, near, we1, we2, we3, gain, offset)]
        + [slab(0), slab(1), slab(99), slab(1)],
        out_specs=[
            slab(1), slab(1), fixed(count, 256), fixed(rows, 256),
            fixed(C, 256), fixed(256, 256), fixed(256, 256), fixed(16, 256),
        ],
        out_shape=[
            shape((rows, K * C), BF),
            shape((rows, K * C), BF),
            shape((count, 256), BF),
            shape((rows, 256), F32),
            shape((C, 256), F32),
            shape((256, 256), F32),
            shape((256, 256), F32),
            shape((16, 256), F32),
        ],
        scratch_shapes=[
            pltpu.VMEM((2, 256, 256), BF),
            pltpu.VMEM((256, 256), BF),
            pltpu.VMEM((2, 256, 256), BF),
            pltpu.VMEM((2, 256, 256), BF),
            pltpu.VMEM((256, 256), BF),
            pltpu.VMEM((2, 256, 256), BF),
            pltpu.VMEM((2, 8, 256), F32),
            pltpu.VMEM((count, 256), F32),
            pltpu.VMEM((2, 256, 256), F32),
            pltpu.VMEM((256, 256), F32),
            pltpu.VMEM((2, 256, 256), F32),
            pltpu.VMEM((2, 2, rows, 256), F32),
            pltpu.VMEM((size, 256), F32),
            pltpu.VMEM((3, size, 256), BF),
            pltpu.VMEM((4, size, 256), BF),
            pltpu.VMEM((size, 256), F32),
            pltpu.VMEM((size, 256), BF),
            pltpu.VMEM((2, size, 256), BF),
            pltpu.VMEM((size, 256), F32),
            pltpu.VMEM((2, size, 256), F32),
            pltpu.VMEM((size, 256), F32),
            pltpu.VMEM((size, 256), F32),
        ],
        compiler_params=LOCAL,
    )(tcol, trow, far_all, near, we1, we2, we3, gain, offset, edges, edges, edges, cot)


def norm_back(upstream, normal, inverse, gain):
    scaled = upstream * gain
    return inverse * (scaled - row_mean(scaled) - normal * row_mean(scaled * normal))


def node_back(
    C, far, near_sum, cot, n1, n2, inv, slope, w3, g1, wf1, wf2, g2, we1, grad_one, resid_out, dgain, v_own
):
    rows, D = cot.shape
    far = far.astype(BF)[:, :C]
    near = near_sum[...].astype(BF)[:, :C]
    grad = cot[...].astype(F32) + dot(near, we1[:, :D]) + dot(far, we1[:, D : 2 * D])
    two = norm_back(grad, n2[...], inv[1][:, 0:1], g2[...])
    dgain[16:24, :] = jnp.broadcast_to(jnp.sum(grad * n2[...], axis=0, keepdims=True), (8, D))
    dgain[24:32, :] = jnp.broadcast_to(jnp.sum(grad, axis=0, keepdims=True), (8, D))
    resid = two.astype(BF)
    resid_out[...] = resid
    inner = (dot_nt(resid, wf2[...]) * slope[...].astype(F32)).astype(BF)
    grad = two + dot_nt(inner, wf1[...])
    one = norm_back(grad, n1[...], inv[0][:, 0:1], g1[...])
    dgain[0:8, :] = jnp.broadcast_to(jnp.sum(grad * n1[...], axis=0, keepdims=True), (8, D))
    dgain[8:16, :] = jnp.broadcast_to(jnp.sum(grad, axis=0, keepdims=True), (8, D))
    grad_one[...] = one
    upper = (one / spread(inv[2], D)).astype(BF)
    v_own[...] = dot_nt(upper, w3[...]).astype(BF)
    return far, near, upper


def node_back_kernel(
    n, C, far_sum, near_sum, cot, node_low, n1, n2, inv, slope, summed,
    w3, g1, wf1, wf2, g2, we1,
    grad_one, vw_all, resid_out, dgain, dw3, dwe_near, dwe_far,
    pair_buf, far_buf, v_own, send, recv, gsend, grecv, own_sem,
):
    place = Place(n)
    rows = cot.shape[0]
    greet([place.sibling] + place.mates)
    far = scatter_sum(place, far_sum, pair_buf, far_buf, send, recv)
    far, near, upper = node_back(
        C, far, near_sum, cot, n1, n2, inv, slope, w3, g1, wf1, wf2, g2, we1,
        grad_one, resid_out, dgain, v_own,
    )
    gather = Gather(place, v_own, vw_all, gsend, grecv)
    gather.start()
    own = pltpu.make_async_copy(v_own, block(vw_all, place.me, rows), own_sem.at[0])
    own.start()
    dw3[...] = dot_tn(summed[...], upper)
    dwe_near[...] = dot_tn(node_low[...], near)
    dwe_far[...] = dot_tn(node_low[...], far)
    own.wait()
    gather.finish()


def node_back_call(n, C, *args):
    cot = args[2]
    rows, D = cot.shape
    shape = jax.ShapeDtypeStruct
    return pl.pallas_call(
        functools.partial(node_back_kernel, n, C),
        in_specs=[WHOLE] * len(args),
        out_specs=[WHOLE] * 7,
        out_shape=[
            shape((rows, D), F32),
            shape((n * rows, D), BF),
            shape((rows, D), BF),
            shape((32, D), F32),
            shape((D, D), F32),
            shape((D, C), F32),
            shape((D, C), F32),
        ],
        scratch_shapes=[
            *comm_scratch(n, rows, 256),
            pltpu.VMEM((rows, D), BF),
            *sems(n),
            *sems(n),
            pltpu.SemaphoreType.DMA((1,)),
        ],
        compiler_params=remote_params(2),
    )(*args)


class Line:
    def __init__(self, place, pieces, x, out, pair_buf, low_buf, high_buf, send_buf, send, recv):
        self.place, self.pieces, self.x, self.out = place, pieces, x, out
        self.pair_buf, self.low_buf, self.high_buf = pair_buf, low_buf, high_buf
        self.send_buf, self.send, self.recv = send_buf, send, recv
        c, q, chips = place.chip, place.core, place.chips
        self.root = chips // 2 - 1 + q
        self.away = jnp.abs(c - self.root)
        self.right = jnp.minimum(c + 1, chips - 1) * 2 + q
        self.left = jnp.maximum(c - 1, 0) * 2 + q
        self.half = x.shape[0] // 2
        self.rows = self.half // pieces

    def part(self, which, p):
        return pl.ds(pl.multiple_of(which * self.half + p * self.rows, self.rows), self.rows)

    def here(self, p):
        return pl.ds(pl.multiple_of(p * self.rows, self.rows), self.rows)

    def link(self, src, dst, p, sent, got, peer):
        n = self.pieces
        return remote(src, dst, self.send.at[sent * n + p], self.recv.at[got * n + p], peer)

    def pair(self, p):
        src = self.x.at[self.part(1 - self.place.core, p)]
        return self.link(src, self.pair_buf.at[self.here(p)], p, 0, 0, self.place.sibling)

    def up(self, p):
        here = self.here(p)
        return self.link(self.send_buf.at[here], self.low_buf.at[here], p, 1, 1, self.right)

    def down(self, p):
        here = self.here(p)
        return self.link(self.send_buf.at[here], self.high_buf.at[here], p, 2, 2, self.left)

    def outward(self, p, sent, got, peer):
        mine = self.out.at[self.part(self.place.core, p)]
        return self.link(mine, mine, p, sent, got, peer)

    def out_left(self, p):
        return self.outward(p, 3, 3, self.left)

    def out_right(self, p):
        return self.outward(p, 5, 3, self.right)

    def across(self, p):
        return self.outward(p, 4, 4, self.place.sibling)

    def each(self, step):
        lax.fori_loop(0, self.pieces, lambda p, z: (step(p), z)[1], 0)

    def start(self):
        self.each(lambda p: self.pair(p).start())

    def reduce(self, p):
        c, root, last = self.place.chip, self.root, self.place.chips - 1
        here, mine_at = self.here(p), self.part(self.place.core, p)
        self.pair(p).wait_recv()
        mine = lambda: self.x[mine_at, :].astype(F32) + self.pair_buf[here, :].astype(F32)

        def end():
            self.send_buf[here, :] = mine().astype(BF)

        def from_low():
            self.up(p).wait_recv()
            self.send_buf[here, :] = (mine() + self.low_buf[here, :].astype(F32)).astype(BF)

        def from_high():
            self.down(p).wait_recv()
            self.send_buf[here, :] = (mine() + self.high_buf[here, :].astype(F32)).astype(BF)

        def at_root():
            self.up(p).wait_recv()
            self.down(p).wait_recv()
            total = mine() + self.low_buf[here, :].astype(F32) + self.high_buf[here, :].astype(F32)
            self.out[mine_at, :] = total.astype(BF)
            self.out_left(p).start()
            self.out_right(p).start()
            self.across(p).start()

        pl.when((c == 0) | (c == last))(end)
        pl.when((c > 0) & (c < root))(from_low)
        pl.when((c > root) & (c < last))(from_high)
        pl.when(c < root)(lambda: self.up(p).start())
        pl.when(c > root)(lambda: self.down(p).start())
        pl.when(c == root)(at_root)

    def spread(self, p):
        c, root, last = self.place.chip, self.root, self.place.chips - 1

        def leftward():
            self.out_left(p).wait_recv()
            pl.when(c > 0)(lambda: self.out_left(p).start())
            self.across(p).start()

        def rightward():
            self.out_right(p).wait_recv()
            pl.when(c < last)(lambda: self.out_right(p).start())
            self.across(p).start()

        pl.when(c < root)(leftward)
        pl.when(c > root)(rightward)

    def slots(self, lag):
        return self.pieces + 2 * lag * (self.place.chips // 2)

    def slot(self, s, lag):
        deep = self.place.chips // 2
        p = s - lag * (deep - self.away)
        pl.when((p >= 0) & (p < self.pieces))(lambda: self.reduce(p))
        o = s - lag * (deep + self.away)
        pl.when((o >= 0) & (o < self.pieces) & (self.away > 0))(lambda: self.spread(o))

    def finish(self):
        c, root, last = self.place.chip, self.root, self.place.chips - 1

        def end(p):
            self.pair(p).wait_send()
            self.across(p).wait_send()
            pl.when(c < root)(lambda: self.up(p).wait_send())
            pl.when(c > root)(lambda: self.down(p).wait_send())
            pl.when((c <= root) & (c > 0))(lambda: self.out_left(p).wait_send())
            pl.when((c >= root) & (c < last))(lambda: self.out_right(p).wait_send())

        self.each(lambda p: self.across(p).wait_recv())
        self.each(end)


def line_scratch(rows, width, pieces):
    return [pltpu.VMEM((rows // 2, width), BF)] * 4 + sems(6 * pieces)


class Exchange:
    def __init__(self, place, n, mine, got, send, recv):
        self.place, self.n, self.mine, self.got = place, n, mine, got
        self.copies = []
        for d in range(1, n):
            peer = lax.rem(place.me + d, n)
            self.copies.append(remote(mine, got.at[place.me], send.at[d], recv.at[d], peer))

    def start(self):
        for copy in self.copies:
            copy.start()
        self.got[self.place.me] = self.mine[...]

    def finish(self):
        for copy in self.copies:
            copy.wait_recv()
        total = self.got[0]
        for e in range(1, self.n):
            total = total + self.got[e]
        for copy in self.copies:
            copy.wait_send()
        return total


EARLY, LATE, LAG = 7, 9, 2
SPREAD_AT = 0


def early_rows(D, C):
    used = D + (2 * D + C) // 2 + C
    unit = 2 * EARLY * 16
    return -(-used // unit) * unit


def pack_early(C, x, gains, dw3, dwe_near, dwe_far, dwe1, dwe2, dwe3, dgain, dg3):
    D = dw3.shape[0]
    x[:D, :] = dw3[...].astype(BF)
    spare = jnp.zeros((D, 256 - C), F32)
    edge1 = jnp.concatenate(
        [
            jnp.concatenate([dwe_near[...], spare], axis=1),
            jnp.concatenate([dwe_far[...], spare], axis=1),
            dwe1[...],
        ],
        axis=0,
    ).astype(BF)
    half = edge1.shape[0] // 2
    x[D : D + half, :256] = edge1[:half]
    x[D : D + half, 256:] = edge1[half:]
    at = D + half
    x[at : at + C, :256] = dwe2[:C, :].astype(BF)
    x[at : at + C, 256:] = dwe3[:C, :].astype(BF)
    if at + C < x.shape[0]:
        x[at + C :, :] = jnp.zeros((x.shape[0] - at - C, D), BF)
    gains[...] = jnp.zeros_like(gains)
    for r in range(4):
        gains[r : r + 1, :] = dgain[8 * r : 8 * r + 1, :]
    for r in range(2):
        gains[4 + r : 5 + r, :256] = dg3[8 * r : 8 * r + 1, :]


def back_start(C, w1, w2, w2t, w_own, w_own_t, zeroed):
    D = w2.shape[0]
    gap = 256 - C
    for ref in (w_own, *zeroed):
        ref[...] = jnp.zeros_like(ref)
    w_own[0, :C, :] = w1[2 * D :, :]
    w_own[1, gap:, :] = w1[2 * D :, :]
    for s in range(2):
        w_own_t[s] = jnp.transpose(w_own[s].astype(F32)).astype(BF)
    w2t[...] = jnp.transpose(w2[...].astype(F32)).astype(BF)


def back_tile(
    g, rows, C, tcol, trow, vw, act1, slope1, slope2, edges, partial, grad_edges,
    w2t, w_own_t, total, a2, ae, source_sum,
):
    half = GROUP // 2 * rows
    ks = [g * GROUP + j for j in ORDER]
    up = gather_table([lane_column(tcol, k) for k in ks], vw)
    upper = up.astype(BF) * slope2[...]
    a2[...] += dot_tn(act1[...], upper)
    lower = dot(upper, w2t[...]).astype(BF) * slope1[...]
    wide = lower.astype(F32)
    acc = wide[:rows]
    for j in range(1, GROUP):
        acc = acc + wide[j * rows : (j + 1) * rows]
    source_sum[...] += acc
    target = jnp.concatenate([trow[pl.ds(k, 1), :] for k in ks], axis=1)
    add_by_target(target, lower, total)
    slabs = slab_pairs(edges[...], C)
    lowers = [lower[:half], lower[half:]]
    own = []
    for s in range(2):
        ae[s] += dot_tn(slabs[s], lowers[s])
        own.append(dot(lowers[s], w_own_t[s]))
    grad_edges[...] = (partial[...].astype(F32) + join_slab(own[0], own[1], rows, C)).astype(BF)


def back_weights(C, dw1, dw2, nodes_all, nodes, total, a2, ae, source_sum):
    D = nodes.shape[1]
    gap = 256 - C
    dw2[...] = a2[...].astype(BF)
    dw1[:D, :] = dot_tn(nodes[...], source_sum[...].astype(BF)).astype(BF)
    dw1[2 * D :, :] = (ae[0][:C, :] + ae[1][gap:, :]).astype(BF)
    a2[...] = jnp.zeros_like(a2)

    def weigh(part):
        a2[...] += dot_tn(nodes_all[part, :], total[part, :].astype(BF))

    by_chunks(total.shape[0], weigh)
    dw1[D : 2 * D, :] = a2[...].astype(BF)


def tail(early, late, scatter, source_sum, grad_one, w1, grad_nodes, feed):
    D = grad_one.shape[1]
    early.start()
    late.start()
    scatter.start()

    def feed_part(f):
        low, resid, wf1, wf2, dwf1, dwf2 = feed
        step = 256
        cols = pl.ds(pl.multiple_of(f * step, step), step)
        act, slope = gelu_full(dot(low[...], wf1[:, cols]))
        dwf2[cols, :] = dot_tn(act, resid[...]).astype(BF)
        inner = (dot_nt(resid[...], wf2[cols, :]) * slope.astype(F32)).astype(BF)
        dwf1[:, cols] = dot_tn(low[...], inner).astype(BF)

    parts = feed[2].shape[1] // 256 if feed else 0

    def slot(s, carry):
        early.slot(s, LAG)
        late.slot(s - EARLY, LAG)
        if feed:
            pl.when((s % 2 == 1) & (s // 2 < parts))(lambda: feed_part(s // 2))
        return carry

    first = SPREAD_AT
    lax.fori_loop(0, first, slot, 0)
    scatter.pass_on()
    lax.fori_loop(first, EARLY + late.slots(LAG), slot, 0)
    source = dot_nt(source_sum[...].astype(BF), w1[:D, :])
    total = scatter.finish()
    grad_nodes[...] = grad_one[...] + source + dot_nt(total.astype(BF), w1[D : 2 * D, :])
    early.finish()
    late.finish()


def back_kernel(n, tiles, C, tcol, trow, nodes, near_sum, g1, g2, dwe1, dwe2, dwe3, dg3, *refs):
    sources, refs = refs[:16], refs[16:]
    act1, slope1, slope2, edges, partial, *refs = refs
    grad_edges, grad_nodes, small, dwf1, dwf2, early_h, late_h, *refs = refs
    held, refs = refs[:16], refs[16:]
    (
        far_sum, low_own, cot, we1, n2, inv, wf2, slope, wf1, n1, w3, w1, w2, summed, node_low, nodes_all
    ) = held
    (
        load_sem, low, lsend, lrecv, vw, v_own, grad_one, resid_own, dgain, dw3, dwe_near, dwe_far,
        resid, bsend, brecv, vsend, vrecv, hsend, hrecv, pair_h, far_h,
        w2t, w_own, w_own_t, total, a2, ae, source_sum, target_sum, gains, got, gsend, grecv,
        pair_buf, far_buf, send, recv, x1, out1, x2, out2, *line_refs,
    ) = refs
    g = pl.program_id(0)
    rows, D = nodes.shape
    place = Place(n)
    loads = Loads(list(zip(sources, held)), load_sem)
    gather = Gather(place, resid_own, resid, bsend, brecv)
    gather_low = Gather(place, low_own, low, lsend, lrecv)
    early = Line(place, EARLY, x1, out1, *line_refs[: len(line_refs) // 2])
    late = Line(place, LATE, x2, out2, *line_refs[len(line_refs) // 2 :])
    exchange = Exchange(place, n, gains, got, gsend, grecv)

    @pl.when(g == 0)
    def _():
        loads.start()
        greet([lax.rem(place.me + d, n) for d in range(1, n)])
        loads.wait(0, 2)
        scatter = Scatter(place, far_sum, pair_h, far_h, hsend, hrecv)
        scatter.start()
        scatter.pass_on()
        mine = pl.ds(pl.multiple_of(place.me * rows, rows), rows)
        low[mine, :] = low_own[...]
        loads.wait(2, 15)
        back_start(C, w1, w2, w2t, w_own, w_own_t, (total, a2, ae, source_sum))
        far, near, upper = node_back(
            C, scatter.finish(), near_sum, cot, n1, n2, inv, slope, w3, g1, wf1, wf2, g2, we1,
            grad_one, resid_own, dgain, v_own,
        )
        spread_v = Gather(place, v_own, vw, vsend, vrecv)
        spread_v.start()
        dw3[...] = dot_tn(summed[...], upper)
        dwe_near[...] = dot_tn(node_low[...], near)
        dwe_far[...] = dot_tn(node_low[...], far)
        pack_early(C, x1, gains, dw3, dwe_near, dwe_far, dwe1, dwe2, dwe3, dgain, dg3)
        vw[mine, :] = v_own[...]
        resid[mine, :] = resid_own[...]
        spread_v.finish()
        exchange.start()

    pl.when(g == 1)(gather_low.start)
    pl.when(g == tiles // 2)(gather.start)
    back_tile(
        g, rows, C, tcol, trow, vw, act1, slope1, slope2, edges, partial, grad_edges,
        w2t, w_own_t, total, a2, ae, source_sum,
    )

    @pl.when(g == tiles - 1)
    def _():
        target_sum[...] = total[...].astype(BF)
        loads.wait(15)
        at = 2 * D + C
        back_weights(
            C, x2.at[pl.ds(0, at)], x2.at[pl.ds(at, D)], nodes_all, nodes, total, a2, ae, source_sum
        )
        small[...] = exchange.finish()
        gather_low.finish()
        gather.finish()
        scatter = Scatter(place, target_sum, pair_buf, far_buf, send, recv)
        tail(
            early, late, scatter, source_sum, grad_one, w1, grad_nodes, (low, resid, wf1, wf2, dwf1, dwf2)
        )
        keep_early = pltpu.make_async_copy(out1, early_h, load_sem.at[16])
        keep_early.start()
        keep_late = pltpu.make_async_copy(out2, late_h, load_sem.at[17])
        keep_late.start()
        keep_early.wait()
        keep_late.wait()


def back_call(n, C, whole, loaded, act1, slope1, slope2, edges, partial):
    rows, D = whole[2].shape
    count = n * rows
    K = edges.shape[1] // C
    tiles = K // GROUP
    size = GROUP * rows
    FF = loaded[8].shape[1]
    early, late = early_rows(D, C), 3 * D + C
    shape = jax.ShapeDtypeStruct
    slab = pl.BlockSpec((rows, GROUP * C), lambda g: (0, g))
    tile = pl.BlockSpec((size, D), lambda g: (g, 0))
    outs = [
        shape((rows, D), F32),
        shape((8, D), F32),
        shape((D, FF), BF),
        shape((FF, D), BF),
    ]
    return pl.pallas_call(
        functools.partial(back_kernel, n, tiles, C),
        grid=(tiles,),
        in_specs=[full(v) for v in whole] + [HBM] * len(loaded) + [tile, tile, tile, slab, slab],
        out_specs=[slab] + [fixed(*v.shape) for v in outs] + [HBM] * 2,
        out_shape=[shape((rows, K * C), BF)]
        + outs
        + [shape((early, D), BF), shape((late, D), BF)],
        scratch_shapes=[pltpu.VMEM(v.shape, v.dtype) for v in loaded]
        + [
            pltpu.SemaphoreType.DMA((18,)),
            pltpu.VMEM((count, D), BF),
            *sems(n),
            pltpu.VMEM((count, D), BF),
            pltpu.VMEM((rows, D), BF),
            pltpu.VMEM((rows, D), F32),
            pltpu.VMEM((rows, D), BF),
            pltpu.VMEM((32, D), F32),
            pltpu.VMEM((D, D), F32),
            pltpu.VMEM((D, C), F32),
            pltpu.VMEM((D, C), F32),
            pltpu.VMEM((count, D), BF),
            *sems(n),
            *sems(n),
            *sems(n),
            *comm_scratch(n, rows, 256),
            pltpu.VMEM((D, D), BF),
            pltpu.VMEM((2, 256, D), BF),
            pltpu.VMEM((2, D, 256), BF),
            pltpu.VMEM((count, D), F32),
            pltpu.VMEM((D, D), F32),
            pltpu.VMEM((2, 256, D), F32),
            pltpu.VMEM((rows, D), F32),
            pltpu.VMEM((count, D), BF),
            pltpu.VMEM((8, D), F32),
            pltpu.VMEM((n, 8, D), F32),
            *sems(n),
            *comm_scratch(n, rows, D),
            *sems(n),
            pltpu.VMEM((early, D), BF),
            pltpu.VMEM((early, D), BF),
            pltpu.VMEM((late, D), BF),
            pltpu.VMEM((late, D), BF),
            *line_scratch(early, D, EARLY),
            *line_scratch(late, D, LATE),
        ],
        compiler_params=remote_params(3),
    )(*whole, *loaded, act1, slope1, slope2, edges, partial)


def message_back_kernel(
    tiles, C, tcol, trow, nodes_all, nodes, vw, w1, w2, act1, slope1, slope2, edges, partial,
    grad_edges, dw1, dw2, target_sum, source_sum, w2t, w_own, w_own_t, total, a2, ae,
):
    g = pl.program_id(0)

    @pl.when(g == 0)
    def _():
        back_start(C, w1, w2, w2t, w_own, w_own_t, (total, a2, ae, source_sum))

    back_tile(
        g, nodes.shape[0], C, tcol, trow, vw, act1, slope1, slope2, edges, partial, grad_edges,
        w2t, w_own_t, total, a2, ae, source_sum,
    )

    @pl.when(g == tiles - 1)
    def _():
        target_sum[...] = total[...].astype(BF)
        back_weights(C, dw1, dw2, nodes_all, nodes, total, a2, ae, source_sum)


def message_back_call(C, tcol, trow, nodes_all, nodes, vw, w1, w2, act1, slope1, slope2, edges, partial):
    rows, D = nodes.shape
    count = vw.shape[0]
    K = edges.shape[1] // C
    tiles = K // GROUP
    size = GROUP * rows
    shape = jax.ShapeDtypeStruct
    slab = pl.BlockSpec((rows, GROUP * C), lambda g: (0, g))
    tile = pl.BlockSpec((size, D), lambda g: (g, 0))
    return pl.pallas_call(
        functools.partial(message_back_kernel, tiles, C),
        grid=(tiles,),
        in_specs=[full(x) for x in (tcol, trow, nodes_all, nodes, vw, w1, w2)]
        + [tile, tile, tile, slab, slab],
        out_specs=[slab, fixed(2 * D + C, D), fixed(D, D), fixed(count, D), fixed(rows, D)],
        out_shape=[
            shape((rows, K * C), BF),
            shape((2 * D + C, D), BF),
            shape((D, D), BF),
            shape((count, D), BF),
            shape((rows, D), F32),
        ],
        scratch_shapes=[
            pltpu.VMEM((D, D), BF),
            pltpu.VMEM((2, 256, D), BF),
            pltpu.VMEM((2, D, 256), BF),
            pltpu.VMEM((count, D), F32),
            pltpu.VMEM((D, D), F32),
            pltpu.VMEM((2, 256, D), F32),
        ],
        compiler_params=LOCAL,
    )(tcol, trow, nodes_all, nodes, vw, w1, w2, act1, slope1, slope2, edges, partial)


def final_kernel(
    n, C, target_sum, source_sum, grad_one, w1, dw1, dw2, dw3, dwe_near, dwe_far, dwe1, dwe2, dwe3,
    dgain, dg3, grad_nodes, out1, out2, small,
    x1, x2, gains, got, gsend, grecv, pair_buf, far_buf, send, recv, *line_refs,
):
    place = Place(n)
    D = grad_one.shape[1]
    pack_early(C, x1, gains, dw3, dwe_near, dwe_far, dwe1, dwe2, dwe3, dgain, dg3)
    at = 2 * D + C
    x2[:at, :] = dw1[...]
    x2[at:, :] = dw2[...]
    greet([lax.rem(place.me + d, n) for d in range(1, n)])
    early = Line(place, EARLY, x1, out1, *line_refs[: len(line_refs) // 2])
    late = Line(place, LATE, x2, out2, *line_refs[len(line_refs) // 2 :])
    exchange = Exchange(place, n, gains, got, gsend, grecv)
    exchange.start()
    small[...] = exchange.finish()
    scatter = Scatter(place, target_sum, pair_buf, far_buf, send, recv)
    tail(early, late, scatter, source_sum, grad_one, w1, grad_nodes, None)


def final_call(n, C, args):
    rows, D = args[2].shape
    early, late = early_rows(D, C), 3 * D + C
    shape = jax.ShapeDtypeStruct
    return pl.pallas_call(
        functools.partial(final_kernel, n, C),
        in_specs=[WHOLE] * len(args),
        out_specs=[WHOLE] * 4,
        out_shape=[
            shape((rows, D), F32),
            shape((early, D), BF),
            shape((late, D), BF),
            shape((8, D), F32),
        ],
        scratch_shapes=[
            pltpu.VMEM((early, D), BF),
            pltpu.VMEM((late, D), BF),
            pltpu.VMEM((8, D), F32),
            pltpu.VMEM((n, 8, D), F32),
            *sems(n),
            *comm_scratch(n, rows, D),
            *sems(n),
            *line_scratch(early, D, EARLY),
            *line_scratch(late, D, LATE),
        ],
        compiler_params=remote_params(4),
    )(*args)


def feed_kernel(low, resid, wf1, wf2, dwf1, dwf2):
    @pl.when(pl.program_id(1) == 0)
    def _():
        dwf1[...] = jnp.zeros_like(dwf1)
        dwf2[...] = jnp.zeros_like(dwf2)

    act, slope = gelu_full(dot(low[...], wf1[...]))
    dwf2[...] += dot_tn(act, resid[...])
    inner = (dot_nt(resid[...], wf2[...]) * slope.astype(F32)).astype(BF)
    dwf1[...] += dot_tn(low[...], inner)


def feed_call(low, resid, wf1, wf2):
    count = low.shape[0]
    D, FF = wf1.shape
    step, rows = min(FF, 512), min(count, TABLE)
    shape = jax.ShapeDtypeStruct
    return pl.pallas_call(
        feed_kernel,
        grid=(FF // step, count // rows),
        in_specs=[
            pl.BlockSpec((rows, D), lambda f, r: (r, 0)),
            pl.BlockSpec((rows, D), lambda f, r: (r, 0)),
            pl.BlockSpec((D, step), lambda f, r: (0, f)),
            pl.BlockSpec((step, D), lambda f, r: (f, 0)),
        ],
        out_specs=[
            pl.BlockSpec((D, step), lambda f, r: (0, f)),
            pl.BlockSpec((step, D), lambda f, r: (f, 0)),
        ],
        out_shape=[shape((D, FF), F32), shape((FF, D), F32)],
        compiler_params=LOCAL,
    )(low, resid, wf1, wf2)


def unpack_kernel(C, steps, late, packed, small, node_in, grad_in, edges, *refs):
    g = pl.program_id(0)
    D = late.shape[1]
    plain = refs[: (len(refs) - 15) // 2]
    w1, w2, w3, grad_edges, one, two, three, node_out, grad_nodes, *outs = refs[len(plain) :]
    gains = outs[len(plain) :]
    grad_edges[...] = edges[...].astype(F32)
    first = 2 * D + C
    for ref, src, base in ((w1, late, 0), (w2, late, first), (w3, packed, 0)):
        step = ref.shape[0]
        ref[...] = src[pl.ds(pl.multiple_of(base + g * step, 16), step), :].astype(F32)
    at = D
    for a, b in zip(plain, outs):
        b[...] = a[...].astype(F32)

    @pl.when(g == steps - 1)
    def _():
        half = (2 * D + C) // 2
        for r in range(2):
            left = 256 * r
            flipped = jnp.transpose(packed[at : at + half, left : left + 256].astype(F32))
            one[:, half * r : half * r + half] = flipped[:C, :]
        end = at + half
        two[...] = packed[end : end + C, :C].astype(F32)
        three[...] = packed[end : end + C, 256 : 256 + C].astype(F32)
        node_out[...] = node_in[...]
        grad_nodes[...] = grad_in[...]
        for r in range(6):
            width = D if r < 4 else C
            gains[r][...] = small[r : r + 1, :width]


def unpack_call(C, late, packed, small, node_out, grad_nodes, edges, arrays):
    steps = 4
    D = packed.shape[1]
    first = 2 * D + C
    shape = jax.ShapeDtypeStruct
    cut = lambda r, c: pl.BlockSpec((r // steps, c), lambda g: (g, 0))
    head = [(first, D), (D, D), (D, D), edges.shape]
    last = [(C, first), (C, C), (C, C)]
    plain = [v.shape for v in arrays]
    gains = [(1, D)] * 4 + [(1, C)] * 2
    return pl.pallas_call(
        functools.partial(unpack_kernel, C, steps),
        grid=(steps,),
        in_specs=[full(v) for v in (late, packed, small, node_out, grad_nodes)] + [cut(*v.shape) for v in (edges, *arrays)],
        out_specs=[cut(*v) for v in head]
        + [fixed(*v) for v in last]
        + [fixed(*node_out.shape)] * 2
        + [cut(*v) for v in plain]
        + [fixed(*v) for v in gains],
        out_shape=[shape(v, F32) for v in head + last]
        + [shape(node_out.shape, BF), shape(node_out.shape, F32)]
        + [shape(v, F32) for v in plain + gains],
        compiler_params=LOCAL,
    )(late, packed, small, node_out, grad_nodes, edges, *arrays)


def body(
    nodes, edges, nbr_owner, nbr_slot, edge_mask, w_msg1, w_msg2, w_msg3, gain_one, offset_one,
    w_ffn1, w_ffn2, gain_two, offset_two, w_edge1, w_edge2, w_edge3, gain_three, offset_three,
    node_cotangent, edge_cotangent,
):
    n = lax.axis_size("edge")
    rows, D = nodes.shape
    C = w_edge2.shape[0]
    we1 = w_edge1.T
    g1, o1, g2, o2 = (v.reshape(1, D) for v in (gain_one, offset_one, gain_two, offset_two))
    (
        act1, slope1, slope2, tcol, trow, node_out, near, low, n1, n2, inv, slope, own_sum,
        nodes_all, far_all,
    ) = forward_call(
        n, C, nodes, nbr_owner[:, :, 0], nbr_slot.T, edge_mask.T, g1, o1, g2, o2,
        [w_msg1, w_msg2, w_msg3, w_ffn1, w_ffn2, we1], edges,
    )
    edge_out, partial, far_sum, near_sum, dwe1, dwe2, dwe3, dg3 = edge_call(
        C, tcol, trow, far_all, near, we1, w_edge2, w_edge3,
        gain_three.reshape(1, C), offset_three.reshape(1, C), edges, edge_cotangent,
    )
    kept = [act1, slope1, slope2, edges, partial]
    if n * rows <= TABLE:
        grad_edges, grad_nodes, small, *dwf, early, late = back_call(
            n, C, [tcol, trow, nodes, near_sum, g1, g2, dwe1, dwe2, dwe3, dg3],
            [
                far_sum, low, node_cotangent, we1, n2, inv, w_ffn2, slope, w_ffn1, n1, w_msg3, w_msg1,
                w_msg2, own_sum, node_out, nodes_all,
            ],
            *kept,
        )
    else:
        grad_one, vw_all, resid, dgain, dw3, dwe_near, dwe_far = node_back_call(
            n, C, far_sum, near_sum, node_cotangent, node_out, n1, n2, inv, slope, own_sum,
            w_msg3, g1, w_ffn1, w_ffn2, g2, we1,
        )
        sums = [dw3, dwe_near, dwe_far, dwe1, dwe2, dwe3, dgain, dg3]
        grad_edges, dw1, dw2, target_sum, source_sum = message_back_call(
            C, tcol, trow, nodes_all, nodes, vw_all, w_msg1, w_msg2, *kept
        )
        grad_nodes, early, late, small = final_call(
            n, C, [target_sum, source_sum, grad_one, w_msg1, dw1, dw2, *sums]
        )
        low, resid = (lax.all_gather(v, "edge", axis=0, tiled=True) for v in (low, resid))
        tot_dwf = feed_call(low, resid, w_ffn1, w_ffn2)
        dwf = []
    (
        tot1, tot2, tot3, grad_edges, we1_t, tot_e2, tot_e3, node_out, grad_nodes, *rest
    ) = unpack_call(C, late, early, small, node_out, grad_nodes, grad_edges, dwf)
    dwf1, dwf2 = rest[:2] if dwf else tot_dwf
    gains = rest[-6:]
    gains = [v.reshape(v.shape[1]) for v in gains]
    return (
        node_out, edge_out, grad_nodes, grad_edges,
        tot1, tot2, tot3, gains[0], gains[1], dwf1, dwf2, gains[2], gains[3],
        we1_t.T, tot_e2, tot_e3, gains[4], gains[5],
    )


def solution(mesh):
    rows = P(("dp", "edge"), None)
    return jax.shard_map(
        body,
        mesh=mesh,
        in_specs=(rows, rows, P(("dp", "edge"), None, None), rows, rows)
        + (P(),) * 14
        + (rows, rows),
        out_specs=(rows,) * 4
        + (P("dp", None),) * 3
        + (P("dp"),) * 2
        + (P("dp", None),) * 2
        + (P("dp"),) * 2
        + (P("dp", None),) * 3
        + (P("dp"),) * 2,
        check_vma=False,
    )
```

```python
import functools

import jax
import jax.numpy as jnp
from jax import lax
from jax.experimental import pallas as pl
from jax.experimental.pallas import tpu as pltpu
from jax.sharding import PartitionSpec as P

BF = jnp.bfloat16
F32 = jnp.float32
I32 = jnp.int32
MESH = pl.DeviceIdType.MESH
MIB = 1024 * 1024
LANES = 128
GROUP = 4
ORDER = (0, 2, 1, 3)
TABLE = 1024
EPS = 1e-05
ROOT = 0.7978845608028654
CUBE = 0.044715 * ROOT


def dot(a, b):
    return jnp.dot(a, b, preferred_element_type=F32)


def dot_tn(a, b):
    return lax.dot_general(a, b, (((0,), (0,)), ((), ())), preferred_element_type=F32)


def dot_nt(a, b):
    return lax.dot_general(a, b, (((1,), (1,)), ((), ())), preferred_element_type=F32)


def gelu_pair(v):
    v = v.astype(BF)
    c = lambda x: jnp.asarray(x, BF)
    z = v * v
    q = c(0.5) + c(0.5) * jnp.tanh(v * (c(ROOT) + c(CUBE) * z))
    act = v * q
    slope = q + (act - act * q) * (c(2.0 * ROOT) + c(6.0 * CUBE) * z)
    return act, slope


def gelu_full(v):
    z = v * v
    q = 0.5 + 0.5 * jnp.tanh(v * (ROOT + CUBE * z))
    act = v * q
    slope = q + (act - act * q) * (2.0 * ROOT + 6.0 * CUBE * z)
    return act.astype(BF), slope.astype(BF)


def row_mean(v):
    return jnp.mean(v, axis=-1, keepdims=True)


def lane_column(ref, k):
    rows = ref.shape[0]
    return jnp.broadcast_to(pltpu.roll(ref[...], LANES - k, axis=1)[:, 0:1], (rows, LANES))


def pick_rows(target, width):
    lane = lax.broadcasted_iota(I32, target.shape, 1)
    one, nil = jnp.ones((), BF), jnp.zeros((), BF)
    t16, l16 = target.astype(jnp.int16), lane.astype(jnp.int16)
    return jnp.concatenate(
        [jnp.where(t16 == l16 + jnp.int16(LANES * c), one, nil) for c in range(width // LANES)], axis=1)


def pick_cols(target, width):
    edges = target.shape[1]
    sub = lax.broadcasted_iota(I32, (width, edges), 0)
    return jnp.where(jnp.broadcast_to(target, (width, edges)).astype(jnp.int16) == sub.astype(jnp.int16), jnp.ones((), BF), jnp.zeros((), BF))


def gather_table(targets, table):
    count = table.shape[0]
    if count <= TABLE:
        hot = jnp.concatenate([pick_rows(t, count) for t in targets], axis=0)
        return dot(hot, table[...])

    def step(c, total):
        base = c * TABLE
        hot = jnp.concatenate([pick_rows(t - base, TABLE) for t in targets], axis=0)
        return total + dot(hot, table[pl.ds(pl.multiple_of(base, TABLE), TABLE), :])

    rows = sum(t.shape[0] for t in targets)
    return lax.fori_loop(0, count // TABLE, step, jnp.zeros((rows, table.shape[1]), F32))


def add_by_target(target, values, total):
    count = total.shape[0]
    if count <= TABLE:
        total[...] += dot(pick_cols(target, count), values)
        return

    def step(c, carry):
        base = c * TABLE
        part = pl.ds(pl.multiple_of(base, TABLE), TABLE)
        total[part, :] += dot(pick_cols(target - base, TABLE), values)
        return carry

    lax.fori_loop(0, count // TABLE, step, 0)


def by_chunks(count, step):
    if count <= TABLE:
        step(pl.ds(0, count))
        return

    def one(c, carry):
        step(pl.ds(pl.multiple_of(c * TABLE, TABLE), TABLE))
        return carry

    lax.fori_loop(0, count // TABLE, one, 0)


def remote(src, dst, send, recv, peer):
    return pltpu.make_async_remote_copy(
        src_ref=src,
        dst_ref=dst,
        send_sem=send,
        recv_sem=recv,
        device_id={"edge": peer},
        device_id_type=MESH,
    )


def greet(peers):
    barrier = pltpu.get_barrier_semaphore()
    for peer in peers:
        pl.semaphore_signal(barrier, inc=1, device_id={"edge": peer}, device_id_type=MESH)
    pl.semaphore_wait(barrier, len(peers))


def block(ref, index, rows):
    return ref.at[pl.ds(pl.multiple_of(index * rows, rows), rows)]


class Place:
    def __init__(self, n):
        self.me = lax.axis_index("edge")
        self.chips = n // 2
        self.chip = self.me // 2
        self.core = lax.rem(self.me, 2)
        self.sibling = self.chip * 2 + 1 - self.core
        self.mates = [self.at(d) for d in range(1, self.chips)]

    def at(self, d):
        return lax.rem(self.chip + d + self.chips, self.chips) * 2 + self.core


class Gather:
    def __init__(self, place, x, out, send, recv):
        rows, chips = x.shape[0], place.chips
        mine = block(out, place.me, rows)
        self.near = remote(x, mine, send.at[0], recv.at[0], place.sibling)
        self.far, self.passed = [], []
        for d in range(1, chips):
            self.far.append(remote(x, mine, send.at[d], recv.at[d], place.mates[d - 1]))
            got = block(out, place.at(-d), rows)
            at = chips + d
            self.passed.append(remote(got, got, send.at[at], recv.at[at], place.sibling))

    def start(self):
        for copy in self.far:
            copy.start()
        self.near.start()

    def finish(self):
        for far, passed in zip(self.far, self.passed):
            far.wait_recv()
            passed.start()
        self.near.wait()
        for copy in self.passed:
            copy.wait()
        for copy in self.far:
            copy.wait_send()


class Scatter:
    def __init__(self, place, x, pair_buf, far_buf, send, recv):
        self.place, self.x = place, x
        self.pair_buf, self.far_buf = pair_buf, far_buf
        chips, self.rows = place.chips, pair_buf.shape[1]
        self.pairs, self.far = [], []
        for d in range(chips):
            theirs = lax.rem(place.chip + d, chips) * 2 + 1 - place.core
            src = block(x, theirs, self.rows)
            self.pairs.append(remote(src, pair_buf.at[d], send.at[d], recv.at[d], place.sibling))
        for d in range(1, chips):
            at = chips + d
            self.far.append(
                remote(pair_buf.at[d], far_buf.at[d], send.at[at], recv.at[at], place.at(d))
            )

    def start(self):
        for copy in self.pairs[1:]:
            copy.start()
        self.pairs[0].start()

    def pass_on(self):
        for d in range(1, self.place.chips):
            self.pairs[d].wait_recv()
            at = pl.ds(pl.multiple_of(self.place.at(d) * self.rows, self.rows), self.rows)
            mine = self.x[at, :].astype(F32) + self.pair_buf[d].astype(F32)
            self.pair_buf[d] = mine.astype(BF)
            self.far[d - 1].start()

    def finish(self):
        self.pairs[0].wait_recv()
        at = pl.ds(pl.multiple_of(self.place.me * self.rows, self.rows), self.rows)
        total = self.x[at, :].astype(F32) + self.pair_buf[0].astype(F32)
        for d in range(1, self.place.chips):
            self.far[d - 1].wait_recv()
            total = total + self.far_buf[d].astype(F32)
        for copy in self.pairs + self.far:
            copy.wait_send()
        return total


def scatter_sum(*refs):
    scatter = Scatter(*refs)
    scatter.start()
    scatter.pass_on()
    return scatter.finish()


def comm_scratch(n, rows, width):
    return [pltpu.VMEM((n // 2, rows, width), BF)] * 2


def sems(count):
    return [pltpu.SemaphoreType.DMA((count,))] * 2


def remote_params(cid):
    return pltpu.CompilerParams(
        collective_id=cid, has_side_effects=True, vmem_limit_bytes=62 * MIB
    )


LOCAL = pltpu.CompilerParams(vmem_limit_bytes=62 * MIB)
WHOLE = pl.BlockSpec(memory_space=pltpu.VMEM)


def slab_pairs(slab, C):
    pairs = slab.shape[1] // (2 * C)
    even = [slab[:, 2 * C * m : 2 * C * m + 256] for m in range(pairs)]
    odd = [slab[:, 2 * C * m + 2 * C - 256 : 2 * C * m + 2 * C] for m in range(pairs)]
    return jnp.concatenate(even, axis=0), jnp.concatenate(odd, axis=0)


def interleave(even, odd, rows):
    parts = []
    for m in range(even.shape[0] // rows):
        parts += [even[m * rows : (m + 1) * rows], odd[m * rows : (m + 1) * rows]]
    return jnp.concatenate(parts, axis=0)


def split_tiles(values, rows):
    count = values.shape[0] // rows
    pick = lambda first: jnp.concatenate(
        [values[k * rows : (k + 1) * rows] for k in range(first, count, 2)], axis=0
    )
    return pick(0), pick(1)


def join_slab(even, odd, rows, C):
    parts = []
    for m in range(even.shape[0] // rows):
        a = even[m * rows : (m + 1) * rows]
        b = odd[m * rows : (m + 1) * rows]
        parts += [a[:, :LANES], a[:, LANES:] + b[:, :LANES], b[:, LANES:]]
    return jnp.concatenate(parts, axis=1)


class Loads:
    def __init__(self, pairs, sem):
        self.copies = [
            pltpu.make_async_copy(src, dst, sem.at[j]) for j, (src, dst) in enumerate(pairs)
        ]

    def start(self):
        for copy in self.copies:
            copy.start()

    def wait(self, first=0, last=None):
        for copy in self.copies[first:last]:
            copy.wait()


def column_of(row):
    return jnp.transpose(jnp.broadcast_to(row, (LANES, row.shape[1])))


def spread(column, width):
    return jnp.concatenate([column] * (width // LANES), axis=1)


def norm_parts(values):
    centred = values - row_mean(values)
    inverse = lax.rsqrt(row_mean(centred * centred) + EPS)
    return centred * inverse, inverse


def forward_kernel(
    n, K, C, nodes, owner, slot, live, g1, o1, g2, o2, w1_h, w2_h, w3_h, wf1_h, wf2_h, we1_h, edges,
    act1, slope1, slope2, tcol, trow, node_out, near, low_out, n1_out, n2_out, inv_out,
    slope_out, sum_out, nodes_h, far_h,
    w1, w2, w3, wf1, wf2, we1, load_sem,
    nodes_all, far_all, lcol, orow, lrow, scol, hist, hist_got, count,
    p_all, p_own, w_own, pre2, total, summed, q_own, pair_buf, far_buf,
    send, recv, hsend, hrecv, rsend, rrecv, qsend, qrecv, own_sem,
):
    i = pl.program_id(0)
    rows, D = nodes.shape
    tiles = K // GROUP
    size = GROUP * rows
    if n * rows > TABLE:
        p_all = summed = nodes_all
    place = Place(n)
    others = [lax.rem(place.me + d, n) for d in range(1, n)]
    loads = Loads(
        [(w1_h, w1), (w2_h, w2), (w3_h, w3), (wf1_h, wf1), (wf2_h, wf2), (we1_h, we1)], load_sem
    )
    keep_nodes = pltpu.make_async_copy(nodes_all, nodes_h, own_sem.at[1])

    @pl.when(i == 0)
    def _():
        loads.start()
        spare = jnp.zeros((LANES - K, rows), I32)
        for k in range(K):
            orow[k : k + 1, :] = owner[k]
        orow[K:, :] = spare
        own_wide = orow[...]
        slot_wide = jnp.concatenate([slot[...], spare], axis=0)
        live_wide = jnp.concatenate([live[...], spare], axis=0).astype(F32)
        target = own_wide * rows + slot_wide
        trow[...] = target
        lrow[...] = live_wide
        tcol[...] = jnp.transpose(target)
        lcol[...] = jnp.transpose(live_wide)
        scol[...] = jnp.transpose(slot_wide)
        pre2[...] = jnp.zeros_like(pre2)
        total[...] = jnp.zeros_like(total)
        w_own[...] = jnp.zeros_like(w_own)
        greet(others)
        gather = Gather(place, nodes, nodes_all, send, recv)
        gather.start()
        own = pltpu.make_async_copy(nodes, block(nodes_all, place.me, rows), own_sem.at[0])
        own.start()

        def tally(g, total):
            ks = [g * GROUP + j for j in range(GROUP)]
            hot = jnp.concatenate([pick_rows(lane_column(scol, k), LANES) for k in ks], axis=0)
            owners = jnp.concatenate([orow[pl.ds(k, 1), :] for k in ks], axis=1)
            lives = jnp.concatenate([lrow[pl.ds(k, 1), :] for k in ks], axis=1)
            sub = lax.broadcasted_iota(I32, (n, size), 0)
            who = jnp.where(
                jnp.broadcast_to(owners, sub.shape) == sub, jnp.broadcast_to(lives, sub.shape), 0.0
            )
            return total + dot(who.astype(BF), hot)

        totals = lax.fori_loop(0, tiles, tally, jnp.zeros((n, LANES), F32))
        for e in range(n):
            hist[e] = jnp.broadcast_to(totals[e : e + 1, :], (8, LANES))
        copies = []
        for d in range(1, n):
            peer = others[d - 1]
            copy = remote(hist.at[peer], hist_got.at[d], hsend.at[d], hrecv.at[d], peer)
            copy.start()
            copies.append(copy)
        loads.wait(0, 2)
        p_own[...] = dot(nodes[...], w1[:D, :])
        w_own[0, :C, :] = w1[2 * D :, :]
        w_own[1, 256 - C :, :] = w1[2 * D :, :]
        tallied = hist[place.me]
        for copy in copies:
            copy.wait_recv()
        for d in range(1, n):
            tallied = tallied + hist_got[d]
        count[...] = tallied
        own.wait()
        gather.finish()
        for copy in copies:
            copy.wait_send()
        keep_nodes.start()
        if n * rows > TABLE:
            keep_nodes.wait()

        def project(part):
            p_all[part, :] = dot(nodes_all[part, :], w1[D : 2 * D, :]).astype(BF)

        by_chunks(n * rows, project)

    last = jnp.clip(i - 1, 0, tiles - 1)
    ks = [last * GROUP + j for j in ORDER]
    act, slope = gelu_pair(pre2[...])
    alive = jnp.concatenate(
        [jnp.concatenate([lane_column(lcol, k)] * (D // LANES), axis=1) for k in ks], axis=0
    ).astype(BF)
    slope2[...] = slope * alive
    act = act * (alive * jnp.where(i >= 1, 1.0, 0.0).astype(BF))
    target = jnp.concatenate([trow[pl.ds(k, 1), :] for k in ks], axis=1)
    add_by_target(target, act, total)

    now = jnp.minimum(i, tiles - 1)
    targets = [lane_column(tcol, now * GROUP + j) for j in ORDER]
    even, odd = slab_pairs(edges[...], C)
    own = jnp.concatenate([dot(even, w_own[0]), dot(odd, w_own[1])], axis=0)
    act, slope = gelu_pair(
        gather_table(targets, p_all) + own + jnp.concatenate([p_own[...]] * GROUP, axis=0)
    )
    act1[...] = act
    slope1[...] = slope
    pre2[...] = dot(act, w2[...])

    @pl.when(i == tiles)
    def _():
        summed[...] = total[...].astype(BF)
        scatter = Scatter(place, summed, pair_buf, far_buf, rsend, rrecv)
        scatter.start()
        scatter.pass_on()
        if n * rows <= TABLE:
            keep_nodes.wait()
        loads.wait(2)
        divisor = 1.0 + column_of(count[0:1, :])
        inv_out[2] = divisor
        mine = scatter.finish().astype(BF)
        sum_out[...] = mine
        resid = nodes[...].astype(F32) + dot(mine, w3[...]) / spread(divisor, D)
        n1, inv1 = norm_parts(resid)
        n1_out[...] = n1
        inv_out[0] = jnp.broadcast_to(inv1, (rows, LANES))
        normed = n1 * g1[...] + o1[...]
        low = normed.astype(BF)
        low_out[...] = low
        act, slope = gelu_full(dot(low, wf1[...]))
        slope_out[...] = slope
        n2, inv2 = norm_parts(normed + dot(act, wf2[...]))
        n2_out[...] = n2
        inv_out[1] = jnp.broadcast_to(inv2, (rows, LANES))
        node_low = (n2 * g2[...] + o2[...]).astype(BF)
        node_out[...] = node_low
        pad = jnp.zeros((rows, 256 - C), F32)
        far = dot_nt(node_low, we1[:, D : 2 * D])
        q_own[...] = jnp.concatenate([far, pad], axis=1).astype(BF)
        gather = Gather(place, q_own, far_all, qsend, qrecv)
        gather.start()
        own = pltpu.make_async_copy(q_own, block(far_all, place.me, rows), own_sem.at[0])
        own.start()
        near[...] = jnp.concatenate([dot_nt(node_low, we1[:, :D]), pad], axis=1)
        own.wait()
        gather.finish()
        keep_far = pltpu.make_async_copy(far_all, far_h, own_sem.at[2])
        keep_far.start()
        keep_far.wait()


def full(x):
    return pl.BlockSpec(
        x.shape, lambda g: (0,) * x.ndim, pipeline_mode=pl.Buffered(buffer_count=1)
    )


def fixed(*s):
    return pl.BlockSpec(s, lambda g: (0,) * len(s), pipeline_mode=pl.Buffered(buffer_count=1))


HBM = pl.BlockSpec(memory_space=pl.ANY)


def forward_call(n, C, nodes, owner, slot, live, g1, o1, g2, o2, weights, edges):
    rows, D = nodes.shape
    K = slot.shape[0]
    FF = weights[3].shape[1]
    tiles = K // GROUP
    size = GROUP * rows
    count = n * rows
    other = count if count <= TABLE else 16
    shape = jax.ShapeDtypeStruct
    lag = lambda d: pl.BlockSpec((size, D), lambda g: (jnp.clip(g - d, 0, tiles - 1), 0))
    small = [nodes, owner, slot, live, g1, o1, g2, o2]
    outs = [
        shape((LANES, rows), I32),
        shape((LANES, rows), I32),
        shape((rows, D), BF),
        shape((rows, 256), F32),
        shape((rows, D), BF),
        shape((rows, D), F32),
        shape((rows, D), F32),
        shape((3, rows, LANES), F32),
        shape((rows, FF), BF),
        shape((rows, D), BF),
    ]
    outs[0] = shape((rows, LANES), I32)
    return pl.pallas_call(
        functools.partial(forward_kernel, n, K, C),
        grid=(tiles + 1,),
        in_specs=[full(v) for v in small]
        + [HBM] * 6
        + [pl.BlockSpec((rows, GROUP * C), lambda g: (0, jnp.minimum(g, tiles - 1)))],
        out_specs=[lag(0), lag(0), lag(1)] + [fixed(*v.shape) for v in outs] + [HBM] * 2,
        out_shape=[shape((K * rows, D), BF)] * 3
        + outs
        + [shape((count, D), BF), shape((count, 256), BF)],
        scratch_shapes=[pltpu.VMEM(v.shape, BF) for v in weights]
        + [
            pltpu.SemaphoreType.DMA((6,)),
            pltpu.VMEM((count, D), BF),
            pltpu.VMEM((count, 256), BF),
            pltpu.VMEM((rows, LANES), F32),
            pltpu.VMEM((LANES, rows), I32),
            pltpu.VMEM((LANES, rows), F32),
            pltpu.VMEM((rows, LANES), I32),
            pltpu.VMEM((n, 8, LANES), F32),
            pltpu.VMEM((n, 8, LANES), F32),
            pltpu.VMEM((8, LANES), F32),
            pltpu.VMEM((other, D), BF),
            pltpu.VMEM((rows, D), F32),
            pltpu.VMEM((2, 256, D), BF),
            pltpu.VMEM((size, D), F32),
            pltpu.VMEM((count, D), F32),
            pltpu.VMEM((other, D), BF),
            pltpu.VMEM((rows, 256), BF),
            *comm_scratch(n, rows, D),
            *sems(n),
            *sems(n),
            *sems(n),
            *sems(n),
            pltpu.SemaphoreType.DMA((3,)),
        ],
        compiler_params=remote_params(0),
    )(*small, *weights, edges)


def edge_kernel(
    tiles, C, tcol, trow, far_all, near, we1, we2, we3, gain, offset, edges1, edges4, edges6, cot,
    edge_out, partial, far_sum, near_sum, dw1, dw2, dw3, dgain,
    w1o, w2p, w3o, w1t, w2t, w3t, gains, total, a1, a2, a3, ag,
    pre1, hid1, slope1, pre2, hid2, slope2, res3, third, up2, up1,
):
    i = pl.program_id(0)
    rows = near.shape[0]
    D2 = we1.shape[1] - C
    gap = 256 - C
    half = GROUP // 2 * rows

    @pl.when(i == 0)
    def _():
        for ref in (w1o, w2p, w3o, w1t, w2t, w3t, gains, total, a1, a2, a3, ag, near_sum,
                    pre1, hid1, slope1, pre2, hid2, slope2, res3, third, up2, up1):
            ref[...] = jnp.zeros_like(ref)
        own = jnp.transpose(we1[:, D2:].astype(F32)).astype(BF)
        w1o[0, :C, :C] = own
        w1o[1, gap:, :C] = own
        w2p[:C, :C] = we2[...]
        w3o[0, :C, :C] = we3[...]
        w3o[1, :C, :] = jnp.concatenate([jnp.zeros((C, gap), F32), we3[...].astype(F32)], axis=1).astype(BF)
        for s in range(2):
            w1t[s] = jnp.transpose(w1o[s].astype(F32)).astype(BF)
            w3t[s] = jnp.transpose(w3o[s].astype(F32)).astype(BF)
        w2t[...] = jnp.transpose(w2p[...].astype(F32)).astype(BF)
        zero = jnp.zeros((1, gap), F32)
        gains[0, 0:1] = jnp.concatenate([gain[...], zero], axis=1)
        gains[0, 1:2] = jnp.concatenate([offset[...], zero], axis=1)
        gains[1, 0:1] = jnp.concatenate([zero, gain[...]], axis=1)
        gains[1, 1:2] = jnp.concatenate([zero, offset[...]], axis=1)

    tile = lambda d: jnp.clip(i - d, 0, tiles - 1)
    sides = [slice(0, half), slice(half, 2 * half)]

    t4 = tile(1)
    valid = jnp.where(i >= 1, 1.0, 0.0)
    slabs = slab_pairs(edges4[...], C)
    cots = slab_pairs(cot[...], C)
    lane = lax.broadcasted_iota(I32, (half, 256), 1)
    outs, grads, ups = [], [], []
    for s in range(2):
        inside = (lane < C) if s == 0 else (lane >= gap)
        keep = lambda v: jnp.where(inside, v, 0.0)
        mean = lambda v: jnp.sum(v, axis=-1, keepdims=True) * (1.0 / C)
        value = keep(slabs[s].astype(F32)) + res3[sides[s], :]
        centred = keep(value - mean(value))
        inverse = lax.rsqrt(mean(centred * centred) + EPS)
        normal = centred * inverse
        outs.append(normal * gains[s, 0:1] + gains[s, 1:2])
        upstream = keep(cots[s].astype(F32)) * valid
        moved = upstream * normal
        for r in range(half // rows):
            part = slice(r * rows, (r + 1) * rows)
            ag[s, 0] += moved[part]
            ag[s, 1] += upstream[part]
        scaled = upstream * gains[s, 0:1]
        grad = inverse * (scaled - mean(scaled) - normal * mean(scaled * normal))
        grad = keep(grad)
        grads.append(grad)
        low3 = grad.astype(BF)
        a3[s] += dot_tn(hid2[sides[s], :], low3)
        ups.append(dot(low3, w3t[s]))
    edge_out[...] = join_slab(outs[0], outs[1], rows, C).astype(BF)

    t5 = tile(1)
    low2 = (jnp.concatenate(ups, axis=0) * slope2[0].astype(F32)).astype(BF)
    a2[...] += dot_tn(hid1[0], low2)
    up1v = dot(low2, w2t[...])

    t6 = tile(1)
    low1 = (up1v * slope1[0].astype(F32)).astype(BF)
    slabs = slab_pairs(edges4[...], C)
    outs = []
    for s in range(2):
        a1[s] += dot_tn(low1[sides[s]], slabs[s])
        outs.append(grads[s] + dot(low1[sides[s]], w1t[s]))
    partial[...] = join_slab(outs[0], outs[1], rows, C).astype(BF)
    wide = low1.astype(F32)
    acc = wide[:rows]
    for j in range(1, GROUP):
        acc = acc + wide[j * rows : (j + 1) * rows]
    near_sum[...] += acc
    target = jnp.concatenate([trow[pl.ds(t6 * GROUP + j, 1), :] for j in ORDER], axis=1)
    add_by_target(target, low1, total)

    t1 = tile(0)
    slabs = slab_pairs(edges1[...], C)
    own = jnp.concatenate([dot(slabs[0], w1o[0]), dot(slabs[1], w1o[1])], axis=0)
    got = gather_table([lane_column(tcol, t1 * GROUP + j) for j in ORDER], far_all)
    pre1v = got + own + jnp.concatenate([near[...]] * GROUP, axis=0)

    t2 = tile(0)
    act, slope = gelu_pair(pre1v)
    hid1[0] = act
    slope1[0] = slope
    pre2v = dot(act, w2p[...])

    t3 = tile(0)
    act, slope = gelu_pair(pre2v)
    hid2[...] = act
    slope2[0] = slope
    for s in range(2):
        res3[sides[s], :] = dot(act[sides[s]], w3o[s])

    @pl.when(i == tiles)
    def _():
        far_sum[...] = total[...].astype(BF)
        dw1[...] = jnp.transpose(a1[0])[:C, :] + jnp.transpose(a1[1])[gap:, :]
        dw2[...] = a2[...]
        shifted = a3[1][:, gap:]
        dw3[...] = a3[0] + jnp.concatenate([shifted, jnp.zeros((256, gap), F32)], axis=1)
        for r in range(2):
            even = jnp.sum(ag[0, r], axis=0, keepdims=True)
            odd = jnp.sum(ag[1, r], axis=0, keepdims=True)
            row = even + jnp.concatenate([odd[:, gap:], jnp.zeros((1, gap), F32)], axis=1)
            dgain[r * 8 : r * 8 + 8, :] = jnp.broadcast_to(row, (8, 256))


def edge_call(C, tcol, trow, far_all, near, we1, we2, we3, gain, offset, edges, cot):
    rows = near.shape[0]
    count = far_all.shape[0]
    K = edges.shape[1] // C
    tiles = K // GROUP
    size = GROUP * rows
    shape = jax.ShapeDtypeStruct
    slab = lambda d: pl.BlockSpec(
        (rows, GROUP * C), lambda g: (0, jnp.clip(g - d, 0, tiles - 1))
    )
    fixed = lambda *s: pl.BlockSpec(
        s, lambda g: (0,) * len(s), pipeline_mode=pl.Buffered(buffer_count=1)
    )
    return pl.pallas_call(
        functools.partial(edge_kernel, tiles, C),
        grid=(tiles + 1,),
        in_specs=[full(x) for x in (tcol, trow, far_all, near, we1, we2, we3, gain, offset)]
        + [slab(0), slab(1), slab(99), slab(1)],
        out_specs=[
            slab(1), slab(1), fixed(count, 256), fixed(rows, 256),
            fixed(C, 256), fixed(256, 256), fixed(256, 256), fixed(16, 256),
        ],
        out_shape=[
            shape((rows, K * C), BF),
            shape((rows, K * C), BF),
            shape((count, 256), BF),
            shape((rows, 256), F32),
            shape((C, 256), F32),
            shape((256, 256), F32),
            shape((256, 256), F32),
            shape((16, 256), F32),
        ],
        scratch_shapes=[
            pltpu.VMEM((2, 256, 256), BF),
            pltpu.VMEM((256, 256), BF),
            pltpu.VMEM((2, 256, 256), BF),
            pltpu.VMEM((2, 256, 256), BF),
            pltpu.VMEM((256, 256), BF),
            pltpu.VMEM((2, 256, 256), BF),
            pltpu.VMEM((2, 8, 256), F32),
            pltpu.VMEM((count, 256), F32),
            pltpu.VMEM((2, 256, 256), F32),
            pltpu.VMEM((256, 256), F32),
            pltpu.VMEM((2, 256, 256), F32),
            pltpu.VMEM((2, 2, rows, 256), F32),
            pltpu.VMEM((size, 256), F32),
            pltpu.VMEM((3, size, 256), BF),
            pltpu.VMEM((4, size, 256), BF),
            pltpu.VMEM((size, 256), F32),
            pltpu.VMEM((size, 256), BF),
            pltpu.VMEM((2, size, 256), BF),
            pltpu.VMEM((size, 256), F32),
            pltpu.VMEM((2, size, 256), F32),
            pltpu.VMEM((size, 256), F32),
            pltpu.VMEM((size, 256), F32),
        ],
        compiler_params=LOCAL,
    )(tcol, trow, far_all, near, we1, we2, we3, gain, offset, edges, edges, edges, cot)


def norm_back(upstream, normal, inverse, gain):
    scaled = upstream * gain
    return inverse * (scaled - row_mean(scaled) - normal * row_mean(scaled * normal))


def node_back(
    C, far, near_sum, cot, n1, n2, inv, slope, w3, g1, wf1, wf2, g2, we1, grad_one, resid_out, dgain, v_own
):
    rows, D = cot.shape
    far = far.astype(BF)[:, :C]
    near = near_sum[...].astype(BF)[:, :C]
    grad = cot[...].astype(F32) + dot(near, we1[:, :D]) + dot(far, we1[:, D : 2 * D])
    two = norm_back(grad, n2[...], inv[1][:, 0:1], g2[...])
    dgain[16:24, :] = jnp.broadcast_to(jnp.sum(grad * n2[...], axis=0, keepdims=True), (8, D))
    dgain[24:32, :] = jnp.broadcast_to(jnp.sum(grad, axis=0, keepdims=True), (8, D))
    resid = two.astype(BF)
    resid_out[...] = resid
    inner = (dot_nt(resid, wf2[...]) * slope[...].astype(F32)).astype(BF)
    grad = two + dot_nt(inner, wf1[...])
    one = norm_back(grad, n1[...], inv[0][:, 0:1], g1[...])
    dgain[0:8, :] = jnp.broadcast_to(jnp.sum(grad * n1[...], axis=0, keepdims=True), (8, D))
    dgain[8:16, :] = jnp.broadcast_to(jnp.sum(grad, axis=0, keepdims=True), (8, D))
    grad_one[...] = one
    upper = (one / spread(inv[2], D)).astype(BF)
    v_own[...] = dot_nt(upper, w3[...]).astype(BF)
    return far, near, upper


def node_back_kernel(
    n, C, far_sum, near_sum, cot, node_low, n1, n2, inv, slope, summed,
    w3, g1, wf1, wf2, g2, we1,
    grad_one, vw_all, resid_out, dgain, dw3, dwe_near, dwe_far,
    pair_buf, far_buf, v_own, send, recv, gsend, grecv, own_sem,
):
    place = Place(n)
    rows = cot.shape[0]
    greet([place.sibling] + place.mates)
    far = scatter_sum(place, far_sum, pair_buf, far_buf, send, recv)
    far, near, upper = node_back(
        C, far, near_sum, cot, n1, n2, inv, slope, w3, g1, wf1, wf2, g2, we1,
        grad_one, resid_out, dgain, v_own,
    )
    gather = Gather(place, v_own, vw_all, gsend, grecv)
    gather.start()
    own = pltpu.make_async_copy(v_own, block(vw_all, place.me, rows), own_sem.at[0])
    own.start()
    dw3[...] = dot_tn(summed[...], upper)
    dwe_near[...] = dot_tn(node_low[...], near)
    dwe_far[...] = dot_tn(node_low[...], far)
    own.wait()
    gather.finish()


def node_back_call(n, C, *args):
    cot = args[2]
    rows, D = cot.shape
    shape = jax.ShapeDtypeStruct
    return pl.pallas_call(
        functools.partial(node_back_kernel, n, C),
        in_specs=[WHOLE] * len(args),
        out_specs=[WHOLE] * 7,
        out_shape=[
            shape((rows, D), F32),
            shape((n * rows, D), BF),
            shape((rows, D), BF),
            shape((32, D), F32),
            shape((D, D), F32),
            shape((D, C), F32),
            shape((D, C), F32),
        ],
        scratch_shapes=[
            *comm_scratch(n, rows, 256),
            pltpu.VMEM((rows, D), BF),
            *sems(n),
            *sems(n),
            pltpu.SemaphoreType.DMA((1,)),
        ],
        compiler_params=remote_params(2),
    )(*args)


class Line:
    def __init__(self, place, pieces, x, out, pair_buf, low_buf, high_buf, send_buf, send, recv):
        self.place, self.pieces, self.x, self.out = place, pieces, x, out
        self.pair_buf, self.low_buf, self.high_buf = pair_buf, low_buf, high_buf
        self.send_buf, self.send, self.recv = send_buf, send, recv
        c, q, chips = place.chip, place.core, place.chips
        self.root = chips // 2 - 1 + q
        self.away = jnp.abs(c - self.root)
        self.right = jnp.minimum(c + 1, chips - 1) * 2 + q
        self.left = jnp.maximum(c - 1, 0) * 2 + q
        self.half = x.shape[0] // 2
        self.rows = self.half // pieces

    def part(self, which, p):
        return pl.ds(pl.multiple_of(which * self.half + p * self.rows, self.rows), self.rows)

    def here(self, p):
        return pl.ds(pl.multiple_of(p * self.rows, self.rows), self.rows)

    def link(self, src, dst, p, sent, got, peer):
        n = self.pieces
        return remote(src, dst, self.send.at[sent * n + p], self.recv.at[got * n + p], peer)

    def pair(self, p):
        src = self.x.at[self.part(1 - self.place.core, p)]
        return self.link(src, self.pair_buf.at[self.here(p)], p, 0, 0, self.place.sibling)

    def up(self, p):
        here = self.here(p)
        return self.link(self.send_buf.at[here], self.low_buf.at[here], p, 1, 1, self.right)

    def down(self, p):
        here = self.here(p)
        return self.link(self.send_buf.at[here], self.high_buf.at[here], p, 2, 2, self.left)

    def outward(self, p, sent, got, peer):
        mine = self.out.at[self.part(self.place.core, p)]
        return self.link(mine, mine, p, sent, got, peer)

    def out_left(self, p):
        return self.outward(p, 3, 3, self.left)

    def out_right(self, p):
        return self.outward(p, 5, 3, self.right)

    def across(self, p):
        return self.outward(p, 4, 4, self.place.sibling)

    def each(self, step):
        lax.fori_loop(0, self.pieces, lambda p, z: (step(p), z)[1], 0)

    def start(self):
        self.each(lambda p: self.pair(p).start())

    def reduce(self, p):
        c, root, last = self.place.chip, self.root, self.place.chips - 1
        here, mine_at = self.here(p), self.part(self.place.core, p)
        self.pair(p).wait_recv()
        mine = lambda: self.x[mine_at, :].astype(F32) + self.pair_buf[here, :].astype(F32)

        def end():
            self.send_buf[here, :] = mine().astype(BF)

        def from_low():
            self.up(p).wait_recv()
            self.send_buf[here, :] = (mine() + self.low_buf[here, :].astype(F32)).astype(BF)

        def from_high():
            self.down(p).wait_recv()
            self.send_buf[here, :] = (mine() + self.high_buf[here, :].astype(F32)).astype(BF)

        def at_root():
            self.up(p).wait_recv()
            self.down(p).wait_recv()
            total = mine() + self.low_buf[here, :].astype(F32) + self.high_buf[here, :].astype(F32)
            self.out[mine_at, :] = total.astype(BF)
            self.out_left(p).start()
            self.out_right(p).start()
            self.across(p).start()

        pl.when((c == 0) | (c == last))(end)
        pl.when((c > 0) & (c < root))(from_low)
        pl.when((c > root) & (c < last))(from_high)
        pl.when(c < root)(lambda: self.up(p).start())
        pl.when(c > root)(lambda: self.down(p).start())
        pl.when(c == root)(at_root)

    def spread(self, p):
        c, root, last = self.place.chip, self.root, self.place.chips - 1

        def leftward():
            self.out_left(p).wait_recv()
            pl.when(c > 0)(lambda: self.out_left(p).start())
            self.across(p).start()

        def rightward():
            self.out_right(p).wait_recv()
            pl.when(c < last)(lambda: self.out_right(p).start())
            self.across(p).start()

        pl.when(c < root)(leftward)
        pl.when(c > root)(rightward)

    def slots(self, lag):
        return self.pieces + 2 * lag * (self.place.chips // 2)

    def slot(self, s, lag):
        deep = self.place.chips // 2
        p = s - lag * (deep - self.away)
        pl.when((p >= 0) & (p < self.pieces))(lambda: self.reduce(p))
        o = s - lag * (deep + self.away)
        pl.when((o >= 0) & (o < self.pieces) & (self.away > 0))(lambda: self.spread(o))

    def finish(self):
        c, root, last = self.place.chip, self.root, self.place.chips - 1

        def end(p):
            self.pair(p).wait_send()
            self.across(p).wait_send()
            pl.when(c < root)(lambda: self.up(p).wait_send())
            pl.when(c > root)(lambda: self.down(p).wait_send())
            pl.when((c <= root) & (c > 0))(lambda: self.out_left(p).wait_send())
            pl.when((c >= root) & (c < last))(lambda: self.out_right(p).wait_send())

        self.each(lambda p: self.across(p).wait_recv())
        self.each(end)


def line_scratch(rows, width, pieces):
    return [pltpu.VMEM((rows // 2, width), BF)] * 4 + sems(6 * pieces)


class Exchange:
    def __init__(self, place, n, mine, got, send, recv):
        self.place, self.n, self.mine, self.got = place, n, mine, got
        self.copies = []
        for d in range(1, n):
            peer = lax.rem(place.me + d, n)
            self.copies.append(remote(mine, got.at[place.me], send.at[d], recv.at[d], peer))

    def start(self):
        for copy in self.copies:
            copy.start()
        self.got[self.place.me] = self.mine[...]

    def finish(self):
        for copy in self.copies:
            copy.wait_recv()
        total = self.got[0]
        for e in range(1, self.n):
            total = total + self.got[e]
        for copy in self.copies:
            copy.wait_send()
        return total


EARLY, LATE, LAG, AHEAD = 7, 9, 2, 7


def early_rows(D, C):
    used = D + (2 * D + C) // 2 + C
    unit = 2 * EARLY * 16
    return -(-used // unit) * unit


def pack_early(C, x, gains, dw3, dwe_near, dwe_far, dwe1, dwe2, dwe3, dgain, dg3):
    D = dw3.shape[0]
    x[:D, :] = dw3[...].astype(BF)
    spare = jnp.zeros((D, 256 - C), F32)
    edge1 = jnp.concatenate(
        [
            jnp.concatenate([dwe_near[...], spare], axis=1),
            jnp.concatenate([dwe_far[...], spare], axis=1),
            dwe1[...],
        ],
        axis=0,
    ).astype(BF)
    half = edge1.shape[0] // 2
    x[D : D + half, :256] = edge1[:half]
    x[D : D + half, 256:] = edge1[half:]
    at = D + half
    x[at : at + C, :256] = dwe2[:C, :].astype(BF)
    x[at : at + C, 256:] = dwe3[:C, :].astype(BF)
    if at + C < x.shape[0]:
        x[at + C :, :] = jnp.zeros((x.shape[0] - at - C, D), BF)
    gains[...] = jnp.zeros_like(gains)
    for r in range(4):
        gains[r : r + 1, :] = dgain[8 * r : 8 * r + 1, :]
    for r in range(2):
        gains[4 + r : 5 + r, :256] = dg3[8 * r : 8 * r + 1, :]


def back_start(C, w1, w2, w2t, w_own, w_own_t, zeroed):
    D = w2.shape[0]
    gap = 256 - C
    for ref in (w_own, *zeroed):
        ref[...] = jnp.zeros_like(ref)
    w_own[0, :C, :] = w1[2 * D :, :]
    w_own[1, gap:, :] = w1[2 * D :, :]
    for s in range(2):
        w_own_t[s] = jnp.transpose(w_own[s].astype(F32)).astype(BF)
    w2t[...] = jnp.transpose(w2[...].astype(F32)).astype(BF)


def back_tile(
    g, rows, C, tcol, trow, vw, act1, slope1, slope2, edges, partial, grad_edges,
    w2t, w_own_t, total, a2, ae, source_sum,
):
    half = GROUP // 2 * rows
    ks = [g * GROUP + j for j in ORDER]
    up = gather_table([lane_column(tcol, k) for k in ks], vw)
    upper = up.astype(BF) * slope2[...]
    a2[...] += dot_tn(act1[...], upper)
    lower = dot(upper, w2t[...]).astype(BF) * slope1[...]
    wide = lower.astype(F32)
    acc = wide[:rows]
    for j in range(1, GROUP):
        acc = acc + wide[j * rows : (j + 1) * rows]
    source_sum[...] += acc
    target = jnp.concatenate([trow[pl.ds(k, 1), :] for k in ks], axis=1)
    add_by_target(target, lower, total)
    slabs = slab_pairs(edges[...], C)
    lowers = [lower[:half], lower[half:]]
    own = []
    for s in range(2):
        ae[s] += dot_tn(slabs[s], lowers[s])
        own.append(dot(lowers[s], w_own_t[s]))
    grad_edges[...] = (partial[...].astype(F32) + join_slab(own[0], own[1], rows, C)).astype(BF)


def back_weights(C, dw1, dw2, nodes_all, nodes, total, a2, ae, source_sum):
    D = nodes.shape[1]
    gap = 256 - C
    dw2[...] = a2[...].astype(BF)
    dw1[:D, :] = dot_tn(nodes[...], source_sum[...].astype(BF)).astype(BF)
    dw1[2 * D :, :] = (ae[0][:C, :] + ae[1][gap:, :]).astype(BF)
    a2[...] = jnp.zeros_like(a2)

    def weigh(part):
        a2[...] += dot_tn(nodes_all[part, :], total[part, :].astype(BF))

    by_chunks(total.shape[0], weigh)
    dw1[D : 2 * D, :] = a2[...].astype(BF)


def tail(early, late, scatter, source_sum, grad_one, w1, grad_nodes, feed):
    D = grad_one.shape[1]
    late.start()
    scatter.start()

    def feed_part(f):
        low, resid, wf1, wf2, dwf1, dwf2 = feed
        step = 256
        cols = pl.ds(pl.multiple_of(f * step, step), step)
        act, slope = gelu_full(dot(low[...], wf1[:, cols]))
        dwf2[cols, :] = dot_tn(act, resid[...]).astype(BF)
        inner = (dot_nt(resid[...], wf2[cols, :]) * slope.astype(F32)).astype(BF)
        dwf1[:, cols] = dot_tn(low[...], inner).astype(BF)

    parts = feed[2].shape[1] // 256 if feed else 0

    def slot(s, carry):
        early.slot(s, LAG)
        late.slot(s - EARLY, LAG)
        if feed:
            f = s - AHEAD
            pl.when((f % 2 == 1) & (f // 2 < parts))(lambda: feed_part(f // 2))
        return carry

    scatter.pass_on()
    lax.fori_loop(AHEAD, EARLY + late.slots(LAG), slot, 0)
    source = dot_nt(source_sum[...].astype(BF), w1[:D, :])
    total = scatter.finish()
    grad_nodes[...] = grad_one[...] + source + dot_nt(total.astype(BF), w1[D : 2 * D, :])
    early.finish()
    late.finish()


def back_kernel(n, tiles, C, tcol, trow, nodes, near_sum, g1, g2, dwe1, dwe2, dwe3, dg3, *refs):
    sources, refs = refs[:16], refs[16:]
    act1, slope1, slope2, edges, partial, *refs = refs
    grad_edges, grad_nodes, small, dwf1, dwf2, early_h, late_h, *refs = refs
    held, refs = refs[:16], refs[16:]
    (
        far_sum, low_own, cot, we1, n2, inv, wf2, slope, wf1, n1, w3, w1, w2, summed, node_low, nodes_all
    ) = held
    (
        load_sem, low, lsend, lrecv, vw, v_own, grad_one, resid_own, dgain, dw3, dwe_near, dwe_far,
        resid, bsend, brecv, vsend, vrecv, hsend, hrecv, pair_h, far_h,
        w2t, w_own, w_own_t, total, a2, ae, source_sum, target_sum, gains, got, gsend, grecv,
        pair_buf, far_buf, send, recv, x1, out1, x2, out2, *line_refs,
    ) = refs
    g = pl.program_id(0)
    rows, D = nodes.shape
    place = Place(n)
    loads = Loads(list(zip(sources, held)), load_sem)
    gather = Gather(place, resid_own, resid, bsend, brecv)
    gather_low = Gather(place, low_own, low, lsend, lrecv)
    early = Line(place, EARLY, x1, out1, *line_refs[: len(line_refs) // 2])
    late = Line(place, LATE, x2, out2, *line_refs[len(line_refs) // 2 :])
    exchange = Exchange(place, n, gains, got, gsend, grecv)

    @pl.when(g == 0)
    def _():
        loads.start()
        greet([lax.rem(place.me + d, n) for d in range(1, n)])
        loads.wait(0, 2)
        scatter = Scatter(place, far_sum, pair_h, far_h, hsend, hrecv)
        scatter.start()
        scatter.pass_on()
        mine = pl.ds(pl.multiple_of(place.me * rows, rows), rows)
        low[mine, :] = low_own[...]
        loads.wait(2, 15)
        back_start(C, w1, w2, w2t, w_own, w_own_t, (total, a2, ae, source_sum))
        far, near, upper = node_back(
            C, scatter.finish(), near_sum, cot, n1, n2, inv, slope, w3, g1, wf1, wf2, g2, we1,
            grad_one, resid_own, dgain, v_own,
        )
        spread_v = Gather(place, v_own, vw, vsend, vrecv)
        spread_v.start()
        dw3[...] = dot_tn(summed[...], upper)
        dwe_near[...] = dot_tn(node_low[...], near)
        dwe_far[...] = dot_tn(node_low[...], far)
        pack_early(C, x1, gains, dw3, dwe_near, dwe_far, dwe1, dwe2, dwe3, dgain, dg3)
        vw[mine, :] = v_own[...]
        resid[mine, :] = resid_own[...]
        spread_v.finish()
        exchange.start()
        early.start()

    pl.when(g == 1)(gather_low.start)
    pl.when(g == 4)(gather.start)
    ahead = g - (tiles - AHEAD)
    pl.when(ahead >= 0)(lambda: early.slot(ahead, LAG))
    back_tile(
        g, rows, C, tcol, trow, vw, act1, slope1, slope2, edges, partial, grad_edges,
        w2t, w_own_t, total, a2, ae, source_sum,
    )

    @pl.when(g == tiles - 1)
    def _():
        target_sum[...] = total[...].astype(BF)
        loads.wait(15)
        at = 2 * D + C
        back_weights(
            C, x2.at[pl.ds(0, at)], x2.at[pl.ds(at, D)], nodes_all, nodes, total, a2, ae, source_sum
        )
        small[...] = exchange.finish()
        gather_low.finish()
        gather.finish()
        scatter = Scatter(place, target_sum, pair_buf, far_buf, send, recv)
        tail(
            early, late, scatter, source_sum, grad_one, w1, grad_nodes, (low, resid, wf1, wf2, dwf1, dwf2)
        )
        keep_early = pltpu.make_async_copy(out1, early_h, load_sem.at[16])
        keep_early.start()
        keep_late = pltpu.make_async_copy(out2, late_h, load_sem.at[17])
        keep_late.start()
        keep_early.wait()
        keep_late.wait()


def back_call(n, C, whole, loaded, act1, slope1, slope2, edges, partial):
    rows, D = whole[2].shape
    count = n * rows
    K = edges.shape[1] // C
    tiles = K // GROUP
    size = GROUP * rows
    FF = loaded[8].shape[1]
    early, late = early_rows(D, C), 3 * D + C
    shape = jax.ShapeDtypeStruct
    slab = pl.BlockSpec((rows, GROUP * C), lambda g: (0, g))
    tile = pl.BlockSpec((size, D), lambda g: (g, 0))
    outs = [
        shape((rows, D), F32),
        shape((8, D), F32),
        shape((D, FF), BF),
        shape((FF, D), BF),
    ]
    return pl.pallas_call(
        functools.partial(back_kernel, n, tiles, C),
        grid=(tiles,),
        in_specs=[full(v) for v in whole] + [HBM] * len(loaded) + [tile, tile, tile, slab, slab],
        out_specs=[slab] + [fixed(*v.shape) for v in outs] + [HBM] * 2,
        out_shape=[shape((rows, K * C), BF)]
        + outs
        + [shape((early, D), BF), shape((late, D), BF)],
        scratch_shapes=[pltpu.VMEM(v.shape, v.dtype) for v in loaded]
        + [
            pltpu.SemaphoreType.DMA((18,)),
            pltpu.VMEM((count, D), BF),
            *sems(n),
            pltpu.VMEM((count, D), BF),
            pltpu.VMEM((rows, D), BF),
            pltpu.VMEM((rows, D), F32),
            pltpu.VMEM((rows, D), BF),
            pltpu.VMEM((32, D), F32),
            pltpu.VMEM((D, D), F32),
            pltpu.VMEM((D, C), F32),
            pltpu.VMEM((D, C), F32),
            pltpu.VMEM((count, D), BF),
            *sems(n),
            *sems(n),
            *sems(n),
            *comm_scratch(n, rows, 256),
            pltpu.VMEM((D, D), BF),
            pltpu.VMEM((2, 256, D), BF),
            pltpu.VMEM((2, D, 256), BF),
            pltpu.VMEM((count, D), F32),
            pltpu.VMEM((D, D), F32),
            pltpu.VMEM((2, 256, D), F32),
            pltpu.VMEM((rows, D), F32),
            pltpu.VMEM((count, D), BF),
            pltpu.VMEM((8, D), F32),
            pltpu.VMEM((n, 8, D), F32),
            *sems(n),
            *comm_scratch(n, rows, D),
            *sems(n),
            pltpu.VMEM((early, D), BF),
            pltpu.VMEM((early, D), BF),
            pltpu.VMEM((late, D), BF),
            pltpu.VMEM((late, D), BF),
            *line_scratch(early, D, EARLY),
            *line_scratch(late, D, LATE),
        ],
        compiler_params=remote_params(3),
    )(*whole, *loaded, act1, slope1, slope2, edges, partial)


def message_back_kernel(
    tiles, C, tcol, trow, nodes_all, nodes, vw, w1, w2, act1, slope1, slope2, edges, partial,
    grad_edges, dw1, dw2, target_sum, source_sum, w2t, w_own, w_own_t, total, a2, ae,
):
    g = pl.program_id(0)

    @pl.when(g == 0)
    def _():
        back_start(C, w1, w2, w2t, w_own, w_own_t, (total, a2, ae, source_sum))

    back_tile(
        g, nodes.shape[0], C, tcol, trow, vw, act1, slope1, slope2, edges, partial, grad_edges,
        w2t, w_own_t, total, a2, ae, source_sum,
    )

    @pl.when(g == tiles - 1)
    def _():
        target_sum[...] = total[...].astype(BF)
        back_weights(C, dw1, dw2, nodes_all, nodes, total, a2, ae, source_sum)


def message_back_call(C, tcol, trow, nodes_all, nodes, vw, w1, w2, act1, slope1, slope2, edges, partial):
    rows, D = nodes.shape
    count = vw.shape[0]
    K = edges.shape[1] // C
    tiles = K // GROUP
    size = GROUP * rows
    shape = jax.ShapeDtypeStruct
    slab = pl.BlockSpec((rows, GROUP * C), lambda g: (0, g))
    tile = pl.BlockSpec((size, D), lambda g: (g, 0))
    return pl.pallas_call(
        functools.partial(message_back_kernel, tiles, C),
        grid=(tiles,),
        in_specs=[full(x) for x in (tcol, trow, nodes_all, nodes, vw, w1, w2)]
        + [tile, tile, tile, slab, slab],
        out_specs=[slab, fixed(2 * D + C, D), fixed(D, D), fixed(count, D), fixed(rows, D)],
        out_shape=[
            shape((rows, K * C), BF),
            shape((2 * D + C, D), BF),
            shape((D, D), BF),
            shape((count, D), BF),
            shape((rows, D), F32),
        ],
        scratch_shapes=[
            pltpu.VMEM((D, D), BF),
            pltpu.VMEM((2, 256, D), BF),
            pltpu.VMEM((2, D, 256), BF),
            pltpu.VMEM((count, D), F32),
            pltpu.VMEM((D, D), F32),
            pltpu.VMEM((2, 256, D), F32),
        ],
        compiler_params=LOCAL,
    )(tcol, trow, nodes_all, nodes, vw, w1, w2, act1, slope1, slope2, edges, partial)


def final_kernel(
    n, C, target_sum, source_sum, grad_one, w1, dw1, dw2, dw3, dwe_near, dwe_far, dwe1, dwe2, dwe3,
    dgain, dg3, grad_nodes, out1, out2, small,
    x1, x2, gains, got, gsend, grecv, pair_buf, far_buf, send, recv, *line_refs,
):
    place = Place(n)
    D = grad_one.shape[1]
    pack_early(C, x1, gains, dw3, dwe_near, dwe_far, dwe1, dwe2, dwe3, dgain, dg3)
    at = 2 * D + C
    x2[:at, :] = dw1[...]
    x2[at:, :] = dw2[...]
    greet([lax.rem(place.me + d, n) for d in range(1, n)])
    early = Line(place, EARLY, x1, out1, *line_refs[: len(line_refs) // 2])
    late = Line(place, LATE, x2, out2, *line_refs[len(line_refs) // 2 :])
    exchange = Exchange(place, n, gains, got, gsend, grecv)
    exchange.start()
    small[...] = exchange.finish()
    scatter = Scatter(place, target_sum, pair_buf, far_buf, send, recv)
    early.start()
    lax.fori_loop(0, AHEAD, lambda s, z: (early.slot(s, LAG), z)[1], 0)
    tail(early, late, scatter, source_sum, grad_one, w1, grad_nodes, None)


def final_call(n, C, args):
    rows, D = args[2].shape
    early, late = early_rows(D, C), 3 * D + C
    shape = jax.ShapeDtypeStruct
    return pl.pallas_call(
        functools.partial(final_kernel, n, C),
        in_specs=[WHOLE] * len(args),
        out_specs=[WHOLE] * 4,
        out_shape=[
            shape((rows, D), F32),
            shape((early, D), BF),
            shape((late, D), BF),
            shape((8, D), F32),
        ],
        scratch_shapes=[
            pltpu.VMEM((early, D), BF),
            pltpu.VMEM((late, D), BF),
            pltpu.VMEM((8, D), F32),
            pltpu.VMEM((n, 8, D), F32),
            *sems(n),
            *comm_scratch(n, rows, D),
            *sems(n),
            *line_scratch(early, D, EARLY),
            *line_scratch(late, D, LATE),
        ],
        compiler_params=remote_params(4),
    )(*args)


def feed_kernel(low, resid, wf1, wf2, dwf1, dwf2):
    @pl.when(pl.program_id(1) == 0)
    def _():
        dwf1[...] = jnp.zeros_like(dwf1)
        dwf2[...] = jnp.zeros_like(dwf2)

    act, slope = gelu_full(dot(low[...], wf1[...]))
    dwf2[...] += dot_tn(act, resid[...])
    inner = (dot_nt(resid[...], wf2[...]) * slope.astype(F32)).astype(BF)
    dwf1[...] += dot_tn(low[...], inner)


def feed_call(low, resid, wf1, wf2):
    count = low.shape[0]
    D, FF = wf1.shape
    step, rows = min(FF, 512), min(count, TABLE)
    shape = jax.ShapeDtypeStruct
    return pl.pallas_call(
        feed_kernel,
        grid=(FF // step, count // rows),
        in_specs=[
            pl.BlockSpec((rows, D), lambda f, r: (r, 0)),
            pl.BlockSpec((rows, D), lambda f, r: (r, 0)),
            pl.BlockSpec((D, step), lambda f, r: (0, f)),
            pl.BlockSpec((step, D), lambda f, r: (f, 0)),
        ],
        out_specs=[
            pl.BlockSpec((D, step), lambda f, r: (0, f)),
            pl.BlockSpec((step, D), lambda f, r: (f, 0)),
        ],
        out_shape=[shape((D, FF), F32), shape((FF, D), F32)],
        compiler_params=LOCAL,
    )(low, resid, wf1, wf2)


def unpack_kernel(C, steps, late, packed, small, node_in, grad_in, edges, *refs):
    g = pl.program_id(0)
    D = late.shape[1]
    plain = refs[: (len(refs) - 15) // 2]
    w1, w2, w3, grad_edges, one, two, three, node_out, grad_nodes, *outs = refs[len(plain) :]
    gains = outs[len(plain) :]
    grad_edges[...] = edges[...].astype(F32)
    first = 2 * D + C
    for ref, src, base in ((w1, late, 0), (w2, late, first), (w3, packed, 0)):
        step = ref.shape[0]
        ref[...] = src[pl.ds(pl.multiple_of(base + g * step, 16), step), :].astype(F32)
    at = D
    for a, b in zip(plain, outs):
        b[...] = a[...].astype(F32)

    @pl.when(g == steps - 1)
    def _():
        half = (2 * D + C) // 2
        for r in range(2):
            left = 256 * r
            flipped = jnp.transpose(packed[at : at + half, left : left + 256].astype(F32))
            one[:, half * r : half * r + half] = flipped[:C, :]
        end = at + half
        two[...] = packed[end : end + C, :C].astype(F32)
        three[...] = packed[end : end + C, 256 : 256 + C].astype(F32)
        node_out[...] = node_in[...]
        grad_nodes[...] = grad_in[...]
        for r in range(6):
            width = D if r < 4 else C
            gains[r][...] = small[r : r + 1, :width]


def unpack_call(C, late, packed, small, node_out, grad_nodes, edges, arrays):
    steps = 4
    D = packed.shape[1]
    first = 2 * D + C
    shape = jax.ShapeDtypeStruct
    cut = lambda r, c: pl.BlockSpec((r // steps, c), lambda g: (g, 0))
    head = [(first, D), (D, D), (D, D), edges.shape]
    last = [(C, first), (C, C), (C, C)]
    plain = [v.shape for v in arrays]
    gains = [(1, D)] * 4 + [(1, C)] * 2
    return pl.pallas_call(
        functools.partial(unpack_kernel, C, steps),
        grid=(steps,),
        in_specs=[full(v) for v in (late, packed, small, node_out, grad_nodes)] + [cut(*v.shape) for v in (edges, *arrays)],
        out_specs=[cut(*v) for v in head]
        + [fixed(*v) for v in last]
        + [fixed(*node_out.shape)] * 2
        + [cut(*v) for v in plain]
        + [fixed(*v) for v in gains],
        out_shape=[shape(v, F32) for v in head + last]
        + [shape(node_out.shape, BF), shape(node_out.shape, F32)]
        + [shape(v, F32) for v in plain + gains],
        compiler_params=LOCAL,
    )(late, packed, small, node_out, grad_nodes, edges, *arrays)


def body(
    nodes, edges, nbr_owner, nbr_slot, edge_mask, w_msg1, w_msg2, w_msg3, gain_one, offset_one,
    w_ffn1, w_ffn2, gain_two, offset_two, w_edge1, w_edge2, w_edge3, gain_three, offset_three,
    node_cotangent, edge_cotangent,
):
    n = lax.axis_size("edge")
    rows, D = nodes.shape
    C = w_edge2.shape[0]
    we1 = w_edge1.T
    g1, o1, g2, o2 = (v.reshape(1, D) for v in (gain_one, offset_one, gain_two, offset_two))
    (
        act1, slope1, slope2, tcol, trow, node_out, near, low, n1, n2, inv, slope, own_sum,
        nodes_all, far_all,
    ) = forward_call(
        n, C, nodes, nbr_owner.transpose(1, 2, 0), nbr_slot.T, edge_mask.T, g1, o1, g2, o2,
        [w_msg1, w_msg2, w_msg3, w_ffn1, w_ffn2, we1], edges,
    )
    edge_out, partial, far_sum, near_sum, dwe1, dwe2, dwe3, dg3 = edge_call(
        C, tcol, trow, far_all, near, we1, w_edge2, w_edge3,
        gain_three.reshape(1, C), offset_three.reshape(1, C), edges, edge_cotangent,
    )
    kept = [act1, slope1, slope2, edges, partial]
    if n * rows <= TABLE:
        grad_edges, grad_nodes, small, *dwf, early, late = back_call(
            n, C, [tcol, trow, nodes, near_sum, g1, g2, dwe1, dwe2, dwe3, dg3],
            [
                far_sum, low, node_cotangent, we1, n2, inv, w_ffn2, slope, w_ffn1, n1, w_msg3, w_msg1,
                w_msg2, own_sum, node_out, nodes_all,
            ],
            *kept,
        )
    else:
        grad_one, vw_all, resid, dgain, dw3, dwe_near, dwe_far = node_back_call(
            n, C, far_sum, near_sum, node_cotangent, node_out, n1, n2, inv, slope, own_sum,
            w_msg3, g1, w_ffn1, w_ffn2, g2, we1,
        )
        sums = [dw3, dwe_near, dwe_far, dwe1, dwe2, dwe3, dgain, dg3]
        grad_edges, dw1, dw2, target_sum, source_sum = message_back_call(
            C, tcol, trow, nodes_all, nodes, vw_all, w_msg1, w_msg2, *kept
        )
        grad_nodes, early, late, small = final_call(
            n, C, [target_sum, source_sum, grad_one, w_msg1, dw1, dw2, *sums]
        )
        low, resid = (lax.all_gather(v, "edge", axis=0, tiled=True) for v in (low, resid))
        tot_dwf = feed_call(low, resid, w_ffn1, w_ffn2)
        dwf = []
    (
        tot1, tot2, tot3, grad_edges, we1_t, tot_e2, tot_e3, node_out, grad_nodes, *rest
    ) = unpack_call(C, late, early, small, node_out, grad_nodes, grad_edges, dwf)
    dwf1, dwf2 = rest[:2] if dwf else tot_dwf
    gains = rest[-6:]
    gains = [v.reshape(v.shape[1]) for v in gains]
    return (
        node_out, edge_out, grad_nodes, grad_edges,
        tot1, tot2, tot3, gains[0], gains[1], dwf1, dwf2, gains[2], gains[3],
        we1_t.T, tot_e2, tot_e3, gains[4], gains[5],
    )


def solution(mesh):
    rows = P(("dp", "edge"), None)
    return jax.shard_map(
        body,
        mesh=mesh,
        in_specs=(rows, rows, P(("dp", "edge"), None, None), rows, rows)
        + (P(),) * 14
        + (rows, rows),
        out_specs=(rows,) * 4
        + (P("dp", None),) * 3
        + (P("dp"),) * 2
        + (P("dp", None),) * 2
        + (P("dp"),) * 2
        + (P("dp", None),) * 3
        + (P("dp"),) * 2,
        check_vma=False,
    )
```

```python
import functools

import jax
import jax.numpy as jnp
from jax import lax
from jax.experimental import pallas as pl
from jax.experimental.pallas import tpu as pltpu
from jax.sharding import PartitionSpec as P

BF = jnp.bfloat16
F32 = jnp.float32
I32 = jnp.int32
MESH = pl.DeviceIdType.MESH
MIB = 1024 * 1024
LANES = 128
GROUP = 4
ORDER = (0, 2, 1, 3)
TABLE = 1024
EPS = 1e-05
ROOT = 0.7978845608028654
CUBE = 0.044715 * ROOT


def dot(a, b):
    return jnp.dot(a, b, preferred_element_type=F32)


def dot_tn(a, b):
    return lax.dot_general(a, b, (((0,), (0,)), ((), ())), preferred_element_type=F32)


def dot_nt(a, b):
    return lax.dot_general(a, b, (((1,), (1,)), ((), ())), preferred_element_type=F32)


def gelu_pair(v):
    v = v.astype(BF)
    c = lambda x: jnp.asarray(x, BF)
    z = v * v
    q = c(0.5) + c(0.5) * jnp.tanh(v * (c(ROOT) + c(CUBE) * z))
    act = v * q
    slope = q + (act - act * q) * (c(2.0 * ROOT) + c(6.0 * CUBE) * z)
    return act, slope


def gelu_full(v):
    z = v * v
    q = 0.5 + 0.5 * jnp.tanh(v * (ROOT + CUBE * z))
    act = v * q
    slope = q + (act - act * q) * (2.0 * ROOT + 6.0 * CUBE * z)
    return act.astype(BF), slope.astype(BF)


def row_mean(v):
    return jnp.mean(v, axis=-1, keepdims=True)


def lane_column(ref, k):
    rows = ref.shape[0]
    return jnp.broadcast_to(pltpu.roll(ref[...], LANES - k, axis=1)[:, 0:1], (rows, LANES))


def pick_rows(target, width):
    lane = lax.broadcasted_iota(I32, target.shape, 1)
    one, nil = jnp.ones((), BF), jnp.zeros((), BF)
    t16, l16 = target.astype(jnp.int16), lane.astype(jnp.int16)
    return jnp.concatenate(
        [jnp.where(t16 == l16 + jnp.int16(LANES * c), one, nil) for c in range(width // LANES)], axis=1)


def pick_cols(target, width):
    edges = target.shape[1]
    sub = lax.broadcasted_iota(I32, (width, edges), 0)
    return jnp.where(jnp.broadcast_to(target, (width, edges)).astype(jnp.int16) == sub.astype(jnp.int16), jnp.ones((), BF), jnp.zeros((), BF))


def gather_table(targets, table):
    count = table.shape[0]
    if count <= TABLE:
        hot = jnp.concatenate([pick_rows(t, count) for t in targets], axis=0)
        return dot(hot, table[...])

    def step(c, total):
        base = c * TABLE
        hot = jnp.concatenate([pick_rows(t - base, TABLE) for t in targets], axis=0)
        return total + dot(hot, table[pl.ds(pl.multiple_of(base, TABLE), TABLE), :])

    rows = sum(t.shape[0] for t in targets)
    return lax.fori_loop(0, count // TABLE, step, jnp.zeros((rows, table.shape[1]), F32))


def add_by_target(target, values, total):
    count = total.shape[0]
    if count <= TABLE:
        total[...] += dot(pick_cols(target, count), values)
        return

    def step(c, carry):
        base = c * TABLE
        part = pl.ds(pl.multiple_of(base, TABLE), TABLE)
        total[part, :] += dot(pick_cols(target - base, TABLE), values)
        return carry

    lax.fori_loop(0, count // TABLE, step, 0)


def by_chunks(count, step):
    if count <= TABLE:
        step(pl.ds(0, count))
        return

    def one(c, carry):
        step(pl.ds(pl.multiple_of(c * TABLE, TABLE), TABLE))
        return carry

    lax.fori_loop(0, count // TABLE, one, 0)


def remote(src, dst, send, recv, peer):
    return pltpu.make_async_remote_copy(
        src_ref=src,
        dst_ref=dst,
        send_sem=send,
        recv_sem=recv,
        device_id={"edge": peer},
        device_id_type=MESH,
    )


def greet(peers):
    barrier = pltpu.get_barrier_semaphore()
    for peer in peers:
        pl.semaphore_signal(barrier, inc=1, device_id={"edge": peer}, device_id_type=MESH)
    pl.semaphore_wait(barrier, len(peers))


def block(ref, index, rows):
    return ref.at[pl.ds(pl.multiple_of(index * rows, rows), rows)]


class Place:
    def __init__(self, n):
        self.me = lax.axis_index("edge")
        self.chips = n // 2
        self.chip = self.me // 2
        self.core = lax.rem(self.me, 2)
        self.sibling = self.chip * 2 + 1 - self.core
        self.mates = [self.at(d) for d in range(1, self.chips)]

    def at(self, d):
        return lax.rem(self.chip + d + self.chips, self.chips) * 2 + self.core


class Gather:
    def __init__(self, place, x, out, send, recv):
        rows, chips = x.shape[0], place.chips
        mine = block(out, place.me, rows)
        self.near = remote(x, mine, send.at[0], recv.at[0], place.sibling)
        self.far, self.passed = [], []
        for d in range(1, chips):
            self.far.append(remote(x, mine, send.at[d], recv.at[d], place.mates[d - 1]))
            got = block(out, place.at(-d), rows)
            at = chips + d
            self.passed.append(remote(got, got, send.at[at], recv.at[at], place.sibling))

    def start(self):
        for copy in self.far:
            copy.start()
        self.near.start()

    def finish(self):
        for far, passed in zip(self.far, self.passed):
            far.wait_recv()
            passed.start()
        self.near.wait()
        for copy in self.passed:
            copy.wait()
        for copy in self.far:
            copy.wait_send()


class Scatter:
    def __init__(self, place, x, pair_buf, far_buf, send, recv):
        self.place, self.x = place, x
        self.pair_buf, self.far_buf = pair_buf, far_buf
        chips, self.rows = place.chips, pair_buf.shape[1]
        self.pairs, self.far = [], []
        for d in range(chips):
            theirs = lax.rem(place.chip + d, chips) * 2 + 1 - place.core
            src = block(x, theirs, self.rows)
            self.pairs.append(remote(src, pair_buf.at[d], send.at[d], recv.at[d], place.sibling))
        for d in range(1, chips):
            at = chips + d
            self.far.append(
                remote(pair_buf.at[d], far_buf.at[d], send.at[at], recv.at[at], place.at(d))
            )

    def start(self):
        for copy in self.pairs[1:]:
            copy.start()
        self.pairs[0].start()

    def pass_on(self):
        for d in range(1, self.place.chips):
            self.pairs[d].wait_recv()
            at = pl.ds(pl.multiple_of(self.place.at(d) * self.rows, self.rows), self.rows)
            mine = self.x[at, :].astype(F32) + self.pair_buf[d].astype(F32)
            self.pair_buf[d] = mine.astype(BF)
            self.far[d - 1].start()

    def finish(self):
        self.pairs[0].wait_recv()
        at = pl.ds(pl.multiple_of(self.place.me * self.rows, self.rows), self.rows)
        total = self.x[at, :].astype(F32) + self.pair_buf[0].astype(F32)
        for d in range(1, self.place.chips):
            self.far[d - 1].wait_recv()
            total = total + self.far_buf[d].astype(F32)
        for copy in self.pairs + self.far:
            copy.wait_send()
        return total


def scatter_sum(*refs):
    scatter = Scatter(*refs)
    scatter.start()
    scatter.pass_on()
    return scatter.finish()


def comm_scratch(n, rows, width):
    return [pltpu.VMEM((n // 2, rows, width), BF)] * 2


def sems(count):
    return [pltpu.SemaphoreType.DMA((count,))] * 2


def remote_params(cid):
    return pltpu.CompilerParams(
        collective_id=cid, has_side_effects=True, vmem_limit_bytes=62 * MIB
    )


LOCAL = pltpu.CompilerParams(vmem_limit_bytes=62 * MIB)
WHOLE = pl.BlockSpec(memory_space=pltpu.VMEM)


def slab_pairs(slab, C):
    pairs = slab.shape[1] // (2 * C)
    even = [slab[:, 2 * C * m : 2 * C * m + 256] for m in range(pairs)]
    odd = [slab[:, 2 * C * m + 2 * C - 256 : 2 * C * m + 2 * C] for m in range(pairs)]
    return jnp.concatenate(even, axis=0), jnp.concatenate(odd, axis=0)


def interleave(even, odd, rows):
    parts = []
    for m in range(even.shape[0] // rows):
        parts += [even[m * rows : (m + 1) * rows], odd[m * rows : (m + 1) * rows]]
    return jnp.concatenate(parts, axis=0)


def split_tiles(values, rows):
    count = values.shape[0] // rows
    pick = lambda first: jnp.concatenate(
        [values[k * rows : (k + 1) * rows] for k in range(first, count, 2)], axis=0
    )
    return pick(0), pick(1)


def join_slab(even, odd, rows, C):
    parts = []
    for m in range(even.shape[0] // rows):
        a = even[m * rows : (m + 1) * rows]
        b = odd[m * rows : (m + 1) * rows]
        parts += [a[:, :LANES], a[:, LANES:] + b[:, :LANES], b[:, LANES:]]
    return jnp.concatenate(parts, axis=1)


class Loads:
    def __init__(self, pairs, sem):
        self.copies = [
            pltpu.make_async_copy(src, dst, sem.at[j]) for j, (src, dst) in enumerate(pairs)
        ]

    def start(self):
        for copy in self.copies:
            copy.start()

    def wait(self, first=0, last=None):
        for copy in self.copies[first:last]:
            copy.wait()


def column_of(row):
    return jnp.transpose(jnp.broadcast_to(row, (LANES, row.shape[1])))


def spread(column, width):
    return jnp.concatenate([column] * (width // LANES), axis=1)


def norm_parts(values):
    centred = values - row_mean(values)
    inverse = lax.rsqrt(row_mean(centred * centred) + EPS)
    return centred * inverse, inverse


def forward_kernel(
    n, K, C, nodes, owner, slot, live, g1, o1, g2, o2, w1_h, w2_h, w3_h, wf1_h, wf2_h, we1_h, edges,
    act1, slope1, slope2, tcol, trow, node_out, near, low_out, n1_out, n2_out, inv_out,
    slope_out, sum_out, nodes_h, far_h,
    w1, w2, w3, wf1, wf2, we1, load_sem,
    nodes_all, far_all, lcol, orow, lrow, scol, hist, hist_got, count,
    p_all, p_own, w_own, pre2, total, summed, q_own, pair_buf, far_buf,
    send, recv, hsend, hrecv, rsend, rrecv, qsend, qrecv, own_sem,
):
    i = pl.program_id(0)
    rows, D = nodes.shape
    tiles = K // GROUP
    size = GROUP * rows
    if n * rows > TABLE:
        p_all = summed = nodes_all
    place = Place(n)
    others = [lax.rem(place.me + d, n) for d in range(1, n)]
    loads = Loads(
        [(w1_h, w1), (w2_h, w2), (w3_h, w3), (wf1_h, wf1), (wf2_h, wf2), (we1_h, we1)], load_sem
    )
    keep_nodes = pltpu.make_async_copy(nodes_all, nodes_h, own_sem.at[1])

    @pl.when(i == 0)
    def _():
        loads.start()
        spare = jnp.zeros((LANES - K, rows), I32)
        for k in range(K):
            orow[k : k + 1, :] = owner[k]
        orow[K:, :] = spare
        own_wide = orow[...]
        slot_wide = jnp.concatenate([slot[...], spare], axis=0)
        live_wide = jnp.concatenate([live[...], spare], axis=0).astype(F32)
        target = own_wide * rows + slot_wide
        trow[...] = target
        lrow[...] = live_wide
        tcol[...] = jnp.transpose(target)
        lcol[...] = jnp.transpose(live_wide)
        scol[...] = jnp.transpose(slot_wide)
        pre2[...] = jnp.zeros_like(pre2)
        total[...] = jnp.zeros_like(total)
        w_own[...] = jnp.zeros_like(w_own)
        greet(others)
        gather = Gather(place, nodes, nodes_all, send, recv)
        gather.start()
        own = pltpu.make_async_copy(nodes, block(nodes_all, place.me, rows), own_sem.at[0])
        own.start()

        def tally(g, total):
            ks = [g * GROUP + j for j in range(GROUP)]
            hot = jnp.concatenate([pick_rows(lane_column(scol, k), LANES) for k in ks], axis=0)
            owners = jnp.concatenate([orow[pl.ds(k, 1), :] for k in ks], axis=1)
            lives = jnp.concatenate([lrow[pl.ds(k, 1), :] for k in ks], axis=1)
            sub = lax.broadcasted_iota(I32, (n, size), 0)
            who = jnp.where(
                jnp.broadcast_to(owners, sub.shape) == sub, jnp.broadcast_to(lives, sub.shape), 0.0
            )
            return total + dot(who.astype(BF), hot)

        totals = lax.fori_loop(0, tiles, tally, jnp.zeros((n, LANES), F32))
        for e in range(n):
            hist[e] = jnp.broadcast_to(totals[e : e + 1, :], (8, LANES))
        copies = []
        for d in range(1, n):
            peer = others[d - 1]
            copy = remote(hist.at[peer], hist_got.at[d], hsend.at[d], hrecv.at[d], peer)
            copy.start()
            copies.append(copy)
        loads.wait(0, 2)
        p_own[...] = dot(nodes[...], w1[:D, :])
        w_own[0, :C, :] = w1[2 * D :, :]
        w_own[1, 256 - C :, :] = w1[2 * D :, :]
        tallied = hist[place.me]
        for copy in copies:
            copy.wait_recv()
        for d in range(1, n):
            tallied = tallied + hist_got[d]
        count[...] = tallied
        own.wait()
        gather.finish()
        for copy in copies:
            copy.wait_send()
        keep_nodes.start()
        if n * rows > TABLE:
            keep_nodes.wait()

        def project(part):
            p_all[part, :] = dot(nodes_all[part, :], w1[D : 2 * D, :]).astype(BF)

        by_chunks(n * rows, project)

    last = jnp.clip(i - 1, 0, tiles - 1)
    ks = [last * GROUP + j for j in ORDER]
    act, slope = gelu_pair(pre2[...])
    alive = jnp.concatenate(
        [jnp.concatenate([lane_column(lcol, k)] * (D // LANES), axis=1) for k in ks], axis=0
    ).astype(BF)
    slope2[...] = slope * alive
    act = act * (alive * jnp.where(i >= 1, 1.0, 0.0).astype(BF))
    target = jnp.concatenate([trow[pl.ds(k, 1), :] for k in ks], axis=1)
    add_by_target(target, act, total)

    now = jnp.minimum(i, tiles - 1)
    targets = [lane_column(tcol, now * GROUP + j) for j in ORDER]
    even, odd = slab_pairs(edges[...], C)
    own = jnp.concatenate([dot(even, w_own[0]), dot(odd, w_own[1])], axis=0)
    act, slope = gelu_pair(
        gather_table(targets, p_all) + own + jnp.concatenate([p_own[...]] * GROUP, axis=0)
    )
    act1[...] = act
    slope1[...] = slope
    pre2[...] = dot(act, w2[...])

    @pl.when(i == tiles)
    def _():
        summed[...] = total[...].astype(BF)
        scatter = Scatter(place, summed, pair_buf, far_buf, rsend, rrecv)
        scatter.start()
        scatter.pass_on()
        if n * rows <= TABLE:
            keep_nodes.wait()
        loads.wait(2)
        divisor = 1.0 + column_of(count[0:1, :])
        inv_out[2] = divisor
        mine = scatter.finish().astype(BF)
        sum_out[...] = mine
        resid = nodes[...].astype(F32) + dot(mine, w3[...]) / spread(divisor, D)
        n1, inv1 = norm_parts(resid)
        n1_out[...] = n1
        inv_out[0] = jnp.broadcast_to(inv1, (rows, LANES))
        normed = n1 * g1[...] + o1[...]
        low = normed.astype(BF)
        low_out[...] = low
        act, slope = gelu_full(dot(low, wf1[...]))
        slope_out[...] = slope
        n2, inv2 = norm_parts(normed + dot(act, wf2[...]))
        n2_out[...] = n2
        inv_out[1] = jnp.broadcast_to(inv2, (rows, LANES))
        node_low = (n2 * g2[...] + o2[...]).astype(BF)
        node_out[...] = node_low
        pad = jnp.zeros((rows, 256 - C), F32)
        far = dot_nt(node_low, we1[:, D : 2 * D])
        q_own[...] = jnp.concatenate([far, pad], axis=1).astype(BF)
        gather = Gather(place, q_own, far_all, qsend, qrecv)
        gather.start()
        own = pltpu.make_async_copy(q_own, block(far_all, place.me, rows), own_sem.at[0])
        own.start()
        near[...] = jnp.concatenate([dot_nt(node_low, we1[:, :D]), pad], axis=1)
        own.wait()
        gather.finish()
        keep_far = pltpu.make_async_copy(far_all, far_h, own_sem.at[2])
        keep_far.start()
        keep_far.wait()


def full(x):
    return pl.BlockSpec(
        x.shape, lambda g: (0,) * x.ndim, pipeline_mode=pl.Buffered(buffer_count=1)
    )


def fixed(*s):
    return pl.BlockSpec(s, lambda g: (0,) * len(s), pipeline_mode=pl.Buffered(buffer_count=1))


HBM = pl.BlockSpec(memory_space=pl.ANY)


def forward_call(n, C, nodes, owner, slot, live, g1, o1, g2, o2, weights, edges):
    rows, D = nodes.shape
    K = slot.shape[0]
    FF = weights[3].shape[1]
    tiles = K // GROUP
    size = GROUP * rows
    count = n * rows
    other = count if count <= TABLE else 16
    shape = jax.ShapeDtypeStruct
    lag = lambda d: pl.BlockSpec((size, D), lambda g: (jnp.clip(g - d, 0, tiles - 1), 0))
    small = [nodes, owner, slot, live, g1, o1, g2, o2]
    outs = [
        shape((LANES, rows), I32),
        shape((LANES, rows), I32),
        shape((rows, D), BF),
        shape((rows, 256), F32),
        shape((rows, D), BF),
        shape((rows, D), F32),
        shape((rows, D), F32),
        shape((3, rows, LANES), F32),
        shape((rows, FF), BF),
        shape((rows, D), BF),
    ]
    outs[0] = shape((rows, LANES), I32)
    return pl.pallas_call(
        functools.partial(forward_kernel, n, K, C),
        grid=(tiles + 1,),
        in_specs=[full(v) for v in small]
        + [HBM] * 6
        + [pl.BlockSpec((rows, GROUP * C), lambda g: (0, jnp.minimum(g, tiles - 1)))],
        out_specs=[lag(0), lag(0), lag(1)] + [fixed(*v.shape) for v in outs] + [HBM] * 2,
        out_shape=[shape((K * rows, D), BF)] * 3
        + outs
        + [shape((count, D), BF), shape((count, 256), BF)],
        scratch_shapes=[pltpu.VMEM(v.shape, BF) for v in weights]
        + [
            pltpu.SemaphoreType.DMA((6,)),
            pltpu.VMEM((count, D), BF),
            pltpu.VMEM((count, 256), BF),
            pltpu.VMEM((rows, LANES), F32),
            pltpu.VMEM((LANES, rows), I32),
            pltpu.VMEM((LANES, rows), F32),
            pltpu.VMEM((rows, LANES), I32),
            pltpu.VMEM((n, 8, LANES), F32),
            pltpu.VMEM((n, 8, LANES), F32),
            pltpu.VMEM((8, LANES), F32),
            pltpu.VMEM((other, D), BF),
            pltpu.VMEM((rows, D), F32),
            pltpu.VMEM((2, 256, D), BF),
            pltpu.VMEM((size, D), F32),
            pltpu.VMEM((count, D), F32),
            pltpu.VMEM((other, D), BF),
            pltpu.VMEM((rows, 256), BF),
            *comm_scratch(n, rows, D),
            *sems(n),
            *sems(n),
            *sems(n),
            *sems(n),
            pltpu.SemaphoreType.DMA((3,)),
        ],
        compiler_params=remote_params(0),
    )(*small, *weights, edges)


def edge_kernel(
    tiles, C, tcol, trow, far_all, near, we1, we2, we3, gain, offset, edges1, edges4, edges6, cot,
    edge_out, partial, far_sum, near_sum, dw1, dw2, dw3, dgain,
    w1o, w2p, w3o, w1t, w2t, w3t, gains, total, a1, a2, a3, ag,
    pre1, hid1, slope1, pre2, hid2, slope2, res3, third, up2, up1,
):
    i = pl.program_id(0)
    rows = near.shape[0]
    D2 = we1.shape[1] - C
    gap = 256 - C
    half = GROUP // 2 * rows

    @pl.when(i == 0)
    def _():
        for ref in (w1o, w2p, w3o, w1t, w2t, w3t, gains, total, a1, a2, a3, ag, near_sum,
                    pre1, hid1, slope1, pre2, hid2, slope2, res3, third, up2, up1):
            ref[...] = jnp.zeros_like(ref)
        own = jnp.transpose(we1[:, D2:].astype(F32)).astype(BF)
        w1o[0, :C, :C] = own
        w1o[1, gap:, :C] = own
        w2p[:C, :C] = we2[...]
        w3o[0, :C, :C] = we3[...]
        w3o[1, :C, :] = jnp.concatenate([jnp.zeros((C, gap), F32), we3[...].astype(F32)], axis=1).astype(BF)
        for s in range(2):
            w1t[s] = jnp.transpose(w1o[s].astype(F32)).astype(BF)
            w3t[s] = jnp.transpose(w3o[s].astype(F32)).astype(BF)
        w2t[...] = jnp.transpose(w2p[...].astype(F32)).astype(BF)
        zero = jnp.zeros((1, gap), F32)
        gains[0, 0:1] = jnp.concatenate([gain[...], zero], axis=1)
        gains[0, 1:2] = jnp.concatenate([offset[...], zero], axis=1)
        gains[1, 0:1] = jnp.concatenate([zero, gain[...]], axis=1)
        gains[1, 1:2] = jnp.concatenate([zero, offset[...]], axis=1)

    tile = lambda d: jnp.clip(i - d, 0, tiles - 1)
    sides = [slice(0, half), slice(half, 2 * half)]

    t4 = tile(1)
    valid = jnp.where(i >= 1, 1.0, 0.0)
    slabs = slab_pairs(edges4[...], C)
    cots = slab_pairs(cot[...], C)
    lane = lax.broadcasted_iota(I32, (half, 256), 1)
    outs, grads, ups = [], [], []
    for s in range(2):
        inside = (lane < C) if s == 0 else (lane >= gap)
        keep = lambda v: jnp.where(inside, v, 0.0)
        mean = lambda v: jnp.sum(v, axis=-1, keepdims=True) * (1.0 / C)
        value = keep(slabs[s].astype(F32)) + res3[sides[s], :]
        centred = keep(value - mean(value))
        inverse = lax.rsqrt(mean(centred * centred) + EPS)
        normal = centred * inverse
        outs.append(normal * gains[s, 0:1] + gains[s, 1:2])
        upstream = cots[s].astype(F32) * valid
        moved = upstream * normal
        for r in range(half // rows):
            part = slice(r * rows, (r + 1) * rows)
            ag[s, 0] += moved[part]
            ag[s, 1] += upstream[part]
        scaled = upstream * gains[s, 0:1]
        grad = inverse * (scaled - mean(scaled) - normal * mean(scaled * normal))
        grad = keep(grad)
        grads.append(grad)
        low3 = grad.astype(BF)
        a3[s] += dot_tn(hid2[sides[s], :], low3)
        ups.append(dot(low3, w3t[s]))
    edge_out[...] = join_slab(outs[0], outs[1], rows, C).astype(BF)

    t5 = tile(1)
    low2 = (jnp.concatenate(ups, axis=0) * slope2[0].astype(F32)).astype(BF)
    a2[...] += dot_tn(hid1[0], low2)
    up1v = dot(low2, w2t[...])

    t6 = tile(1)
    low1 = (up1v * slope1[0].astype(F32)).astype(BF)
    slabs = slab_pairs(edges4[...], C)
    outs = []
    for s in range(2):
        a1[s] += dot_tn(low1[sides[s]], slabs[s])
        outs.append(grads[s] + dot(low1[sides[s]], w1t[s]))
    partial[...] = join_slab(outs[0], outs[1], rows, C).astype(BF)
    wide = low1.astype(F32)
    acc = wide[:rows]
    for j in range(1, GROUP):
        acc = acc + wide[j * rows : (j + 1) * rows]
    near_sum[...] += acc
    target = jnp.concatenate([trow[pl.ds(t6 * GROUP + j, 1), :] for j in ORDER], axis=1)
    add_by_target(target, low1, total)

    t1 = tile(0)
    slabs = slab_pairs(edges1[...], C)
    own = jnp.concatenate([dot(slabs[0], w1o[0]), dot(slabs[1], w1o[1])], axis=0)
    got = gather_table([lane_column(tcol, t1 * GROUP + j) for j in ORDER], far_all)
    pre1v = got + own + jnp.concatenate([near[...]] * GROUP, axis=0)

    t2 = tile(0)
    act, slope = gelu_pair(pre1v)
    hid1[0] = act
    slope1[0] = slope
    pre2v = dot(act, w2p[...])

    t3 = tile(0)
    act, slope = gelu_pair(pre2v)
    hid2[...] = act
    slope2[0] = slope
    for s in range(2):
        res3[sides[s], :] = dot(act[sides[s]], w3o[s])

    @pl.when(i == tiles)
    def _():
        far_sum[...] = total[...].astype(BF)
        dw1[...] = jnp.transpose(a1[0])[:C, :] + jnp.transpose(a1[1])[gap:, :]
        dw2[...] = a2[...]
        shifted = a3[1][:, gap:]
        dw3[...] = a3[0] + jnp.concatenate([shifted, jnp.zeros((256, gap), F32)], axis=1)
        for r in range(2):
            even = jnp.sum(ag[0, r], axis=0, keepdims=True)
            odd = jnp.sum(ag[1, r], axis=0, keepdims=True)
            row = even + jnp.concatenate([odd[:, gap:], jnp.zeros((1, gap), F32)], axis=1)
            dgain[r * 8 : r * 8 + 8, :] = jnp.broadcast_to(row, (8, 256))


def edge_call(C, tcol, trow, far_all, near, we1, we2, we3, gain, offset, edges, cot):
    rows = near.shape[0]
    count = far_all.shape[0]
    K = edges.shape[1] // C
    tiles = K // GROUP
    size = GROUP * rows
    shape = jax.ShapeDtypeStruct
    slab = lambda d: pl.BlockSpec(
        (rows, GROUP * C), lambda g: (0, jnp.clip(g - d, 0, tiles - 1))
    )
    fixed = lambda *s: pl.BlockSpec(
        s, lambda g: (0,) * len(s), pipeline_mode=pl.Buffered(buffer_count=1)
    )
    return pl.pallas_call(
        functools.partial(edge_kernel, tiles, C),
        grid=(tiles + 1,),
        in_specs=[full(x) for x in (tcol, trow, far_all, near, we1, we2, we3, gain, offset)]
        + [slab(0), slab(1), slab(99), slab(1)],
        out_specs=[
            slab(1), slab(1), fixed(count, 256), fixed(rows, 256),
            fixed(C, 256), fixed(256, 256), fixed(256, 256), fixed(16, 256),
        ],
        out_shape=[
            shape((rows, K * C), BF),
            shape((rows, K * C), BF),
            shape((count, 256), BF),
            shape((rows, 256), F32),
            shape((C, 256), F32),
            shape((256, 256), F32),
            shape((256, 256), F32),
            shape((16, 256), F32),
        ],
        scratch_shapes=[
            pltpu.VMEM((2, 256, 256), BF),
            pltpu.VMEM((256, 256), BF),
            pltpu.VMEM((2, 256, 256), BF),
            pltpu.VMEM((2, 256, 256), BF),
            pltpu.VMEM((256, 256), BF),
            pltpu.VMEM((2, 256, 256), BF),
            pltpu.VMEM((2, 8, 256), F32),
            pltpu.VMEM((count, 256), F32),
            pltpu.VMEM((2, 256, 256), F32),
            pltpu.VMEM((256, 256), F32),
            pltpu.VMEM((2, 256, 256), F32),
            pltpu.VMEM((2, 2, rows, 256), F32),
            pltpu.VMEM((size, 256), F32),
            pltpu.VMEM((3, size, 256), BF),
            pltpu.VMEM((4, size, 256), BF),
            pltpu.VMEM((size, 256), F32),
            pltpu.VMEM((size, 256), BF),
            pltpu.VMEM((2, size, 256), BF),
            pltpu.VMEM((size, 256), F32),
            pltpu.VMEM((2, size, 256), F32),
            pltpu.VMEM((size, 256), F32),
            pltpu.VMEM((size, 256), F32),
        ],
        compiler_params=LOCAL,
    )(tcol, trow, far_all, near, we1, we2, we3, gain, offset, edges, edges, edges, cot)


def norm_back(upstream, normal, inverse, gain):
    scaled = upstream * gain
    return inverse * (scaled - row_mean(scaled) - normal * row_mean(scaled * normal))


def node_back(
    C, far, near_sum, cot, n1, n2, inv, slope, w3, g1, wf1, wf2, g2, we1, grad_one, resid_out, dgain, v_own
):
    rows, D = cot.shape
    far = far.astype(BF)[:, :C]
    near = near_sum[...].astype(BF)[:, :C]
    grad = cot[...].astype(F32) + dot(near, we1[:, :D]) + dot(far, we1[:, D : 2 * D])
    two = norm_back(grad, n2[...], inv[1][:, 0:1], g2[...])
    dgain[16:24, :] = jnp.broadcast_to(jnp.sum(grad * n2[...], axis=0, keepdims=True), (8, D))
    dgain[24:32, :] = jnp.broadcast_to(jnp.sum(grad, axis=0, keepdims=True), (8, D))
    resid = two.astype(BF)
    resid_out[...] = resid
    inner = (dot_nt(resid, wf2[...]) * slope[...].astype(F32)).astype(BF)
    grad = two + dot_nt(inner, wf1[...])
    one = norm_back(grad, n1[...], inv[0][:, 0:1], g1[...])
    dgain[0:8, :] = jnp.broadcast_to(jnp.sum(grad * n1[...], axis=0, keepdims=True), (8, D))
    dgain[8:16, :] = jnp.broadcast_to(jnp.sum(grad, axis=0, keepdims=True), (8, D))
    grad_one[...] = one
    upper = (one / spread(inv[2], D)).astype(BF)
    v_own[...] = dot_nt(upper, w3[...]).astype(BF)
    return far, near, upper


def node_back_kernel(
    n, C, far_sum, near_sum, cot, node_low, n1, n2, inv, slope, summed,
    w3, g1, wf1, wf2, g2, we1,
    grad_one, vw_all, resid_out, dgain, dw3, dwe_near, dwe_far,
    pair_buf, far_buf, v_own, send, recv, gsend, grecv, own_sem,
):
    place = Place(n)
    rows = cot.shape[0]
    greet([place.sibling] + place.mates)
    far = scatter_sum(place, far_sum, pair_buf, far_buf, send, recv)
    far, near, upper = node_back(
        C, far, near_sum, cot, n1, n2, inv, slope, w3, g1, wf1, wf2, g2, we1,
        grad_one, resid_out, dgain, v_own,
    )
    gather = Gather(place, v_own, vw_all, gsend, grecv)
    gather.start()
    own = pltpu.make_async_copy(v_own, block(vw_all, place.me, rows), own_sem.at[0])
    own.start()
    dw3[...] = dot_tn(summed[...], upper)
    dwe_near[...] = dot_tn(node_low[...], near)
    dwe_far[...] = dot_tn(node_low[...], far)
    own.wait()
    gather.finish()


def node_back_call(n, C, *args):
    cot = args[2]
    rows, D = cot.shape
    shape = jax.ShapeDtypeStruct
    return pl.pallas_call(
        functools.partial(node_back_kernel, n, C),
        in_specs=[WHOLE] * len(args),
        out_specs=[WHOLE] * 7,
        out_shape=[
            shape((rows, D), F32),
            shape((n * rows, D), BF),
            shape((rows, D), BF),
            shape((32, D), F32),
            shape((D, D), F32),
            shape((D, C), F32),
            shape((D, C), F32),
        ],
        scratch_shapes=[
            *comm_scratch(n, rows, 256),
            pltpu.VMEM((rows, D), BF),
            *sems(n),
            *sems(n),
            pltpu.SemaphoreType.DMA((1,)),
        ],
        compiler_params=remote_params(2),
    )(*args)


class Line:
    def __init__(self, place, pieces, x, out, pair_buf, low_buf, high_buf, send_buf, send, recv):
        self.place, self.pieces, self.x, self.out = place, pieces, x, out
        self.pair_buf, self.low_buf, self.high_buf = pair_buf, low_buf, high_buf
        self.send_buf, self.send, self.recv = send_buf, send, recv
        c, q, chips = place.chip, place.core, place.chips
        self.root = chips // 2 - 1 + q
        self.away = jnp.abs(c - self.root)
        self.right = jnp.minimum(c + 1, chips - 1) * 2 + q
        self.left = jnp.maximum(c - 1, 0) * 2 + q
        self.half = x.shape[0] // 2
        self.rows = self.half // pieces

    def part(self, which, p):
        return pl.ds(pl.multiple_of(which * self.half + p * self.rows, self.rows), self.rows)

    def here(self, p):
        return pl.ds(pl.multiple_of(p * self.rows, self.rows), self.rows)

    def link(self, src, dst, p, sent, got, peer):
        n = self.pieces
        return remote(src, dst, self.send.at[sent * n + p], self.recv.at[got * n + p], peer)

    def pair(self, p):
        src = self.x.at[self.part(1 - self.place.core, p)]
        return self.link(src, self.pair_buf.at[self.here(p)], p, 0, 0, self.place.sibling)

    def up(self, p):
        here = self.here(p)
        return self.link(self.send_buf.at[here], self.low_buf.at[here], p, 1, 1, self.right)

    def down(self, p):
        here = self.here(p)
        return self.link(self.send_buf.at[here], self.high_buf.at[here], p, 2, 2, self.left)

    def outward(self, p, sent, got, peer):
        mine = self.out.at[self.part(self.place.core, p)]
        return self.link(mine, mine, p, sent, got, peer)

    def out_left(self, p):
        return self.outward(p, 3, 3, self.left)

    def out_right(self, p):
        return self.outward(p, 5, 3, self.right)

    def across(self, p):
        return self.outward(p, 4, 4, self.place.sibling)

    def each(self, step):
        lax.fori_loop(0, self.pieces, lambda p, z: (step(p), z)[1], 0)

    def start(self):
        self.each(lambda p: self.pair(p).start())

    def reduce(self, p):
        c, root, last = self.place.chip, self.root, self.place.chips - 1
        here, mine_at = self.here(p), self.part(self.place.core, p)
        self.pair(p).wait_recv()
        mine = lambda: self.x[mine_at, :].astype(F32) + self.pair_buf[here, :].astype(F32)

        def end():
            self.send_buf[here, :] = mine().astype(BF)

        def from_low():
            self.up(p).wait_recv()
            self.send_buf[here, :] = (mine() + self.low_buf[here, :].astype(F32)).astype(BF)

        def from_high():
            self.down(p).wait_recv()
            self.send_buf[here, :] = (mine() + self.high_buf[here, :].astype(F32)).astype(BF)

        def at_root():
            self.up(p).wait_recv()
            self.down(p).wait_recv()
            total = mine() + self.low_buf[here, :].astype(F32) + self.high_buf[here, :].astype(F32)
            self.out[mine_at, :] = total.astype(BF)
            self.out_left(p).start()
            self.out_right(p).start()
            self.across(p).start()

        pl.when((c == 0) | (c == last))(end)
        pl.when((c > 0) & (c < root))(from_low)
        pl.when((c > root) & (c < last))(from_high)
        pl.when(c < root)(lambda: self.up(p).start())
        pl.when(c > root)(lambda: self.down(p).start())
        pl.when(c == root)(at_root)

    def spread(self, p):
        c, root, last = self.place.chip, self.root, self.place.chips - 1

        def leftward():
            self.out_left(p).wait_recv()
            pl.when(c > 0)(lambda: self.out_left(p).start())
            self.across(p).start()

        def rightward():
            self.out_right(p).wait_recv()
            pl.when(c < last)(lambda: self.out_right(p).start())
            self.across(p).start()

        pl.when(c < root)(leftward)
        pl.when(c > root)(rightward)

    def slots(self, lag):
        return self.pieces + 2 * lag * (self.place.chips // 2)

    def slot(self, s, lag):
        deep = self.place.chips // 2
        p = s - lag * (deep - self.away)
        pl.when((p >= 0) & (p < self.pieces))(lambda: self.reduce(p))
        o = s - lag * (deep + self.away)
        pl.when((o >= 0) & (o < self.pieces) & (self.away > 0))(lambda: self.spread(o))

    def finish(self):
        c, root, last = self.place.chip, self.root, self.place.chips - 1

        def end(p):
            self.pair(p).wait_send()
            self.across(p).wait_send()
            pl.when(c < root)(lambda: self.up(p).wait_send())
            pl.when(c > root)(lambda: self.down(p).wait_send())
            pl.when((c <= root) & (c > 0))(lambda: self.out_left(p).wait_send())
            pl.when((c >= root) & (c < last))(lambda: self.out_right(p).wait_send())

        self.each(lambda p: self.across(p).wait_recv())
        self.each(end)


def line_scratch(rows, width, pieces):
    return [pltpu.VMEM((rows // 2, width), BF)] * 4 + sems(6 * pieces)


class Exchange:
    def __init__(self, place, n, mine, got, send, recv):
        self.place, self.n, self.mine, self.got = place, n, mine, got
        self.copies = []
        for d in range(1, n):
            peer = lax.rem(place.me + d, n)
            self.copies.append(remote(mine, got.at[place.me], send.at[d], recv.at[d], peer))

    def start(self):
        for copy in self.copies:
            copy.start()
        self.got[self.place.me] = self.mine[...]

    def finish(self):
        for copy in self.copies:
            copy.wait_recv()
        total = self.got[0]
        for e in range(1, self.n):
            total = total + self.got[e]
        for copy in self.copies:
            copy.wait_send()
        return total


EARLY, LATE, LAG, AHEAD = 7, 9, 2, 7


def early_rows(D, C):
    used = D + (2 * D + C) // 2 + C
    unit = 2 * EARLY * 16
    return -(-used // unit) * unit


def pack_early(C, x, gains, dw3, dwe_near, dwe_far, dwe1, dwe2, dwe3, dgain, dg3):
    D = dw3.shape[0]
    x[:D, :] = dw3[...].astype(BF)
    spare = jnp.zeros((D, 256 - C), F32)
    edge1 = jnp.concatenate(
        [
            jnp.concatenate([dwe_near[...], spare], axis=1),
            jnp.concatenate([dwe_far[...], spare], axis=1),
            dwe1[...],
        ],
        axis=0,
    ).astype(BF)
    half = edge1.shape[0] // 2
    x[D : D + half, :256] = edge1[:half]
    x[D : D + half, 256:] = edge1[half:]
    at = D + half
    x[at : at + C, :256] = dwe2[:C, :].astype(BF)
    x[at : at + C, 256:] = dwe3[:C, :].astype(BF)
    if at + C < x.shape[0]:
        x[at + C :, :] = jnp.zeros((x.shape[0] - at - C, D), BF)
    gains[...] = jnp.zeros_like(gains)
    for r in range(4):
        gains[r : r + 1, :] = dgain[8 * r : 8 * r + 1, :]
    for r in range(2):
        gains[4 + r : 5 + r, :256] = dg3[8 * r : 8 * r + 1, :]


def back_start(C, w1, w2, w2t, w_own, w_own_t, zeroed):
    D = w2.shape[0]
    gap = 256 - C
    for ref in (w_own, *zeroed):
        ref[...] = jnp.zeros_like(ref)
    w_own[0, :C, :] = w1[2 * D :, :]
    w_own[1, gap:, :] = w1[2 * D :, :]
    for s in range(2):
        w_own_t[s] = jnp.transpose(w_own[s].astype(F32)).astype(BF)
    w2t[...] = jnp.transpose(w2[...].astype(F32)).astype(BF)


def back_tile(
    g, rows, C, tcol, trow, vw, act1, slope1, slope2, edges, partial, grad_edges,
    w2t, w_own_t, total, a2, ae, source_sum,
):
    half = GROUP // 2 * rows
    ks = [g * GROUP + j for j in ORDER]
    up = gather_table([lane_column(tcol, k) for k in ks], vw)
    upper = up.astype(BF) * slope2[...]
    a2[...] += dot_tn(act1[...], upper)
    lower = dot(upper, w2t[...]).astype(BF) * slope1[...]
    wide = lower.astype(F32)
    acc = wide[:rows]
    for j in range(1, GROUP):
        acc = acc + wide[j * rows : (j + 1) * rows]
    source_sum[...] += acc
    target = jnp.concatenate([trow[pl.ds(k, 1), :] for k in ks], axis=1)
    add_by_target(target, lower, total)
    slabs = slab_pairs(edges[...], C)
    lowers = [lower[:half], lower[half:]]
    own = []
    for s in range(2):
        ae[s] += dot_tn(slabs[s], lowers[s])
        own.append(dot(lowers[s], w_own_t[s]))
    grad_edges[...] = (partial[...].astype(F32) + join_slab(own[0], own[1], rows, C)).astype(BF)


def back_weights(C, dw1, dw2, nodes_all, nodes, total, a2, ae, source_sum):
    D = nodes.shape[1]
    gap = 256 - C
    dw2[...] = a2[...].astype(BF)
    dw1[:D, :] = dot_tn(nodes[...], source_sum[...].astype(BF)).astype(BF)
    dw1[2 * D :, :] = (ae[0][:C, :] + ae[1][gap:, :]).astype(BF)
    a2[...] = jnp.zeros_like(a2)

    def weigh(part):
        a2[...] += dot_tn(nodes_all[part, :], total[part, :].astype(BF))

    by_chunks(total.shape[0], weigh)
    dw1[D : 2 * D, :] = a2[...].astype(BF)


def tail(early, late, scatter, source_sum, grad_one, w1, grad_nodes, feed):
    D = grad_one.shape[1]
    late.start()
    scatter.start()

    def feed_part(f):
        low, resid, wf1, wf2, dwf1, dwf2 = feed
        step = 256
        cols = pl.ds(pl.multiple_of(f * step, step), step)
        act, slope = gelu_full(dot(low[...], wf1[:, cols]))
        dwf2[cols, :] = dot_tn(act, resid[...]).astype(BF)
        inner = (dot_nt(resid[...], wf2[cols, :]) * slope.astype(F32)).astype(BF)
        dwf1[:, cols] = dot_tn(low[...], inner).astype(BF)

    parts = feed[2].shape[1] // 256 if feed else 0

    def slot(s, carry):
        early.slot(s, LAG)
        late.slot(s - EARLY, LAG)
        if feed:
            f = s - AHEAD
            pl.when((f % 2 == 1) & (f // 2 < parts))(lambda: feed_part(f // 2))
        return carry

    lax.fori_loop(AHEAD, AHEAD + 14, slot, 0)
    scatter.pass_on()
    lax.fori_loop(AHEAD + 14, EARLY + late.slots(LAG), slot, 0)
    source = dot_nt(source_sum[...].astype(BF), w1[:D, :])
    total = scatter.finish()
    grad_nodes[...] = grad_one[...] + source + dot_nt(total.astype(BF), w1[D : 2 * D, :])
    early.finish()
    late.finish()


def back_kernel(n, tiles, C, tcol, trow, nodes, near_sum, g1, g2, dwe1, dwe2, dwe3, dg3, *refs):
    sources, refs = refs[:16], refs[16:]
    act1, slope1, slope2, edges, partial, *refs = refs
    grad_edges, grad_nodes, small, dwf1, dwf2, early_h, late_h, *refs = refs
    held, refs = refs[:16], refs[16:]
    (
        far_sum, low_own, cot, we1, n2, inv, wf2, slope, wf1, n1, w3, w1, w2, summed, node_low, nodes_all
    ) = held
    (
        load_sem, low, lsend, lrecv, vw, v_own, grad_one, resid_own, dgain, dw3, dwe_near, dwe_far,
        resid, bsend, brecv, vsend, vrecv, hsend, hrecv, pair_h, far_h,
        w2t, w_own, w_own_t, total, a2, ae, source_sum, target_sum, gains, got, gsend, grecv,
        pair_buf, far_buf, send, recv, x1, out1, x2, out2, *line_refs,
    ) = refs
    g = pl.program_id(0)
    rows, D = nodes.shape
    place = Place(n)
    loads = Loads(list(zip(sources, held)), load_sem)
    gather = Gather(place, resid_own, resid, bsend, brecv)
    gather_low = Gather(place, low_own, low, lsend, lrecv)
    early = Line(place, EARLY, x1, out1, *line_refs[: len(line_refs) // 2])
    late = Line(place, LATE, x2, out2, *line_refs[len(line_refs) // 2 :])
    exchange = Exchange(place, n, gains, got, gsend, grecv)

    @pl.when(g == 0)
    def _():
        loads.start()
        greet([lax.rem(place.me + d, n) for d in range(1, n)])
        loads.wait(0, 2)
        scatter = Scatter(place, far_sum, pair_h, far_h, hsend, hrecv)
        scatter.start()
        scatter.pass_on()
        mine = pl.ds(pl.multiple_of(place.me * rows, rows), rows)
        low[mine, :] = low_own[...]
        loads.wait(2, 15)
        back_start(C, w1, w2, w2t, w_own, w_own_t, (total, a2, ae, source_sum))
        far, near, upper = node_back(
            C, scatter.finish(), near_sum, cot, n1, n2, inv, slope, w3, g1, wf1, wf2, g2, we1,
            grad_one, resid_own, dgain, v_own,
        )
        spread_v = Gather(place, v_own, vw, vsend, vrecv)
        spread_v.start()
        dw3[...] = dot_tn(summed[...], upper)
        dwe_near[...] = dot_tn(node_low[...], near)
        dwe_far[...] = dot_tn(node_low[...], far)
        pack_early(C, x1, gains, dw3, dwe_near, dwe_far, dwe1, dwe2, dwe3, dgain, dg3)
        vw[mine, :] = v_own[...]
        resid[mine, :] = resid_own[...]
        spread_v.finish()
        exchange.start()
        early.start()

    pl.when(g == 1)(gather_low.start)
    pl.when(g == 4)(gather.start)
    ahead = g - (tiles - AHEAD)
    pl.when(ahead >= 0)(lambda: early.slot(ahead, LAG))
    back_tile(
        g, rows, C, tcol, trow, vw, act1, slope1, slope2, edges, partial, grad_edges,
        w2t, w_own_t, total, a2, ae, source_sum,
    )

    @pl.when(g == tiles - 1)
    def _():
        target_sum[...] = total[...].astype(BF)
        loads.wait(15)
        at = 2 * D + C
        back_weights(
            C, x2.at[pl.ds(0, at)], x2.at[pl.ds(at, D)], nodes_all, nodes, total, a2, ae, source_sum
        )
        small[...] = exchange.finish()
        gather_low.finish()
        gather.finish()
        scatter = Scatter(place, target_sum, pair_buf, far_buf, send, recv)
        tail(
            early, late, scatter, source_sum, grad_one, w1, grad_nodes, (low, resid, wf1, wf2, dwf1, dwf2)
        )
        keep_early = pltpu.make_async_copy(out1, early_h, load_sem.at[16])
        keep_early.start()
        keep_late = pltpu.make_async_copy(out2, late_h, load_sem.at[17])
        keep_late.start()
        keep_early.wait()
        keep_late.wait()


def back_call(n, C, whole, loaded, act1, slope1, slope2, edges, partial):
    rows, D = whole[2].shape
    count = n * rows
    K = edges.shape[1] // C
    tiles = K // GROUP
    size = GROUP * rows
    FF = loaded[8].shape[1]
    early, late = early_rows(D, C), 3 * D + C
    shape = jax.ShapeDtypeStruct
    slab = pl.BlockSpec((rows, GROUP * C), lambda g: (0, g))
    tile = pl.BlockSpec((size, D), lambda g: (g, 0))
    outs = [
        shape((rows, D), F32),
        shape((8, D), F32),
        shape((D, FF), BF),
        shape((FF, D), BF),
    ]
    return pl.pallas_call(
        functools.partial(back_kernel, n, tiles, C),
        grid=(tiles,),
        in_specs=[full(v) for v in whole] + [HBM] * len(loaded) + [tile, tile, tile, slab, slab],
        out_specs=[slab] + [fixed(*v.shape) for v in outs] + [HBM] * 2,
        out_shape=[shape((rows, K * C), BF)]
        + outs
        + [shape((early, D), BF), shape((late, D), BF)],
        scratch_shapes=[pltpu.VMEM(v.shape, v.dtype) for v in loaded]
        + [
            pltpu.SemaphoreType.DMA((18,)),
            pltpu.VMEM((count, D), BF),
            *sems(n),
            pltpu.VMEM((count, D), BF),
            pltpu.VMEM((rows, D), BF),
            pltpu.VMEM((rows, D), F32),
            pltpu.VMEM((rows, D), BF),
            pltpu.VMEM((32, D), F32),
            pltpu.VMEM((D, D), F32),
            pltpu.VMEM((D, C), F32),
            pltpu.VMEM((D, C), F32),
            pltpu.VMEM((count, D), BF),
            *sems(n),
            *sems(n),
            *sems(n),
            *comm_scratch(n, rows, 256),
            pltpu.VMEM((D, D), BF),
            pltpu.VMEM((2, 256, D), BF),
            pltpu.VMEM((2, D, 256), BF),
            pltpu.VMEM((count, D), F32),
            pltpu.VMEM((D, D), F32),
            pltpu.VMEM((2, 256, D), F32),
            pltpu.VMEM((rows, D), F32),
            pltpu.VMEM((count, D), BF),
            pltpu.VMEM((8, D), F32),
            pltpu.VMEM((n, 8, D), F32),
            *sems(n),
            *comm_scratch(n, rows, D),
            *sems(n),
            pltpu.VMEM((early, D), BF),
            pltpu.VMEM((early, D), BF),
            pltpu.VMEM((late, D), BF),
            pltpu.VMEM((late, D), BF),
            *line_scratch(early, D, EARLY),
            *line_scratch(late, D, LATE),
        ],
        compiler_params=remote_params(3),
    )(*whole, *loaded, act1, slope1, slope2, edges, partial)


def message_back_kernel(
    tiles, C, tcol, trow, nodes_all, nodes, vw, w1, w2, act1, slope1, slope2, edges, partial,
    grad_edges, dw1, dw2, target_sum, source_sum, w2t, w_own, w_own_t, total, a2, ae,
):
    g = pl.program_id(0)

    @pl.when(g == 0)
    def _():
        back_start(C, w1, w2, w2t, w_own, w_own_t, (total, a2, ae, source_sum))

    back_tile(
        g, nodes.shape[0], C, tcol, trow, vw, act1, slope1, slope2, edges, partial, grad_edges,
        w2t, w_own_t, total, a2, ae, source_sum,
    )

    @pl.when(g == tiles - 1)
    def _():
        target_sum[...] = total[...].astype(BF)
        back_weights(C, dw1, dw2, nodes_all, nodes, total, a2, ae, source_sum)


def message_back_call(C, tcol, trow, nodes_all, nodes, vw, w1, w2, act1, slope1, slope2, edges, partial):
    rows, D = nodes.shape
    count = vw.shape[0]
    K = edges.shape[1] // C
    tiles = K // GROUP
    size = GROUP * rows
    shape = jax.ShapeDtypeStruct
    slab = pl.BlockSpec((rows, GROUP * C), lambda g: (0, g))
    tile = pl.BlockSpec((size, D), lambda g: (g, 0))
    return pl.pallas_call(
        functools.partial(message_back_kernel, tiles, C),
        grid=(tiles,),
        in_specs=[full(x) for x in (tcol, trow, nodes_all, nodes, vw, w1, w2)]
        + [tile, tile, tile, slab, slab],
        out_specs=[slab, fixed(2 * D + C, D), fixed(D, D), fixed(count, D), fixed(rows, D)],
        out_shape=[
            shape((rows, K * C), BF),
            shape((2 * D + C, D), BF),
            shape((D, D), BF),
            shape((count, D), BF),
            shape((rows, D), F32),
        ],
        scratch_shapes=[
            pltpu.VMEM((D, D), BF),
            pltpu.VMEM((2, 256, D), BF),
            pltpu.VMEM((2, D, 256), BF),
            pltpu.VMEM((count, D), F32),
            pltpu.VMEM((D, D), F32),
            pltpu.VMEM((2, 256, D), F32),
        ],
        compiler_params=LOCAL,
    )(tcol, trow, nodes_all, nodes, vw, w1, w2, act1, slope1, slope2, edges, partial)


def final_kernel(
    n, C, target_sum, source_sum, grad_one, w1, dw1, dw2, dw3, dwe_near, dwe_far, dwe1, dwe2, dwe3,
    dgain, dg3, grad_nodes, out1, out2, small,
    x1, x2, gains, got, gsend, grecv, pair_buf, far_buf, send, recv, *line_refs,
):
    place = Place(n)
    D = grad_one.shape[1]
    pack_early(C, x1, gains, dw3, dwe_near, dwe_far, dwe1, dwe2, dwe3, dgain, dg3)
    at = 2 * D + C
    x2[:at, :] = dw1[...]
    x2[at:, :] = dw2[...]
    greet([lax.rem(place.me + d, n) for d in range(1, n)])
    early = Line(place, EARLY, x1, out1, *line_refs[: len(line_refs) // 2])
    late = Line(place, LATE, x2, out2, *line_refs[len(line_refs) // 2 :])
    exchange = Exchange(place, n, gains, got, gsend, grecv)
    exchange.start()
    small[...] = exchange.finish()
    scatter = Scatter(place, target_sum, pair_buf, far_buf, send, recv)
    early.start()
    lax.fori_loop(0, AHEAD, lambda s, z: (early.slot(s, LAG), z)[1], 0)
    tail(early, late, scatter, source_sum, grad_one, w1, grad_nodes, None)


def final_call(n, C, args):
    rows, D = args[2].shape
    early, late = early_rows(D, C), 3 * D + C
    shape = jax.ShapeDtypeStruct
    return pl.pallas_call(
        functools.partial(final_kernel, n, C),
        in_specs=[WHOLE] * len(args),
        out_specs=[WHOLE] * 4,
        out_shape=[
            shape((rows, D), F32),
            shape((early, D), BF),
            shape((late, D), BF),
            shape((8, D), F32),
        ],
        scratch_shapes=[
            pltpu.VMEM((early, D), BF),
            pltpu.VMEM((late, D), BF),
            pltpu.VMEM((8, D), F32),
            pltpu.VMEM((n, 8, D), F32),
            *sems(n),
            *comm_scratch(n, rows, D),
            *sems(n),
            *line_scratch(early, D, EARLY),
            *line_scratch(late, D, LATE),
        ],
        compiler_params=remote_params(4),
    )(*args)


def feed_kernel(low, resid, wf1, wf2, dwf1, dwf2):
    @pl.when(pl.program_id(1) == 0)
    def _():
        dwf1[...] = jnp.zeros_like(dwf1)
        dwf2[...] = jnp.zeros_like(dwf2)

    act, slope = gelu_full(dot(low[...], wf1[...]))
    dwf2[...] += dot_tn(act, resid[...])
    inner = (dot_nt(resid[...], wf2[...]) * slope.astype(F32)).astype(BF)
    dwf1[...] += dot_tn(low[...], inner)


def feed_call(low, resid, wf1, wf2):
    count = low.shape[0]
    D, FF = wf1.shape
    step, rows = min(FF, 512), min(count, TABLE)
    shape = jax.ShapeDtypeStruct
    return pl.pallas_call(
        feed_kernel,
        grid=(FF // step, count // rows),
        in_specs=[
            pl.BlockSpec((rows, D), lambda f, r: (r, 0)),
            pl.BlockSpec((rows, D), lambda f, r: (r, 0)),
            pl.BlockSpec((D, step), lambda f, r: (0, f)),
            pl.BlockSpec((step, D), lambda f, r: (f, 0)),
        ],
        out_specs=[
            pl.BlockSpec((D, step), lambda f, r: (0, f)),
            pl.BlockSpec((step, D), lambda f, r: (f, 0)),
        ],
        out_shape=[shape((D, FF), F32), shape((FF, D), F32)],
        compiler_params=LOCAL,
    )(low, resid, wf1, wf2)


def unpack_kernel(C, steps, late, packed, small, node_in, grad_in, edges, *refs):
    g = pl.program_id(0)
    D = late.shape[1]
    plain = refs[: (len(refs) - 15) // 2]
    w1, w2, w3, grad_edges, one, two, three, node_out, grad_nodes, *outs = refs[len(plain) :]
    gains = outs[len(plain) :]
    grad_edges[...] = edges[...].astype(F32)
    first = 2 * D + C
    for ref, src, base in ((w1, late, 0), (w2, late, first), (w3, packed, 0)):
        step = ref.shape[0]
        ref[...] = src[pl.ds(pl.multiple_of(base + g * step, 16), step), :].astype(F32)
    at = D
    for a, b in zip(plain, outs):
        b[...] = a[...].astype(F32)

    @pl.when(g == steps - 1)
    def _():
        half = (2 * D + C) // 2
        for r in range(2):
            left = 256 * r
            flipped = jnp.transpose(packed[at : at + half, left : left + 256].astype(F32))
            one[:, half * r : half * r + half] = flipped[:C, :]
        end = at + half
        two[...] = packed[end : end + C, :C].astype(F32)
        three[...] = packed[end : end + C, 256 : 256 + C].astype(F32)
        node_out[...] = node_in[...]
        grad_nodes[...] = grad_in[...]
        for r in range(6):
            width = D if r < 4 else C
            gains[r][...] = small[r : r + 1, :width]


def unpack_call(C, late, packed, small, node_out, grad_nodes, edges, arrays):
    steps = 2
    D = packed.shape[1]
    first = 2 * D + C
    shape = jax.ShapeDtypeStruct
    cut = lambda r, c: pl.BlockSpec((r // steps, c), lambda g: (g, 0))
    head = [(first, D), (D, D), (D, D), edges.shape]
    last = [(C, first), (C, C), (C, C)]
    plain = [v.shape for v in arrays]
    gains = [(1, D)] * 4 + [(1, C)] * 2
    return pl.pallas_call(
        functools.partial(unpack_kernel, C, steps),
        grid=(steps,),
        in_specs=[full(v) for v in (late, packed, small, node_out, grad_nodes)] + [cut(*v.shape) for v in (edges, *arrays)],
        out_specs=[cut(*v) for v in head]
        + [fixed(*v) for v in last]
        + [fixed(*node_out.shape)] * 2
        + [cut(*v) for v in plain]
        + [fixed(*v) for v in gains],
        out_shape=[shape(v, F32) for v in head + last]
        + [shape(node_out.shape, BF), shape(node_out.shape, F32)]
        + [shape(v, F32) for v in plain + gains],
        compiler_params=LOCAL,
    )(late, packed, small, node_out, grad_nodes, edges, *arrays)


def body(
    nodes, edges, nbr_owner, nbr_slot, edge_mask, w_msg1, w_msg2, w_msg3, gain_one, offset_one,
    w_ffn1, w_ffn2, gain_two, offset_two, w_edge1, w_edge2, w_edge3, gain_three, offset_three,
    node_cotangent, edge_cotangent,
):
    n = lax.axis_size("edge")
    rows, D = nodes.shape
    C = w_edge2.shape[0]
    we1 = w_edge1.T
    g1, o1, g2, o2 = (v.reshape(1, D) for v in (gain_one, offset_one, gain_two, offset_two))
    (
        act1, slope1, slope2, tcol, trow, node_out, near, low, n1, n2, inv, slope, own_sum,
        nodes_all, far_all,
    ) = forward_call(
        n, C, nodes, nbr_owner.transpose(1, 2, 0), nbr_slot.T, edge_mask.T, g1, o1, g2, o2,
        [w_msg1, w_msg2, w_msg3, w_ffn1, w_ffn2, we1], edges,
    )
    edge_out, partial, far_sum, near_sum, dwe1, dwe2, dwe3, dg3 = edge_call(
        C, tcol, trow, far_all, near, we1, w_edge2, w_edge3,
        gain_three.reshape(1, C), offset_three.reshape(1, C), edges, edge_cotangent,
    )
    kept = [act1, slope1, slope2, edges, partial]
    if n * rows <= TABLE:
        grad_edges, grad_nodes, small, *dwf, early, late = back_call(
            n, C, [tcol, trow, nodes, near_sum, g1, g2, dwe1, dwe2, dwe3, dg3],
            [
                far_sum, low, node_cotangent, we1, n2, inv, w_ffn2, slope, w_ffn1, n1, w_msg3, w_msg1,
                w_msg2, own_sum, node_out, nodes_all,
            ],
            *kept,
        )
    else:
        grad_one, vw_all, resid, dgain, dw3, dwe_near, dwe_far = node_back_call(
            n, C, far_sum, near_sum, node_cotangent, node_out, n1, n2, inv, slope, own_sum,
            w_msg3, g1, w_ffn1, w_ffn2, g2, we1,
        )
        sums = [dw3, dwe_near, dwe_far, dwe1, dwe2, dwe3, dgain, dg3]
        grad_edges, dw1, dw2, target_sum, source_sum = message_back_call(
            C, tcol, trow, nodes_all, nodes, vw_all, w_msg1, w_msg2, *kept
        )
        grad_nodes, early, late, small = final_call(
            n, C, [target_sum, source_sum, grad_one, w_msg1, dw1, dw2, *sums]
        )
        low, resid = (lax.all_gather(v, "edge", axis=0, tiled=True) for v in (low, resid))
        tot_dwf = feed_call(low, resid, w_ffn1, w_ffn2)
        dwf = []
    (
        tot1, tot2, tot3, grad_edges, we1_t, tot_e2, tot_e3, node_out, grad_nodes, *rest
    ) = unpack_call(C, late, early, small, node_out, grad_nodes, grad_edges, dwf)
    dwf1, dwf2 = rest[:2] if dwf else tot_dwf
    gains = rest[-6:]
    gains = [v.reshape(v.shape[1]) for v in gains]
    return (
        node_out, edge_out, grad_nodes, grad_edges,
        tot1, tot2, tot3, gains[0], gains[1], dwf1, dwf2, gains[2], gains[3],
        we1_t.T, tot_e2, tot_e3, gains[4], gains[5],
    )


def solution(mesh):
    rows = P(("dp", "edge"), None)
    return jax.shard_map(
        body,
        mesh=mesh,
        in_specs=(rows, rows, P(("dp", "edge"), None, None), rows, rows)
        + (P(),) * 14
        + (rows, rows),
        out_specs=(rows,) * 4
        + (P("dp", None),) * 3
        + (P("dp"),) * 2
        + (P("dp", None),) * 2
        + (P("dp"),) * 2
        + (P("dp", None),) * 3
        + (P("dp"),) * 2,
        check_vma=False,
    )
```

```python
import functools

import jax
import jax.numpy as jnp
from jax import lax
from jax.experimental import pallas as pl
from jax.experimental.pallas import tpu as pltpu
from jax.sharding import PartitionSpec as P

BF = jnp.bfloat16
F32 = jnp.float32
I32 = jnp.int32
MESH = pl.DeviceIdType.MESH
MIB = 1024 * 1024
LANES = 128
GROUP = 4
ORDER = (0, 2, 1, 3)
TABLE = 1024
EPS = 1e-05
ROOT = 0.7978845608028654
CUBE = 0.044715 * ROOT


def dot(a, b):
    return jnp.dot(a, b, preferred_element_type=F32)


def dot_tn(a, b):
    return lax.dot_general(a, b, (((0,), (0,)), ((), ())), preferred_element_type=F32)


def dot_nt(a, b):
    return lax.dot_general(a, b, (((1,), (1,)), ((), ())), preferred_element_type=F32)


def gelu_pair(v):
    v = v.astype(BF)
    c = lambda x: jnp.asarray(x, BF)
    z = v * v
    q = c(0.5) + c(0.5) * jnp.tanh(v * (c(ROOT) + c(CUBE) * z))
    act = v * q
    slope = q + (act - act * q) * (c(2.0 * ROOT) + c(6.0 * CUBE) * z)
    return act, slope


def gelu_full(v):
    z = v * v
    q = 0.5 + 0.5 * jnp.tanh(v * (ROOT + CUBE * z))
    act = v * q
    slope = q + (act - act * q) * (2.0 * ROOT + 6.0 * CUBE * z)
    return act.astype(BF), slope.astype(BF)


def row_mean(v):
    return jnp.mean(v, axis=-1, keepdims=True)


def lane_column(ref, k):
    rows = ref.shape[0]
    return jnp.broadcast_to(pltpu.roll(ref[...], LANES - k, axis=1)[:, 0:1], (rows, LANES))


def pick_rows(target, width):
    lane = lax.broadcasted_iota(I32, target.shape, 1)
    one, nil = jnp.ones((), BF), jnp.zeros((), BF)
    t16, l16 = target.astype(jnp.int16), lane.astype(jnp.int16)
    return jnp.concatenate(
        [jnp.where(t16 == l16 + jnp.int16(LANES * c), one, nil) for c in range(width // LANES)], axis=1)


def pick_cols(target, width):
    edges = target.shape[1]
    sub = lax.broadcasted_iota(I32, (width, edges), 0)
    return jnp.where(jnp.broadcast_to(target, (width, edges)).astype(jnp.int16) == sub.astype(jnp.int16), jnp.ones((), BF), jnp.zeros((), BF))


def gather_table(targets, table):
    count = table.shape[0]
    if count <= TABLE:
        hot = jnp.concatenate([pick_rows(t, count) for t in targets], axis=0)
        return dot(hot, table[...])

    def step(c, total):
        base = c * TABLE
        hot = jnp.concatenate([pick_rows(t - base, TABLE) for t in targets], axis=0)
        return total + dot(hot, table[pl.ds(pl.multiple_of(base, TABLE), TABLE), :])

    rows = sum(t.shape[0] for t in targets)
    return lax.fori_loop(0, count // TABLE, step, jnp.zeros((rows, table.shape[1]), F32))


def add_by_target(target, values, total):
    count = total.shape[0]
    if count <= TABLE:
        total[...] += dot(pick_cols(target, count), values)
        return

    def step(c, carry):
        base = c * TABLE
        part = pl.ds(pl.multiple_of(base, TABLE), TABLE)
        total[part, :] += dot(pick_cols(target - base, TABLE), values)
        return carry

    lax.fori_loop(0, count // TABLE, step, 0)


def by_chunks(count, step):
    if count <= TABLE:
        step(pl.ds(0, count))
        return

    def one(c, carry):
        step(pl.ds(pl.multiple_of(c * TABLE, TABLE), TABLE))
        return carry

    lax.fori_loop(0, count // TABLE, one, 0)


def remote(src, dst, send, recv, peer):
    return pltpu.make_async_remote_copy(
        src_ref=src,
        dst_ref=dst,
        send_sem=send,
        recv_sem=recv,
        device_id={"edge": peer},
        device_id_type=MESH,
    )


def greet(peers):
    barrier = pltpu.get_barrier_semaphore()
    for peer in peers:
        pl.semaphore_signal(barrier, inc=1, device_id={"edge": peer}, device_id_type=MESH)
    pl.semaphore_wait(barrier, len(peers))


def block(ref, index, rows):
    return ref.at[pl.ds(pl.multiple_of(index * rows, rows), rows)]


class Place:
    def __init__(self, n):
        self.me = lax.axis_index("edge")
        self.chips = n // 2
        self.chip = self.me // 2
        self.core = lax.rem(self.me, 2)
        self.sibling = self.chip * 2 + 1 - self.core
        self.mates = [self.at(d) for d in range(1, self.chips)]

    def at(self, d):
        return lax.rem(self.chip + d + self.chips, self.chips) * 2 + self.core


class Gather:
    def __init__(self, place, x, out, send, recv):
        rows, chips = x.shape[0], place.chips
        mine = block(out, place.me, rows)
        self.near = remote(x, mine, send.at[0], recv.at[0], place.sibling)
        self.far, self.passed = [], []
        for d in range(1, chips):
            self.far.append(remote(x, mine, send.at[d], recv.at[d], place.mates[d - 1]))
            got = block(out, place.at(-d), rows)
            at = chips + d
            self.passed.append(remote(got, got, send.at[at], recv.at[at], place.sibling))

    def start(self):
        for copy in self.far:
            copy.start()
        self.near.start()

    def finish(self):
        for far, passed in zip(self.far, self.passed):
            far.wait_recv()
            passed.start()
        self.near.wait()
        for copy in self.passed:
            copy.wait()
        for copy in self.far:
            copy.wait_send()


class Scatter:
    def __init__(self, place, x, pair_buf, far_buf, send, recv):
        self.place, self.x = place, x
        self.pair_buf, self.far_buf = pair_buf, far_buf
        chips, self.rows = place.chips, pair_buf.shape[1]
        self.pairs, self.far = [], []
        for d in range(chips):
            theirs = lax.rem(place.chip + d, chips) * 2 + 1 - place.core
            src = block(x, theirs, self.rows)
            self.pairs.append(remote(src, pair_buf.at[d], send.at[d], recv.at[d], place.sibling))
        for d in range(1, chips):
            at = chips + d
            self.far.append(
                remote(pair_buf.at[d], far_buf.at[d], send.at[at], recv.at[at], place.at(d))
            )

    def start(self):
        for copy in self.pairs[1:]:
            copy.start()
        self.pairs[0].start()

    def pass_on(self):
        for d in range(1, self.place.chips):
            self.pairs[d].wait_recv()
            at = pl.ds(pl.multiple_of(self.place.at(d) * self.rows, self.rows), self.rows)
            mine = self.x[at, :].astype(F32) + self.pair_buf[d].astype(F32)
            self.pair_buf[d] = mine.astype(BF)
            self.far[d - 1].start()

    def finish(self):
        self.pairs[0].wait_recv()
        at = pl.ds(pl.multiple_of(self.place.me * self.rows, self.rows), self.rows)
        total = self.x[at, :].astype(F32) + self.pair_buf[0].astype(F32)
        for d in range(1, self.place.chips):
            self.far[d - 1].wait_recv()
            total = total + self.far_buf[d].astype(F32)
        for copy in self.pairs + self.far:
            copy.wait_send()
        return total


def scatter_sum(*refs):
    scatter = Scatter(*refs)
    scatter.start()
    scatter.pass_on()
    return scatter.finish()


def comm_scratch(n, rows, width):
    return [pltpu.VMEM((n // 2, rows, width), BF)] * 2


def sems(count):
    return [pltpu.SemaphoreType.DMA((count,))] * 2


def remote_params(cid):
    return pltpu.CompilerParams(
        collective_id=cid, has_side_effects=True, vmem_limit_bytes=62 * MIB
    )


LOCAL = pltpu.CompilerParams(vmem_limit_bytes=62 * MIB)
WHOLE = pl.BlockSpec(memory_space=pltpu.VMEM)


def slab_pairs(slab, C):
    pairs = slab.shape[1] // (2 * C)
    even = [slab[:, 2 * C * m : 2 * C * m + 256] for m in range(pairs)]
    odd = [slab[:, 2 * C * m + 2 * C - 256 : 2 * C * m + 2 * C] for m in range(pairs)]
    return jnp.concatenate(even, axis=0), jnp.concatenate(odd, axis=0)


def interleave(even, odd, rows):
    parts = []
    for m in range(even.shape[0] // rows):
        parts += [even[m * rows : (m + 1) * rows], odd[m * rows : (m + 1) * rows]]
    return jnp.concatenate(parts, axis=0)


def split_tiles(values, rows):
    count = values.shape[0] // rows
    pick = lambda first: jnp.concatenate(
        [values[k * rows : (k + 1) * rows] for k in range(first, count, 2)], axis=0
    )
    return pick(0), pick(1)


def join_slab(even, odd, rows, C):
    parts = []
    for m in range(even.shape[0] // rows):
        a = even[m * rows : (m + 1) * rows]
        b = odd[m * rows : (m + 1) * rows]
        parts += [a[:, :LANES], a[:, LANES:] + b[:, :LANES], b[:, LANES:]]
    return jnp.concatenate(parts, axis=1)


class Loads:
    def __init__(self, pairs, sem):
        self.copies = [
            pltpu.make_async_copy(src, dst, sem.at[j]) for j, (src, dst) in enumerate(pairs)
        ]

    def start(self):
        for copy in self.copies:
            copy.start()

    def wait(self, first=0, last=None):
        for copy in self.copies[first:last]:
            copy.wait()


def column_of(row):
    return jnp.transpose(jnp.broadcast_to(row, (LANES, row.shape[1])))


def spread(column, width):
    return jnp.concatenate([column] * (width // LANES), axis=1)


def norm_parts(values):
    centred = values - row_mean(values)
    inverse = lax.rsqrt(row_mean(centred * centred) + EPS)
    return centred * inverse, inverse


def forward_kernel(
    n, K, C, nodes, owner, slot, live, g1, o1, g2, o2, w1_h, w2_h, w3_h, wf1_h, wf2_h, we1_h, edges,
    act1, slope1, slope2, tcol, trow, node_out, near, low_out, n1_out, n2_out, inv_out,
    slope_out, sum_out, nodes_h, far_h,
    w1, w2, w3, wf1, wf2, we1, load_sem,
    nodes_all, far_all, lcol, orow, lrow, scol, hist, hist_got, count,
    p_all, p_own, w_own, pre2, total, summed, q_own, pair_buf, far_buf,
    send, recv, hsend, hrecv, rsend, rrecv, qsend, qrecv, own_sem,
):
    i = pl.program_id(0)
    rows, D = nodes.shape
    tiles = K // GROUP
    size = GROUP * rows
    if n * rows > TABLE:
        p_all = summed = nodes_all
    place = Place(n)
    others = [lax.rem(place.me + d, n) for d in range(1, n)]
    loads = Loads(
        [(w1_h, w1), (w2_h, w2), (w3_h, w3), (wf1_h, wf1), (wf2_h, wf2), (we1_h, we1)], load_sem
    )
    keep_nodes = pltpu.make_async_copy(nodes_all, nodes_h, own_sem.at[1])

    @pl.when(i == 0)
    def _():
        loads.start()
        spare = jnp.zeros((LANES - K, rows), I32)
        for k in range(K):
            orow[k : k + 1, :] = owner[k]
        orow[K:, :] = spare
        own_wide = orow[...]
        slot_wide = jnp.concatenate([slot[...], spare], axis=0)
        live_wide = jnp.concatenate([live[...], spare], axis=0).astype(F32)
        target = own_wide * rows + slot_wide
        trow[...] = target
        lrow[...] = live_wide
        tcol[...] = jnp.transpose(target)
        lcol[...] = jnp.transpose(live_wide)
        scol[...] = jnp.transpose(slot_wide)
        pre2[...] = jnp.zeros_like(pre2)
        total[...] = jnp.zeros_like(total)
        w_own[...] = jnp.zeros_like(w_own)
        greet(others)
        gather = Gather(place, nodes, nodes_all, send, recv)
        gather.start()
        own = pltpu.make_async_copy(nodes, block(nodes_all, place.me, rows), own_sem.at[0])
        own.start()

        def tally(g, total):
            ks = [g * GROUP + j for j in range(GROUP)]
            hot = jnp.concatenate([pick_rows(lane_column(scol, k), LANES) for k in ks], axis=0)
            owners = jnp.concatenate([orow[pl.ds(k, 1), :] for k in ks], axis=1)
            lives = jnp.concatenate([lrow[pl.ds(k, 1), :] for k in ks], axis=1)
            sub = lax.broadcasted_iota(I32, (n, size), 0)
            who = jnp.where(
                jnp.broadcast_to(owners, sub.shape) == sub, jnp.broadcast_to(lives, sub.shape), 0.0
            )
            return total + dot(who.astype(BF), hot)

        totals = lax.fori_loop(0, tiles, tally, jnp.zeros((n, LANES), F32))
        for e in range(n):
            hist[e] = jnp.broadcast_to(totals[e : e + 1, :], (8, LANES))
        copies = []
        for d in range(1, n):
            peer = others[d - 1]
            copy = remote(hist.at[peer], hist_got.at[d], hsend.at[d], hrecv.at[d], peer)
            copy.start()
            copies.append(copy)
        loads.wait(0, 2)
        p_own[...] = dot(nodes[...], w1[:D, :])
        w_own[0, :C, :] = w1[2 * D :, :]
        w_own[1, 256 - C :, :] = w1[2 * D :, :]
        tallied = hist[place.me]
        for copy in copies:
            copy.wait_recv()
        for d in range(1, n):
            tallied = tallied + hist_got[d]
        count[...] = tallied
        own.wait()
        gather.finish()
        for copy in copies:
            copy.wait_send()
        keep_nodes.start()
        if n * rows > TABLE:
            keep_nodes.wait()

        def project(part):
            p_all[part, :] = dot(nodes_all[part, :], w1[D : 2 * D, :]).astype(BF)

        by_chunks(n * rows, project)

    last = jnp.clip(i - 1, 0, tiles - 1)
    ks = [last * GROUP + j for j in ORDER]
    act, slope = gelu_pair(pre2[...])
    alive = jnp.concatenate(
        [jnp.concatenate([lane_column(lcol, k)] * (D // LANES), axis=1) for k in ks], axis=0
    ).astype(BF)
    slope2[...] = slope * alive
    act = act * (alive * jnp.where(i >= 1, 1.0, 0.0).astype(BF))
    target = jnp.concatenate([trow[pl.ds(k, 1), :] for k in ks], axis=1)
    add_by_target(target, act, total)

    now = jnp.minimum(i, tiles - 1)
    targets = [lane_column(tcol, now * GROUP + j) for j in ORDER]
    even, odd = slab_pairs(edges[...], C)
    own = jnp.concatenate([dot(even, w_own[0]), dot(odd, w_own[1])], axis=0)
    act, slope = gelu_pair(
        gather_table(targets, p_all) + own + jnp.concatenate([p_own[...]] * GROUP, axis=0)
    )
    act1[...] = act
    slope1[...] = slope
    pre2[...] = dot(act, w2[...])

    @pl.when(i == tiles)
    def _():
        summed[...] = total[...].astype(BF)
        scatter = Scatter(place, summed, pair_buf, far_buf, rsend, rrecv)
        scatter.start()
        scatter.pass_on()
        if n * rows <= TABLE:
            keep_nodes.wait()
        loads.wait(2)
        divisor = 1.0 + column_of(count[0:1, :])
        inv_out[2] = divisor
        mine = scatter.finish().astype(BF)
        sum_out[...] = mine
        resid = nodes[...].astype(F32) + dot(mine, w3[...]) / spread(divisor, D)
        n1, inv1 = norm_parts(resid)
        n1_out[...] = n1
        inv_out[0] = jnp.broadcast_to(inv1, (rows, LANES))
        normed = n1 * g1[...] + o1[...]
        low = normed.astype(BF)
        low_out[...] = low
        act, slope = gelu_full(dot(low, wf1[...]))
        slope_out[...] = slope
        n2, inv2 = norm_parts(normed + dot(act, wf2[...]))
        n2_out[...] = n2
        inv_out[1] = jnp.broadcast_to(inv2, (rows, LANES))
        node_low = (n2 * g2[...] + o2[...]).astype(BF)
        node_out[...] = node_low
        pad = jnp.zeros((rows, 256 - C), F32)
        far = dot_nt(node_low, we1[:, D : 2 * D])
        q_own[...] = jnp.concatenate([far, pad], axis=1).astype(BF)
        gather = Gather(place, q_own, far_all, qsend, qrecv)
        gather.start()
        own = pltpu.make_async_copy(q_own, block(far_all, place.me, rows), own_sem.at[0])
        own.start()
        near[...] = jnp.concatenate([dot_nt(node_low, we1[:, :D]), pad], axis=1)
        own.wait()
        gather.finish()
        keep_far = pltpu.make_async_copy(far_all, far_h, own_sem.at[2])
        keep_far.start()
        keep_far.wait()


def full(x):
    return pl.BlockSpec(
        x.shape, lambda g: (0,) * x.ndim, pipeline_mode=pl.Buffered(buffer_count=1)
    )


def fixed(*s):
    return pl.BlockSpec(s, lambda g: (0,) * len(s), pipeline_mode=pl.Buffered(buffer_count=1))


HBM = pl.BlockSpec(memory_space=pl.ANY)


def forward_call(n, C, nodes, owner, slot, live, g1, o1, g2, o2, weights, edges):
    rows, D = nodes.shape
    K = slot.shape[0]
    FF = weights[3].shape[1]
    tiles = K // GROUP
    size = GROUP * rows
    count = n * rows
    other = count if count <= TABLE else 16
    shape = jax.ShapeDtypeStruct
    lag = lambda d: pl.BlockSpec((size, D), lambda g: (jnp.clip(g - d, 0, tiles - 1), 0))
    small = [nodes, owner, slot, live, g1, o1, g2, o2]
    outs = [
        shape((LANES, rows), I32),
        shape((LANES, rows), I32),
        shape((rows, D), BF),
        shape((rows, 256), F32),
        shape((rows, D), BF),
        shape((rows, D), F32),
        shape((rows, D), F32),
        shape((3, rows, LANES), F32),
        shape((rows, FF), BF),
        shape((rows, D), BF),
    ]
    outs[0] = shape((rows, LANES), I32)
    return pl.pallas_call(
        functools.partial(forward_kernel, n, K, C),
        grid=(tiles + 1,),
        in_specs=[full(v) for v in small]
        + [HBM] * 6
        + [pl.BlockSpec((rows, GROUP * C), lambda g: (0, jnp.minimum(g, tiles - 1)))],
        out_specs=[lag(0), lag(0), lag(1)] + [fixed(*v.shape) for v in outs] + [HBM] * 2,
        out_shape=[shape((K * rows, D), BF)] * 3
        + outs
        + [shape((count, D), BF), shape((count, 256), BF)],
        scratch_shapes=[pltpu.VMEM(v.shape, BF) for v in weights]
        + [
            pltpu.SemaphoreType.DMA((6,)),
            pltpu.VMEM((count, D), BF),
            pltpu.VMEM((count, 256), BF),
            pltpu.VMEM((rows, LANES), F32),
            pltpu.VMEM((LANES, rows), I32),
            pltpu.VMEM((LANES, rows), F32),
            pltpu.VMEM((rows, LANES), I32),
            pltpu.VMEM((n, 8, LANES), F32),
            pltpu.VMEM((n, 8, LANES), F32),
            pltpu.VMEM((8, LANES), F32),
            pltpu.VMEM((other, D), BF),
            pltpu.VMEM((rows, D), F32),
            pltpu.VMEM((2, 256, D), BF),
            pltpu.VMEM((size, D), F32),
            pltpu.VMEM((count, D), F32),
            pltpu.VMEM((other, D), BF),
            pltpu.VMEM((rows, 256), BF),
            *comm_scratch(n, rows, D),
            *sems(n),
            *sems(n),
            *sems(n),
            *sems(n),
            pltpu.SemaphoreType.DMA((3,)),
        ],
        compiler_params=remote_params(0),
    )(*small, *weights, edges)


def edge_kernel(
    tiles, C, tcol, trow, far_all, near, we1, we2, we3, gain, offset, edges1, edges4, edges6, cot,
    edge_out, partial, far_sum, near_sum, dw1, dw2, dw3, dgain,
    w1o, w2p, w3o, w1t, w2t, w3t, gains, total, a1, a2, a3, ag,
    pre1, hid1, slope1, pre2, hid2, slope2, res3, third, up2, up1,
):
    i = pl.program_id(0)
    rows = near.shape[0]
    D2 = we1.shape[1] - C
    gap = 256 - C
    half = GROUP // 2 * rows

    @pl.when(i == 0)
    def _():
        for ref in (w1o, w2p, w3o, w1t, w2t, w3t, gains, total, a1, a2, a3, ag, near_sum,
                    pre1, hid1, slope1, pre2, hid2, slope2, res3, third, up2, up1):
            ref[...] = jnp.zeros_like(ref)
        own = jnp.transpose(we1[:, D2:].astype(F32)).astype(BF)
        w1o[0, :C, :C] = own
        w1o[1, gap:, :C] = own
        w2p[:C, :C] = we2[...]
        w3o[0, :C, :C] = we3[...]
        w3o[1, :C, :] = jnp.concatenate([jnp.zeros((C, gap), F32), we3[...].astype(F32)], axis=1).astype(BF)
        for s in range(2):
            w1t[s] = jnp.transpose(w1o[s].astype(F32)).astype(BF)
            w3t[s] = jnp.transpose(w3o[s].astype(F32)).astype(BF)
        w2t[...] = jnp.transpose(w2p[...].astype(F32)).astype(BF)
        zero = jnp.zeros((1, gap), F32)
        gains[0, 0:1] = jnp.concatenate([gain[...], zero], axis=1)
        gains[0, 1:2] = jnp.concatenate([offset[...], zero], axis=1)
        gains[1, 0:1] = jnp.concatenate([zero, gain[...]], axis=1)
        gains[1, 1:2] = jnp.concatenate([zero, offset[...]], axis=1)

    tile = lambda d: jnp.clip(i - d, 0, tiles - 1)
    sides = [slice(0, half), slice(half, 2 * half)]

    t4 = tile(1)
    valid = jnp.where(i >= 1, 1.0, 0.0)
    slabs = slab_pairs(edges4[...], C)
    cots = slab_pairs(cot[...], C)
    lane = lax.broadcasted_iota(I32, (half, 256), 1)
    outs, grads, ups = [], [], []
    for s in range(2):
        inside = (lane < C) if s == 0 else (lane >= gap)
        keep = lambda v: jnp.where(inside, v, 0.0)
        mean = lambda v: jnp.sum(v, axis=-1, keepdims=True) * (1.0 / C)
        value = keep(slabs[s].astype(F32)) + res3[sides[s], :]
        centred = keep(value - mean(value))
        inverse = lax.rsqrt(mean(centred * centred) + EPS)
        normal = centred * inverse
        outs.append(normal * gains[s, 0:1] + gains[s, 1:2])
        upstream = cots[s].astype(F32) * valid
        moved = upstream * normal
        for r in range(half // rows):
            part = slice(r * rows, (r + 1) * rows)
            ag[s, 0] += moved[part]
            ag[s, 1] += upstream[part]
        scaled = upstream * gains[s, 0:1]
        grad = inverse * (scaled - mean(scaled) - normal * mean(scaled * normal))
        grad = keep(grad)
        grads.append(grad)
        low3 = grad.astype(BF)
        a3[s] += dot_tn(hid2[sides[s], :], low3)
        ups.append(dot(low3, w3t[s]))
    edge_out[...] = join_slab(outs[0], outs[1], rows, C).astype(BF)

    t5 = tile(1)
    low2 = (jnp.concatenate(ups, axis=0) * slope2[0].astype(F32)).astype(BF)
    a2[...] += dot_tn(hid1[0], low2)
    up1v = dot(low2, w2t[...])

    t6 = tile(1)
    low1 = (up1v * slope1[0].astype(F32)).astype(BF)
    slabs = slab_pairs(edges4[...], C)
    outs = []
    for s in range(2):
        a1[s] += dot_tn(low1[sides[s]], slabs[s])
        outs.append(grads[s] + dot(low1[sides[s]], w1t[s]))
    partial[...] = join_slab(outs[0], outs[1], rows, C).astype(BF)
    wide = low1.astype(F32)
    acc = wide[:rows]
    for j in range(1, GROUP):
        acc = acc + wide[j * rows : (j + 1) * rows]
    near_sum[...] += acc
    target = jnp.concatenate([trow[pl.ds(t6 * GROUP + j, 1), :] for j in ORDER], axis=1)
    add_by_target(target, low1, total)

    t1 = tile(0)
    slabs = slab_pairs(edges1[...], C)
    own = jnp.concatenate([dot(slabs[0], w1o[0]), dot(slabs[1], w1o[1])], axis=0)
    got = gather_table([lane_column(tcol, t1 * GROUP + j) for j in ORDER], far_all)
    pre1v = got + own + jnp.concatenate([near[...]] * GROUP, axis=0)

    t2 = tile(0)
    act, slope = gelu_pair(pre1v)
    hid1[0] = act
    slope1[0] = slope
    pre2v = dot(act, w2p[...])

    t3 = tile(0)
    act, slope = gelu_pair(pre2v)
    hid2[...] = act
    slope2[0] = slope
    for s in range(2):
        res3[sides[s], :] = dot(act[sides[s]], w3o[s])

    @pl.when(i == tiles)
    def _():
        far_sum[...] = total[...].astype(BF)
        dw1[...] = jnp.transpose(a1[0])[:C, :] + jnp.transpose(a1[1])[gap:, :]
        dw2[...] = a2[...]
        shifted = a3[1][:, gap:]
        dw3[...] = a3[0] + jnp.concatenate([shifted, jnp.zeros((256, gap), F32)], axis=1)
        for r in range(2):
            even = jnp.sum(ag[0, r], axis=0, keepdims=True)
            odd = jnp.sum(ag[1, r], axis=0, keepdims=True)
            row = even + jnp.concatenate([odd[:, gap:], jnp.zeros((1, gap), F32)], axis=1)
            dgain[r * 8 : r * 8 + 8, :] = jnp.broadcast_to(row, (8, 256))


def edge_call(C, tcol, trow, far_all, near, we1, we2, we3, gain, offset, edges, cot):
    rows = near.shape[0]
    count = far_all.shape[0]
    K = edges.shape[1] // C
    tiles = K // GROUP
    size = GROUP * rows
    shape = jax.ShapeDtypeStruct
    slab = lambda d: pl.BlockSpec(
        (rows, GROUP * C), lambda g: (0, jnp.clip(g - d, 0, tiles - 1))
    )
    fixed = lambda *s: pl.BlockSpec(
        s, lambda g: (0,) * len(s), pipeline_mode=pl.Buffered(buffer_count=1)
    )
    return pl.pallas_call(
        functools.partial(edge_kernel, tiles, C),
        grid=(tiles + 1,),
        in_specs=[full(x) for x in (tcol, trow, far_all, near, we1, we2, we3, gain, offset)]
        + [slab(0), slab(1), slab(99), slab(1)],
        out_specs=[
            slab(1), slab(1), fixed(count, 256), fixed(rows, 256),
            fixed(C, 256), fixed(256, 256), fixed(256, 256), fixed(16, 256),
        ],
        out_shape=[
            shape((rows, K * C), BF),
            shape((rows, K * C), BF),
            shape((count, 256), BF),
            shape((rows, 256), F32),
            shape((C, 256), F32),
            shape((256, 256), F32),
            shape((256, 256), F32),
            shape((16, 256), F32),
        ],
        scratch_shapes=[
            pltpu.VMEM((2, 256, 256), BF),
            pltpu.VMEM((256, 256), BF),
            pltpu.VMEM((2, 256, 256), BF),
            pltpu.VMEM((2, 256, 256), BF),
            pltpu.VMEM((256, 256), BF),
            pltpu.VMEM((2, 256, 256), BF),
            pltpu.VMEM((2, 8, 256), F32),
            pltpu.VMEM((count, 256), F32),
            pltpu.VMEM((2, 256, 256), F32),
            pltpu.VMEM((256, 256), F32),
            pltpu.VMEM((2, 256, 256), F32),
            pltpu.VMEM((2, 2, rows, 256), F32),
            pltpu.VMEM((size, 256), F32),
            pltpu.VMEM((3, size, 256), BF),
            pltpu.VMEM((4, size, 256), BF),
            pltpu.VMEM((size, 256), F32),
            pltpu.VMEM((size, 256), BF),
            pltpu.VMEM((2, size, 256), BF),
            pltpu.VMEM((size, 256), F32),
            pltpu.VMEM((2, size, 256), F32),
            pltpu.VMEM((size, 256), F32),
            pltpu.VMEM((size, 256), F32),
        ],
        compiler_params=LOCAL,
    )(tcol, trow, far_all, near, we1, we2, we3, gain, offset, edges, edges, edges, cot)


def norm_back(upstream, normal, inverse, gain):
    scaled = upstream * gain
    return inverse * (scaled - row_mean(scaled) - normal * row_mean(scaled * normal))


def node_back(
    C, far, near_sum, cot, n1, n2, inv, slope, w3, g1, wf1, wf2, g2, we1, grad_one, resid_out, dgain, v_own
):
    rows, D = cot.shape
    far = far.astype(BF)[:, :C]
    near = near_sum[...].astype(BF)[:, :C]
    grad = cot[...].astype(F32) + dot(near, we1[:, :D]) + dot(far, we1[:, D : 2 * D])
    two = norm_back(grad, n2[...], inv[1][:, 0:1], g2[...])
    dgain[16:24, :] = jnp.broadcast_to(jnp.sum(grad * n2[...], axis=0, keepdims=True), (8, D))
    dgain[24:32, :] = jnp.broadcast_to(jnp.sum(grad, axis=0, keepdims=True), (8, D))
    resid = two.astype(BF)
    resid_out[...] = resid
    inner = (dot_nt(resid, wf2[...]) * slope[...].astype(F32)).astype(BF)
    grad = two + dot_nt(inner, wf1[...])
    one = norm_back(grad, n1[...], inv[0][:, 0:1], g1[...])
    dgain[0:8, :] = jnp.broadcast_to(jnp.sum(grad * n1[...], axis=0, keepdims=True), (8, D))
    dgain[8:16, :] = jnp.broadcast_to(jnp.sum(grad, axis=0, keepdims=True), (8, D))
    grad_one[...] = one
    upper = (one / spread(inv[2], D)).astype(BF)
    v_own[...] = dot_nt(upper, w3[...]).astype(BF)
    return far, near, upper


def node_back_kernel(
    n, C, far_sum, near_sum, cot, node_low, n1, n2, inv, slope, summed,
    w3, g1, wf1, wf2, g2, we1,
    grad_one, vw_all, resid_out, dgain, dw3, dwe_near, dwe_far,
    pair_buf, far_buf, v_own, send, recv, gsend, grecv, own_sem,
):
    place = Place(n)
    rows = cot.shape[0]
    greet([place.sibling] + place.mates)
    far = scatter_sum(place, far_sum, pair_buf, far_buf, send, recv)
    far, near, upper = node_back(
        C, far, near_sum, cot, n1, n2, inv, slope, w3, g1, wf1, wf2, g2, we1,
        grad_one, resid_out, dgain, v_own,
    )
    gather = Gather(place, v_own, vw_all, gsend, grecv)
    gather.start()
    own = pltpu.make_async_copy(v_own, block(vw_all, place.me, rows), own_sem.at[0])
    own.start()
    dw3[...] = dot_tn(summed[...], upper)
    dwe_near[...] = dot_tn(node_low[...], near)
    dwe_far[...] = dot_tn(node_low[...], far)
    own.wait()
    gather.finish()


def node_back_call(n, C, *args):
    cot = args[2]
    rows, D = cot.shape
    shape = jax.ShapeDtypeStruct
    return pl.pallas_call(
        functools.partial(node_back_kernel, n, C),
        in_specs=[WHOLE] * len(args),
        out_specs=[WHOLE] * 7,
        out_shape=[
            shape((rows, D), F32),
            shape((n * rows, D), BF),
            shape((rows, D), BF),
            shape((32, D), F32),
            shape((D, D), F32),
            shape((D, C), F32),
            shape((D, C), F32),
        ],
        scratch_shapes=[
            *comm_scratch(n, rows, 256),
            pltpu.VMEM((rows, D), BF),
            *sems(n),
            *sems(n),
            pltpu.SemaphoreType.DMA((1,)),
        ],
        compiler_params=remote_params(2),
    )(*args)


class Line:
    def __init__(self, place, pieces, x, out, pair_buf, low_buf, high_buf, send_buf, send, recv):
        self.place, self.pieces, self.x, self.out = place, pieces, x, out
        self.pair_buf, self.low_buf, self.high_buf = pair_buf, low_buf, high_buf
        self.send_buf, self.send, self.recv = send_buf, send, recv
        c, q, chips = place.chip, place.core, place.chips
        self.root = chips // 2 - 1 + q
        self.away = jnp.abs(c - self.root)
        self.right = jnp.minimum(c + 1, chips - 1) * 2 + q
        self.left = jnp.maximum(c - 1, 0) * 2 + q
        self.half = x.shape[0] // 2
        self.rows = self.half // pieces

    def part(self, which, p):
        return pl.ds(pl.multiple_of(which * self.half + p * self.rows, self.rows), self.rows)

    def here(self, p):
        return pl.ds(pl.multiple_of(p * self.rows, self.rows), self.rows)

    def link(self, src, dst, p, sent, got, peer):
        n = self.pieces
        return remote(src, dst, self.send.at[sent * n + p], self.recv.at[got * n + p], peer)

    def pair(self, p):
        src = self.x.at[self.part(1 - self.place.core, p)]
        return self.link(src, self.pair_buf.at[self.here(p)], p, 0, 0, self.place.sibling)

    def up(self, p):
        here = self.here(p)
        return self.link(self.send_buf.at[here], self.low_buf.at[here], p, 1, 1, self.right)

    def down(self, p):
        here = self.here(p)
        return self.link(self.send_buf.at[here], self.high_buf.at[here], p, 2, 2, self.left)

    def outward(self, p, sent, got, peer):
        mine = self.out.at[self.part(self.place.core, p)]
        return self.link(mine, mine, p, sent, got, peer)

    def out_left(self, p):
        return self.outward(p, 3, 3, self.left)

    def out_right(self, p):
        return self.outward(p, 5, 3, self.right)

    def across(self, p):
        return self.outward(p, 4, 4, self.place.sibling)

    def each(self, step):
        lax.fori_loop(0, self.pieces, lambda p, z: (step(p), z)[1], 0)

    def start(self):
        self.each(lambda p: self.pair(p).start())

    def reduce(self, p):
        c, root, last = self.place.chip, self.root, self.place.chips - 1
        here, mine_at = self.here(p), self.part(self.place.core, p)
        self.pair(p).wait_recv()
        mine = lambda: self.x[mine_at, :].astype(F32) + self.pair_buf[here, :].astype(F32)

        def end():
            self.send_buf[here, :] = mine().astype(BF)

        def from_low():
            self.up(p).wait_recv()
            self.send_buf[here, :] = (mine() + self.low_buf[here, :].astype(F32)).astype(BF)

        def from_high():
            self.down(p).wait_recv()
            self.send_buf[here, :] = (mine() + self.high_buf[here, :].astype(F32)).astype(BF)

        def at_root():
            self.up(p).wait_recv()
            self.down(p).wait_recv()
            total = mine() + self.low_buf[here, :].astype(F32) + self.high_buf[here, :].astype(F32)
            self.out[mine_at, :] = total.astype(BF)
            self.out_left(p).start()
            self.out_right(p).start()
            self.across(p).start()

        pl.when((c == 0) | (c == last))(end)
        pl.when((c > 0) & (c < root))(from_low)
        pl.when((c > root) & (c < last))(from_high)
        pl.when(c < root)(lambda: self.up(p).start())
        pl.when(c > root)(lambda: self.down(p).start())
        pl.when(c == root)(at_root)

    def spread(self, p):
        c, root, last = self.place.chip, self.root, self.place.chips - 1

        def leftward():
            self.out_left(p).wait_recv()
            pl.when(c > 0)(lambda: self.out_left(p).start())
            self.across(p).start()

        def rightward():
            self.out_right(p).wait_recv()
            pl.when(c < last)(lambda: self.out_right(p).start())
            self.across(p).start()

        pl.when(c < root)(leftward)
        pl.when(c > root)(rightward)

    def slots(self, lag):
        return self.pieces + 2 * lag * (self.place.chips // 2)

    def slot(self, s, lag):
        deep = self.place.chips // 2
        p = s - lag * (deep - self.away)
        pl.when((p >= 0) & (p < self.pieces))(lambda: self.reduce(p))
        o = s - lag * (deep + self.away)
        pl.when((o >= 0) & (o < self.pieces) & (self.away > 0))(lambda: self.spread(o))

    def finish(self):
        c, root, last = self.place.chip, self.root, self.place.chips - 1

        def end(p):
            self.pair(p).wait_send()
            self.across(p).wait_send()
            pl.when(c < root)(lambda: self.up(p).wait_send())
            pl.when(c > root)(lambda: self.down(p).wait_send())
            pl.when((c <= root) & (c > 0))(lambda: self.out_left(p).wait_send())
            pl.when((c >= root) & (c < last))(lambda: self.out_right(p).wait_send())

        self.each(lambda p: self.across(p).wait_recv())
        self.each(end)


def line_scratch(rows, width, pieces):
    return [pltpu.VMEM((rows // 2, width), BF)] * 4 + sems(6 * pieces)


class Exchange:
    def __init__(self, place, n, mine, got, send, recv):
        self.place, self.n, self.mine, self.got = place, n, mine, got
        self.copies = []
        for d in range(1, n):
            peer = lax.rem(place.me + d, n)
            self.copies.append(remote(mine, got.at[place.me], send.at[d], recv.at[d], peer))

    def start(self):
        for copy in self.copies:
            copy.start()
        self.got[self.place.me] = self.mine[...]

    def finish(self):
        for copy in self.copies:
            copy.wait_recv()
        total = self.got[0]
        for e in range(1, self.n):
            total = total + self.got[e]
        for copy in self.copies:
            copy.wait_send()
        return total


EARLY, LATE, LAG, AHEAD = 7, 9, 2, 7


def early_rows(D, C):
    used = D + (2 * D + C) // 2 + C
    unit = 2 * EARLY * 16
    return -(-used // unit) * unit


def pack_early(C, x, gains, dw3, dwe_near, dwe_far, dwe1, dwe2, dwe3, dgain, dg3):
    D = dw3.shape[0]
    x[:D, :] = dw3[...].astype(BF)
    spare = jnp.zeros((D, 256 - C), F32)
    edge1 = jnp.concatenate(
        [
            jnp.concatenate([dwe_near[...], spare], axis=1),
            jnp.concatenate([dwe_far[...], spare], axis=1),
            dwe1[...],
        ],
        axis=0,
    ).astype(BF)
    half = edge1.shape[0] // 2
    x[D : D + half, :256] = edge1[:half]
    x[D : D + half, 256:] = edge1[half:]
    at = D + half
    x[at : at + C, :256] = dwe2[:C, :].astype(BF)
    x[at : at + C, 256:] = dwe3[:C, :].astype(BF)
    if at + C < x.shape[0]:
        x[at + C :, :] = jnp.zeros((x.shape[0] - at - C, D), BF)
    gains[...] = jnp.zeros_like(gains)
    for r in range(4):
        gains[r : r + 1, :] = dgain[8 * r : 8 * r + 1, :]
    for r in range(2):
        gains[4 + r : 5 + r, :256] = dg3[8 * r : 8 * r + 1, :]


def back_start(C, w1, w2, w2t, w_own, w_own_t, zeroed):
    D = w2.shape[0]
    gap = 256 - C
    for ref in (w_own, *zeroed):
        ref[...] = jnp.zeros_like(ref)
    w_own[0, :C, :] = w1[2 * D :, :]
    w_own[1, gap:, :] = w1[2 * D :, :]
    for s in range(2):
        w_own_t[s] = jnp.transpose(w_own[s].astype(F32)).astype(BF)
    w2t[...] = jnp.transpose(w2[...].astype(F32)).astype(BF)


def back_tile(
    g, rows, C, tcol, trow, vw, act1, slope1, slope2, edges, partial, grad_edges,
    w2t, w_own_t, total, a2, ae, source_sum,
):
    half = GROUP // 2 * rows
    ks = [g * GROUP + j for j in ORDER]
    up = gather_table([lane_column(tcol, k) for k in ks], vw)
    upper = up.astype(BF) * slope2[...]
    a2[...] += dot_tn(act1[...], upper)
    lower = dot(upper, w2t[...]).astype(BF) * slope1[...]
    wide = lower.astype(F32)
    acc = wide[:rows]
    for j in range(1, GROUP):
        acc = acc + wide[j * rows : (j + 1) * rows]
    source_sum[...] += acc
    target = jnp.concatenate([trow[pl.ds(k, 1), :] for k in ks], axis=1)
    add_by_target(target, lower, total)
    slabs = slab_pairs(edges[...], C)
    lowers = [lower[:half], lower[half:]]
    own = []
    for s in range(2):
        ae[s] += dot_tn(slabs[s], lowers[s])
        own.append(dot(lowers[s], w_own_t[s]))
    grad_edges[...] = (partial[...].astype(F32) + join_slab(own[0], own[1], rows, C)).astype(BF)


def back_weights(C, dw1, dw2, nodes_all, nodes, total, a2, ae, source_sum):
    D = nodes.shape[1]
    gap = 256 - C
    dw2[...] = a2[...].astype(BF)
    dw1[:D, :] = dot_tn(nodes[...], source_sum[...].astype(BF)).astype(BF)
    dw1[2 * D :, :] = (ae[0][:C, :] + ae[1][gap:, :]).astype(BF)
    a2[...] = jnp.zeros_like(a2)

    def weigh(part):
        a2[...] += dot_tn(nodes_all[part, :], total[part, :].astype(BF))

    by_chunks(total.shape[0], weigh)
    dw1[D : 2 * D, :] = a2[...].astype(BF)


def tail(early, late, scatter, source_sum, grad_one, w1, grad_nodes, feed, ready=None):
    D = grad_one.shape[1]
    late.start()
    scatter.start()
    if ready:
        ready()

    def feed_part(f):
        low, resid, wf1, wf2, dwf1, dwf2 = feed
        step = 256
        cols = pl.ds(pl.multiple_of(f * step, step), step)
        act, slope = gelu_full(dot(low[...], wf1[:, cols]))
        dwf2[cols, :] = dot_tn(act, resid[...]).astype(BF)
        inner = (dot_nt(resid[...], wf2[cols, :]) * slope.astype(F32)).astype(BF)
        dwf1[:, cols] = dot_tn(low[...], inner).astype(BF)

    parts = feed[2].shape[1] // 256 if feed else 0

    def slot(s, carry):
        early.slot(s, LAG)
        late.slot(s - EARLY, LAG)
        if feed:
            f = s - AHEAD
            pl.when((f % 2 == 1) & (f // 2 < parts))(lambda: feed_part(f // 2))
        return carry

    lax.fori_loop(AHEAD, AHEAD + 14, slot, 0)
    scatter.pass_on()
    lax.fori_loop(AHEAD + 14, EARLY + late.slots(LAG), slot, 0)
    source = dot_nt(source_sum[...].astype(BF), w1[:D, :])
    total = scatter.finish()
    grad_nodes[...] = grad_one[...] + source + dot_nt(total.astype(BF), w1[D : 2 * D, :])
    early.finish()
    late.finish()


def back_kernel(n, tiles, C, tcol, trow, nodes, near_sum, g1, g2, dwe1, dwe2, dwe3, dg3, *refs):
    sources, refs = refs[:16], refs[16:]
    act1, slope1, slope2, edges, partial, *refs = refs
    grad_edges, grad_nodes, small, dwf1, dwf2, early_h, late_h, *refs = refs
    held, refs = refs[:16], refs[16:]
    (
        far_sum, low_own, cot, we1, n2, inv, wf2, slope, wf1, n1, w3, w1, w2, summed, node_low, nodes_all
    ) = held
    (
        load_sem, low, lsend, lrecv, vw, v_own, grad_one, resid_own, dgain, dw3, dwe_near, dwe_far,
        resid, bsend, brecv, vsend, vrecv, hsend, hrecv, pair_h, far_h,
        w2t, w_own, w_own_t, total, a2, ae, source_sum, target_sum, gains, got, gsend, grecv,
        pair_buf, far_buf, send, recv, x1, out1, x2, out2, *line_refs,
    ) = refs
    g = pl.program_id(0)
    rows, D = nodes.shape
    place = Place(n)
    loads = Loads(list(zip(sources, held)), load_sem)
    gather = Gather(place, resid_own, resid, bsend, brecv)
    gather_low = Gather(place, low_own, low, lsend, lrecv)
    early = Line(place, EARLY, x1, out1, *line_refs[: len(line_refs) // 2])
    late = Line(place, LATE, x2, out2, *line_refs[len(line_refs) // 2 :])
    exchange = Exchange(place, n, gains, got, gsend, grecv)

    @pl.when(g == 0)
    def _():
        loads.start()
        greet([lax.rem(place.me + d, n) for d in range(1, n)])
        loads.wait(0, 2)
        scatter = Scatter(place, far_sum, pair_h, far_h, hsend, hrecv)
        scatter.start()
        scatter.pass_on()
        mine = pl.ds(pl.multiple_of(place.me * rows, rows), rows)
        low[mine, :] = low_own[...]
        loads.wait(2, 15)
        back_start(C, w1, w2, w2t, w_own, w_own_t, (total, a2, ae, source_sum))
        far, near, upper = node_back(
            C, scatter.finish(), near_sum, cot, n1, n2, inv, slope, w3, g1, wf1, wf2, g2, we1,
            grad_one, resid_own, dgain, v_own,
        )
        spread_v = Gather(place, v_own, vw, vsend, vrecv)
        spread_v.start()
        dw3[...] = dot_tn(summed[...], upper)
        dwe_near[...] = dot_tn(node_low[...], near)
        dwe_far[...] = dot_tn(node_low[...], far)
        pack_early(C, x1, gains, dw3, dwe_near, dwe_far, dwe1, dwe2, dwe3, dgain, dg3)
        vw[mine, :] = v_own[...]
        resid[mine, :] = resid_own[...]
        spread_v.finish()
        exchange.start()
        early.start()

    pl.when(g == 1)(gather_low.start)
    pl.when(g == 4)(gather.start)
    ahead = g - (tiles - AHEAD)
    pl.when(ahead >= 0)(lambda: early.slot(ahead, LAG))
    back_tile(
        g, rows, C, tcol, trow, vw, act1, slope1, slope2, edges, partial, grad_edges,
        w2t, w_own_t, total, a2, ae, source_sum,
    )

    @pl.when(g == tiles - 1)
    def _():
        target_sum[...] = total[...].astype(BF)
        loads.wait(15)
        at = 2 * D + C
        back_weights(
            C, x2.at[pl.ds(0, at)], x2.at[pl.ds(at, D)], nodes_all, nodes, total, a2, ae, source_sum
        )

        def ready():
            gather_low.finish()
            gather.finish()
            small[...] = exchange.finish()

        scatter = Scatter(place, target_sum, pair_buf, far_buf, send, recv)
        tail(
            early, late, scatter, source_sum, grad_one, w1, grad_nodes, (low, resid, wf1, wf2, dwf1, dwf2),
            ready,
        )
        keep_early = pltpu.make_async_copy(out1, early_h, load_sem.at[16])
        keep_early.start()
        keep_late = pltpu.make_async_copy(out2, late_h, load_sem.at[17])
        keep_late.start()
        keep_early.wait()
        keep_late.wait()


def back_call(n, C, whole, loaded, act1, slope1, slope2, edges, partial):
    rows, D = whole[2].shape
    count = n * rows
    K = edges.shape[1] // C
    tiles = K // GROUP
    size = GROUP * rows
    FF = loaded[8].shape[1]
    early, late = early_rows(D, C), 3 * D + C
    shape = jax.ShapeDtypeStruct
    slab = pl.BlockSpec((rows, GROUP * C), lambda g: (0, g))
    tile = pl.BlockSpec((size, D), lambda g: (g, 0))
    outs = [
        shape((rows, D), F32),
        shape((8, D), F32),
        shape((D, FF), BF),
        shape((FF, D), BF),
    ]
    return pl.pallas_call(
        functools.partial(back_kernel, n, tiles, C),
        grid=(tiles,),
        in_specs=[full(v) for v in whole] + [HBM] * len(loaded) + [tile, tile, tile, slab, slab],
        out_specs=[slab] + [fixed(*v.shape) for v in outs] + [HBM] * 2,
        out_shape=[shape((rows, K * C), BF)]
        + outs
        + [shape((early, D), BF), shape((late, D), BF)],
        scratch_shapes=[pltpu.VMEM(v.shape, v.dtype) for v in loaded]
        + [
            pltpu.SemaphoreType.DMA((18,)),
            pltpu.VMEM((count, D), BF),
            *sems(n),
            pltpu.VMEM((count, D), BF),
            pltpu.VMEM((rows, D), BF),
            pltpu.VMEM((rows, D), F32),
            pltpu.VMEM((rows, D), BF),
            pltpu.VMEM((32, D), F32),
            pltpu.VMEM((D, D), F32),
            pltpu.VMEM((D, C), F32),
            pltpu.VMEM((D, C), F32),
            pltpu.VMEM((count, D), BF),
            *sems(n),
            *sems(n),
            *sems(n),
            *comm_scratch(n, rows, 256),
            pltpu.VMEM((D, D), BF),
            pltpu.VMEM((2, 256, D), BF),
            pltpu.VMEM((2, D, 256), BF),
            pltpu.VMEM((count, D), F32),
            pltpu.VMEM((D, D), F32),
            pltpu.VMEM((2, 256, D), F32),
            pltpu.VMEM((rows, D), F32),
            pltpu.VMEM((count, D), BF),
            pltpu.VMEM((8, D), F32),
            pltpu.VMEM((n, 8, D), F32),
            *sems(n),
            *comm_scratch(n, rows, D),
            *sems(n),
            pltpu.VMEM((early, D), BF),
            pltpu.VMEM((early, D), BF),
            pltpu.VMEM((late, D), BF),
            pltpu.VMEM((late, D), BF),
            *line_scratch(early, D, EARLY),
            *line_scratch(late, D, LATE),
        ],
        compiler_params=remote_params(3),
    )(*whole, *loaded, act1, slope1, slope2, edges, partial)


def message_back_kernel(
    tiles, C, tcol, trow, nodes_all, nodes, vw, w1, w2, act1, slope1, slope2, edges, partial,
    grad_edges, dw1, dw2, target_sum, source_sum, w2t, w_own, w_own_t, total, a2, ae,
):
    g = pl.program_id(0)

    @pl.when(g == 0)
    def _():
        back_start(C, w1, w2, w2t, w_own, w_own_t, (total, a2, ae, source_sum))

    back_tile(
        g, nodes.shape[0], C, tcol, trow, vw, act1, slope1, slope2, edges, partial, grad_edges,
        w2t, w_own_t, total, a2, ae, source_sum,
    )

    @pl.when(g == tiles - 1)
    def _():
        target_sum[...] = total[...].astype(BF)
        back_weights(C, dw1, dw2, nodes_all, nodes, total, a2, ae, source_sum)


def message_back_call(C, tcol, trow, nodes_all, nodes, vw, w1, w2, act1, slope1, slope2, edges, partial):
    rows, D = nodes.shape
    count = vw.shape[0]
    K = edges.shape[1] // C
    tiles = K // GROUP
    size = GROUP * rows
    shape = jax.ShapeDtypeStruct
    slab = pl.BlockSpec((rows, GROUP * C), lambda g: (0, g))
    tile = pl.BlockSpec((size, D), lambda g: (g, 0))
    return pl.pallas_call(
        functools.partial(message_back_kernel, tiles, C),
        grid=(tiles,),
        in_specs=[full(x) for x in (tcol, trow, nodes_all, nodes, vw, w1, w2)]
        + [tile, tile, tile, slab, slab],
        out_specs=[slab, fixed(2 * D + C, D), fixed(D, D), fixed(count, D), fixed(rows, D)],
        out_shape=[
            shape((rows, K * C), BF),
            shape((2 * D + C, D), BF),
            shape((D, D), BF),
            shape((count, D), BF),
            shape((rows, D), F32),
        ],
        scratch_shapes=[
            pltpu.VMEM((D, D), BF),
            pltpu.VMEM((2, 256, D), BF),
            pltpu.VMEM((2, D, 256), BF),
            pltpu.VMEM((count, D), F32),
            pltpu.VMEM((D, D), F32),
            pltpu.VMEM((2, 256, D), F32),
        ],
        compiler_params=LOCAL,
    )(tcol, trow, nodes_all, nodes, vw, w1, w2, act1, slope1, slope2, edges, partial)


def final_kernel(
    n, C, target_sum, source_sum, grad_one, w1, dw1, dw2, dw3, dwe_near, dwe_far, dwe1, dwe2, dwe3,
    dgain, dg3, grad_nodes, out1, out2, small,
    x1, x2, gains, got, gsend, grecv, pair_buf, far_buf, send, recv, *line_refs,
):
    place = Place(n)
    D = grad_one.shape[1]
    pack_early(C, x1, gains, dw3, dwe_near, dwe_far, dwe1, dwe2, dwe3, dgain, dg3)
    at = 2 * D + C
    x2[:at, :] = dw1[...]
    x2[at:, :] = dw2[...]
    greet([lax.rem(place.me + d, n) for d in range(1, n)])
    early = Line(place, EARLY, x1, out1, *line_refs[: len(line_refs) // 2])
    late = Line(place, LATE, x2, out2, *line_refs[len(line_refs) // 2 :])
    exchange = Exchange(place, n, gains, got, gsend, grecv)
    exchange.start()
    small[...] = exchange.finish()
    scatter = Scatter(place, target_sum, pair_buf, far_buf, send, recv)
    early.start()
    lax.fori_loop(0, AHEAD, lambda s, z: (early.slot(s, LAG), z)[1], 0)
    tail(early, late, scatter, source_sum, grad_one, w1, grad_nodes, None)


def final_call(n, C, args):
    rows, D = args[2].shape
    early, late = early_rows(D, C), 3 * D + C
    shape = jax.ShapeDtypeStruct
    return pl.pallas_call(
        functools.partial(final_kernel, n, C),
        in_specs=[WHOLE] * len(args),
        out_specs=[WHOLE] * 4,
        out_shape=[
            shape((rows, D), F32),
            shape((early, D), BF),
            shape((late, D), BF),
            shape((8, D), F32),
        ],
        scratch_shapes=[
            pltpu.VMEM((early, D), BF),
            pltpu.VMEM((late, D), BF),
            pltpu.VMEM((8, D), F32),
            pltpu.VMEM((n, 8, D), F32),
            *sems(n),
            *comm_scratch(n, rows, D),
            *sems(n),
            *line_scratch(early, D, EARLY),
            *line_scratch(late, D, LATE),
        ],
        compiler_params=remote_params(4),
    )(*args)


def feed_kernel(low, resid, wf1, wf2, dwf1, dwf2):
    @pl.when(pl.program_id(1) == 0)
    def _():
        dwf1[...] = jnp.zeros_like(dwf1)
        dwf2[...] = jnp.zeros_like(dwf2)

    act, slope = gelu_full(dot(low[...], wf1[...]))
    dwf2[...] += dot_tn(act, resid[...])
    inner = (dot_nt(resid[...], wf2[...]) * slope.astype(F32)).astype(BF)
    dwf1[...] += dot_tn(low[...], inner)


def feed_call(low, resid, wf1, wf2):
    count = low.shape[0]
    D, FF = wf1.shape
    step, rows = min(FF, 512), min(count, TABLE)
    shape = jax.ShapeDtypeStruct
    return pl.pallas_call(
        feed_kernel,
        grid=(FF // step, count // rows),
        in_specs=[
            pl.BlockSpec((rows, D), lambda f, r: (r, 0)),
            pl.BlockSpec((rows, D), lambda f, r: (r, 0)),
            pl.BlockSpec((D, step), lambda f, r: (0, f)),
            pl.BlockSpec((step, D), lambda f, r: (f, 0)),
        ],
        out_specs=[
            pl.BlockSpec((D, step), lambda f, r: (0, f)),
            pl.BlockSpec((step, D), lambda f, r: (f, 0)),
        ],
        out_shape=[shape((D, FF), F32), shape((FF, D), F32)],
        compiler_params=LOCAL,
    )(low, resid, wf1, wf2)


def unpack_kernel(C, steps, late, packed, small, node_in, grad_in, edges, *refs):
    g = pl.program_id(0)
    D = late.shape[1]
    plain = refs[: (len(refs) - 15) // 2]
    w1, w2, w3, grad_edges, one, two, three, node_out, grad_nodes, *outs = refs[len(plain) :]
    gains = outs[len(plain) :]
    grad_edges[...] = edges[...].astype(F32)
    first = 2 * D + C
    for ref, src, base in ((w1, late, 0), (w2, late, first), (w3, packed, 0)):
        step = ref.shape[0]
        ref[...] = src[pl.ds(pl.multiple_of(base + g * step, 16), step), :].astype(F32)
    at = D
    for a, b in zip(plain, outs):
        b[...] = a[...].astype(F32)

    @pl.when(g == steps - 1)
    def _():
        half = (2 * D + C) // 2
        for r in range(2):
            left = 256 * r
            flipped = jnp.transpose(packed[at : at + half, left : left + 256].astype(F32))
            one[:, half * r : half * r + half] = flipped[:C, :]
        end = at + half
        two[...] = packed[end : end + C, :C].astype(F32)
        three[...] = packed[end : end + C, 256 : 256 + C].astype(F32)
        node_out[...] = node_in[...]
        grad_nodes[...] = grad_in[...]
        for r in range(6):
            width = D if r < 4 else C
            gains[r][...] = small[r : r + 1, :width]


def unpack_call(C, late, packed, small, node_out, grad_nodes, edges, arrays):
    steps = 2
    D = packed.shape[1]
    first = 2 * D + C
    shape = jax.ShapeDtypeStruct
    cut = lambda r, c: pl.BlockSpec((r // steps, c), lambda g: (g, 0))
    head = [(first, D), (D, D), (D, D), edges.shape]
    last = [(C, first), (C, C), (C, C)]
    plain = [v.shape for v in arrays]
    gains = [(1, D)] * 4 + [(1, C)] * 2
    return pl.pallas_call(
        functools.partial(unpack_kernel, C, steps),
        grid=(steps,),
        in_specs=[full(v) for v in (late, packed, small, node_out, grad_nodes)] + [cut(*v.shape) for v in (edges, *arrays)],
        out_specs=[cut(*v) for v in head]
        + [fixed(*v) for v in last]
        + [fixed(*node_out.shape)] * 2
        + [cut(*v) for v in plain]
        + [fixed(*v) for v in gains],
        out_shape=[shape(v, F32) for v in head + last]
        + [shape(node_out.shape, BF), shape(node_out.shape, F32)]
        + [shape(v, F32) for v in plain + gains],
        compiler_params=LOCAL,
    )(late, packed, small, node_out, grad_nodes, edges, *arrays)


def body(
    nodes, edges, nbr_owner, nbr_slot, edge_mask, w_msg1, w_msg2, w_msg3, gain_one, offset_one,
    w_ffn1, w_ffn2, gain_two, offset_two, w_edge1, w_edge2, w_edge3, gain_three, offset_three,
    node_cotangent, edge_cotangent,
):
    n = lax.axis_size("edge")
    rows, D = nodes.shape
    C = w_edge2.shape[0]
    we1 = w_edge1.T
    g1, o1, g2, o2 = (v.reshape(1, D) for v in (gain_one, offset_one, gain_two, offset_two))
    (
        act1, slope1, slope2, tcol, trow, node_out, near, low, n1, n2, inv, slope, own_sum,
        nodes_all, far_all,
    ) = forward_call(
        n, C, nodes, nbr_owner.transpose(1, 2, 0), nbr_slot.T, edge_mask.T, g1, o1, g2, o2,
        [w_msg1, w_msg2, w_msg3, w_ffn1, w_ffn2, we1], edges,
    )
    edge_out, partial, far_sum, near_sum, dwe1, dwe2, dwe3, dg3 = edge_call(
        C, tcol, trow, far_all, near, we1, w_edge2, w_edge3,
        gain_three.reshape(1, C), offset_three.reshape(1, C), edges, edge_cotangent,
    )
    kept = [act1, slope1, slope2, edges, partial]
    if n * rows <= TABLE:
        grad_edges, grad_nodes, small, *dwf, early, late = back_call(
            n, C, [tcol, trow, nodes, near_sum, g1, g2, dwe1, dwe2, dwe3, dg3],
            [
                far_sum, low, node_cotangent, we1, n2, inv, w_ffn2, slope, w_ffn1, n1, w_msg3, w_msg1,
                w_msg2, own_sum, node_out, nodes_all,
            ],
            *kept,
        )
    else:
        grad_one, vw_all, resid, dgain, dw3, dwe_near, dwe_far = node_back_call(
            n, C, far_sum, near_sum, node_cotangent, node_out, n1, n2, inv, slope, own_sum,
            w_msg3, g1, w_ffn1, w_ffn2, g2, we1,
        )
        sums = [dw3, dwe_near, dwe_far, dwe1, dwe2, dwe3, dgain, dg3]
        grad_edges, dw1, dw2, target_sum, source_sum = message_back_call(
            C, tcol, trow, nodes_all, nodes, vw_all, w_msg1, w_msg2, *kept
        )
        grad_nodes, early, late, small = final_call(
            n, C, [target_sum, source_sum, grad_one, w_msg1, dw1, dw2, *sums]
        )
        low, resid = (lax.all_gather(v, "edge", axis=0, tiled=True) for v in (low, resid))
        tot_dwf = feed_call(low, resid, w_ffn1, w_ffn2)
        dwf = []
    (
        tot1, tot2, tot3, grad_edges, we1_t, tot_e2, tot_e3, node_out, grad_nodes, *rest
    ) = unpack_call(C, late, early, small, node_out, grad_nodes, grad_edges, dwf)
    dwf1, dwf2 = rest[:2] if dwf else tot_dwf
    gains = rest[-6:]
    gains = [v.reshape(v.shape[1]) for v in gains]
    return (
        node_out, edge_out, grad_nodes, grad_edges,
        tot1, tot2, tot3, gains[0], gains[1], dwf1, dwf2, gains[2], gains[3],
        we1_t.T, tot_e2, tot_e3, gains[4], gains[5],
    )


def solution(mesh):
    rows = P(("dp", "edge"), None)
    return jax.shard_map(
        body,
        mesh=mesh,
        in_specs=(rows, rows, P(("dp", "edge"), None, None), rows, rows)
        + (P(),) * 14
        + (rows, rows),
        out_specs=(rows,) * 4
        + (P("dp", None),) * 3
        + (P("dp"),) * 2
        + (P("dp", None),) * 2
        + (P("dp"),) * 2
        + (P("dp", None),) * 3
        + (P("dp"),) * 2,
        check_vma=False,
    )
```
